32 devices in a mesh: sa: 4 (over z), sb: 4 (over y, x), noise: 2 (over core).
Axes of the slice: x: 2, y: 2, z: 4, core: 2. Of those that a mesh axis runs over, the one named last changes fastest.
Arguments:
- base: bfloat16 [512, 1536], P(('sa', 'sb')), may hold values from -6 to 6
- noise: bfloat16 [4, 512, 1536], P('noise', ('sa', 'sb')), may hold values from -3 to 3
- cot: bfloat16 [512, 1536], P(('sa', 'sb')), may hold values from -6 to 6
- convolution_weight: bfloat16 [3, 1536, 384], P(None, 'sa'), may hold values from -0.15625 to 0.15625
- mix_w: bfloat16 [384, 1536], P('sa'), may hold values from -0.625 to 0.625
- norm_gain: float32 [1536], replicated, may hold values from 0.1 to 1.9
- qkv_w: bfloat16 [1536, 896], P('sa'), may hold values from -1 to 1
- out_w: bfloat16 [384, 1536], P('sa'), may hold values from -1.25 to 1.25
- band_width: int32 [4], replicated, may hold values from 1 to 32, as said below
- pairs: int32 [16, 2], replicated, may hold values from 0 to 3, as said below
Outputs:
- saliency: float32 [512, 1536], P(('sa', 'sb'))
The draws below stay inside these ranges and needn't reach their ends.
Inputs may be any that keep to these rules, and one draw needn't show every extreme that they name: `band_width`: one head has band half-width exactly 32. Tile t holds bins t * 128 to (t + 1) * 128 - 1; both tiles of a pair lie in the same stretch of 128 bins that starts at a multiple of 128; pairs may repeat.
All inputs are finite; a program needn't handle non-finite values.
Results may differ from the reference program's by a relative error of at most 0.018.
Values may be sent and summed in bfloat16 or wider, within the bound.
No kernel may reach another device: no remote copies, remote signals or barrier semaphores. Data moves between devices by JAX's collectives and lax.ppermute only.
A program may use at most 64 MiB of HBM per device.

```python
import jax
import jax.numpy as jnp
from jax import lax

D = 1536
HID = 384
HEADS = 4
KEY = 64
VAL = 96
DILATION_BINS = 16
BAND = 32
TILE = 128
PAIRS_STR = 4
BINS_DEV = 32
QKV = 896
STRETCH = 128
LENGTH = 512
SAMPLES = 4
TILES = 4
NPAIRS = 16
N_SA = 4
N_SB = 4


def draw_qkv_w(key, part):
    values = jax.random.normal(key, (D, QKV), jnp.float32) * D ** (-0.5)
    return jnp.clip(values, -1.0, 1.0).astype(jnp.bfloat16)


def draw_band_width(key, part):
    first, second = jax.random.split(jax.random.fold_in(key, 17))
    widths = jax.random.randint(first, (HEADS,), 1, BAND + 1, dtype=jnp.int32)
    chosen = jax.random.randint(second, (), 0, HEADS, dtype=jnp.int32)
    return jnp.where(jnp.arange(HEADS, dtype=jnp.int32) == chosen, BAND, widths).astype(jnp.int32)


def draw_pairs(key, part):
    per_stretch = STRETCH // TILE
    subkeys = jax.random.split(key, 3)
    stretch_id = jnp.repeat(jnp.arange(N_SA, dtype=jnp.int32), PAIRS_STR)
    first_pick = jax.random.randint(subkeys[0], (NPAIRS,), 0, per_stretch, dtype=jnp.int32)
    second_pick = jax.random.randint(subkeys[1], (NPAIRS,), 0, per_stretch, dtype=jnp.int32)
    query_tile = stretch_id * per_stretch + first_pick * second_pick // per_stretch
    key_tile = stretch_id * per_stretch + jax.random.randint(subkeys[2], (NPAIRS,), 0, per_stretch, dtype=jnp.int32)
    return jnp.stack([query_tile, key_tile], axis=1).astype(jnp.int32)


def level_of(own_key, dims, cuts, least, largest):
    loudness = 1.0
    for position, shards_of in cuts:
        steps = jax.random.uniform(jax.random.fold_in(jax.random.fold_in(own_key, 6), position), (shards_of,), jnp.float32, least / len(cuts), largest / len(cuts))
        loudness = loudness * jnp.repeat(jnp.exp(steps), dims[position] // shards_of).reshape((-1,) + (1,) * (len(dims) - 1 - position))
    return loudness


def scatter_about(own_key, extent, spread, most, cuts=(), kind=jnp.bfloat16):
    loudness = level_of(own_key, extent, cuts, -0.22, 0.18) if cuts else 1.0
    array = jax.random.normal(own_key, extent, jnp.float32) * spread * loudness
    return jnp.minimum(jnp.maximum(array, -most), most).astype(kind)


def setup_inputs(seed: int = 0) -> dict:
    keys = jax.random.split(jax.random.key(seed), 11)
    base = scatter_about(keys[0], (LENGTH, D), 1.0, 6.0, ((0, 16),))
    noise = scatter_about(keys[1], (SAMPLES, LENGTH, D), 0.5, 3.0, ((0, 2), (1, 16)))
    cot = scatter_about(keys[2], (LENGTH, D), 1.0, 6.0, ((0, 16),))
    convolution_weight = scatter_about(keys[3], (3, D, HID), D ** -0.5, 0.15625, ((1, 4),))
    mix_w = scatter_about(keys[4], (HID, D), (HID // 4) ** -0.5, 0.625, ((0, 4),))
    norm_gain = jnp.clip(1.0 + 0.18 * jax.random.normal(keys[5], (D,), jnp.float32), 0.1, 1.9)
    qkv_w = draw_qkv_w(jax.random.fold_in(keys[10], 71), 0)
    out_w = scatter_about(keys[7], (HEADS * VAL, D), (HEADS * VAL // 16) ** -0.5, 1.25, ((0, 4),))
    band_width = draw_band_width(jax.random.fold_in(keys[10], 71), 0)
    pairs = draw_pairs(jax.random.fold_in(keys[10], 71), 0)
    return {"base": base, "noise": noise, "cot": cot, "convolution_weight": convolution_weight, "mix_w": mix_w, "norm_gain": norm_gain, "qkv_w": qkv_w, "out_w": out_w, "band_width": band_width, "pairs": pairs}


ROOT_TWO_PI = 0.7978845608
CUBIC = 0.044715

def gelu_tanh(values):
    inner = ROOT_TWO_PI * (values + CUBIC * values * values * values)
    return 0.5 * values * (1.0 + jnp.tanh(inner))

def gelu_slope(values):
    tangent = jnp.tanh(ROOT_TWO_PI * (values + CUBIC * values * values * values))
    return 0.5 * (1.0 + tangent) + 0.5 * values * (1.0 - tangent * tangent) * ROOT_TWO_PI * (1.0 + 3.0 * CUBIC * values * values)

def rounded(values):
    return lax.optimization_barrier(values.astype(jnp.bfloat16)).astype(jnp.float32)

def reference(base, noise, cot, convolution_weight, mix_w, norm_gain, qkv_w, out_w, band_width, pairs):
    sequence_length = base.shape[0]
    heads_key = HEADS * KEY
    heads_val = HEADS * VAL
    scale = KEY ** (-0.5)
    tile_ids = jnp.arange(TILES, dtype=jnp.int32)
    pick_query = (pairs[:, 0][:, None] == tile_ids[None, :]).astype(jnp.float32)
    pick_key = (pairs[:, 1][:, None] == tile_ids[None, :]).astype(jnp.float32)
    table = jnp.dot(pick_query.T, pick_key) > 0.5
    d_att = jnp.dot(cot, out_w.T, preferred_element_type=jnp.float32).astype(jnp.bfloat16)
    d_att_heads = d_att.reshape(sequence_length, HEADS, VAL)
    width = STRETCH + 2 * BAND
    blocks = sequence_length // BINS_DEV

    def one_sample(noise_row):
        noisy = base.astype(jnp.float32) + noise_row.astype(jnp.float32)
        gelu_input = gelu_tanh(noisy).astype(jnp.bfloat16)
        padded_input = jnp.pad(gelu_input, ((DILATION_BINS, DILATION_BINS), (0, 0)))
        hidden_state = jnp.zeros((sequence_length, HID), jnp.float32)
        for tap_index in range(3):
            hidden_state = hidden_state + jnp.dot(padded_input[tap_index * DILATION_BINS:tap_index * DILATION_BINS + sequence_length], convolution_weight[tap_index], preferred_element_type=jnp.float32)
        act = gelu_tanh(hidden_state).astype(jnp.bfloat16)
        resid = noisy + jnp.dot(act, mix_w, preferred_element_type=jnp.float32)
        inv_rms = lax.rsqrt(lax.optimization_barrier(jnp.mean(resid * resid, axis=-1, keepdims=True)) + 1e-06)
        normed = (resid * inv_rms * norm_gain).astype(jnp.bfloat16)
        proj = jnp.dot(normed, qkv_w, preferred_element_type=jnp.float32).astype(jnp.bfloat16)
        queries = proj[:, :heads_key].reshape(sequence_length, HEADS, KEY)
        key_vals = jnp.pad(proj[:, heads_key:], ((BAND, BAND), (0, 0)))

        def step(carry, block):
            row_first = block * BINS_DEV
            stretch_id = block // N_SB
            col_first = stretch_id * STRETCH
            query_blk = lax.dynamic_slice(queries, (row_first, jnp.int32(0), jnp.int32(0)), (BINS_DEV, HEADS, KEY)).astype(jnp.float32)
            window = lax.dynamic_slice(key_vals, (col_first, jnp.int32(0)), (width, heads_key + heads_val))
            key_blk = window[:, :heads_key].reshape(width, HEADS, KEY).astype(jnp.float32)
            val_blk = window[:, heads_key:].reshape(width, HEADS, VAL).astype(jnp.float32)
            rows = row_first + jnp.arange(BINS_DEV, dtype=jnp.int32)
            cols = col_first - BAND + jnp.arange(width, dtype=jnp.int32)
            inside = (cols >= 0) & (cols < sequence_length)
            apart = jnp.abs(rows[:, None] - cols[None, :])
            in_band = apart[None] <= band_width[:, None, None]
            same = (cols >= col_first) & (cols < col_first + STRETCH)
            query_tile = rows // TILE
            key_tile = jnp.clip(cols, 0, sequence_length - 1) // TILE
            paired = table[query_tile][:, key_tile] & same[None, :]
            allowed = inside[None, None, :] & (in_band | paired[None])
            score = jnp.einsum('ihd,jhd->hij', query_blk, key_blk) * scale
            score = jnp.where(allowed, score, -1e+30)
            top = lax.optimization_barrier(jnp.max(score, axis=-1))
            total = lax.optimization_barrier(jnp.sum(jnp.where(allowed, jnp.exp(score - top[..., None]), 0.0), axis=-1))
            lse = top + jnp.log(total)
            prob = jnp.where(allowed, jnp.exp(score - lse[..., None]), 0.0)
            prob_b = rounded(prob)
            attn = jnp.einsum('hij,jhe->ihe', prob_b, val_blk)
            grad_blk = lax.dynamic_slice(d_att_heads, (row_first, jnp.int32(0), jnp.int32(0)), (BINS_DEV, HEADS, VAL)).astype(jnp.float32)
            delta = lax.optimization_barrier(jnp.sum(grad_blk * attn, axis=-1))
            d_prob = jnp.einsum('ihe,jhe->hij', grad_blk, val_blk)
            d_score = rounded(prob * (d_prob - delta.T[..., None]) * scale)
            d_query = jnp.einsum('hij,jhd->ihd', d_score, key_blk)
            d_key = jnp.einsum('hij,ihd->jhd', d_score, query_blk)
            d_value = jnp.einsum('hij,ihe->jhe', prob_b, grad_blk)
            d_window = jnp.concatenate([d_key.reshape(width, heads_key), d_value.reshape(width, heads_val)], axis=1)
            current = lax.dynamic_slice(carry, (col_first, jnp.int32(0)), (width, heads_key + heads_val))
            carry = lax.dynamic_update_slice(carry, current + d_window, (col_first, jnp.int32(0)))
            return (carry, d_query.reshape(BINS_DEV, heads_key))
        start = jnp.zeros((sequence_length + 2 * BAND, heads_key + heads_val), jnp.float32)
        d_kv_pad, d_query = lax.scan(step, start, jnp.arange(blocks, dtype=jnp.int32))
        d_query = d_query.reshape(sequence_length, heads_key)
        d_proj = jnp.concatenate([d_query, d_kv_pad[BAND:BAND + sequence_length]], axis=1).astype(jnp.bfloat16)
        d_normed = jnp.dot(d_proj, qkv_w.T, preferred_element_type=jnp.float32)
        gained = norm_gain * d_normed
        d_resid = cot.astype(jnp.float32) + inv_rms * gained - resid * inv_rms * inv_rms * inv_rms * lax.optimization_barrier(jnp.mean(resid * gained, axis=-1, keepdims=True))
        d_act = jnp.dot(d_resid.astype(jnp.bfloat16), mix_w.T, preferred_element_type=jnp.float32)
        hidden_gradient = (d_act * gelu_slope(hidden_state)).astype(jnp.bfloat16)
        gradient_padded = jnp.pad(hidden_gradient, ((DILATION_BINS, DILATION_BINS), (0, 0)))
        d_gelu_in = jnp.zeros((sequence_length, D), jnp.float32)
        for tap_index in range(3):
            start_offset = (2 - tap_index) * DILATION_BINS
            d_gelu_in = d_gelu_in + jnp.dot(gradient_padded[start_offset:start_offset + sequence_length], convolution_weight[tap_index].T, preferred_element_type=jnp.float32)
        return d_resid + d_gelu_in * gelu_slope(noisy)
    summed = jnp.zeros((sequence_length, D), jnp.float32)
    for sample in range(SAMPLES):
        summed = summed + one_sample(noise[sample])
    return summed / SAMPLES
```

```python
import jax
import jax.numpy as jnp
from jax import lax
from jax.sharding import PartitionSpec as P

HID = 384
HEADS = 4
KEY = 64
VAL = 96
DILATION_BINS = 16
BAND = 32
TILE = 128


ROOT_TWO_PI = 0.7978845608
CUBIC = 0.044715


def extended(value, sides, width):
    for axis, dim in sides:
        peers, length = (lax.axis_size(axis), value.shape[dim])
        up = [(i, (i + 1) % peers) for i in range(peers - 1)]
        down = [(j, i) for i, j in up]
        last = lax.slice_in_dim(value, length - width, length, axis=dim)
        leading = lax.slice_in_dim(value, 0, width, axis=dim)
        before = lax.ppermute(last, axis, up)
        after = lax.ppermute(leading, axis, down)
        value = jnp.concatenate([before, value, after], axis=dim)
    return value


def from_behind(block, axis, distance):
    devices = range(lax.axis_size(axis))
    route = [(i - distance, i) for i in devices if i - distance in devices]
    return lax.ppermute(block, axis, route)


def gelu_tanh(values):
    inner = ROOT_TWO_PI * (values + CUBIC * values * values * values)
    return 0.5 * values * (1.0 + jnp.tanh(inner))


def gelu_slope(values):
    tangent = jnp.tanh(ROOT_TWO_PI * (values + CUBIC * values * values * values))
    return 0.5 * (1.0 + tangent) + 0.5 * values * (1.0 - tangent * tangent) * ROOT_TWO_PI * (
        1.0 + 3.0 * CUBIC * values * values
    )


def gathered_weights(convolution_weight, mix_w, qkv_w, out_w):
    n_sa, n_sb, n_noise = (lax.axis_size("sa"), lax.axis_size("sb"), lax.axis_size("noise"))
    parts = n_sb * n_noise
    part = lax.axis_index("sb") * n_noise + lax.axis_index("noise")
    arrays = (convolution_weight, mix_w, qkv_w, out_w)
    flat = [a.reshape(parts, -1) for a in arrays]
    sizes = [f.shape[1] for f in flat]
    mine = jnp.concatenate(
        [lax.dynamic_index_in_dim(f, part, 0, keepdims=False).reshape(-1, 128) for f in flat], axis=0
    )
    everything = lax.all_gather(mine, ("sa", "sb", "noise"), axis=0, tiled=False)
    everything = everything.reshape(n_sa, parts, -1, 128)
    full, first = [], 0
    for a, size in zip(arrays, sizes):
        rows = size // 128
        full.append(everything[:, :, first : first + rows].reshape((n_sa,) + a.shape))
        first += rows
    conv, mix, qkv, out = full
    conv = jnp.transpose(conv, (1, 0, 2, 3)).reshape(conv.shape[1], -1, conv.shape[3])
    return conv, mix.reshape(-1, mix.shape[2]), qkv.reshape(-1, qkv.shape[2]), out.reshape(-1, out.shape[2])


def shards(base, noise, cot, convolution_weight, mix_w, norm_gain, qkv_w, out_w, band_width, pairs):
    conv_full, mix_full, qkv_full, out_full = gathered_weights(convolution_weight, mix_w, qkv_w, out_w)
    sequence_bins = base.shape[0]
    samples_dev = noise.shape[0]
    stretch = sequence_bins * lax.axis_size("sb")
    sequence_length = stretch * lax.axis_size("sa")
    heads_key = HEADS * KEY
    heads_val = HEADS * VAL
    width = sequence_bins + 2 * BAND
    scale = KEY ** (-0.5)
    stretch_first = lax.axis_index("sa") * stretch
    first_row = stretch_first + lax.axis_index("sb") * sequence_bins
    row_pos = first_row + jnp.arange(sequence_bins, dtype=jnp.int32)
    ext_pos = first_row - BAND + jnp.arange(width, dtype=jnp.int32)
    stretch_pos = stretch_first + jnp.arange(stretch, dtype=jnp.int32)
    tiles = sequence_length // TILE
    tile_ids = jnp.arange(tiles, dtype=jnp.int32)
    pick_query = (pairs[:, 0][:, None] == tile_ids[None, :]).astype(jnp.float32)
    pick_key = (pairs[:, 1][:, None] == tile_ids[None, :]).astype(jnp.float32)
    table = jnp.dot(pick_query.T, pick_key)
    own_select = ((row_pos // TILE)[:, None] == tile_ids[None, :]).astype(jnp.float32)
    stretch_select = ((stretch_pos // TILE)[:, None] == tile_ids[None, :]).astype(jnp.float32)
    pair_own_rows = jnp.dot(jnp.dot(own_select, table), stretch_select.T) > 0.5
    pair_own_keys = jnp.dot(jnp.dot(stretch_select, table), own_select.T) > 0.5
    inside = (ext_pos >= 0) & (ext_pos < sequence_length)
    band_mask = inside[None, None, :] & (
        jnp.abs(row_pos[:, None] - ext_pos[None, :])[None] <= band_width[:, None, None]
    )
    far_rows = jnp.abs(row_pos[:, None] - stretch_pos[None, :])[None] > band_width[:, None, None]
    pair_mask = pair_own_rows[None] & far_rows
    key_mask = pair_own_keys[None] & jnp.transpose(far_rows, (0, 2, 1))
    noisy = base.astype(jnp.float32)[None] + noise.astype(jnp.float32)
    gelu_input = gelu_tanh(noisy).astype(jnp.bfloat16)
    gelu_extended = extended(gelu_input, ((("sa", "sb"), 1),), DILATION_BINS)
    hidden_state = jnp.zeros((samples_dev, sequence_bins, HID), jnp.float32)
    for tap_index in range(3):
        hidden_state = hidden_state + jnp.einsum(
            "nbd,dc->nbc",
            gelu_extended[:, tap_index * DILATION_BINS : tap_index * DILATION_BINS + sequence_bins],
            conv_full[tap_index],
            preferred_element_type=jnp.float32,
        )
    act = gelu_tanh(hidden_state).astype(jnp.bfloat16)
    resid = noisy + jnp.einsum("nbc,cd->nbd", act, mix_full, preferred_element_type=jnp.float32)
    inv_rms = lax.rsqrt(jnp.mean(resid * resid, axis=-1, keepdims=True) + 1e-06)
    normed = (resid * inv_rms * norm_gain).astype(jnp.bfloat16)
    proj = jnp.einsum("nbd,dc->nbc", normed, qkv_full, preferred_element_type=jnp.float32).astype(
        jnp.bfloat16
    )
    queries = proj[..., :heads_key].reshape(samples_dev, sequence_bins, HEADS, KEY)
    key_vals = proj[..., heads_key:]
    kv_ext = extended(key_vals, ((("sa", "sb"), 1),), BAND)
    kv_all = lax.all_gather(key_vals, "sb", axis=1, tiled=True)
    keys_ext = kv_ext[..., :heads_key].reshape(samples_dev, width, HEADS, KEY)
    vals_ext = kv_ext[..., heads_key:].reshape(samples_dev, width, HEADS, VAL)
    keys_all = kv_all[..., :heads_key].reshape(samples_dev, stretch, HEADS, KEY)
    vals_all = kv_all[..., heads_key:].reshape(samples_dev, stretch, HEADS, VAL)
    score_band = (
        jnp.einsum("nihd,njhd->nhij", queries, keys_ext, preferred_element_type=jnp.float32) * scale
    )
    score_band = jnp.where(band_mask[None], score_band, -1e30)
    raw_pair = jnp.einsum("nihd,njhd->nhij", queries, keys_all, preferred_element_type=jnp.float32)
    score_pair = jnp.where(pair_mask[None], raw_pair * scale, -1e30)
    top = jnp.maximum(jnp.max(score_band, axis=-1), jnp.max(score_pair, axis=-1))
    total = jnp.sum(jnp.where(band_mask[None], jnp.exp(score_band - top[..., None]), 0.0), axis=-1)
    total = total + jnp.sum(
        jnp.where(pair_mask[None], jnp.exp(score_pair - top[..., None]), 0.0), axis=-1
    )
    lse = top + jnp.log(total)
    prob_band = jnp.where(band_mask[None], jnp.exp(score_band - lse[..., None]), 0.0)
    prob_pair = jnp.where(pair_mask[None], jnp.exp(score_pair - lse[..., None]), 0.0)
    band_b = prob_band.astype(jnp.bfloat16)
    pair_b = prob_pair.astype(jnp.bfloat16)
    attn = jnp.einsum("nhij,njhe->nihe", band_b, vals_ext, preferred_element_type=jnp.float32)
    attn = attn + jnp.einsum(
        "nhij,njhe->nihe", pair_b, vals_all, preferred_element_type=jnp.float32
    )
    d_att = jnp.dot(cot, out_full.T, preferred_element_type=jnp.float32).astype(jnp.bfloat16)
    d_att_heads = d_att.reshape(sequence_bins, HEADS, VAL)
    delta = jnp.transpose(jnp.sum(d_att_heads.astype(jnp.float32)[None] * attn, axis=-1), (0, 2, 1))
    d_prob_band = jnp.einsum(
        "ihe,njhe->nhij", d_att_heads, vals_ext, preferred_element_type=jnp.float32
    )
    d_prob_pair = jnp.einsum(
        "ihe,njhe->nhij", d_att_heads, vals_all, preferred_element_type=jnp.float32
    )
    d_score_band = (prob_band * (d_prob_band - delta[..., None]) * scale).astype(jnp.bfloat16)
    d_score_pair = (prob_pair * (d_prob_pair - delta[..., None]) * scale).astype(jnp.bfloat16)
    d_query = jnp.einsum(
        "nhij,njhd->nihd", d_score_band, keys_ext, preferred_element_type=jnp.float32
    )
    d_query = d_query + jnp.einsum(
        "nhij,njhd->nihd", d_score_pair, keys_all, preferred_element_type=jnp.float32
    )
    d_key_ext = jnp.einsum(
        "nhij,nihd->njhd", d_score_band, queries, preferred_element_type=jnp.float32
    )
    d_val_ext = jnp.einsum(
        "nhij,ihe->njhe", band_b, d_att_heads, preferred_element_type=jnp.float32
    )
    d_kv_ext = jnp.concatenate(
        [
            d_key_ext.reshape(samples_dev, width, heads_key),
            d_val_ext.reshape(samples_dev, width, heads_val),
        ],
        axis=2,
    )
    from_right = from_behind(d_kv_ext[:, :BAND].astype(jnp.bfloat16), ("sa", "sb"), -1).astype(
        jnp.float32
    )
    from_left = from_behind(
        d_kv_ext[:, BAND + sequence_bins :].astype(jnp.bfloat16), ("sa", "sb"), 1
    ).astype(jnp.float32)
    d_key_vals = d_kv_ext[:, BAND : BAND + sequence_bins]
    d_key_vals = d_key_vals + from_left
    d_key_vals = d_key_vals + from_right
    statistics = jnp.stack([lse, delta], axis=1)
    query_rows = proj[..., :heads_key]
    queries_all, d_att_all = (
        lax.all_gather(query_rows, "sb", axis=1, tiled=True),
        lax.all_gather(d_att, "sb", axis=0, tiled=True),
    )
    stats_all = lax.all_gather(statistics, "sb", axis=3, tiled=True)
    queries_all = queries_all.reshape(samples_dev, stretch, HEADS, KEY)
    d_att_all = d_att_all.reshape(stretch, HEADS, VAL)
    keys_own = key_vals[..., :heads_key].reshape(samples_dev, sequence_bins, HEADS, KEY)
    vals_own = key_vals[..., heads_key:].reshape(samples_dev, sequence_bins, HEADS, VAL)
    score_key = (
        jnp.einsum("nihd,njhd->nhij", queries_all, keys_own, preferred_element_type=jnp.float32)
        * scale
    )
    prob_key = jnp.where(key_mask[None], jnp.exp(score_key - stats_all[:, 0][..., None]), 0.0)
    d_val_pair = jnp.einsum(
        "nhij,ihe->njhe",
        prob_key.astype(jnp.bfloat16),
        d_att_all,
        preferred_element_type=jnp.float32,
    )
    d_prob_key = jnp.einsum(
        "ihe,njhe->nhij", d_att_all, vals_own, preferred_element_type=jnp.float32
    )
    d_score_key = (prob_key * (d_prob_key - stats_all[:, 1][..., None]) * scale).astype(
        jnp.bfloat16
    )
    d_key_pair = jnp.einsum(
        "nhij,nihd->njhd", d_score_key, queries_all, preferred_element_type=jnp.float32
    )
    d_key_vals = d_key_vals + jnp.concatenate(
        [
            d_key_pair.reshape(samples_dev, sequence_bins, heads_key),
            d_val_pair.reshape(samples_dev, sequence_bins, heads_val),
        ],
        axis=2,
    )
    d_proj = jnp.concatenate(
        [d_query.reshape(samples_dev, sequence_bins, heads_key), d_key_vals], axis=2
    ).astype(jnp.bfloat16)
    d_normed = jnp.einsum("nbc,dc->nbd", d_proj, qkv_full, preferred_element_type=jnp.float32)
    gained = norm_gain * d_normed
    d_resid = (
        cot.astype(jnp.float32)[None]
        + inv_rms * gained
        - resid * inv_rms * inv_rms * inv_rms * jnp.mean(resid * gained, axis=-1, keepdims=True)
    )
    d_act = jnp.einsum(
        "nbd,cd->nbc", d_resid.astype(jnp.bfloat16), mix_full, preferred_element_type=jnp.float32
    )
    hidden_gradient = (d_act * gelu_slope(hidden_state)).astype(jnp.bfloat16)
    gradient_extended = extended(hidden_gradient, ((("sa", "sb"), 1),), DILATION_BINS)
    d_gelu_in = jnp.zeros((samples_dev, sequence_bins, base.shape[1]), jnp.float32)
    for tap_index in range(3):
        start_offset = (2 - tap_index) * DILATION_BINS
        d_gelu_in = d_gelu_in + jnp.einsum(
            "nbc,dc->nbd",
            gradient_extended[:, start_offset : start_offset + sequence_bins],
            conv_full[tap_index],
            preferred_element_type=jnp.float32,
        )
    grads = d_resid + d_gelu_in * gelu_slope(noisy)
    own = jnp.sum(grads, axis=0)
    n_noise = lax.axis_size("noise")
    passing = own.astype(jnp.bfloat16)
    summed = passing.astype(jnp.float32)
    for _ in range(n_noise - 1):
        passing = lax.ppermute(passing, "noise", [(i, (i + 1) % n_noise) for i in range(n_noise)])
        summed = summed + passing.astype(jnp.float32)
    return summed / (samples_dev * lax.axis_size("noise"))


def solution(mesh):
    return jax.shard_map(
        shards,
        mesh=mesh,
        in_specs=(
            P(("sa", "sb"), None),
            P("noise", ("sa", "sb"), None),
            P(("sa", "sb"), None),
            P(None, "sa", None),
            P("sa", None),
            P(),
            P("sa", None),
            P("sa", None),
            P(),
            P(),
        ),
        out_specs=P(("sa", "sb"), None),
        check_vma=False,
    )
```

```python
import jax
import jax.numpy as jnp
from jax import lax
from jax.experimental import pallas as pl
from jax.experimental.pallas import tpu as pltpu
from jax.sharding import PartitionSpec as P

HID = 384
HEADS = 4
KEY = 64
VAL = 96
DILATION_BINS = 16
BAND = 32
TILE = 128


ROOT_TWO_PI = 0.7978845608
CUBIC = 0.044715


def extended(value, sides, width):
    for axis, dim in sides:
        peers, length = (lax.axis_size(axis), value.shape[dim])
        up = [(i, (i + 1) % peers) for i in range(peers - 1)]
        down = [(j, i) for i, j in up]
        last = lax.slice_in_dim(value, length - width, length, axis=dim)
        leading = lax.slice_in_dim(value, 0, width, axis=dim)
        before = lax.ppermute(last, axis, up)
        after = lax.ppermute(leading, axis, down)
        value = jnp.concatenate([before, value, after], axis=dim)
    return value


def from_behind(block, axis, distance):
    devices = range(lax.axis_size(axis))
    route = [(i - distance, i) for i in devices if i - distance in devices]
    return lax.ppermute(block, axis, route)


def gelu_tanh(values):
    inner = ROOT_TWO_PI * (values + CUBIC * values * values * values)
    return 0.5 * values * (1.0 + jnp.tanh(inner))


def gelu_slope(values):
    tangent = jnp.tanh(ROOT_TWO_PI * (values + CUBIC * values * values * values))
    return 0.5 * (1.0 + tangent) + 0.5 * values * (1.0 - tangent * tangent) * ROOT_TWO_PI * (
        1.0 + 3.0 * CUBIC * values * values
    )


def shards(base, noise, cot, convolution_weight, mix_w, norm_gain, qkv_w, out_w, band_width, pairs):
    conv_full, mix_full, qkv_full, out_full = (
        lax.all_gather(convolution_weight, "sa", axis=1, tiled=True),
        lax.all_gather(mix_w, "sa", axis=0, tiled=True),
        lax.all_gather(qkv_w, "sa", axis=0, tiled=True),
        lax.all_gather(out_w, "sa", axis=0, tiled=True),
    )
    sequence_bins = base.shape[0]
    samples_dev = noise.shape[0]
    stretch = sequence_bins * lax.axis_size("sb")
    sequence_length = stretch * lax.axis_size("sa")
    heads_key = HEADS * KEY
    heads_val = HEADS * VAL
    width = sequence_bins + 2 * BAND
    scale = KEY ** (-0.5)
    stretch_first = lax.axis_index("sa") * stretch
    first_row = stretch_first + lax.axis_index("sb") * sequence_bins
    row_pos = first_row + jnp.arange(sequence_bins, dtype=jnp.int32)
    ext_pos = first_row - BAND + jnp.arange(width, dtype=jnp.int32)
    stretch_pos = stretch_first + jnp.arange(stretch, dtype=jnp.int32)
    tiles = sequence_length // TILE
    tile_ids = jnp.arange(tiles, dtype=jnp.int32)
    pick_query = (pairs[:, 0][:, None] == tile_ids[None, :]).astype(jnp.float32)
    pick_key = (pairs[:, 1][:, None] == tile_ids[None, :]).astype(jnp.float32)
    table = jnp.dot(pick_query.T, pick_key)
    own_select = ((row_pos // TILE)[:, None] == tile_ids[None, :]).astype(jnp.float32)
    stretch_select = ((stretch_pos // TILE)[:, None] == tile_ids[None, :]).astype(jnp.float32)
    pair_own_rows = jnp.dot(jnp.dot(own_select, table), stretch_select.T) > 0.5
    pair_own_keys = jnp.dot(jnp.dot(stretch_select, table), own_select.T) > 0.5
    inside = (ext_pos >= 0) & (ext_pos < sequence_length)
    band_mask = inside[None, None, :] & (
        jnp.abs(row_pos[:, None] - ext_pos[None, :])[None] <= band_width[:, None, None]
    )
    far_rows = jnp.abs(row_pos[:, None] - stretch_pos[None, :])[None] > band_width[:, None, None]
    pair_mask = pair_own_rows[None] & far_rows
    key_mask = pair_own_keys[None] & jnp.transpose(far_rows, (0, 2, 1))
    noisy = base.astype(jnp.float32)[None] + noise.astype(jnp.float32)
    gelu_input = gelu_tanh(noisy).astype(jnp.bfloat16)
    gelu_extended = extended(gelu_input, ((("sa", "sb"), 1),), DILATION_BINS)
    hidden_state = jnp.zeros((samples_dev, sequence_bins, HID), jnp.float32)
    for tap_index in range(3):
        hidden_state = hidden_state + jnp.einsum(
            "nbd,dc->nbc",
            gelu_extended[:, tap_index * DILATION_BINS : tap_index * DILATION_BINS + sequence_bins],
            conv_full[tap_index],
            preferred_element_type=jnp.float32,
        )
    act = gelu_tanh(hidden_state).astype(jnp.bfloat16)
    resid = noisy + jnp.einsum("nbc,cd->nbd", act, mix_full, preferred_element_type=jnp.float32)
    inv_rms = lax.rsqrt(jnp.mean(resid * resid, axis=-1, keepdims=True) + 1e-06)
    normed = (resid * inv_rms * norm_gain).astype(jnp.bfloat16)
    proj = jnp.einsum("nbd,dc->nbc", normed, qkv_full, preferred_element_type=jnp.float32).astype(
        jnp.bfloat16
    )
    queries = proj[..., :heads_key].reshape(samples_dev, sequence_bins, HEADS, KEY)
    key_vals = proj[..., heads_key:]
    kv_ext = extended(key_vals, ((("sa", "sb"), 1),), BAND)
    kv_all = lax.all_gather(key_vals, "sb", axis=1, tiled=True)
    keys_ext = kv_ext[..., :heads_key].reshape(samples_dev, width, HEADS, KEY)
    vals_ext = kv_ext[..., heads_key:].reshape(samples_dev, width, HEADS, VAL)
    keys_all = kv_all[..., :heads_key].reshape(samples_dev, stretch, HEADS, KEY)
    vals_all = kv_all[..., heads_key:].reshape(samples_dev, stretch, HEADS, VAL)
    score_band = (
        jnp.einsum("nihd,njhd->nhij", queries, keys_ext, preferred_element_type=jnp.float32) * scale
    )
    score_band = jnp.where(band_mask[None], score_band, -1e30)
    raw_pair = jnp.einsum("nihd,njhd->nhij", queries, keys_all, preferred_element_type=jnp.float32)
    score_pair = jnp.where(pair_mask[None], raw_pair * scale, -1e30)
    top = jnp.maximum(jnp.max(score_band, axis=-1), jnp.max(score_pair, axis=-1))
    total = jnp.sum(jnp.where(band_mask[None], jnp.exp(score_band - top[..., None]), 0.0), axis=-1)
    total = total + jnp.sum(
        jnp.where(pair_mask[None], jnp.exp(score_pair - top[..., None]), 0.0), axis=-1
    )
    lse = top + jnp.log(total)
    prob_band = jnp.where(band_mask[None], jnp.exp(score_band - lse[..., None]), 0.0)
    prob_pair = jnp.where(pair_mask[None], jnp.exp(score_pair - lse[..., None]), 0.0)
    band_b = prob_band.astype(jnp.bfloat16)
    pair_b = prob_pair.astype(jnp.bfloat16)
    attn = jnp.einsum("nhij,njhe->nihe", band_b, vals_ext, preferred_element_type=jnp.float32)
    attn = attn + jnp.einsum(
        "nhij,njhe->nihe", pair_b, vals_all, preferred_element_type=jnp.float32
    )
    d_att = jnp.dot(cot, out_full.T, preferred_element_type=jnp.float32).astype(jnp.bfloat16)
    d_att_heads = d_att.reshape(sequence_bins, HEADS, VAL)
    delta = jnp.transpose(jnp.sum(d_att_heads.astype(jnp.float32)[None] * attn, axis=-1), (0, 2, 1))
    d_prob_band = jnp.einsum(
        "ihe,njhe->nhij", d_att_heads, vals_ext, preferred_element_type=jnp.float32
    )
    d_prob_pair = jnp.einsum(
        "ihe,njhe->nhij", d_att_heads, vals_all, preferred_element_type=jnp.float32
    )
    d_score_band = (prob_band * (d_prob_band - delta[..., None]) * scale).astype(jnp.bfloat16)
    d_score_pair = (prob_pair * (d_prob_pair - delta[..., None]) * scale).astype(jnp.bfloat16)
    d_query = jnp.einsum(
        "nhij,njhd->nihd", d_score_band, keys_ext, preferred_element_type=jnp.float32
    )
    d_query = d_query + jnp.einsum(
        "nhij,njhd->nihd", d_score_pair, keys_all, preferred_element_type=jnp.float32
    )
    d_key_ext = jnp.einsum(
        "nhij,nihd->njhd", d_score_band, queries, preferred_element_type=jnp.float32
    )
    d_val_ext = jnp.einsum(
        "nhij,ihe->njhe", band_b, d_att_heads, preferred_element_type=jnp.float32
    )
    d_kv_ext = jnp.concatenate(
        [
            d_key_ext.reshape(samples_dev, width, heads_key),
            d_val_ext.reshape(samples_dev, width, heads_val),
        ],
        axis=2,
    )
    from_right = from_behind(d_kv_ext[:, :BAND].astype(jnp.bfloat16), ("sa", "sb"), -1).astype(
        jnp.float32
    )
    from_left = from_behind(
        d_kv_ext[:, BAND + sequence_bins :].astype(jnp.bfloat16), ("sa", "sb"), 1
    ).astype(jnp.float32)
    d_key_vals = d_kv_ext[:, BAND : BAND + sequence_bins]
    d_key_vals = d_key_vals + from_left
    d_key_vals = d_key_vals + from_right
    statistics = jnp.stack([lse, delta], axis=1)
    query_rows = proj[..., :heads_key]
    queries_all, d_att_all = (
        lax.all_gather(query_rows, "sb", axis=1, tiled=True),
        lax.all_gather(d_att, "sb", axis=0, tiled=True),
    )
    stats_all = lax.all_gather(statistics, "sb", axis=3, tiled=True)
    queries_all = queries_all.reshape(samples_dev, stretch, HEADS, KEY)
    d_att_all = d_att_all.reshape(stretch, HEADS, VAL)
    keys_own = key_vals[..., :heads_key].reshape(samples_dev, sequence_bins, HEADS, KEY)
    vals_own = key_vals[..., heads_key:].reshape(samples_dev, sequence_bins, HEADS, VAL)
    score_key = (
        jnp.einsum("nihd,njhd->nhij", queries_all, keys_own, preferred_element_type=jnp.float32)
        * scale
    )
    prob_key = jnp.where(key_mask[None], jnp.exp(score_key - stats_all[:, 0][..., None]), 0.0)
    d_val_pair = jnp.einsum(
        "nhij,ihe->njhe",
        prob_key.astype(jnp.bfloat16),
        d_att_all,
        preferred_element_type=jnp.float32,
    )
    d_prob_key = jnp.einsum(
        "ihe,njhe->nhij", d_att_all, vals_own, preferred_element_type=jnp.float32
    )
    d_score_key = (prob_key * (d_prob_key - stats_all[:, 1][..., None]) * scale).astype(
        jnp.bfloat16
    )
    d_key_pair = jnp.einsum(
        "nhij,nihd->njhd", d_score_key, queries_all, preferred_element_type=jnp.float32
    )
    d_key_vals = d_key_vals + jnp.concatenate(
        [
            d_key_pair.reshape(samples_dev, sequence_bins, heads_key),
            d_val_pair.reshape(samples_dev, sequence_bins, heads_val),
        ],
        axis=2,
    )
    d_proj = jnp.concatenate(
        [d_query.reshape(samples_dev, sequence_bins, heads_key), d_key_vals], axis=2
    ).astype(jnp.bfloat16)
    d_normed = jnp.einsum("nbc,dc->nbd", d_proj, qkv_full, preferred_element_type=jnp.float32)
    gained = norm_gain * d_normed
    d_resid = (
        cot.astype(jnp.float32)[None]
        + inv_rms * gained
        - resid * inv_rms * inv_rms * inv_rms * jnp.mean(resid * gained, axis=-1, keepdims=True)
    )
    d_act = jnp.einsum(
        "nbd,cd->nbc", d_resid.astype(jnp.bfloat16), mix_full, preferred_element_type=jnp.float32
    )
    hidden_gradient = (d_act * gelu_slope(hidden_state)).astype(jnp.bfloat16)
    gradient_extended = extended(hidden_gradient, ((("sa", "sb"), 1),), DILATION_BINS)
    d_gelu_in = jnp.zeros((samples_dev, sequence_bins, base.shape[1]), jnp.float32)
    for tap_index in range(3):
        start_offset = (2 - tap_index) * DILATION_BINS
        d_gelu_in = d_gelu_in + jnp.einsum(
            "nbc,dc->nbd",
            gradient_extended[:, start_offset : start_offset + sequence_bins],
            conv_full[tap_index],
            preferred_element_type=jnp.float32,
        )
    grads = d_resid + d_gelu_in * gelu_slope(noisy)
    summed = lax.psum(jnp.sum(grads, axis=0).astype(jnp.bfloat16), "noise").astype(jnp.float32)
    return summed / (samples_dev * lax.axis_size("noise"))


def permuted(value, pairs):
    return lax.ppermute(value, ("sa", "sb", "noise"), pairs)


def routes(n_sa, route):
    flat = lambda z, y, x, c: ((z * 2 + y) * 2 + x) * 2 + c
    pairs = []
    for z in range(n_sa):
        for y in range(2):
            for x in range(2):
                for c in range(2):
                    target = route(z, y, x, c)
                    if target is not None and 0 <= target[0] < n_sa:
                        pairs.append((flat(z, y, x, c), flat(*target)))
    return pairs


def pack_kernel(info, conv, mix, qkv, out, packed, sems):
    b, n = info[1], info[2]
    part = b * 2 + n
    rows = pl.ds(pl.multiple_of(part * 48, 16), 48)
    half = pl.ds(pl.multiple_of(n * 48, 16), 48)
    columns = pl.ds(pl.multiple_of(b * 384, 128), 384)
    copies = [(conv.at[t, rows, :], packed.at[pl.ds(48 * t, 48), :]) for t in range(3)]
    copies.append((mix.at[half, columns], packed.at[pl.ds(144, 48), :]))
    copies.append((out.at[half, columns], packed.at[pl.ds(192, 48), :]))
    for k in range(2):
        copies.append((qkv.at[rows, pl.ds(384 * k, 384)], packed.at[pl.ds(240 + 48 * k, 48), :]))
    for k in range(3):
        third = pl.ds(pl.multiple_of(part * 48 + 16 * k, 16), 16)
        copies.append((qkv.at[third, pl.ds(768, 128)], packed.at[pl.ds(336, 16), pl.ds(128 * k, 128)]))
    started = [pltpu.make_async_copy(s, d, sems.at[i]) for i, (s, d) in enumerate(copies)]
    for copy in started:
        copy.start()
    for copy in started:
        copy.wait()


def nt(a, b):
    return lax.dot_general(a, b, (((1,), (1,)), ((), ())), preferred_element_type=jnp.float32)


def tn(a, b):
    return lax.dot_general(a, b, (((0,), (0,)), ((), ())), preferred_element_type=jnp.float32)


def nn(a, b):
    return jnp.dot(a, b, preferred_element_type=jnp.float32)


CHUNK = 384


def chunk(c):
    return pl.ds(pl.multiple_of(c * CHUNK, 128), CHUNK)


def forward_kernel(
    info, band, noise, base, cot, gathered, gain,
    d_q_out, d_kv_out, send, resid_out, inv_out, hidden_out, conv_out, mix_out, qkv_out,
    conv, mix, qkv, out, noisy, gelu_in, sems,
):
    length = info[5]
    first = info[0] * 128
    pair_flag = info[4]

    def unpack(i, _):
        part = lax.rem(i, 8)
        z = i // 8
        b, n = part // 2, lax.rem(part, 2)
        rows = pl.ds(pl.multiple_of(z * 384 + part * 48, 16), 48)
        half = pl.ds(pl.multiple_of(z * 96 + n * 48, 16), 48)
        columns = pl.ds(pl.multiple_of(b * 384, 128), 384)
        for t in range(3):
            conv[t, rows, :] = gathered[i, pl.ds(48 * t, 48), :]
        mix[half, columns] = gathered[i, pl.ds(144, 48), :]
        out[half, columns] = gathered[i, pl.ds(192, 48), :]
        for k in range(2):
            qkv[rows, pl.ds(384 * k, 384)] = gathered[i, pl.ds(240 + 48 * k, 48), :]
        for k in range(3):
            third = pl.ds(pl.multiple_of(z * 384 + part * 48 + 16 * k, 16), 16)
            qkv[third, pl.ds(768, 128)] = gathered[i, pl.ds(336, 16), pl.ds(128 * k, 128)]
        return 0

    lax.fori_loop(0, gathered.shape[0], unpack, 0)
    copies = [
        pltpu.make_async_copy(s, d, sems.at[i])
        for i, (s, d) in enumerate(((conv, conv_out), (mix, mix_out), (qkv, qkv_out)))
    ]
    for copy in copies:
        copy.start()

    def activate(c, _):
        values = base[:, chunk(c)].astype(jnp.float32) + noise[:, chunk(c)].astype(jnp.float32)
        noisy[:, chunk(c)] = values
        gelu_in[:, chunk(c)] = gelu_tanh(values).astype(jnp.bfloat16)
        return 0

    lax.fori_loop(0, 4, activate, 0)

    def convolve(c, total):
        for t in range(3):
            total = total + nn(gelu_in[pl.ds(16 * t, 192), chunk(c)], conv[t, chunk(c), :])
        return total

    hidden = lax.fori_loop(0, 4, convolve, jnp.zeros((192, HID), jnp.float32))
    hidden_out[...] = hidden[32:160]
    act = gelu_tanh(hidden).astype(jnp.bfloat16)

    def mixing(c, squares):
        resid = noisy[pl.ds(16, 192), chunk(c)] + nn(act, mix[:, chunk(c)])
        noisy[pl.ds(16, 192), chunk(c)] = resid
        resid_out[:, chunk(c)] = resid[32:160]
        return squares + jnp.sum(resid * resid, axis=1, keepdims=True)

    squares = lax.fori_loop(0, 4, mixing, jnp.zeros((192, 1), jnp.float32))
    inv_rms = lax.rsqrt(squares * (1.0 / 1536) + 1e-06)
    inv_out[...] = inv_rms[32:160]

    def project(c, total):
        normed = (noisy[pl.ds(16, 192), chunk(c)] * inv_rms * gain[:, chunk(c)]).astype(jnp.bfloat16)
        return total + nn(normed, qkv[chunk(c), :])

    proj = lax.fori_loop(0, 4, project, jnp.zeros((192, 896), jnp.float32)).astype(jnp.bfloat16)

    def attended(c, total):
        return total + nt(cot[:, chunk(c)], out[:, chunk(c)])

    d_att = lax.fori_loop(0, 4, attended, jnp.zeros((128, HEADS * VAL), jnp.float32)).astype(jnp.bfloat16)

    row = lax.broadcasted_iota(jnp.int32, (128, 192), 0)
    column = lax.broadcasted_iota(jnp.int32, (128, 192), 1) - 32
    inside = (column + first >= 0) & (column + first < length)
    paired = (column >= 0) & (column < 128) & (pair_flag > 0)
    apart = jnp.abs(row - column)
    scale = KEY ** (-0.5)
    d_queries, d_keys, d_values = [], [], []
    for h in range(HEADS):
        q = proj[32:160, KEY * h : KEY * (h + 1)]
        k = proj[:, HEADS * KEY + KEY * h : HEADS * KEY + KEY * (h + 1)]
        v = proj[:, 2 * HEADS * KEY + VAL * h : 2 * HEADS * KEY + VAL * (h + 1)]
        d_att_h = d_att[:, VAL * h : VAL * (h + 1)]
        allowed = inside & (paired | (apart <= band[h]))
        score = jnp.where(allowed, nt(q, k) * scale, -1e30)
        top = jnp.max(score, axis=1, keepdims=True)
        raised = jnp.where(allowed, jnp.exp(score - top), 0.0)
        prob = raised / jnp.sum(raised, axis=1, keepdims=True)
        prob_b = prob.astype(jnp.bfloat16)
        attn = nn(prob_b, v)
        delta = jnp.sum(d_att_h.astype(jnp.float32) * attn, axis=1, keepdims=True)
        d_score = (prob * (nt(d_att_h, v) - delta) * scale).astype(jnp.bfloat16)
        d_queries.append(nn(d_score, k))
        d_keys.append(tn(d_score, q))
        d_values.append(tn(prob_b, d_att_h))
    d_q_out[...] = jnp.concatenate(d_queries, axis=1)
    d_kv = jnp.concatenate(d_keys + d_values, axis=1)
    d_kv_out[...] = d_kv[32:160]

    @pl.when(info[2] == 0)
    def _():
        send[...] = d_kv[:32].astype(jnp.bfloat16)

    @pl.when(info[2] == 1)
    def _():
        send[...] = d_kv[160:].astype(jnp.bfloat16)

    for copy in copies:
        copy.wait()


def norm_kernel(
    info, d_q, d_kv, received, resid, inv_rms_ref, hidden, cot, gain, mix, qkv,
    d_hidden_out, d_resid_out, send, total_kv, gained, d_resid_all,
):
    n = info[2]
    total_kv[...] = d_kv[...]
    edge = pl.ds(pl.multiple_of(n * 96, 32), 32)
    total_kv[edge, :] = total_kv[edge, :] + received[...].astype(jnp.float32)
    d_proj = jnp.concatenate([d_q[...], total_kv[...]], axis=1).astype(jnp.bfloat16)
    inv_rms = inv_rms_ref[...]

    def back(c, mean):
        part = gain[:, chunk(c)] * nt(d_proj, qkv[chunk(c), :])
        gained[:, chunk(c)] = part
        return mean + jnp.sum(resid[:, chunk(c)] * part, axis=1, keepdims=True)

    mean = lax.fori_loop(0, 4, back, jnp.zeros((128, 1), jnp.float32)) * (1.0 / 1536)
    cubed = inv_rms * inv_rms * inv_rms * mean

    def residual(c, total):
        d_resid = (
            cot[:, chunk(c)].astype(jnp.float32)
            + inv_rms * gained[:, chunk(c)]
            - resid[:, chunk(c)] * cubed
        )
        d_resid_all[:, chunk(c)] = d_resid
        return total + nt(d_resid.astype(jnp.bfloat16), mix[:, chunk(c)])

    d_act = lax.fori_loop(0, 4, residual, jnp.zeros((128, HID), jnp.float32))
    d_hidden = (d_act * gelu_slope(hidden[...])).astype(jnp.bfloat16)
    d_hidden_out[...] = d_hidden
    d_resid_out[...] = d_resid_all[pl.ds(pl.multiple_of(n * 64, 64), 64), :]

    @pl.when(n == 0)
    def _():
        send[...] = d_hidden[:16]

    @pl.when(n == 1)
    def _():
        send[...] = d_hidden[112:]


def taps_kernel(info, d_hidden, received, d_resid, noise, base, conv, keep, send, extended_ref, grads):
    n, x = info[2], info[3]

    @pl.when(n == 0)
    def _():
        extended_ref[pl.ds(0, 16), :] = received[...]
        extended_ref[pl.ds(16, 80), :] = d_hidden[pl.ds(0, 80), :]

    @pl.when(n == 1)
    def _():
        extended_ref[pl.ds(0, 80), :] = d_hidden[pl.ds(48, 80), :]
        extended_ref[pl.ds(80, 16), :] = received[...]

    rows = pl.ds(pl.multiple_of(48 + 64 * n, 16), 64)

    def taps(c, _):
        noisy = base[rows, chunk(c)].astype(jnp.float32) + noise[rows, chunk(c)].astype(jnp.float32)
        total = nt(extended_ref[pl.ds(32, 64), :], conv[0, chunk(c), :])
        total = total + nt(extended_ref[pl.ds(16, 64), :], conv[1, chunk(c), :])
        total = total + nt(extended_ref[pl.ds(0, 64), :], conv[2, chunk(c), :])
        grads[:, chunk(c)] = d_resid[:, chunk(c)] + total * gelu_slope(noisy)
        return 0

    lax.fori_loop(0, 4, taps, 0)
    keep[...] = grads[pl.ds(pl.multiple_of(32 * x, 32), 32), :]
    send[...] = grads[pl.ds(pl.multiple_of(32 - 32 * x, 32), 32), :].astype(jnp.bfloat16)


def vmem(count):
    return [pl.BlockSpec(memory_space=pltpu.VMEM)] * count


def smem(count):
    return [pl.BlockSpec(memory_space=pltpu.SMEM)] * count


def hbm(count):
    return [pl.BlockSpec(memory_space=pl.ANY)] * count


LIMIT = pltpu.CompilerParams(vmem_limit_bytes=56 * 1024 * 1024)
f32, bf16 = (jnp.float32, jnp.bfloat16)


def shaped(*shape, dtype=jnp.float32):
    return jax.ShapeDtypeStruct(shape, dtype)


def stretch_shards(
    base, noise, cot, convolution_weight, mix_w, norm_gain, qkv_w, out_w, band_width, pairs
):
    n_sa = lax.axis_size("sa")
    z, b, n = (lax.axis_index("sa"), lax.axis_index("sb"), lax.axis_index("noise"))
    y, x = (b >> 1, b & 1)
    flag = jnp.any((pairs[:, 0] == z) & (pairs[:, 1] == z)).astype(jnp.int32)
    info = jnp.stack([z, b, n, x, flag, jnp.int32(n_sa * 128)]).astype(jnp.int32)
    features = base.shape[1]

    packed = pl.pallas_call(
        pack_kernel,
        out_shape=shaped(352, CHUNK, dtype=bf16),
        in_specs=smem(1) + hbm(4),
        out_specs=pl.BlockSpec(memory_space=pl.ANY),
        scratch_shapes=[pltpu.SemaphoreType.DMA((10,))],
    )(info, convolution_weight, mix_w, qkv_w, out_w)
    gathered = lax.all_gather(packed, ("sa", "sb", "noise"), axis=0, tiled=False)
    gathered = gathered.reshape(-1, 352, CHUNK)

    def to_sample(shift):
        return routes(n_sa, lambda z, y, x, c: (z, c, (x + shift) % 2, y))

    got = [
        permuted(jnp.where(x == shift, noise[0], noise[1]), to_sample(shift))
        for shift in range(2)
    ]
    even = x == 0
    noise_half = jnp.concatenate([jnp.where(even, got[0], got[1]), jnp.where(even, got[1], got[0])], axis=0)
    both = jnp.stack([base, cot])
    across = permuted(both, routes(n_sa, lambda z, y, x, c: (z, 1 - y, x, 1 - c) if y != c else None))
    current = jnp.where(y == n, both, across)
    beside = permuted(current, routes(n_sa, lambda z, y, x, c: (z, y, 1 - x, c)))
    halves = jnp.concatenate([jnp.where(even, current, beside), jnp.where(even, beside, current)], axis=1)
    edge_route = routes(n_sa, lambda z, y, x, c: (z - 1, y, x, 1) if c == 0 else (z + 1, y, x, 0))
    core_route = routes(n_sa, lambda z, y, x, c: (z, y, x, 1 - c))
    mine = jnp.stack([noise_half, halves[0]])
    edge = permuted(jnp.where(n == 0, mine[:, :48], mine[:, 16:]), edge_route)
    wide = jnp.concatenate([jnp.where(n == 0, edge, mine[:, :48])] + [jnp.where(n == 0, mine, jnp.concatenate([mine[:, 48:], edge], axis=1))], axis=1)
    swap = permuted(jnp.concatenate([wide.reshape(224, features), halves[1]], axis=0), core_route)
    wide_other = swap[:224].reshape(2, 112, features)
    whole = jnp.concatenate([jnp.where(n == 0, wide, wide_other), jnp.where(n == 0, wide_other, wide)], axis=1)
    noise_rows, base_rows = whole[0], whole[1]
    cot_rows = jnp.concatenate(
        [jnp.where(n == 0, halves[1], swap[224:]), jnp.where(n == 0, swap[224:], halves[1])], axis=0
    )
    gain = norm_gain.reshape(1, features)

    d_q, d_kv, send, resid, inv_rms, hidden, conv, mix, qkv = pl.pallas_call(
        forward_kernel,
        out_shape=(
            shaped(128, 256), shaped(128, 640), shaped(32, 640, dtype=bf16), shaped(128, features),
            shaped(128, 1), shaped(128, HID), shaped(3, features, HID, dtype=bf16),
            shaped(HID, features, dtype=bf16), shaped(features, 896, dtype=bf16),
        ),
        in_specs=smem(2) + vmem(5),
        out_specs=tuple(vmem(6) + hbm(3)),
        scratch_shapes=[
            pltpu.VMEM((3, features, HID), bf16), pltpu.VMEM((HID, features), bf16),
            pltpu.VMEM((features, 896), bf16), pltpu.VMEM((HEADS * VAL, features), bf16),
            pltpu.VMEM((224, features), f32), pltpu.VMEM((224, features), bf16),
            pltpu.SemaphoreType.DMA((3,)),
        ],
        compiler_params=LIMIT,
    )(info, band_width, noise_rows, base_rows, cot_rows, gathered, gain)

    received = permuted(send, edge_route)
    d_hidden, d_resid, send = pl.pallas_call(
        norm_kernel,
        out_shape=(shaped(128, HID, dtype=bf16), shaped(64, features), shaped(16, HID, dtype=bf16)),
        in_specs=smem(1) + vmem(10),
        out_specs=tuple(vmem(3)),
        scratch_shapes=[
            pltpu.VMEM((128, 640), f32), pltpu.VMEM((128, features), f32), pltpu.VMEM((128, features), f32),
        ],
        compiler_params=LIMIT,
    )(info, d_q, d_kv, received, resid, inv_rms, hidden, cot_rows, gain, mix, qkv)

    received = permuted(send, edge_route)
    keep, send = pl.pallas_call(
        taps_kernel,
        out_shape=(shaped(32, features), shaped(32, features, dtype=bf16)),
        in_specs=smem(1) + vmem(6),
        out_specs=tuple(vmem(2)),
        scratch_shapes=[pltpu.VMEM((96, HID), bf16), pltpu.VMEM((64, features), f32)],
        compiler_params=LIMIT,
    )(info, d_hidden, received, d_resid, noise_rows, base_rows, conv)

    received = permuted(send, routes(n_sa, lambda z, y, x, c: (z, y, 1 - x, c)))
    partial = (keep + received.astype(f32)).astype(bf16)
    first_sum = permuted(
        partial, routes(n_sa, lambda z, y, x, c: (z, c, x, c) if y != c else (z, y, x, 1 - c))
    )
    second_sum = permuted(partial, routes(n_sa, lambda z, y, x, c: (z, c, x, 1 - c) if y != c else None))
    other = jnp.where(y == n, partial, second_sum)
    return (first_sum.astype(f32) + other.astype(f32)) * 0.25


def solution(mesh):
    fits = mesh.shape["sb"] == 4 and mesh.shape["noise"] == 2 and HEADS == 4

    def body(*arrays):
        if fits and arrays[0].shape[0] == 32 and arrays[1].shape[0] == 2 and TILE == 128:
            if arrays[0].shape[1] == 1536 and mesh.shape["sa"] == 4:
                return stretch_shards(*arrays)
        return shards(*arrays)

    return jax.shard_map(
        body,
        mesh=mesh,
        in_specs=(
            P(("sa", "sb"), None),
            P("noise", ("sa", "sb"), None),
            P(("sa", "sb"), None),
            P(None, "sa", None),
            P("sa", None),
            P(),
            P("sa", None),
            P("sa", None),
            P(),
            P(),
        ),
        out_specs=P(("sa", "sb"), None),
        check_vma=False,
    )
```

```python
import jax
import jax.numpy as jnp
from jax import lax
from jax.experimental import pallas as pl
from jax.experimental.pallas import tpu as pltpu
from jax.sharding import PartitionSpec as P

HID = 384
HEADS = 4
KEY = 64
VAL = 96
DILATION_BINS = 16
BAND = 32
TILE = 128


ROOT_TWO_PI = 0.7978845608
CUBIC = 0.044715


def extended(value, sides, width):
    for axis, dim in sides:
        peers, length = (lax.axis_size(axis), value.shape[dim])
        up = [(i, (i + 1) % peers) for i in range(peers - 1)]
        down = [(j, i) for i, j in up]
        last = lax.slice_in_dim(value, length - width, length, axis=dim)
        leading = lax.slice_in_dim(value, 0, width, axis=dim)
        before = lax.ppermute(last, axis, up)
        after = lax.ppermute(leading, axis, down)
        value = jnp.concatenate([before, value, after], axis=dim)
    return value


def from_behind(block, axis, distance):
    devices = range(lax.axis_size(axis))
    route = [(i - distance, i) for i in devices if i - distance in devices]
    return lax.ppermute(block, axis, route)


def gelu_tanh(values):
    inner = ROOT_TWO_PI * (values + CUBIC * values * values * values)
    return 0.5 * values * (1.0 + jnp.tanh(inner))


def gelu_slope(values):
    tangent = jnp.tanh(ROOT_TWO_PI * (values + CUBIC * values * values * values))
    return 0.5 * (1.0 + tangent) + 0.5 * values * (1.0 - tangent * tangent) * ROOT_TWO_PI * (
        1.0 + 3.0 * CUBIC * values * values
    )


def shards(base, noise, cot, convolution_weight, mix_w, norm_gain, qkv_w, out_w, band_width, pairs):
    conv_full, mix_full, qkv_full, out_full = (
        lax.all_gather(convolution_weight, "sa", axis=1, tiled=True),
        lax.all_gather(mix_w, "sa", axis=0, tiled=True),
        lax.all_gather(qkv_w, "sa", axis=0, tiled=True),
        lax.all_gather(out_w, "sa", axis=0, tiled=True),
    )
    sequence_bins = base.shape[0]
    samples_dev = noise.shape[0]
    stretch = sequence_bins * lax.axis_size("sb")
    sequence_length = stretch * lax.axis_size("sa")
    heads_key = HEADS * KEY
    heads_val = HEADS * VAL
    width = sequence_bins + 2 * BAND
    scale = KEY ** (-0.5)
    stretch_first = lax.axis_index("sa") * stretch
    first_row = stretch_first + lax.axis_index("sb") * sequence_bins
    row_pos = first_row + jnp.arange(sequence_bins, dtype=jnp.int32)
    ext_pos = first_row - BAND + jnp.arange(width, dtype=jnp.int32)
    stretch_pos = stretch_first + jnp.arange(stretch, dtype=jnp.int32)
    tiles = sequence_length // TILE
    tile_ids = jnp.arange(tiles, dtype=jnp.int32)
    pick_query = (pairs[:, 0][:, None] == tile_ids[None, :]).astype(jnp.float32)
    pick_key = (pairs[:, 1][:, None] == tile_ids[None, :]).astype(jnp.float32)
    table = jnp.dot(pick_query.T, pick_key)
    own_select = ((row_pos // TILE)[:, None] == tile_ids[None, :]).astype(jnp.float32)
    stretch_select = ((stretch_pos // TILE)[:, None] == tile_ids[None, :]).astype(jnp.float32)
    pair_own_rows = jnp.dot(jnp.dot(own_select, table), stretch_select.T) > 0.5
    pair_own_keys = jnp.dot(jnp.dot(stretch_select, table), own_select.T) > 0.5
    inside = (ext_pos >= 0) & (ext_pos < sequence_length)
    band_mask = inside[None, None, :] & (
        jnp.abs(row_pos[:, None] - ext_pos[None, :])[None] <= band_width[:, None, None]
    )
    far_rows = jnp.abs(row_pos[:, None] - stretch_pos[None, :])[None] > band_width[:, None, None]
    pair_mask = pair_own_rows[None] & far_rows
    key_mask = pair_own_keys[None] & jnp.transpose(far_rows, (0, 2, 1))
    noisy = base.astype(jnp.float32)[None] + noise.astype(jnp.float32)
    gelu_input = gelu_tanh(noisy).astype(jnp.bfloat16)
    gelu_extended = extended(gelu_input, ((("sa", "sb"), 1),), DILATION_BINS)
    hidden_state = jnp.zeros((samples_dev, sequence_bins, HID), jnp.float32)
    for tap_index in range(3):
        hidden_state = hidden_state + jnp.einsum(
            "nbd,dc->nbc",
            gelu_extended[:, tap_index * DILATION_BINS : tap_index * DILATION_BINS + sequence_bins],
            conv_full[tap_index],
            preferred_element_type=jnp.float32,
        )
    act = gelu_tanh(hidden_state).astype(jnp.bfloat16)
    resid = noisy + jnp.einsum("nbc,cd->nbd", act, mix_full, preferred_element_type=jnp.float32)
    inv_rms = lax.rsqrt(jnp.mean(resid * resid, axis=-1, keepdims=True) + 1e-06)
    normed = (resid * inv_rms * norm_gain).astype(jnp.bfloat16)
    proj = jnp.einsum("nbd,dc->nbc", normed, qkv_full, preferred_element_type=jnp.float32).astype(
        jnp.bfloat16
    )
    queries = proj[..., :heads_key].reshape(samples_dev, sequence_bins, HEADS, KEY)
    key_vals = proj[..., heads_key:]
    kv_ext = extended(key_vals, ((("sa", "sb"), 1),), BAND)
    kv_all = lax.all_gather(key_vals, "sb", axis=1, tiled=True)
    keys_ext = kv_ext[..., :heads_key].reshape(samples_dev, width, HEADS, KEY)
    vals_ext = kv_ext[..., heads_key:].reshape(samples_dev, width, HEADS, VAL)
    keys_all = kv_all[..., :heads_key].reshape(samples_dev, stretch, HEADS, KEY)
    vals_all = kv_all[..., heads_key:].reshape(samples_dev, stretch, HEADS, VAL)
    score_band = (
        jnp.einsum("nihd,njhd->nhij", queries, keys_ext, preferred_element_type=jnp.float32) * scale
    )
    score_band = jnp.where(band_mask[None], score_band, -1e30)
    raw_pair = jnp.einsum("nihd,njhd->nhij", queries, keys_all, preferred_element_type=jnp.float32)
    score_pair = jnp.where(pair_mask[None], raw_pair * scale, -1e30)
    top = jnp.maximum(jnp.max(score_band, axis=-1), jnp.max(score_pair, axis=-1))
    total = jnp.sum(jnp.where(band_mask[None], jnp.exp(score_band - top[..., None]), 0.0), axis=-1)
    total = total + jnp.sum(
        jnp.where(pair_mask[None], jnp.exp(score_pair - top[..., None]), 0.0), axis=-1
    )
    lse = top + jnp.log(total)
    prob_band = jnp.where(band_mask[None], jnp.exp(score_band - lse[..., None]), 0.0)
    prob_pair = jnp.where(pair_mask[None], jnp.exp(score_pair - lse[..., None]), 0.0)
    band_b = prob_band.astype(jnp.bfloat16)
    pair_b = prob_pair.astype(jnp.bfloat16)
    attn = jnp.einsum("nhij,njhe->nihe", band_b, vals_ext, preferred_element_type=jnp.float32)
    attn = attn + jnp.einsum(
        "nhij,njhe->nihe", pair_b, vals_all, preferred_element_type=jnp.float32
    )
    d_att = jnp.dot(cot, out_full.T, preferred_element_type=jnp.float32).astype(jnp.bfloat16)
    d_att_heads = d_att.reshape(sequence_bins, HEADS, VAL)
    delta = jnp.transpose(jnp.sum(d_att_heads.astype(jnp.float32)[None] * attn, axis=-1), (0, 2, 1))
    d_prob_band = jnp.einsum(
        "ihe,njhe->nhij", d_att_heads, vals_ext, preferred_element_type=jnp.float32
    )
    d_prob_pair = jnp.einsum(
        "ihe,njhe->nhij", d_att_heads, vals_all, preferred_element_type=jnp.float32
    )
    d_score_band = (prob_band * (d_prob_band - delta[..., None]) * scale).astype(jnp.bfloat16)
    d_score_pair = (prob_pair * (d_prob_pair - delta[..., None]) * scale).astype(jnp.bfloat16)
    d_query = jnp.einsum(
        "nhij,njhd->nihd", d_score_band, keys_ext, preferred_element_type=jnp.float32
    )
    d_query = d_query + jnp.einsum(
        "nhij,njhd->nihd", d_score_pair, keys_all, preferred_element_type=jnp.float32
    )
    d_key_ext = jnp.einsum(
        "nhij,nihd->njhd", d_score_band, queries, preferred_element_type=jnp.float32
    )
    d_val_ext = jnp.einsum(
        "nhij,ihe->njhe", band_b, d_att_heads, preferred_element_type=jnp.float32
    )
    d_kv_ext = jnp.concatenate(
        [
            d_key_ext.reshape(samples_dev, width, heads_key),
            d_val_ext.reshape(samples_dev, width, heads_val),
        ],
        axis=2,
    )
    from_right = from_behind(d_kv_ext[:, :BAND].astype(jnp.bfloat16), ("sa", "sb"), -1).astype(
        jnp.float32
    )
    from_left = from_behind(
        d_kv_ext[:, BAND + sequence_bins :].astype(jnp.bfloat16), ("sa", "sb"), 1
    ).astype(jnp.float32)
    d_key_vals = d_kv_ext[:, BAND : BAND + sequence_bins]
    d_key_vals = d_key_vals + from_left
    d_key_vals = d_key_vals + from_right
    statistics = jnp.stack([lse, delta], axis=1)
    query_rows = proj[..., :heads_key]
    queries_all, d_att_all = (
        lax.all_gather(query_rows, "sb", axis=1, tiled=True),
        lax.all_gather(d_att, "sb", axis=0, tiled=True),
    )
    stats_all = lax.all_gather(statistics, "sb", axis=3, tiled=True)
    queries_all = queries_all.reshape(samples_dev, stretch, HEADS, KEY)
    d_att_all = d_att_all.reshape(stretch, HEADS, VAL)
    keys_own = key_vals[..., :heads_key].reshape(samples_dev, sequence_bins, HEADS, KEY)
    vals_own = key_vals[..., heads_key:].reshape(samples_dev, sequence_bins, HEADS, VAL)
    score_key = (
        jnp.einsum("nihd,njhd->nhij", queries_all, keys_own, preferred_element_type=jnp.float32)
        * scale
    )
    prob_key = jnp.where(key_mask[None], jnp.exp(score_key - stats_all[:, 0][..., None]), 0.0)
    d_val_pair = jnp.einsum(
        "nhij,ihe->njhe",
        prob_key.astype(jnp.bfloat16),
        d_att_all,
        preferred_element_type=jnp.float32,
    )
    d_prob_key = jnp.einsum(
        "ihe,njhe->nhij", d_att_all, vals_own, preferred_element_type=jnp.float32
    )
    d_score_key = (prob_key * (d_prob_key - stats_all[:, 1][..., None]) * scale).astype(
        jnp.bfloat16
    )
    d_key_pair = jnp.einsum(
        "nhij,nihd->njhd", d_score_key, queries_all, preferred_element_type=jnp.float32
    )
    d_key_vals = d_key_vals + jnp.concatenate(
        [
            d_key_pair.reshape(samples_dev, sequence_bins, heads_key),
            d_val_pair.reshape(samples_dev, sequence_bins, heads_val),
        ],
        axis=2,
    )
    d_proj = jnp.concatenate(
        [d_query.reshape(samples_dev, sequence_bins, heads_key), d_key_vals], axis=2
    ).astype(jnp.bfloat16)
    d_normed = jnp.einsum("nbc,dc->nbd", d_proj, qkv_full, preferred_element_type=jnp.float32)
    gained = norm_gain * d_normed
    d_resid = (
        cot.astype(jnp.float32)[None]
        + inv_rms * gained
        - resid * inv_rms * inv_rms * inv_rms * jnp.mean(resid * gained, axis=-1, keepdims=True)
    )
    d_act = jnp.einsum(
        "nbd,cd->nbc", d_resid.astype(jnp.bfloat16), mix_full, preferred_element_type=jnp.float32
    )
    hidden_gradient = (d_act * gelu_slope(hidden_state)).astype(jnp.bfloat16)
    gradient_extended = extended(hidden_gradient, ((("sa", "sb"), 1),), DILATION_BINS)
    d_gelu_in = jnp.zeros((samples_dev, sequence_bins, base.shape[1]), jnp.float32)
    for tap_index in range(3):
        start_offset = (2 - tap_index) * DILATION_BINS
        d_gelu_in = d_gelu_in + jnp.einsum(
            "nbc,dc->nbd",
            gradient_extended[:, start_offset : start_offset + sequence_bins],
            conv_full[tap_index],
            preferred_element_type=jnp.float32,
        )
    grads = d_resid + d_gelu_in * gelu_slope(noisy)
    summed = lax.psum(jnp.sum(grads, axis=0).astype(jnp.bfloat16), "noise").astype(jnp.float32)
    return summed / (samples_dev * lax.axis_size("noise"))


def permuted(value, pairs):
    return lax.ppermute(value, ("sa", "sb", "noise"), pairs)


def routes(n_sa, route):
    flat = lambda z, y, x, c: ((z * 2 + y) * 2 + x) * 2 + c
    pairs = []
    for z in range(n_sa):
        for y in range(2):
            for x in range(2):
                for c in range(2):
                    target = route(z, y, x, c)
                    if target is not None and 0 <= target[0] < n_sa:
                        pairs.append((flat(z, y, x, c), flat(*target)))
    return pairs


def position():
    b = lax.axis_index("sb")
    return lax.axis_index("sa"), b // 2, lax.rem(b, 2), lax.axis_index("noise")


def pack_kernel(conv, mix, qkv, out, early, late):
    z, y, x, n = position()
    b = 2 * y + x
    part = b * 2 + n
    rows = pl.ds(pl.multiple_of(part * 48, 16), 48)
    half = pl.ds(pl.multiple_of(n * 48, 16), 48)
    columns = pl.ds(pl.multiple_of(b * 384, 128), 384)
    for t in range(3):
        early[pl.ds(48 * t, 48), :] = conv[t, rows, :]
    early[pl.ds(144, 48), :] = mix[half, columns]
    late[pl.ds(0, 48), :] = out[half, columns]
    for k in range(2):
        late[pl.ds(48 + 48 * k, 48), :] = qkv[rows, pl.ds(384 * k, 384)]
    for k in range(3):
        third = pl.ds(pl.multiple_of(part * 48 + 16 * k, 16), 16)
        late[pl.ds(144, 16), pl.ds(128 * k, 128)] = qkv[third, pl.ds(768, 128)]


def nt(a, b):
    return lax.dot_general(a, b, (((1,), (1,)), ((), ())), preferred_element_type=jnp.float32)


def tn(a, b):
    return lax.dot_general(a, b, (((0,), (0,)), ((), ())), preferred_element_type=jnp.float32)


def nn(a, b):
    return jnp.dot(a, b, preferred_element_type=jnp.float32)


CHUNK = 384


def chunk(c):
    return pl.ds(pl.multiple_of(c * CHUNK, 128), CHUNK)


def pieces(mine, other, n, i):
    first, second = mine[i], other[i]
    return jnp.where(n == 0, first, second), jnp.where(n == 0, second, first)


def forward_kernel(
    noise, base, mine, other, gain, normed_out, resid_out, inv_out, hidden_out, conv_out, mix_out,
    conv, mix, noisy, gelu_in, sems,
):
    z, y, x, n = position()

    def unpack(i, _):
        source, b = i // 4, lax.rem(i, 4)
        for core, piece in enumerate(pieces(mine, other, n, i)):
            rows = pl.ds(pl.multiple_of(source * 384 + (b * 2 + core) * 48, 16), 48)
            half = pl.ds(pl.multiple_of(source * 96 + core * 48, 16), 48)
            columns = pl.ds(pl.multiple_of(b * 384, 128), 384)
            for t in range(3):
                conv[t, rows, :] = piece[48 * t : 48 * t + 48]
            mix[half, columns] = piece[144:192]
        return 0

    lax.fori_loop(0, mine.shape[0], unpack, 0)
    copies = [
        pltpu.make_async_copy(s, d, sems.at[i]) for i, (s, d) in enumerate(((conv, conv_out), (mix, mix_out)))
    ]
    for copy in copies:
        copy.start()

    def activate(c, _):
        values = base[:, chunk(c)].astype(jnp.float32) + noise[:, chunk(c)].astype(jnp.float32)
        noisy[:, chunk(c)] = values
        gelu_in[:, chunk(c)] = gelu_tanh(values).astype(jnp.bfloat16)
        return 0

    lax.fori_loop(0, 4, activate, 0)

    def convolve(c, total):
        for t in range(3):
            total = total + nn(gelu_in[pl.ds(16 * t, 192), chunk(c)], conv[t, chunk(c), :])
        return total

    hidden = lax.fori_loop(0, 4, convolve, jnp.zeros((192, HID), jnp.float32))
    hidden_out[...] = hidden[32:160]
    act = gelu_tanh(hidden).astype(jnp.bfloat16)

    def mixing(c, squares):
        resid = noisy[pl.ds(16, 192), chunk(c)] + nn(act, mix[:, chunk(c)])
        noisy[pl.ds(16, 192), chunk(c)] = resid
        resid_out[:, chunk(c)] = resid[32:160]
        return squares + jnp.sum(resid * resid, axis=1, keepdims=True)

    squares = lax.fori_loop(0, 4, mixing, jnp.zeros((192, 1), jnp.float32))
    inv_rms = lax.rsqrt(squares * (1.0 / 1536) + 1e-06)
    inv_out[...] = inv_rms[32:160]

    def normalise(c, _):
        normed = noisy[pl.ds(16, 192), chunk(c)] * inv_rms * gain[:, chunk(c)]
        normed_out[:, chunk(c)] = normed.astype(jnp.bfloat16)
        return 0

    lax.fori_loop(0, 4, normalise, 0)
    for copy in copies:
        copy.wait()


def attention_kernel(
    band, pairs, normed, cot, mine, other, d_q_out, d_kv_out, send, qkv_out, qkv, out, sems,
):
    z, y, x, n = position()
    length = lax.axis_size("sa") * 128
    first = z * 128
    pair_flag = jnp.int32(0)
    for i in range(pairs.shape[0]):
        pair_flag = pair_flag | ((pairs[i, 0] == z) & (pairs[i, 1] == z)).astype(jnp.int32)

    proj = jnp.zeros((192, 896), jnp.float32)
    for source in range(4):
        for b in range(4):
            for core, piece in enumerate(pieces(mine, other, n, 4 * source + b)):
                row = source * 384 + (b * 2 + core) * 48
                out[pl.ds(source * 96 + core * 48, 48), pl.ds(b * 384, 384)] = piece[:48]
                for k in range(2):
                    qkv[pl.ds(row, 48), pl.ds(384 * k, 384)] = piece[48 + 48 * k : 96 + 48 * k]
                for k in range(3):
                    qkv[pl.ds(row + 16 * k, 16), pl.ds(768, 128)] = piece[144:160, 128 * k : 128 * k + 128]
        rows = pl.ds(source * 384, 384)
        proj = proj + nn(normed[:, rows], qkv[rows, :])
    proj = proj.astype(jnp.bfloat16)
    copy = pltpu.make_async_copy(qkv, qkv_out, sems.at[0])
    copy.start()
    d_att = nt(cot[...], out[...]).astype(jnp.bfloat16)

    row = lax.broadcasted_iota(jnp.int32, (128, 192), 0)
    column = lax.broadcasted_iota(jnp.int32, (128, 192), 1) - 32
    inside = (column + first >= 0) & (column + first < length)
    paired = (column >= 0) & (column < 128) & (pair_flag > 0)
    apart = jnp.abs(row - column)
    scale = KEY ** (-0.5)
    d_queries, d_keys, d_values = [], [], []
    for h in range(HEADS):
        q = proj[32:160, KEY * h : KEY * (h + 1)]
        k = proj[:, HEADS * KEY + KEY * h : HEADS * KEY + KEY * (h + 1)]
        v = proj[:, 2 * HEADS * KEY + VAL * h : 2 * HEADS * KEY + VAL * (h + 1)]
        d_att_h = d_att[:, VAL * h : VAL * (h + 1)]
        allowed = inside & (paired | (apart <= band[h]))
        score = jnp.where(allowed, nt(q, k) * scale, -1e30)
        top = jnp.max(score, axis=1, keepdims=True)
        raised = jnp.where(allowed, jnp.exp(score - top), 0.0)
        prob = raised / jnp.sum(raised, axis=1, keepdims=True)
        prob_b = prob.astype(jnp.bfloat16)
        attn = nn(prob_b, v)
        delta = jnp.sum(d_att_h.astype(jnp.float32) * attn, axis=1, keepdims=True)
        d_score = (prob * (nt(d_att_h, v) - delta) * scale).astype(jnp.bfloat16)
        d_queries.append(nn(d_score, k))
        d_keys.append(tn(d_score, q))
        d_values.append(tn(prob_b, d_att_h))
    d_q_out[...] = jnp.concatenate(d_queries, axis=1)
    d_kv = jnp.concatenate(d_keys + d_values, axis=1)
    d_kv_out[...] = d_kv[32:160]
    send[...] = jnp.where(n == 0, d_kv[:32], d_kv[160:]).astype(jnp.bfloat16)
    copy.wait()


def norm_kernel(
    d_q, d_kv, received, resid, inv_rms_ref, hidden, cot, gain, mix, qkv,
    d_hidden_out, d_resid_out, send, total_kv, gained, d_resid_all,
):
    z, y, x, n = position()
    total_kv[...] = d_kv[...]
    edge = pl.ds(pl.multiple_of(n * 96, 32), 32)
    total_kv[edge, :] = total_kv[edge, :] + received[...].astype(jnp.float32)
    d_proj = jnp.concatenate([d_q[...], total_kv[...]], axis=1).astype(jnp.bfloat16)
    inv_rms = inv_rms_ref[...]

    def back(c, mean):
        part = gain[:, chunk(c)] * nt(d_proj, qkv[chunk(c), :])
        gained[:, chunk(c)] = part
        return mean + jnp.sum(resid[:, chunk(c)] * part, axis=1, keepdims=True)

    mean = lax.fori_loop(0, 4, back, jnp.zeros((128, 1), jnp.float32)) * (1.0 / 1536)
    cubed = inv_rms * inv_rms * inv_rms * mean

    def residual(c, total):
        d_resid = (
            cot[:, chunk(c)].astype(jnp.float32)
            + inv_rms * gained[:, chunk(c)]
            - resid[:, chunk(c)] * cubed
        )
        d_resid_all[:, chunk(c)] = d_resid
        return total + nt(d_resid.astype(jnp.bfloat16), mix[:, chunk(c)])

    d_act = lax.fori_loop(0, 4, residual, jnp.zeros((128, HID), jnp.float32))
    d_hidden = (d_act * gelu_slope(hidden[...])).astype(jnp.bfloat16)
    d_hidden_out[...] = d_hidden
    d_resid_out[...] = d_resid_all[pl.ds(pl.multiple_of(n * 64, 64), 64), :]

    @pl.when(n == 0)
    def _():
        send[...] = d_hidden[:16]

    @pl.when(n == 1)
    def _():
        send[...] = d_hidden[112:]


def taps_kernel(d_hidden, received, d_resid, noise, base, conv, keep, send, extended_ref, grads):
    z, y, x, n = position()

    @pl.when(n == 0)
    def _():
        extended_ref[pl.ds(0, 16), :] = received[...]
        extended_ref[pl.ds(16, 80), :] = d_hidden[pl.ds(0, 80), :]

    @pl.when(n == 1)
    def _():
        extended_ref[pl.ds(0, 80), :] = d_hidden[pl.ds(48, 80), :]
        extended_ref[pl.ds(80, 16), :] = received[...]

    rows = pl.ds(pl.multiple_of(48 + 64 * n, 16), 64)

    def taps(c, _):
        noisy = base[rows, chunk(c)].astype(jnp.float32) + noise[rows, chunk(c)].astype(jnp.float32)
        total = nt(extended_ref[pl.ds(32, 64), :], conv[0, chunk(c), :])
        total = total + nt(extended_ref[pl.ds(16, 64), :], conv[1, chunk(c), :])
        total = total + nt(extended_ref[pl.ds(0, 64), :], conv[2, chunk(c), :])
        grads[:, chunk(c)] = d_resid[:, chunk(c)] + total * gelu_slope(noisy)
        return 0

    lax.fori_loop(0, 4, taps, 0)
    keep[...] = grads[pl.ds(pl.multiple_of(32 * x, 32), 32), :]
    send[...] = grads[pl.ds(pl.multiple_of(32 - 32 * x, 32), 32), :].astype(jnp.bfloat16)


def vmem(count):
    return [pl.BlockSpec(memory_space=pltpu.VMEM)] * count


def smem(count):
    return [pl.BlockSpec(memory_space=pltpu.SMEM)] * count


def hbm(count):
    return [pl.BlockSpec(memory_space=pl.ANY)] * count


def limit(mebibytes):
    return pltpu.CompilerParams(vmem_limit_bytes=mebibytes * 1024 * 1024)


f32, bf16 = (jnp.float32, jnp.bfloat16)


def shaped(*shape, dtype=jnp.float32):
    return jax.ShapeDtypeStruct(shape, dtype)


def stretch_shards(
    base, noise, cot, convolution_weight, mix_w, norm_gain, qkv_w, out_w, band_width, pairs
):
    n_sa = lax.axis_size("sa")
    z, b, n = (lax.axis_index("sa"), lax.axis_index("sb"), lax.axis_index("noise"))
    y, x = (b >> 1, b & 1)
    features = base.shape[1]

    early, late = pl.pallas_call(
        pack_kernel,
        out_shape=(shaped(192, CHUNK, dtype=bf16), shaped(160, CHUNK, dtype=bf16)),
        in_specs=vmem(4),
        out_specs=tuple(vmem(2)),
        compiler_params=limit(8),
    )(convolution_weight, mix_w, qkv_w, out_w)
    early = lax.all_gather(early, ("sa", "sb"), axis=0, tiled=False)
    late = lax.all_gather(late, ("sa", "sb"), axis=0, tiled=False)

    def to_sample(shift):
        return routes(n_sa, lambda z, y, x, c: (z, c, (x + shift) % 2, y))

    got = [
        permuted(jnp.where(x == shift, noise[0], noise[1]), to_sample(shift))
        for shift in range(2)
    ]
    even = x == 0
    noise_half = jnp.concatenate([jnp.where(even, got[0], got[1]), jnp.where(even, got[1], got[0])], axis=0)
    both = jnp.stack([base, cot])
    across = permuted(both, routes(n_sa, lambda z, y, x, c: (z, 1 - y, x, 1 - c) if y != c else None))
    current = jnp.where(y == n, both, across)
    beside = permuted(current, routes(n_sa, lambda z, y, x, c: (z, y, 1 - x, c)))
    halves = jnp.concatenate([jnp.where(even, current, beside), jnp.where(even, beside, current)], axis=1)
    edge_route = routes(n_sa, lambda z, y, x, c: (z - 1, y, x, 1) if c == 0 else (z + 1, y, x, 0))
    core_route = routes(n_sa, lambda z, y, x, c: (z, y, x, 1 - c))
    mine = jnp.stack([noise_half, halves[0]])
    edge = permuted(jnp.where(n == 0, mine[:, :48], mine[:, 16:]), edge_route)
    wide = jnp.concatenate([jnp.where(n == 0, edge, mine[:, :48])] + [jnp.where(n == 0, mine, jnp.concatenate([mine[:, 48:], edge], axis=1))], axis=1)
    swap = permuted(jnp.concatenate([wide.reshape(224, features), halves[1]], axis=0), core_route)
    wide_other = swap[:224].reshape(2, 112, features)
    whole = jnp.concatenate([jnp.where(n == 0, wide, wide_other), jnp.where(n == 0, wide_other, wide)], axis=1)
    noise_rows, base_rows = whole[0], whole[1]
    cot_rows = jnp.concatenate(
        [jnp.where(n == 0, halves[1], swap[224:]), jnp.where(n == 0, swap[224:], halves[1])], axis=0
    )
    gain = norm_gain.reshape(1, features)

    early_other = permuted(early, core_route)
    normed, resid, inv_rms, hidden, conv, mix = pl.pallas_call(
        forward_kernel,
        out_shape=(
            shaped(192, features, dtype=bf16), shaped(128, features), shaped(128, 1), shaped(128, HID),
            shaped(3, features, HID, dtype=bf16), shaped(HID, features, dtype=bf16),
        ),
        in_specs=vmem(5),
        out_specs=tuple(vmem(4) + hbm(2)),
        scratch_shapes=[
            pltpu.VMEM((3, features, HID), bf16), pltpu.VMEM((HID, features), bf16),
            pltpu.VMEM((224, features), f32), pltpu.VMEM((224, features), bf16),
            pltpu.SemaphoreType.DMA((2,)),
        ],
        compiler_params=limit(28),
    )(noise_rows, base_rows, early, early_other, gain)
    late_other = permuted(late, core_route)
    d_q, d_kv, send, qkv = pl.pallas_call(
        attention_kernel,
        out_shape=(
            shaped(128, 256), shaped(128, 640), shaped(32, 640, dtype=bf16), shaped(features, 896, dtype=bf16)
        ),
        in_specs=smem(2) + vmem(4),
        out_specs=tuple(vmem(3) + hbm(1)),
        scratch_shapes=[
            pltpu.VMEM((features, 896), bf16), pltpu.VMEM((HEADS * VAL, features), bf16),
            pltpu.SemaphoreType.DMA((1,)),
        ],
        compiler_params=limit(24),
    )(band_width, pairs, normed, cot_rows, late, late_other)

    received = permuted(send, edge_route)
    d_hidden, d_resid, send = pl.pallas_call(
        norm_kernel,
        out_shape=(shaped(128, HID, dtype=bf16), shaped(64, features), shaped(16, HID, dtype=bf16)),
        in_specs=vmem(10),
        out_specs=tuple(vmem(3)),
        scratch_shapes=[
            pltpu.VMEM((128, 640), f32), pltpu.VMEM((128, features), f32), pltpu.VMEM((128, features), f32),
        ],
        compiler_params=limit(16),
    )(d_q, d_kv, received, resid, inv_rms, hidden, cot_rows, gain, mix, qkv)

    received = permuted(send, edge_route)
    keep, send = pl.pallas_call(
        taps_kernel,
        out_shape=(shaped(32, features), shaped(32, features, dtype=bf16)),
        in_specs=vmem(6),
        out_specs=tuple(vmem(2)),
        scratch_shapes=[pltpu.VMEM((96, HID), bf16), pltpu.VMEM((64, features), f32)],
        compiler_params=limit(16),
    )(d_hidden, received, d_resid, noise_rows, base_rows, conv)

    received = permuted(send, routes(n_sa, lambda z, y, x, c: (z, y, 1 - x, c)))
    partial = (keep + received.astype(f32)).astype(bf16)
    first_sum = permuted(
        partial, routes(n_sa, lambda z, y, x, c: (z, c, x, c) if y != c else (z, y, x, 1 - c))
    )
    second_sum = permuted(partial, routes(n_sa, lambda z, y, x, c: (z, c, x, 1 - c) if y != c else None))
    other = jnp.where(y == n, partial, second_sum)
    return (first_sum.astype(f32) + other.astype(f32)) * 0.25


def solution(mesh):
    fits = mesh.shape["sb"] == 4 and mesh.shape["noise"] == 2 and HEADS == 4

    def body(*arrays):
        if fits and arrays[0].shape[0] == 32 and arrays[1].shape[0] == 2 and TILE == 128:
            if arrays[0].shape[1] == 1536 and mesh.shape["sa"] == 4:
                return stretch_shards(*arrays)
        return shards(*arrays)

    return jax.shard_map(
        body,
        mesh=mesh,
        in_specs=(
            P(("sa", "sb"), None),
            P("noise", ("sa", "sb"), None),
            P(("sa", "sb"), None),
            P(None, "sa", None),
            P("sa", None),
            P(),
            P("sa", None),
            P("sa", None),
            P(),
            P(),
        ),
        out_specs=P(("sa", "sb"), None),
        check_vma=False,
    )
```

```python
import jax
import jax.numpy as jnp
from jax import lax
from jax.experimental import pallas as pl
from jax.experimental.pallas import tpu as pltpu
from jax.sharding import PartitionSpec as P

HID = 384
HEADS = 4
KEY = 64
VAL = 96
DILATION_BINS = 16
BAND = 32
TILE = 128


ROOT_TWO_PI = 0.7978845608
CUBIC = 0.044715


def extended(value, sides, width):
    for axis, dim in sides:
        peers, length = (lax.axis_size(axis), value.shape[dim])
        up = [(i, (i + 1) % peers) for i in range(peers - 1)]
        down = [(j, i) for i, j in up]
        last = lax.slice_in_dim(value, length - width, length, axis=dim)
        leading = lax.slice_in_dim(value, 0, width, axis=dim)
        before = lax.ppermute(last, axis, up)
        after = lax.ppermute(leading, axis, down)
        value = jnp.concatenate([before, value, after], axis=dim)
    return value


def from_behind(block, axis, distance):
    devices = range(lax.axis_size(axis))
    route = [(i - distance, i) for i in devices if i - distance in devices]
    return lax.ppermute(block, axis, route)


def gelu_tanh(values):
    inner = ROOT_TWO_PI * (values + CUBIC * values * values * values)
    return 0.5 * values * (1.0 + jnp.tanh(inner))


def gelu_slope(values):
    tangent = jnp.tanh(ROOT_TWO_PI * (values + CUBIC * values * values * values))
    return 0.5 * (1.0 + tangent) + 0.5 * values * (1.0 - tangent * tangent) * ROOT_TWO_PI * (
        1.0 + 3.0 * CUBIC * values * values
    )


def shards(base, noise, cot, convolution_weight, mix_w, norm_gain, qkv_w, out_w, band_width, pairs):
    conv_full, mix_full, qkv_full, out_full = (
        lax.all_gather(convolution_weight, "sa", axis=1, tiled=True),
        lax.all_gather(mix_w, "sa", axis=0, tiled=True),
        lax.all_gather(qkv_w, "sa", axis=0, tiled=True),
        lax.all_gather(out_w, "sa", axis=0, tiled=True),
    )
    sequence_bins = base.shape[0]
    samples_dev = noise.shape[0]
    stretch = sequence_bins * lax.axis_size("sb")
    sequence_length = stretch * lax.axis_size("sa")
    heads_key = HEADS * KEY
    heads_val = HEADS * VAL
    width = sequence_bins + 2 * BAND
    scale = KEY ** (-0.5)
    stretch_first = lax.axis_index("sa") * stretch
    first_row = stretch_first + lax.axis_index("sb") * sequence_bins
    row_pos = first_row + jnp.arange(sequence_bins, dtype=jnp.int32)
    ext_pos = first_row - BAND + jnp.arange(width, dtype=jnp.int32)
    stretch_pos = stretch_first + jnp.arange(stretch, dtype=jnp.int32)
    tiles = sequence_length // TILE
    tile_ids = jnp.arange(tiles, dtype=jnp.int32)
    pick_query = (pairs[:, 0][:, None] == tile_ids[None, :]).astype(jnp.float32)
    pick_key = (pairs[:, 1][:, None] == tile_ids[None, :]).astype(jnp.float32)
    table = jnp.dot(pick_query.T, pick_key)
    own_select = ((row_pos // TILE)[:, None] == tile_ids[None, :]).astype(jnp.float32)
    stretch_select = ((stretch_pos // TILE)[:, None] == tile_ids[None, :]).astype(jnp.float32)
    pair_own_rows = jnp.dot(jnp.dot(own_select, table), stretch_select.T) > 0.5
    pair_own_keys = jnp.dot(jnp.dot(stretch_select, table), own_select.T) > 0.5
    inside = (ext_pos >= 0) & (ext_pos < sequence_length)
    band_mask = inside[None, None, :] & (
        jnp.abs(row_pos[:, None] - ext_pos[None, :])[None] <= band_width[:, None, None]
    )
    far_rows = jnp.abs(row_pos[:, None] - stretch_pos[None, :])[None] > band_width[:, None, None]
    pair_mask = pair_own_rows[None] & far_rows
    key_mask = pair_own_keys[None] & jnp.transpose(far_rows, (0, 2, 1))
    noisy = base.astype(jnp.float32)[None] + noise.astype(jnp.float32)
    gelu_input = gelu_tanh(noisy).astype(jnp.bfloat16)
    gelu_extended = extended(gelu_input, ((("sa", "sb"), 1),), DILATION_BINS)
    hidden_state = jnp.zeros((samples_dev, sequence_bins, HID), jnp.float32)
    for tap_index in range(3):
        hidden_state = hidden_state + jnp.einsum(
            "nbd,dc->nbc",
            gelu_extended[:, tap_index * DILATION_BINS : tap_index * DILATION_BINS + sequence_bins],
            conv_full[tap_index],
            preferred_element_type=jnp.float32,
        )
    act = gelu_tanh(hidden_state).astype(jnp.bfloat16)
    resid = noisy + jnp.einsum("nbc,cd->nbd", act, mix_full, preferred_element_type=jnp.float32)
    inv_rms = lax.rsqrt(jnp.mean(resid * resid, axis=-1, keepdims=True) + 1e-06)
    normed = (resid * inv_rms * norm_gain).astype(jnp.bfloat16)
    proj = jnp.einsum("nbd,dc->nbc", normed, qkv_full, preferred_element_type=jnp.float32).astype(
        jnp.bfloat16
    )
    queries = proj[..., :heads_key].reshape(samples_dev, sequence_bins, HEADS, KEY)
    key_vals = proj[..., heads_key:]
    kv_ext = extended(key_vals, ((("sa", "sb"), 1),), BAND)
    kv_all = lax.all_gather(key_vals, "sb", axis=1, tiled=True)
    keys_ext = kv_ext[..., :heads_key].reshape(samples_dev, width, HEADS, KEY)
    vals_ext = kv_ext[..., heads_key:].reshape(samples_dev, width, HEADS, VAL)
    keys_all = kv_all[..., :heads_key].reshape(samples_dev, stretch, HEADS, KEY)
    vals_all = kv_all[..., heads_key:].reshape(samples_dev, stretch, HEADS, VAL)
    score_band = (
        jnp.einsum("nihd,njhd->nhij", queries, keys_ext, preferred_element_type=jnp.float32) * scale
    )
    score_band = jnp.where(band_mask[None], score_band, -1e30)
    raw_pair = jnp.einsum("nihd,njhd->nhij", queries, keys_all, preferred_element_type=jnp.float32)
    score_pair = jnp.where(pair_mask[None], raw_pair * scale, -1e30)
    top = jnp.maximum(jnp.max(score_band, axis=-1), jnp.max(score_pair, axis=-1))
    total = jnp.sum(jnp.where(band_mask[None], jnp.exp(score_band - top[..., None]), 0.0), axis=-1)
    total = total + jnp.sum(
        jnp.where(pair_mask[None], jnp.exp(score_pair - top[..., None]), 0.0), axis=-1
    )
    lse = top + jnp.log(total)
    prob_band = jnp.where(band_mask[None], jnp.exp(score_band - lse[..., None]), 0.0)
    prob_pair = jnp.where(pair_mask[None], jnp.exp(score_pair - lse[..., None]), 0.0)
    band_b = prob_band.astype(jnp.bfloat16)
    pair_b = prob_pair.astype(jnp.bfloat16)
    attn = jnp.einsum("nhij,njhe->nihe", band_b, vals_ext, preferred_element_type=jnp.float32)
    attn = attn + jnp.einsum(
        "nhij,njhe->nihe", pair_b, vals_all, preferred_element_type=jnp.float32
    )
    d_att = jnp.dot(cot, out_full.T, preferred_element_type=jnp.float32).astype(jnp.bfloat16)
    d_att_heads = d_att.reshape(sequence_bins, HEADS, VAL)
    delta = jnp.transpose(jnp.sum(d_att_heads.astype(jnp.float32)[None] * attn, axis=-1), (0, 2, 1))
    d_prob_band = jnp.einsum(
        "ihe,njhe->nhij", d_att_heads, vals_ext, preferred_element_type=jnp.float32
    )
    d_prob_pair = jnp.einsum(
        "ihe,njhe->nhij", d_att_heads, vals_all, preferred_element_type=jnp.float32
    )
    d_score_band = (prob_band * (d_prob_band - delta[..., None]) * scale).astype(jnp.bfloat16)
    d_score_pair = (prob_pair * (d_prob_pair - delta[..., None]) * scale).astype(jnp.bfloat16)
    d_query = jnp.einsum(
        "nhij,njhd->nihd", d_score_band, keys_ext, preferred_element_type=jnp.float32
    )
    d_query = d_query + jnp.einsum(
        "nhij,njhd->nihd", d_score_pair, keys_all, preferred_element_type=jnp.float32
    )
    d_key_ext = jnp.einsum(
        "nhij,nihd->njhd", d_score_band, queries, preferred_element_type=jnp.float32
    )
    d_val_ext = jnp.einsum(
        "nhij,ihe->njhe", band_b, d_att_heads, preferred_element_type=jnp.float32
    )
    d_kv_ext = jnp.concatenate(
        [
            d_key_ext.reshape(samples_dev, width, heads_key),
            d_val_ext.reshape(samples_dev, width, heads_val),
        ],
        axis=2,
    )
    from_right = from_behind(d_kv_ext[:, :BAND].astype(jnp.bfloat16), ("sa", "sb"), -1).astype(
        jnp.float32
    )
    from_left = from_behind(
        d_kv_ext[:, BAND + sequence_bins :].astype(jnp.bfloat16), ("sa", "sb"), 1
    ).astype(jnp.float32)
    d_key_vals = d_kv_ext[:, BAND : BAND + sequence_bins]
    d_key_vals = d_key_vals + from_left
    d_key_vals = d_key_vals + from_right
    statistics = jnp.stack([lse, delta], axis=1)
    query_rows = proj[..., :heads_key]
    queries_all, d_att_all = (
        lax.all_gather(query_rows, "sb", axis=1, tiled=True),
        lax.all_gather(d_att, "sb", axis=0, tiled=True),
    )
    stats_all = lax.all_gather(statistics, "sb", axis=3, tiled=True)
    queries_all = queries_all.reshape(samples_dev, stretch, HEADS, KEY)
    d_att_all = d_att_all.reshape(stretch, HEADS, VAL)
    keys_own = key_vals[..., :heads_key].reshape(samples_dev, sequence_bins, HEADS, KEY)
    vals_own = key_vals[..., heads_key:].reshape(samples_dev, sequence_bins, HEADS, VAL)
    score_key = (
        jnp.einsum("nihd,njhd->nhij", queries_all, keys_own, preferred_element_type=jnp.float32)
        * scale
    )
    prob_key = jnp.where(key_mask[None], jnp.exp(score_key - stats_all[:, 0][..., None]), 0.0)
    d_val_pair = jnp.einsum(
        "nhij,ihe->njhe",
        prob_key.astype(jnp.bfloat16),
        d_att_all,
        preferred_element_type=jnp.float32,
    )
    d_prob_key = jnp.einsum(
        "ihe,njhe->nhij", d_att_all, vals_own, preferred_element_type=jnp.float32
    )
    d_score_key = (prob_key * (d_prob_key - stats_all[:, 1][..., None]) * scale).astype(
        jnp.bfloat16
    )
    d_key_pair = jnp.einsum(
        "nhij,nihd->njhd", d_score_key, queries_all, preferred_element_type=jnp.float32
    )
    d_key_vals = d_key_vals + jnp.concatenate(
        [
            d_key_pair.reshape(samples_dev, sequence_bins, heads_key),
            d_val_pair.reshape(samples_dev, sequence_bins, heads_val),
        ],
        axis=2,
    )
    d_proj = jnp.concatenate(
        [d_query.reshape(samples_dev, sequence_bins, heads_key), d_key_vals], axis=2
    ).astype(jnp.bfloat16)
    d_normed = jnp.einsum("nbc,dc->nbd", d_proj, qkv_full, preferred_element_type=jnp.float32)
    gained = norm_gain * d_normed
    d_resid = (
        cot.astype(jnp.float32)[None]
        + inv_rms * gained
        - resid * inv_rms * inv_rms * inv_rms * jnp.mean(resid * gained, axis=-1, keepdims=True)
    )
    d_act = jnp.einsum(
        "nbd,cd->nbc", d_resid.astype(jnp.bfloat16), mix_full, preferred_element_type=jnp.float32
    )
    hidden_gradient = (d_act * gelu_slope(hidden_state)).astype(jnp.bfloat16)
    gradient_extended = extended(hidden_gradient, ((("sa", "sb"), 1),), DILATION_BINS)
    d_gelu_in = jnp.zeros((samples_dev, sequence_bins, base.shape[1]), jnp.float32)
    for tap_index in range(3):
        start_offset = (2 - tap_index) * DILATION_BINS
        d_gelu_in = d_gelu_in + jnp.einsum(
            "nbc,dc->nbd",
            gradient_extended[:, start_offset : start_offset + sequence_bins],
            conv_full[tap_index],
            preferred_element_type=jnp.float32,
        )
    grads = d_resid + d_gelu_in * gelu_slope(noisy)
    summed = lax.psum(jnp.sum(grads, axis=0).astype(jnp.bfloat16), "noise").astype(jnp.float32)
    return summed / (samples_dev * lax.axis_size("noise"))


def permuted(value, pairs):
    return lax.ppermute(value, ("sa", "sb", "noise"), pairs)


def routes(n_sa, route):
    flat = lambda z, y, x, c: ((z * 2 + y) * 2 + x) * 2 + c
    pairs = []
    for z in range(n_sa):
        for y in range(2):
            for x in range(2):
                for c in range(2):
                    target = route(z, y, x, c)
                    if target is not None and 0 <= target[0] < n_sa:
                        pairs.append((flat(z, y, x, c), flat(*target)))
    return pairs


def position():
    b = lax.axis_index("sb")
    return lax.axis_index("sa"), b // 2, lax.rem(b, 2), lax.axis_index("noise")


def pack_kernel(conv, mix, qkv, out, early, late):
    z, y, x, n = position()
    b = 2 * y + x
    part = b * 2 + n
    rows = pl.ds(pl.multiple_of(part * 48, 16), 48)
    half = pl.ds(pl.multiple_of(n * 48, 16), 48)
    columns = pl.ds(pl.multiple_of(b * 384, 128), 384)
    for t in range(3):
        early[pl.ds(48 * t, 48), :] = conv[t, rows, :]
    early[pl.ds(144, 48), :] = mix[half, columns]
    late[pl.ds(0, 48), :] = out[half, columns]
    for k in range(2):
        late[pl.ds(48 + 48 * k, 48), :] = qkv[rows, pl.ds(384 * k, 384)]
    for k in range(3):
        third = pl.ds(pl.multiple_of(part * 48 + 16 * k, 16), 16)
        late[pl.ds(144, 16), pl.ds(128 * k, 128)] = qkv[third, pl.ds(768, 128)]


def nt(a, b):
    return lax.dot_general(a, b, (((1,), (1,)), ((), ())), preferred_element_type=jnp.float32)


def tn(a, b):
    return lax.dot_general(a, b, (((0,), (0,)), ((), ())), preferred_element_type=jnp.float32)


def nn(a, b):
    return jnp.dot(a, b, preferred_element_type=jnp.float32)


CHUNK = 384


def chunk(c):
    return pl.ds(pl.multiple_of(c * CHUNK, 128), CHUNK)


def arrived(z, y, x, n, same, other):
    for j in range(3):
        for core, (straight, beside, across, diagonal_a, diagonal_b) in enumerate((same, other)):
            half = diagonal_a.shape[1]
            for dy in range(2):
                for dx in range(2):
                    if dy and dx:
                        first, second = diagonal_a[j], diagonal_b[j]
                    else:
                        whole = across if dy else beside if dx else straight
                        first, second = whole[j, pl.ds(0, half), :], whole[j, pl.ds(half, half), :]
                    yield j, z ^ (j + 1), y ^ dy, x ^ dx, n ^ core, first, second


def times(value, factor, unit):
    return pl.multiple_of(value * factor, unit)


def forward_kernel(
    noise, base, *refs,
):
    own_conv, own_mix = refs[:2]
    same, other = refs[2:7], refs[7:12]
    (
        gain, normed_out, resid_out, inv_out, hidden_out, conv_out, mix_out,
        conv, mix, noisy, gelu_in, sems,
    ) = refs[12:]
    z, y, x, n = position()

    for t in range(3):
        conv[t, pl.ds(times(z, 384, 128), 384), :] = own_conv[t]
    mix[pl.ds(times(z, 96, 32), 96), :] = own_mix[...]
    for _, sz, sy, sx, sn, first, second in arrived(z, y, x, n, same, other):
        b = 2 * sy + sx
        rows = pl.ds(pl.multiple_of(sz * 384 + (b * 2 + sn) * 48, 16), 48)
        conv[0, rows, :] = first[:48]
        conv[1, rows, :] = first[48:]
        conv[2, rows, :] = second[:48]
        mix[pl.ds(pl.multiple_of(sz * 96 + sn * 48, 16), 48), pl.ds(times(b, 384, 128), 384)] = second[48:]
    copies = [
        pltpu.make_async_copy(s, d, sems.at[i]) for i, (s, d) in enumerate(((conv, conv_out), (mix, mix_out)))
    ]
    for copy in copies:
        copy.start()

    def activate(c, _):
        values = base[:, chunk(c)].astype(jnp.float32) + noise[:, chunk(c)].astype(jnp.float32)
        noisy[:, chunk(c)] = values
        gelu_in[:, chunk(c)] = gelu_tanh(values).astype(jnp.bfloat16)
        return 0

    lax.fori_loop(0, 4, activate, 0)

    def convolve(c, total):
        for t in range(3):
            total = total + nn(gelu_in[pl.ds(16 * t, 192), chunk(c)], conv[t, chunk(c), :])
        return total

    hidden = lax.fori_loop(0, 4, convolve, jnp.zeros((192, HID), jnp.float32))
    hidden_out[...] = hidden[32:160]
    act = gelu_tanh(hidden).astype(jnp.bfloat16)

    def mixing(c, squares):
        resid = noisy[pl.ds(16, 192), chunk(c)] + nn(act, mix[:, chunk(c)])
        noisy[pl.ds(16, 192), chunk(c)] = resid
        resid_out[:, chunk(c)] = resid[32:160]
        return squares + jnp.sum(resid * resid, axis=1, keepdims=True)

    squares = lax.fori_loop(0, 4, mixing, jnp.zeros((192, 1), jnp.float32))
    inv_rms = lax.rsqrt(squares * (1.0 / 1536) + 1e-06)
    inv_out[...] = inv_rms[32:160]

    def normalise(c, _):
        normed = noisy[pl.ds(16, 192), chunk(c)] * inv_rms * gain[:, chunk(c)]
        normed_out[:, chunk(c)] = normed.astype(jnp.bfloat16)
        return 0

    lax.fori_loop(0, 4, normalise, 0)
    for copy in copies:
        copy.wait()


def attention_kernel(band, pairs, normed, cot, *refs):
    own_qkv, own_out = refs[:2]
    same, other = refs[2:7], refs[7:12]
    d_q_out, d_kv_out, send, qkv_out, qkv, out, sems = refs[12:]
    z, y, x, n = position()
    length = lax.axis_size("sa") * 128
    first_bin = z * 128
    pair_flag = jnp.int32(0)
    for i in range(pairs.shape[0]):
        pair_flag = pair_flag | ((pairs[i, 0] == z) & (pairs[i, 1] == z)).astype(jnp.int32)

    own_rows = pl.ds(times(z, 384, 128), 384)
    qkv[own_rows, :] = own_qkv[...]
    out[pl.ds(times(z, 96, 32), 96), :] = own_out[...]
    proj = nn(normed[:, own_rows], own_qkv[...])
    done = 0
    for j, sz, sy, sx, sn, first, second in arrived(z, y, x, n, same, other):
        b = 2 * sy + sx
        row = sz * 384 + (b * 2 + sn) * 48
        out[pl.ds(pl.multiple_of(sz * 96 + sn * 48, 16), 48), pl.ds(times(b, 384, 128), 384)] = first[:48]
        qkv[pl.ds(pl.multiple_of(row, 16), 32), pl.ds(0, 384)] = first[48:]
        qkv[pl.ds(pl.multiple_of(row + 32, 16), 16), pl.ds(0, 384)] = second[:16]
        qkv[pl.ds(pl.multiple_of(row, 16), 48), pl.ds(384, 384)] = second[16:64]
        for k in range(3):
            third = pl.ds(pl.multiple_of(row + 16 * k, 16), 16)
            qkv[third, pl.ds(768, 128)] = second[64:, 128 * k : 128 * k + 128]
        done += 1
        if done % 8 == 0:
            rows = pl.ds(times(sz, 384, 128), 384)
            proj = proj + nn(normed[:, rows], qkv[rows, :])
    proj = proj.astype(jnp.bfloat16)
    copy = pltpu.make_async_copy(qkv, qkv_out, sems.at[0])
    copy.start()
    d_att = nt(cot[...], out[...]).astype(jnp.bfloat16)

    row = lax.broadcasted_iota(jnp.int32, (128, 192), 0)
    column = lax.broadcasted_iota(jnp.int32, (128, 192), 1) - 32
    inside = (column + first_bin >= 0) & (column + first_bin < length)
    paired = (column >= 0) & (column < 128) & (pair_flag > 0)
    apart = jnp.abs(row - column)
    scale = KEY ** (-0.5)
    d_queries, d_keys, d_values = [], [], []
    for h in range(HEADS):
        q = proj[32:160, KEY * h : KEY * (h + 1)]
        k = proj[:, HEADS * KEY + KEY * h : HEADS * KEY + KEY * (h + 1)]
        v = proj[:, 2 * HEADS * KEY + VAL * h : 2 * HEADS * KEY + VAL * (h + 1)]
        d_att_h = d_att[:, VAL * h : VAL * (h + 1)]
        allowed = inside & (paired | (apart <= band[h]))
        score = jnp.where(allowed, nt(q, k) * scale, -1e30)
        top = jnp.max(score, axis=1, keepdims=True)
        raised = jnp.where(allowed, jnp.exp(score - top), 0.0)
        prob = raised / jnp.sum(raised, axis=1, keepdims=True)
        prob_b = prob.astype(jnp.bfloat16)
        attn = nn(prob_b, v)
        delta = jnp.sum(d_att_h.astype(jnp.float32) * attn, axis=1, keepdims=True)
        d_score = (prob * (nt(d_att_h, v) - delta) * scale).astype(jnp.bfloat16)
        d_queries.append(nn(d_score, k))
        d_keys.append(tn(d_score, q))
        d_values.append(tn(prob_b, d_att_h))
    d_q_out[...] = jnp.concatenate(d_queries, axis=1)
    d_kv = jnp.concatenate(d_keys + d_values, axis=1)
    d_kv_out[...] = d_kv[32:160]
    send[...] = jnp.where(n == 0, d_kv[:32], d_kv[160:]).astype(jnp.bfloat16)
    copy.wait()


def norm_kernel(
    d_q, d_kv, received, resid, inv_rms_ref, hidden, cot, gain, mix, qkv,
    d_hidden_out, d_resid_out, send, total_kv, gained, d_resid_all,
):
    z, y, x, n = position()
    total_kv[...] = d_kv[...]
    edge = pl.ds(pl.multiple_of(n * 96, 32), 32)
    total_kv[edge, :] = total_kv[edge, :] + received[...].astype(jnp.float32)
    d_proj = jnp.concatenate([d_q[...], total_kv[...]], axis=1).astype(jnp.bfloat16)
    inv_rms = inv_rms_ref[...]

    def back(c, mean):
        part = gain[:, chunk(c)] * nt(d_proj, qkv[chunk(c), :])
        gained[:, chunk(c)] = part
        return mean + jnp.sum(resid[:, chunk(c)] * part, axis=1, keepdims=True)

    mean = lax.fori_loop(0, 4, back, jnp.zeros((128, 1), jnp.float32)) * (1.0 / 1536)
    cubed = inv_rms * inv_rms * inv_rms * mean

    def residual(c, total):
        d_resid = (
            cot[:, chunk(c)].astype(jnp.float32)
            + inv_rms * gained[:, chunk(c)]
            - resid[:, chunk(c)] * cubed
        )
        d_resid_all[:, chunk(c)] = d_resid
        return total + nt(d_resid.astype(jnp.bfloat16), mix[:, chunk(c)])

    d_act = lax.fori_loop(0, 4, residual, jnp.zeros((128, HID), jnp.float32))
    d_hidden = (d_act * gelu_slope(hidden[...])).astype(jnp.bfloat16)
    d_hidden_out[...] = d_hidden
    d_resid_out[...] = d_resid_all[pl.ds(pl.multiple_of(n * 64, 64), 64), :]

    @pl.when(n == 0)
    def _():
        send[...] = d_hidden[:16]

    @pl.when(n == 1)
    def _():
        send[...] = d_hidden[112:]


def taps_kernel(d_hidden, received, d_resid, noise, base, conv, keep, send, extended_ref, grads):
    z, y, x, n = position()

    @pl.when(n == 0)
    def _():
        extended_ref[pl.ds(0, 16), :] = received[...]
        extended_ref[pl.ds(16, 80), :] = d_hidden[pl.ds(0, 80), :]

    @pl.when(n == 1)
    def _():
        extended_ref[pl.ds(0, 80), :] = d_hidden[pl.ds(48, 80), :]
        extended_ref[pl.ds(80, 16), :] = received[...]

    rows = pl.ds(pl.multiple_of(48 + 64 * n, 16), 64)

    def taps(c, _):
        noisy = base[rows, chunk(c)].astype(jnp.float32) + noise[rows, chunk(c)].astype(jnp.float32)
        total = nt(extended_ref[pl.ds(32, 64), :], conv[0, chunk(c), :])
        total = total + nt(extended_ref[pl.ds(16, 64), :], conv[1, chunk(c), :])
        total = total + nt(extended_ref[pl.ds(0, 64), :], conv[2, chunk(c), :])
        grads[:, chunk(c)] = d_resid[:, chunk(c)] + total * gelu_slope(noisy)
        return 0

    lax.fori_loop(0, 4, taps, 0)
    keep[...] = grads[pl.ds(pl.multiple_of(32 * x, 32), 32), :]
    send[...] = grads[pl.ds(pl.multiple_of(32 - 32 * x, 32), 32), :].astype(jnp.bfloat16)


def vmem(count):
    return [pl.BlockSpec(memory_space=pltpu.VMEM)] * count


def smem(count):
    return [pl.BlockSpec(memory_space=pltpu.SMEM)] * count


def hbm(count):
    return [pl.BlockSpec(memory_space=pl.ANY)] * count


def limit(mebibytes):
    return pltpu.CompilerParams(vmem_limit_bytes=mebibytes * 1024 * 1024)


f32, bf16 = (jnp.float32, jnp.bfloat16)


def shaped(*shape, dtype=jnp.float32):
    return jax.ShapeDtypeStruct(shape, dtype)


def stretch_shards(
    base, noise, cot, convolution_weight, mix_w, norm_gain, qkv_w, out_w, band_width, pairs
):
    n_sa = lax.axis_size("sa")
    z, b, n = (lax.axis_index("sa"), lax.axis_index("sb"), lax.axis_index("noise"))
    y, x = (b >> 1, b & 1)
    features = base.shape[1]

    early, late = pl.pallas_call(
        pack_kernel,
        out_shape=(shaped(192, CHUNK, dtype=bf16), shaped(160, CHUNK, dtype=bf16)),
        in_specs=vmem(4),
        out_specs=tuple(vmem(2)),
        compiler_params=limit(8),
    )(convolution_weight, mix_w, qkv_w, out_w)
    def along_z(step):
        return routes(n_sa, lambda z, y, x, c: (z ^ step, y, x, c))

    x_route = routes(n_sa, lambda z, y, x, c: (z, y, 1 - x, c))
    y_route = routes(n_sa, lambda z, y, x, c: (z, 1 - y, x, c))
    core_route = routes(n_sa, lambda z, y, x, c: (z, y, x, 1 - c))

    def collected(piece):
        half = piece.shape[0] // 2
        straight = jnp.stack([permuted(piece, along_z(step)) for step in range(1, 4)])
        beside, across = permuted(straight, x_route), permuted(straight, y_route)
        diagonal_a = permuted(beside[:, :half], y_route)
        diagonal_b = permuted(across[:, half:], x_route)
        same = (straight, beside, across, diagonal_a, diagonal_b)
        return same + tuple(permuted(part, core_route) for part in same)

    early, late = collected(early), collected(late)

    def to_sample(shift):
        return routes(n_sa, lambda z, y, x, c: (z, c, (x + shift) % 2, y))

    got = [
        permuted(jnp.where(x == shift, noise[0], noise[1]), to_sample(shift))
        for shift in range(2)
    ]
    even = x == 0
    noise_half = jnp.concatenate([jnp.where(even, got[0], got[1]), jnp.where(even, got[1], got[0])], axis=0)
    both = jnp.stack([base, cot])
    across = permuted(both, routes(n_sa, lambda z, y, x, c: (z, 1 - y, x, 1 - c) if y != c else None))
    current = jnp.where(y == n, both, across)
    beside = permuted(current, x_route)
    halves = jnp.concatenate([jnp.where(even, current, beside), jnp.where(even, beside, current)], axis=1)
    edge_route = routes(n_sa, lambda z, y, x, c: (z - 1, y, x, 1) if c == 0 else (z + 1, y, x, 0))
    mine = jnp.stack([noise_half, halves[0]])
    edge = permuted(jnp.where(n == 0, mine[:, :48], mine[:, 16:]), edge_route)
    wide = jnp.concatenate([jnp.where(n == 0, edge, mine[:, :48])] + [jnp.where(n == 0, mine, jnp.concatenate([mine[:, 48:], edge], axis=1))], axis=1)
    swap = permuted(jnp.concatenate([wide.reshape(224, features), halves[1]], axis=0), core_route)
    wide_other = swap[:224].reshape(2, 112, features)
    whole = jnp.concatenate([jnp.where(n == 0, wide, wide_other), jnp.where(n == 0, wide_other, wide)], axis=1)
    noise_rows, base_rows = whole[0], whole[1]
    cot_rows = jnp.concatenate(
        [jnp.where(n == 0, halves[1], swap[224:]), jnp.where(n == 0, swap[224:], halves[1])], axis=0
    )
    gain = norm_gain.reshape(1, features)

    normed, resid, inv_rms, hidden, conv, mix = pl.pallas_call(
        forward_kernel,
        out_shape=(
            shaped(192, features, dtype=bf16), shaped(128, features), shaped(128, 1), shaped(128, HID),
            shaped(3, features, HID, dtype=bf16), shaped(HID, features, dtype=bf16),
        ),
        in_specs=vmem(15),
        out_specs=tuple(vmem(4) + hbm(2)),
        scratch_shapes=[
            pltpu.VMEM((3, features, HID), bf16), pltpu.VMEM((HID, features), bf16),
            pltpu.VMEM((224, features), f32), pltpu.VMEM((224, features), bf16),
            pltpu.SemaphoreType.DMA((2,)),
        ],
        compiler_params=limit(28),
    )(noise_rows, base_rows, convolution_weight, mix_w, *early, gain)
    d_q, d_kv, send, qkv = pl.pallas_call(
        attention_kernel,
        out_shape=(
            shaped(128, 256), shaped(128, 640), shaped(32, 640, dtype=bf16), shaped(features, 896, dtype=bf16)
        ),
        in_specs=smem(2) + vmem(14),
        out_specs=tuple(vmem(3) + hbm(1)),
        scratch_shapes=[
            pltpu.VMEM((features, 896), bf16), pltpu.VMEM((HEADS * VAL, features), bf16),
            pltpu.SemaphoreType.DMA((1,)),
        ],
        compiler_params=limit(24),
    )(band_width, pairs, normed, cot_rows, qkv_w, out_w, *late)

    received = permuted(send, edge_route)
    d_hidden, d_resid, send = pl.pallas_call(
        norm_kernel,
        out_shape=(shaped(128, HID, dtype=bf16), shaped(64, features), shaped(16, HID, dtype=bf16)),
        in_specs=vmem(10),
        out_specs=tuple(vmem(3)),
        scratch_shapes=[
            pltpu.VMEM((128, 640), f32), pltpu.VMEM((128, features), f32), pltpu.VMEM((128, features), f32),
        ],
        compiler_params=limit(16),
    )(d_q, d_kv, received, resid, inv_rms, hidden, cot_rows, gain, mix, qkv)

    received = permuted(send, edge_route)
    keep, send = pl.pallas_call(
        taps_kernel,
        out_shape=(shaped(32, features), shaped(32, features, dtype=bf16)),
        in_specs=vmem(6),
        out_specs=tuple(vmem(2)),
        scratch_shapes=[pltpu.VMEM((96, HID), bf16), pltpu.VMEM((64, features), f32)],
        compiler_params=limit(16),
    )(d_hidden, received, d_resid, noise_rows, base_rows, conv)

    received = permuted(send, x_route)
    partial = (keep + received.astype(f32)).astype(bf16)
    first_sum = permuted(
        partial, routes(n_sa, lambda z, y, x, c: (z, c, x, c) if y != c else (z, y, x, 1 - c))
    )
    second_sum = permuted(partial, routes(n_sa, lambda z, y, x, c: (z, c, x, 1 - c) if y != c else None))
    other = jnp.where(y == n, partial, second_sum)
    return (first_sum.astype(f32) + other.astype(f32)) * 0.25


def solution(mesh):
    fits = mesh.shape["sb"] == 4 and mesh.shape["noise"] == 2 and HEADS == 4

    def body(*arrays):
        if fits and arrays[0].shape[0] == 32 and arrays[1].shape[0] == 2 and TILE == 128:
            if arrays[0].shape[1] == 1536 and mesh.shape["sa"] == 4:
                return stretch_shards(*arrays)
        return shards(*arrays)

    return jax.shard_map(
        body,
        mesh=mesh,
        in_specs=(
            P(("sa", "sb"), None),
            P("noise", ("sa", "sb"), None),
            P(("sa", "sb"), None),
            P(None, "sa", None),
            P("sa", None),
            P(),
            P("sa", None),
            P("sa", None),
            P(),
            P(),
        ),
        out_specs=P(("sa", "sb"), None),
        check_vma=False,
    )
```

```python
import jax
import jax.numpy as jnp
from jax import lax
from jax.experimental import pallas as pl
from jax.experimental.pallas import tpu as pltpu
from jax.sharding import PartitionSpec as P

HID = 384
HEADS = 4
KEY = 64
VAL = 96
DILATION_BINS = 16
BAND = 32
TILE = 128


ROOT_TWO_PI = 0.7978845608
CUBIC = 0.044715


def extended(value, sides, width):
    for axis, dim in sides:
        peers, length = (lax.axis_size(axis), value.shape[dim])
        up = [(i, (i + 1) % peers) for i in range(peers - 1)]
        down = [(j, i) for i, j in up]
        last = lax.slice_in_dim(value, length - width, length, axis=dim)
        leading = lax.slice_in_dim(value, 0, width, axis=dim)
        before = lax.ppermute(last, axis, up)
        after = lax.ppermute(leading, axis, down)
        value = jnp.concatenate([before, value, after], axis=dim)
    return value


def from_behind(block, axis, distance):
    devices = range(lax.axis_size(axis))
    route = [(i - distance, i) for i in devices if i - distance in devices]
    return lax.ppermute(block, axis, route)


def gelu_tanh(values):
    inner = ROOT_TWO_PI * (values + CUBIC * values * values * values)
    return 0.5 * values * (1.0 + jnp.tanh(inner))


def gelu_slope(values):
    tangent = jnp.tanh(ROOT_TWO_PI * (values + CUBIC * values * values * values))
    return 0.5 * (1.0 + tangent) + 0.5 * values * (1.0 - tangent * tangent) * ROOT_TWO_PI * (
        1.0 + 3.0 * CUBIC * values * values
    )


def shards(base, noise, cot, convolution_weight, mix_w, norm_gain, qkv_w, out_w, band_width, pairs):
    conv_full, mix_full, qkv_full, out_full = (
        lax.all_gather(convolution_weight, "sa", axis=1, tiled=True),
        lax.all_gather(mix_w, "sa", axis=0, tiled=True),
        lax.all_gather(qkv_w, "sa", axis=0, tiled=True),
        lax.all_gather(out_w, "sa", axis=0, tiled=True),
    )
    sequence_bins = base.shape[0]
    samples_dev = noise.shape[0]
    stretch = sequence_bins * lax.axis_size("sb")
    sequence_length = stretch * lax.axis_size("sa")
    heads_key = HEADS * KEY
    heads_val = HEADS * VAL
    width = sequence_bins + 2 * BAND
    scale = KEY ** (-0.5)
    stretch_first = lax.axis_index("sa") * stretch
    first_row = stretch_first + lax.axis_index("sb") * sequence_bins
    row_pos = first_row + jnp.arange(sequence_bins, dtype=jnp.int32)
    ext_pos = first_row - BAND + jnp.arange(width, dtype=jnp.int32)
    stretch_pos = stretch_first + jnp.arange(stretch, dtype=jnp.int32)
    tiles = sequence_length // TILE
    tile_ids = jnp.arange(tiles, dtype=jnp.int32)
    pick_query = (pairs[:, 0][:, None] == tile_ids[None, :]).astype(jnp.float32)
    pick_key = (pairs[:, 1][:, None] == tile_ids[None, :]).astype(jnp.float32)
    table = jnp.dot(pick_query.T, pick_key)
    own_select = ((row_pos // TILE)[:, None] == tile_ids[None, :]).astype(jnp.float32)
    stretch_select = ((stretch_pos // TILE)[:, None] == tile_ids[None, :]).astype(jnp.float32)
    pair_own_rows = jnp.dot(jnp.dot(own_select, table), stretch_select.T) > 0.5
    pair_own_keys = jnp.dot(jnp.dot(stretch_select, table), own_select.T) > 0.5
    inside = (ext_pos >= 0) & (ext_pos < sequence_length)
    band_mask = inside[None, None, :] & (
        jnp.abs(row_pos[:, None] - ext_pos[None, :])[None] <= band_width[:, None, None]
    )
    far_rows = jnp.abs(row_pos[:, None] - stretch_pos[None, :])[None] > band_width[:, None, None]
    pair_mask = pair_own_rows[None] & far_rows
    key_mask = pair_own_keys[None] & jnp.transpose(far_rows, (0, 2, 1))
    noisy = base.astype(jnp.float32)[None] + noise.astype(jnp.float32)
    gelu_input = gelu_tanh(noisy).astype(jnp.bfloat16)
    gelu_extended = extended(gelu_input, ((("sa", "sb"), 1),), DILATION_BINS)
    hidden_state = jnp.zeros((samples_dev, sequence_bins, HID), jnp.float32)
    for tap_index in range(3):
        hidden_state = hidden_state + jnp.einsum(
            "nbd,dc->nbc",
            gelu_extended[:, tap_index * DILATION_BINS : tap_index * DILATION_BINS + sequence_bins],
            conv_full[tap_index],
            preferred_element_type=jnp.float32,
        )
    act = gelu_tanh(hidden_state).astype(jnp.bfloat16)
    resid = noisy + jnp.einsum("nbc,cd->nbd", act, mix_full, preferred_element_type=jnp.float32)
    inv_rms = lax.rsqrt(jnp.mean(resid * resid, axis=-1, keepdims=True) + 1e-06)
    normed = (resid * inv_rms * norm_gain).astype(jnp.bfloat16)
    proj = jnp.einsum("nbd,dc->nbc", normed, qkv_full, preferred_element_type=jnp.float32).astype(
        jnp.bfloat16
    )
    queries = proj[..., :heads_key].reshape(samples_dev, sequence_bins, HEADS, KEY)
    key_vals = proj[..., heads_key:]
    kv_ext = extended(key_vals, ((("sa", "sb"), 1),), BAND)
    kv_all = lax.all_gather(key_vals, "sb", axis=1, tiled=True)
    keys_ext = kv_ext[..., :heads_key].reshape(samples_dev, width, HEADS, KEY)
    vals_ext = kv_ext[..., heads_key:].reshape(samples_dev, width, HEADS, VAL)
    keys_all = kv_all[..., :heads_key].reshape(samples_dev, stretch, HEADS, KEY)
    vals_all = kv_all[..., heads_key:].reshape(samples_dev, stretch, HEADS, VAL)
    score_band = (
        jnp.einsum("nihd,njhd->nhij", queries, keys_ext, preferred_element_type=jnp.float32) * scale
    )
    score_band = jnp.where(band_mask[None], score_band, -1e30)
    raw_pair = jnp.einsum("nihd,njhd->nhij", queries, keys_all, preferred_element_type=jnp.float32)
    score_pair = jnp.where(pair_mask[None], raw_pair * scale, -1e30)
    top = jnp.maximum(jnp.max(score_band, axis=-1), jnp.max(score_pair, axis=-1))
    total = jnp.sum(jnp.where(band_mask[None], jnp.exp(score_band - top[..., None]), 0.0), axis=-1)
    total = total + jnp.sum(
        jnp.where(pair_mask[None], jnp.exp(score_pair - top[..., None]), 0.0), axis=-1
    )
    lse = top + jnp.log(total)
    prob_band = jnp.where(band_mask[None], jnp.exp(score_band - lse[..., None]), 0.0)
    prob_pair = jnp.where(pair_mask[None], jnp.exp(score_pair - lse[..., None]), 0.0)
    band_b = prob_band.astype(jnp.bfloat16)
    pair_b = prob_pair.astype(jnp.bfloat16)
    attn = jnp.einsum("nhij,njhe->nihe", band_b, vals_ext, preferred_element_type=jnp.float32)
    attn = attn + jnp.einsum(
        "nhij,njhe->nihe", pair_b, vals_all, preferred_element_type=jnp.float32
    )
    d_att = jnp.dot(cot, out_full.T, preferred_element_type=jnp.float32).astype(jnp.bfloat16)
    d_att_heads = d_att.reshape(sequence_bins, HEADS, VAL)
    delta = jnp.transpose(jnp.sum(d_att_heads.astype(jnp.float32)[None] * attn, axis=-1), (0, 2, 1))
    d_prob_band = jnp.einsum(
        "ihe,njhe->nhij", d_att_heads, vals_ext, preferred_element_type=jnp.float32
    )
    d_prob_pair = jnp.einsum(
        "ihe,njhe->nhij", d_att_heads, vals_all, preferred_element_type=jnp.float32
    )
    d_score_band = (prob_band * (d_prob_band - delta[..., None]) * scale).astype(jnp.bfloat16)
    d_score_pair = (prob_pair * (d_prob_pair - delta[..., None]) * scale).astype(jnp.bfloat16)
    d_query = jnp.einsum(
        "nhij,njhd->nihd", d_score_band, keys_ext, preferred_element_type=jnp.float32
    )
    d_query = d_query + jnp.einsum(
        "nhij,njhd->nihd", d_score_pair, keys_all, preferred_element_type=jnp.float32
    )
    d_key_ext = jnp.einsum(
        "nhij,nihd->njhd", d_score_band, queries, preferred_element_type=jnp.float32
    )
    d_val_ext = jnp.einsum(
        "nhij,ihe->njhe", band_b, d_att_heads, preferred_element_type=jnp.float32
    )
    d_kv_ext = jnp.concatenate(
        [
            d_key_ext.reshape(samples_dev, width, heads_key),
            d_val_ext.reshape(samples_dev, width, heads_val),
        ],
        axis=2,
    )
    from_right = from_behind(d_kv_ext[:, :BAND].astype(jnp.bfloat16), ("sa", "sb"), -1).astype(
        jnp.float32
    )
    from_left = from_behind(
        d_kv_ext[:, BAND + sequence_bins :].astype(jnp.bfloat16), ("sa", "sb"), 1
    ).astype(jnp.float32)
    d_key_vals = d_kv_ext[:, BAND : BAND + sequence_bins]
    d_key_vals = d_key_vals + from_left
    d_key_vals = d_key_vals + from_right
    statistics = jnp.stack([lse, delta], axis=1)
    query_rows = proj[..., :heads_key]
    queries_all, d_att_all = (
        lax.all_gather(query_rows, "sb", axis=1, tiled=True),
        lax.all_gather(d_att, "sb", axis=0, tiled=True),
    )
    stats_all = lax.all_gather(statistics, "sb", axis=3, tiled=True)
    queries_all = queries_all.reshape(samples_dev, stretch, HEADS, KEY)
    d_att_all = d_att_all.reshape(stretch, HEADS, VAL)
    keys_own = key_vals[..., :heads_key].reshape(samples_dev, sequence_bins, HEADS, KEY)
    vals_own = key_vals[..., heads_key:].reshape(samples_dev, sequence_bins, HEADS, VAL)
    score_key = (
        jnp.einsum("nihd,njhd->nhij", queries_all, keys_own, preferred_element_type=jnp.float32)
        * scale
    )
    prob_key = jnp.where(key_mask[None], jnp.exp(score_key - stats_all[:, 0][..., None]), 0.0)
    d_val_pair = jnp.einsum(
        "nhij,ihe->njhe",
        prob_key.astype(jnp.bfloat16),
        d_att_all,
        preferred_element_type=jnp.float32,
    )
    d_prob_key = jnp.einsum(
        "ihe,njhe->nhij", d_att_all, vals_own, preferred_element_type=jnp.float32
    )
    d_score_key = (prob_key * (d_prob_key - stats_all[:, 1][..., None]) * scale).astype(
        jnp.bfloat16
    )
    d_key_pair = jnp.einsum(
        "nhij,nihd->njhd", d_score_key, queries_all, preferred_element_type=jnp.float32
    )
    d_key_vals = d_key_vals + jnp.concatenate(
        [
            d_key_pair.reshape(samples_dev, sequence_bins, heads_key),
            d_val_pair.reshape(samples_dev, sequence_bins, heads_val),
        ],
        axis=2,
    )
    d_proj = jnp.concatenate(
        [d_query.reshape(samples_dev, sequence_bins, heads_key), d_key_vals], axis=2
    ).astype(jnp.bfloat16)
    d_normed = jnp.einsum("nbc,dc->nbd", d_proj, qkv_full, preferred_element_type=jnp.float32)
    gained = norm_gain * d_normed
    d_resid = (
        cot.astype(jnp.float32)[None]
        + inv_rms * gained
        - resid * inv_rms * inv_rms * inv_rms * jnp.mean(resid * gained, axis=-1, keepdims=True)
    )
    d_act = jnp.einsum(
        "nbd,cd->nbc", d_resid.astype(jnp.bfloat16), mix_full, preferred_element_type=jnp.float32
    )
    hidden_gradient = (d_act * gelu_slope(hidden_state)).astype(jnp.bfloat16)
    gradient_extended = extended(hidden_gradient, ((("sa", "sb"), 1),), DILATION_BINS)
    d_gelu_in = jnp.zeros((samples_dev, sequence_bins, base.shape[1]), jnp.float32)
    for tap_index in range(3):
        start_offset = (2 - tap_index) * DILATION_BINS
        d_gelu_in = d_gelu_in + jnp.einsum(
            "nbc,dc->nbd",
            gradient_extended[:, start_offset : start_offset + sequence_bins],
            conv_full[tap_index],
            preferred_element_type=jnp.float32,
        )
    grads = d_resid + d_gelu_in * gelu_slope(noisy)
    summed = lax.psum(jnp.sum(grads, axis=0).astype(jnp.bfloat16), "noise").astype(jnp.float32)
    return summed / (samples_dev * lax.axis_size("noise"))


def permuted(value, pairs):
    return lax.ppermute(value, ("sa", "sb", "noise"), pairs)


def routes(n_sa, route):
    flat = lambda z, y, x, c: ((z * 2 + y) * 2 + x) * 2 + c
    pairs = []
    for z in range(n_sa):
        for y in range(2):
            for x in range(2):
                for c in range(2):
                    target = route(z, y, x, c)
                    if target is not None and 0 <= target[0] < n_sa:
                        pairs.append((flat(z, y, x, c), flat(*target)))
    return pairs


def position():
    b = lax.axis_index("sb")
    return lax.axis_index("sa"), b // 2, lax.rem(b, 2), lax.axis_index("noise")


def half_index():
    return lax.rem(lax.axis_index("noise") + lax.axis_index("sa"), 2)


def pack_kernel(conv, mix, qkv, out, early, late):
    z, y, x, n = position()
    b = 2 * y + x
    part = b * 2 + n
    rows = pl.ds(pl.multiple_of(part * 48, 16), 48)
    half = pl.ds(pl.multiple_of(n * 48, 16), 48)
    columns = pl.ds(pl.multiple_of(b * 384, 128), 384)
    for t in range(3):
        early[pl.ds(48 * t, 48), :] = conv[t, rows, :]
    early[pl.ds(144, 48), :] = mix[half, columns]
    late[pl.ds(0, 48), :] = out[half, columns]
    for k in range(2):
        late[pl.ds(48 + 48 * k, 48), :] = qkv[rows, pl.ds(384 * k, 384)]
    for k in range(3):
        third = pl.ds(pl.multiple_of(part * 48 + 16 * k, 16), 16)
        late[pl.ds(144, 16), pl.ds(128 * k, 128)] = qkv[third, pl.ds(768, 128)]


def nt(a, b):
    return lax.dot_general(a, b, (((1,), (1,)), ((), ())), preferred_element_type=jnp.float32)


def tn(a, b):
    return lax.dot_general(a, b, (((0,), (0,)), ((), ())), preferred_element_type=jnp.float32)


def nn(a, b):
    return jnp.dot(a, b, preferred_element_type=jnp.float32)


CHUNK = 384


def chunk(c):
    return pl.ds(pl.multiple_of(c * CHUNK, 128), CHUNK)


def arrived(z, y, x, n, same, other):
    for j in range(3):
        for core, (straight, beside, across, diagonal_a, diagonal_b) in enumerate((same, other)):
            half = diagonal_a.shape[1]
            for dy in range(2):
                for dx in range(2):
                    if dy and dx:
                        first, second = diagonal_a[j], diagonal_b[j]
                    else:
                        whole = across if dy else beside if dx else straight
                        first, second = whole[j, pl.ds(0, half), :], whole[j, pl.ds(half, half), :]
                    yield j, z ^ (j + 1), y ^ dy, x ^ dx, n ^ core, first, second


def times(value, factor, unit):
    return pl.multiple_of(value * factor, unit)


def forward_kernel(
    blocks_even, blocks_odd, edge, other_even, other_odd, other_edge, *refs,
):
    own_conv, own_mix = refs[:2]
    same, other = refs[2:7], refs[7:12]
    (
        gain, normed_out, resid_out, inv_out, hidden_out, conv_out, mix_out,
        conv, mix, noisy, gelu_in, sems,
    ) = refs[12:]
    z, y, x, n = position()

    for t in range(3):
        conv[t, pl.ds(times(z, 384, 128), 384), :] = own_conv[t]
    mix[pl.ds(times(z, 96, 32), 96), :] = own_mix[...]
    for _, sz, sy, sx, sn, first, second in arrived(z, y, x, n, same, other):
        b = 2 * sy + sx
        rows = pl.ds(pl.multiple_of(sz * 384 + (b * 2 + sn) * 48, 16), 48)
        conv[0, rows, :] = first[:48]
        conv[1, rows, :] = first[48:]
        conv[2, rows, :] = second[:48]
        mix[pl.ds(pl.multiple_of(sz * 96 + sn * 48, 16), 48), pl.ds(times(b, 384, 128), 384)] = second[48:]
    copies = [
        pltpu.make_async_copy(s, d, sems.at[i]) for i, (s, d) in enumerate(((conv, conv_out), (mix, mix_out)))
    ]
    for copy in copies:
        copy.start()

    m = half_index()
    for half, (even, odd, outer) in (
        (m, (blocks_even, blocks_odd, edge)), (1 - m, (other_even, other_odd, other_edge))
    ):
        noisy[pl.ds(times(half, 176, 16), 48), :] = outer[...].astype(jnp.float32)
        for shift, block in enumerate((even, odd)):
            row = 48 + 64 * half + 32 * lax.rem(x + shift, 2)
            noisy[pl.ds(pl.multiple_of(row, 16), 32), :] = block[...].astype(jnp.float32)

    def activate(c, _):
        gelu_in[:, chunk(c)] = gelu_tanh(noisy[:, chunk(c)]).astype(jnp.bfloat16)
        return 0

    lax.fori_loop(0, 4, activate, 0)

    def convolve(c, total):
        for t in range(3):
            total = total + nn(gelu_in[pl.ds(16 * t, 192), chunk(c)], conv[t, chunk(c), :])
        return total

    hidden = lax.fori_loop(0, 4, convolve, jnp.zeros((192, HID), jnp.float32))
    hidden_out[...] = hidden[32:160]
    act = gelu_tanh(hidden).astype(jnp.bfloat16)

    def mixing(c, squares):
        resid = noisy[pl.ds(16, 192), chunk(c)] + nn(act, mix[:, chunk(c)])
        noisy[pl.ds(16, 192), chunk(c)] = resid
        resid_out[:, chunk(c)] = resid[32:160]
        return squares + jnp.sum(resid * resid, axis=1, keepdims=True)

    squares = lax.fori_loop(0, 4, mixing, jnp.zeros((192, 1), jnp.float32))
    inv_rms = lax.rsqrt(squares * (1.0 / 1536) + 1e-06)
    inv_out[...] = inv_rms[32:160]

    def normalise(c, _):
        normed = noisy[pl.ds(16, 192), chunk(c)] * inv_rms * gain[:, chunk(c)]
        normed_out[:, chunk(c)] = normed.astype(jnp.bfloat16)
        return 0

    lax.fori_loop(0, 4, normalise, 0)
    for copy in copies:
        copy.wait()


def attention_kernel(band, pairs, normed, cot_block, cot_beside, other_block, other_beside, *refs):
    own_qkv, own_out = refs[:2]
    same, other = refs[2:7], refs[7:12]
    d_q_out, d_kv_out, send, qkv_out, cot_out, qkv, out, sems = refs[12:]
    z, y, x, n = position()
    length = lax.axis_size("sa") * 128
    first_bin = z * 128
    pair_flag = jnp.int32(0)
    for i in range(pairs.shape[0]):
        pair_flag = pair_flag | ((pairs[i, 0] == z) & (pairs[i, 1] == z)).astype(jnp.int32)

    own_rows = pl.ds(times(z, 384, 128), 384)
    qkv[own_rows, :] = own_qkv[...]
    out[pl.ds(times(z, 96, 32), 96), :] = own_out[...]
    proj = nn(normed[:, own_rows], own_qkv[...])
    done = 0
    for j, sz, sy, sx, sn, first, second in arrived(z, y, x, n, same, other):
        b = 2 * sy + sx
        row = sz * 384 + (b * 2 + sn) * 48
        out[pl.ds(pl.multiple_of(sz * 96 + sn * 48, 16), 48), pl.ds(times(b, 384, 128), 384)] = first[:48]
        qkv[pl.ds(pl.multiple_of(row, 16), 32), pl.ds(0, 384)] = first[48:]
        qkv[pl.ds(pl.multiple_of(row + 32, 16), 16), pl.ds(0, 384)] = second[:16]
        qkv[pl.ds(pl.multiple_of(row, 16), 48), pl.ds(384, 384)] = second[16:64]
        for k in range(3):
            third = pl.ds(pl.multiple_of(row + 16 * k, 16), 16)
            qkv[third, pl.ds(768, 128)] = second[64:, 128 * k : 128 * k + 128]
        done += 1
        if done % 8 == 0:
            rows = pl.ds(times(sz, 384, 128), 384)
            proj = proj + nn(normed[:, rows], qkv[rows, :])
    proj = proj.astype(jnp.bfloat16)
    copy = pltpu.make_async_copy(qkv, qkv_out, sems.at[0])
    copy.start()
    m = half_index()
    for half, (block, beside) in ((m, (cot_block, cot_beside)), (1 - m, (other_block, other_beside))):
        for shift, rows in enumerate((block, beside)):
            row = 64 * half + 32 * lax.rem(x + shift, 2)
            cot_out[pl.ds(pl.multiple_of(row, 32), 32), :] = rows[...]
    d_att = nt(cot_out[...], out[...]).astype(jnp.bfloat16)

    row = lax.broadcasted_iota(jnp.int32, (128, 192), 0)
    column = lax.broadcasted_iota(jnp.int32, (128, 192), 1) - 32
    inside = (column + first_bin >= 0) & (column + first_bin < length)
    paired = (column >= 0) & (column < 128) & (pair_flag > 0)
    apart = jnp.abs(row - column)
    scale = KEY ** (-0.5)
    d_queries, d_keys, d_values = [], [], []
    for h in range(HEADS):
        q = proj[32:160, KEY * h : KEY * (h + 1)]
        k = proj[:, HEADS * KEY + KEY * h : HEADS * KEY + KEY * (h + 1)]
        v = proj[:, 2 * HEADS * KEY + VAL * h : 2 * HEADS * KEY + VAL * (h + 1)]
        d_att_h = d_att[:, VAL * h : VAL * (h + 1)]
        allowed = inside & (paired | (apart <= band[h]))
        score = jnp.where(allowed, nt(q, k) * scale, -1e30)
        top = jnp.max(score, axis=1, keepdims=True)
        raised = jnp.where(allowed, jnp.exp(score - top), 0.0)
        prob = raised / jnp.sum(raised, axis=1, keepdims=True)
        prob_b = prob.astype(jnp.bfloat16)
        attn = nn(prob_b, v)
        delta = jnp.sum(d_att_h.astype(jnp.float32) * attn, axis=1, keepdims=True)
        d_score = (prob * (nt(d_att_h, v) - delta) * scale).astype(jnp.bfloat16)
        d_queries.append(nn(d_score, k))
        d_keys.append(tn(d_score, q))
        d_values.append(tn(prob_b, d_att_h))
    d_q_out[...] = jnp.concatenate(d_queries, axis=1)
    d_kv = jnp.concatenate(d_keys + d_values, axis=1)
    d_kv_out[...] = d_kv[32:160]
    send[...] = jnp.where(m == 0, d_kv[:32], d_kv[160:]).astype(jnp.bfloat16)
    copy.wait()


def norm_kernel(
    d_q, d_kv, received, resid, inv_rms_ref, hidden, cot, gain, mix, qkv,
    d_hidden_out, d_resid_out, send, total_kv, gained, d_resid_all,
):
    n = half_index()
    total_kv[...] = d_kv[...]
    edge = pl.ds(pl.multiple_of(n * 96, 32), 32)
    total_kv[edge, :] = total_kv[edge, :] + received[...].astype(jnp.float32)
    d_proj = jnp.concatenate([d_q[...], total_kv[...]], axis=1).astype(jnp.bfloat16)
    inv_rms = inv_rms_ref[...]

    def back(c, mean):
        part = gain[:, chunk(c)] * nt(d_proj, qkv[chunk(c), :])
        gained[:, chunk(c)] = part
        return mean + jnp.sum(resid[:, chunk(c)] * part, axis=1, keepdims=True)

    mean = lax.fori_loop(0, 4, back, jnp.zeros((128, 1), jnp.float32)) * (1.0 / 1536)
    cubed = inv_rms * inv_rms * inv_rms * mean

    def residual(c, total):
        d_resid = (
            cot[:, chunk(c)].astype(jnp.float32)
            + inv_rms * gained[:, chunk(c)]
            - resid[:, chunk(c)] * cubed
        )
        d_resid_all[:, chunk(c)] = d_resid
        return total + nt(d_resid.astype(jnp.bfloat16), mix[:, chunk(c)])

    d_act = lax.fori_loop(0, 4, residual, jnp.zeros((128, HID), jnp.float32))
    d_hidden = (d_act * gelu_slope(hidden[...])).astype(jnp.bfloat16)
    d_hidden_out[...] = d_hidden
    d_resid_out[...] = d_resid_all[pl.ds(pl.multiple_of(n * 64, 64), 64), :]

    @pl.when(n == 0)
    def _():
        send[...] = d_hidden[:16]

    @pl.when(n == 1)
    def _():
        send[...] = d_hidden[112:]


def taps_kernel(d_hidden, received, d_resid, blocks_even, blocks_odd, conv, keep, send, extended_ref, noisy, grads):
    x, n = lax.rem(lax.axis_index("sb"), 2), half_index()

    @pl.when(n == 0)
    def _():
        extended_ref[pl.ds(0, 16), :] = received[...]
        extended_ref[pl.ds(16, 80), :] = d_hidden[pl.ds(0, 80), :]

    @pl.when(n == 1)
    def _():
        extended_ref[pl.ds(0, 80), :] = d_hidden[pl.ds(48, 80), :]
        extended_ref[pl.ds(80, 16), :] = received[...]

    for shift, block in enumerate((blocks_even, blocks_odd)):
        noisy[pl.ds(times(lax.rem(x + shift, 2), 32, 32), 32), :] = block[...].astype(jnp.float32)

    def taps(c, _):
        total = nt(extended_ref[pl.ds(32, 64), :], conv[0, chunk(c), :])
        total = total + nt(extended_ref[pl.ds(16, 64), :], conv[1, chunk(c), :])
        total = total + nt(extended_ref[pl.ds(0, 64), :], conv[2, chunk(c), :])
        grads[:, chunk(c)] = d_resid[:, chunk(c)] + total * gelu_slope(noisy[:, chunk(c)])
        return 0

    lax.fori_loop(0, 4, taps, 0)
    keep[...] = grads[pl.ds(pl.multiple_of(32 * x, 32), 32), :]
    send[...] = grads[pl.ds(pl.multiple_of(32 - 32 * x, 32), 32), :].astype(jnp.bfloat16)


def vmem(count):
    return [pl.BlockSpec(memory_space=pltpu.VMEM)] * count


def smem(count):
    return [pl.BlockSpec(memory_space=pltpu.SMEM)] * count


def hbm(count):
    return [pl.BlockSpec(memory_space=pl.ANY)] * count


def limit(mebibytes):
    return pltpu.CompilerParams(vmem_limit_bytes=mebibytes * 1024 * 1024)


f32, bf16 = (jnp.float32, jnp.bfloat16)


def shaped(*shape, dtype=jnp.float32):
    return jax.ShapeDtypeStruct(shape, dtype)


def stretch_shards(
    base, noise, cot, convolution_weight, mix_w, norm_gain, qkv_w, out_w, band_width, pairs
):
    n_sa = lax.axis_size("sa")
    b = lax.axis_index("sb")
    m = half_index()
    y, x = (b >> 1, b & 1)
    features = base.shape[1]

    early, late = pl.pallas_call(
        pack_kernel,
        out_shape=(shaped(192, CHUNK, dtype=bf16), shaped(160, CHUNK, dtype=bf16)),
        in_specs=vmem(4),
        out_specs=tuple(vmem(2)),
        compiler_params=limit(8),
    )(convolution_weight, mix_w, qkv_w, out_w)
    def along_z(step):
        return routes(n_sa, lambda z, y, x, c: (z ^ step, y, x, c))

    x_route = routes(n_sa, lambda z, y, x, c: (z, y, 1 - x, c))
    y_route = routes(n_sa, lambda z, y, x, c: (z, 1 - y, x, c))
    core_route = routes(n_sa, lambda z, y, x, c: (z, y, x, 1 - c))

    def collected(piece, nearest):
        half = piece.shape[0] // 2
        straight = jnp.stack([nearest] + [permuted(piece, along_z(step)) for step in range(2, 4)])
        beside, across = permuted(straight, x_route), permuted(straight, y_route)
        diagonal_a = permuted(beside[:, :half], y_route)
        diagonal_b = permuted(across[:, half:], x_route)
        same = (straight, beside, across, diagonal_a, diagonal_b)
        return same, tuple(permuted(part, core_route) for part in same[:3])

    nearest = permuted(early, along_z(1))
    early, early_other = collected(early, nearest)
    early += early_other + tuple(permuted(part, core_route) for part in early[3:])
    late, _ = lax.optimization_barrier((late, early[0]))
    late, late_other = collected(late, permuted(late, along_z(1)))
    noise, base, _ = lax.optimization_barrier((noise, base, early[0]))
    cot, _ = lax.optimization_barrier((cot, late[0]))

    def to_sample(shift):
        return routes(n_sa, lambda z, y, x, c: (z, c, (x + shift) % 2, y ^ (z & 1)))

    noisy = (base.astype(f32)[None] + noise.astype(f32)).astype(bf16)
    even = x == 0
    blocks = [
        permuted(jnp.where(x == shift, noisy[0], noisy[1]), to_sample(shift)) for shift in range(2)
    ]
    edge_route = routes(
        n_sa, lambda z, y, x, c: (z - 1, y, x, c) if c ^ (z & 1) == 0 else (z + 1, y, x, c)
    )
    low, high = jnp.where(even, blocks[0], blocks[1]), jnp.where(even, blocks[1], blocks[0])
    outer = jnp.concatenate(
        [jnp.where(m == 0, low[:16], low[16:]), jnp.where(m == 0, low[16:], high[:16]), jnp.where(m == 0, high[:16], high[16:])]
    )
    mine = (blocks[0], blocks[1], permuted(outer, edge_route))
    noisy_rows = mine + tuple(permuted(part, core_route) for part in mine)
    across = permuted(
        cot, routes(n_sa, lambda z, y, x, c: (z, 1 - y, x, c) if y == c ^ (z & 1) else None)
    )
    cot_block = jnp.where(y == m, cot, across)
    cot_rows = (cot_block, permuted(cot_block, x_route))
    cot_rows = cot_rows + tuple(permuted(part, core_route) for part in cot_rows)
    gain = norm_gain.reshape(1, features)

    normed, resid, inv_rms, hidden, conv, mix = pl.pallas_call(
        forward_kernel,
        out_shape=(
            shaped(192, features, dtype=bf16), shaped(128, features), shaped(128, 1), shaped(128, HID),
            shaped(3, features, HID, dtype=bf16), shaped(HID, features, dtype=bf16),
        ),
        in_specs=vmem(19),
        out_specs=tuple(vmem(4) + hbm(2)),
        scratch_shapes=[
            pltpu.VMEM((3, features, HID), bf16), pltpu.VMEM((HID, features), bf16),
            pltpu.VMEM((224, features), f32), pltpu.VMEM((224, features), bf16),
            pltpu.SemaphoreType.DMA((2,)),
        ],
        compiler_params=limit(28),
    )(*noisy_rows, convolution_weight, mix_w, *early, gain)
    *diagonals, normed = lax.optimization_barrier((*late[3:], normed))
    late += late_other + tuple(permuted(part, core_route) for part in diagonals)
    d_q, d_kv, send, qkv, cot_all = pl.pallas_call(
        attention_kernel,
        out_shape=(
            shaped(128, 256), shaped(128, 640), shaped(32, 640, dtype=bf16), shaped(features, 896, dtype=bf16),
            shaped(128, features, dtype=bf16),
        ),
        in_specs=smem(2) + vmem(17),
        out_specs=tuple(vmem(3) + hbm(1) + vmem(1)),
        scratch_shapes=[
            pltpu.VMEM((features, 896), bf16), pltpu.VMEM((HEADS * VAL, features), bf16),
            pltpu.SemaphoreType.DMA((1,)),
        ],
        compiler_params=limit(24),
    )(band_width, pairs, normed, *cot_rows, qkv_w, out_w, *late)

    received = permuted(send, edge_route)
    d_hidden, d_resid, send = pl.pallas_call(
        norm_kernel,
        out_shape=(shaped(128, HID, dtype=bf16), shaped(64, features), shaped(16, HID, dtype=bf16)),
        in_specs=vmem(10),
        out_specs=tuple(vmem(3)),
        scratch_shapes=[
            pltpu.VMEM((128, 640), f32), pltpu.VMEM((128, features), f32), pltpu.VMEM((128, features), f32),
        ],
        compiler_params=limit(16),
    )(d_q, d_kv, received, resid, inv_rms, hidden, cot_all, gain, mix, qkv)

    received = permuted(send, edge_route)
    keep, send = pl.pallas_call(
        taps_kernel,
        out_shape=(shaped(32, features), shaped(32, features, dtype=bf16)),
        in_specs=vmem(6),
        out_specs=tuple(vmem(2)),
        scratch_shapes=[
            pltpu.VMEM((96, HID), bf16), pltpu.VMEM((64, features), f32), pltpu.VMEM((64, features), f32),
        ],
        compiler_params=limit(16),
    )(d_hidden, received, d_resid, *blocks, conv)

    received = permuted(send, x_route)
    partial = (keep + received.astype(f32)).astype(bf16)
    first_sum = permuted(
        partial, routes(n_sa, lambda z, y, x, c: (z, 1 - y, x, c) if y != c ^ (z & 1) else (z, y, x, 1 - c))
    )
    second_sum = permuted(partial, routes(n_sa, lambda z, y, x, c: (z, 1 - y, x, 1 - c) if y != c ^ (z & 1) else None))
    other = jnp.where(y == m, partial, second_sum)
    return (first_sum.astype(f32) + other.astype(f32)) * 0.25


def solution(mesh):
    fits = mesh.shape["sb"] == 4 and mesh.shape["noise"] == 2 and HEADS == 4

    def body(*arrays):
        if fits and arrays[0].shape[0] == 32 and arrays[1].shape[0] == 2 and TILE == 128:
            if arrays[0].shape[1] == 1536 and mesh.shape["sa"] == 4:
                return stretch_shards(*arrays)
        return shards(*arrays)

    return jax.shard_map(
        body,
        mesh=mesh,
        in_specs=(
            P(("sa", "sb"), None),
            P("noise", ("sa", "sb"), None),
            P(("sa", "sb"), None),
            P(None, "sa", None),
            P("sa", None),
            P(),
            P("sa", None),
            P("sa", None),
            P(),
            P(),
        ),
        out_specs=P(("sa", "sb"), None),
        check_vma=False,
    )
```

```python
import jax
import jax.numpy as jnp
from jax import lax
from jax.experimental import pallas as pl
from jax.experimental.pallas import tpu as pltpu
from jax.sharding import PartitionSpec as P

HID = 384
HEADS = 4
KEY = 64
VAL = 96
DILATION_BINS = 16
BAND = 32
TILE = 128


ROOT_TWO_PI = 0.7978845608
CUBIC = 0.044715


def extended(value, sides, width):
    for axis, dim in sides:
        peers, length = (lax.axis_size(axis), value.shape[dim])
        up = [(i, (i + 1) % peers) for i in range(peers - 1)]
        down = [(j, i) for i, j in up]
        last = lax.slice_in_dim(value, length - width, length, axis=dim)
        leading = lax.slice_in_dim(value, 0, width, axis=dim)
        before = lax.ppermute(last, axis, up)
        after = lax.ppermute(leading, axis, down)
        value = jnp.concatenate([before, value, after], axis=dim)
    return value


def from_behind(block, axis, distance):
    devices = range(lax.axis_size(axis))
    route = [(i - distance, i) for i in devices if i - distance in devices]
    return lax.ppermute(block, axis, route)


def gelu_tanh(values):
    inner = ROOT_TWO_PI * (values + CUBIC * values * values * values)
    return 0.5 * values * (1.0 + jnp.tanh(inner))


def gelu_slope(values):
    tangent = jnp.tanh(ROOT_TWO_PI * (values + CUBIC * values * values * values))
    return 0.5 * (1.0 + tangent) + 0.5 * values * (1.0 - tangent * tangent) * ROOT_TWO_PI * (
        1.0 + 3.0 * CUBIC * values * values
    )


def shards(base, noise, cot, convolution_weight, mix_w, norm_gain, qkv_w, out_w, band_width, pairs):
    conv_full, mix_full, qkv_full, out_full = (
        lax.all_gather(convolution_weight, "sa", axis=1, tiled=True),
        lax.all_gather(mix_w, "sa", axis=0, tiled=True),
        lax.all_gather(qkv_w, "sa", axis=0, tiled=True),
        lax.all_gather(out_w, "sa", axis=0, tiled=True),
    )
    sequence_bins = base.shape[0]
    samples_dev = noise.shape[0]
    stretch = sequence_bins * lax.axis_size("sb")
    sequence_length = stretch * lax.axis_size("sa")
    heads_key = HEADS * KEY
    heads_val = HEADS * VAL
    width = sequence_bins + 2 * BAND
    scale = KEY ** (-0.5)
    stretch_first = lax.axis_index("sa") * stretch
    first_row = stretch_first + lax.axis_index("sb") * sequence_bins
    row_pos = first_row + jnp.arange(sequence_bins, dtype=jnp.int32)
    ext_pos = first_row - BAND + jnp.arange(width, dtype=jnp.int32)
    stretch_pos = stretch_first + jnp.arange(stretch, dtype=jnp.int32)
    tiles = sequence_length // TILE
    tile_ids = jnp.arange(tiles, dtype=jnp.int32)
    pick_query = (pairs[:, 0][:, None] == tile_ids[None, :]).astype(jnp.float32)
    pick_key = (pairs[:, 1][:, None] == tile_ids[None, :]).astype(jnp.float32)
    table = jnp.dot(pick_query.T, pick_key)
    own_select = ((row_pos // TILE)[:, None] == tile_ids[None, :]).astype(jnp.float32)
    stretch_select = ((stretch_pos // TILE)[:, None] == tile_ids[None, :]).astype(jnp.float32)
    pair_own_rows = jnp.dot(jnp.dot(own_select, table), stretch_select.T) > 0.5
    pair_own_keys = jnp.dot(jnp.dot(stretch_select, table), own_select.T) > 0.5
    inside = (ext_pos >= 0) & (ext_pos < sequence_length)
    band_mask = inside[None, None, :] & (
        jnp.abs(row_pos[:, None] - ext_pos[None, :])[None] <= band_width[:, None, None]
    )
    far_rows = jnp.abs(row_pos[:, None] - stretch_pos[None, :])[None] > band_width[:, None, None]
    pair_mask = pair_own_rows[None] & far_rows
    key_mask = pair_own_keys[None] & jnp.transpose(far_rows, (0, 2, 1))
    noisy = base.astype(jnp.float32)[None] + noise.astype(jnp.float32)
    gelu_input = gelu_tanh(noisy).astype(jnp.bfloat16)
    gelu_extended = extended(gelu_input, ((("sa", "sb"), 1),), DILATION_BINS)
    hidden_state = jnp.zeros((samples_dev, sequence_bins, HID), jnp.float32)
    for tap_index in range(3):
        hidden_state = hidden_state + jnp.einsum(
            "nbd,dc->nbc",
            gelu_extended[:, tap_index * DILATION_BINS : tap_index * DILATION_BINS + sequence_bins],
            conv_full[tap_index],
            preferred_element_type=jnp.float32,
        )
    act = gelu_tanh(hidden_state).astype(jnp.bfloat16)
    resid = noisy + jnp.einsum("nbc,cd->nbd", act, mix_full, preferred_element_type=jnp.float32)
    inv_rms = lax.rsqrt(jnp.mean(resid * resid, axis=-1, keepdims=True) + 1e-06)
    normed = (resid * inv_rms * norm_gain).astype(jnp.bfloat16)
    proj = jnp.einsum("nbd,dc->nbc", normed, qkv_full, preferred_element_type=jnp.float32).astype(
        jnp.bfloat16
    )
    queries = proj[..., :heads_key].reshape(samples_dev, sequence_bins, HEADS, KEY)
    key_vals = proj[..., heads_key:]
    kv_ext = extended(key_vals, ((("sa", "sb"), 1),), BAND)
    kv_all = lax.all_gather(key_vals, "sb", axis=1, tiled=True)
    keys_ext = kv_ext[..., :heads_key].reshape(samples_dev, width, HEADS, KEY)
    vals_ext = kv_ext[..., heads_key:].reshape(samples_dev, width, HEADS, VAL)
    keys_all = kv_all[..., :heads_key].reshape(samples_dev, stretch, HEADS, KEY)
    vals_all = kv_all[..., heads_key:].reshape(samples_dev, stretch, HEADS, VAL)
    score_band = (
        jnp.einsum("nihd,njhd->nhij", queries, keys_ext, preferred_element_type=jnp.float32) * scale
    )
    score_band = jnp.where(band_mask[None], score_band, -1e30)
    raw_pair = jnp.einsum("nihd,njhd->nhij", queries, keys_all, preferred_element_type=jnp.float32)
    score_pair = jnp.where(pair_mask[None], raw_pair * scale, -1e30)
    top = jnp.maximum(jnp.max(score_band, axis=-1), jnp.max(score_pair, axis=-1))
    total = jnp.sum(jnp.where(band_mask[None], jnp.exp(score_band - top[..., None]), 0.0), axis=-1)
    total = total + jnp.sum(
        jnp.where(pair_mask[None], jnp.exp(score_pair - top[..., None]), 0.0), axis=-1
    )
    lse = top + jnp.log(total)
    prob_band = jnp.where(band_mask[None], jnp.exp(score_band - lse[..., None]), 0.0)
    prob_pair = jnp.where(pair_mask[None], jnp.exp(score_pair - lse[..., None]), 0.0)
    band_b = prob_band.astype(jnp.bfloat16)
    pair_b = prob_pair.astype(jnp.bfloat16)
    attn = jnp.einsum("nhij,njhe->nihe", band_b, vals_ext, preferred_element_type=jnp.float32)
    attn = attn + jnp.einsum(
        "nhij,njhe->nihe", pair_b, vals_all, preferred_element_type=jnp.float32
    )
    d_att = jnp.dot(cot, out_full.T, preferred_element_type=jnp.float32).astype(jnp.bfloat16)
    d_att_heads = d_att.reshape(sequence_bins, HEADS, VAL)
    delta = jnp.transpose(jnp.sum(d_att_heads.astype(jnp.float32)[None] * attn, axis=-1), (0, 2, 1))
    d_prob_band = jnp.einsum(
        "ihe,njhe->nhij", d_att_heads, vals_ext, preferred_element_type=jnp.float32
    )
    d_prob_pair = jnp.einsum(
        "ihe,njhe->nhij", d_att_heads, vals_all, preferred_element_type=jnp.float32
    )
    d_score_band = (prob_band * (d_prob_band - delta[..., None]) * scale).astype(jnp.bfloat16)
    d_score_pair = (prob_pair * (d_prob_pair - delta[..., None]) * scale).astype(jnp.bfloat16)
    d_query = jnp.einsum(
        "nhij,njhd->nihd", d_score_band, keys_ext, preferred_element_type=jnp.float32
    )
    d_query = d_query + jnp.einsum(
        "nhij,njhd->nihd", d_score_pair, keys_all, preferred_element_type=jnp.float32
    )
    d_key_ext = jnp.einsum(
        "nhij,nihd->njhd", d_score_band, queries, preferred_element_type=jnp.float32
    )
    d_val_ext = jnp.einsum(
        "nhij,ihe->njhe", band_b, d_att_heads, preferred_element_type=jnp.float32
    )
    d_kv_ext = jnp.concatenate(
        [
            d_key_ext.reshape(samples_dev, width, heads_key),
            d_val_ext.reshape(samples_dev, width, heads_val),
        ],
        axis=2,
    )
    from_right = from_behind(d_kv_ext[:, :BAND].astype(jnp.bfloat16), ("sa", "sb"), -1).astype(
        jnp.float32
    )
    from_left = from_behind(
        d_kv_ext[:, BAND + sequence_bins :].astype(jnp.bfloat16), ("sa", "sb"), 1
    ).astype(jnp.float32)
    d_key_vals = d_kv_ext[:, BAND : BAND + sequence_bins]
    d_key_vals = d_key_vals + from_left
    d_key_vals = d_key_vals + from_right
    statistics = jnp.stack([lse, delta], axis=1)
    query_rows = proj[..., :heads_key]
    queries_all, d_att_all = (
        lax.all_gather(query_rows, "sb", axis=1, tiled=True),
        lax.all_gather(d_att, "sb", axis=0, tiled=True),
    )
    stats_all = lax.all_gather(statistics, "sb", axis=3, tiled=True)
    queries_all = queries_all.reshape(samples_dev, stretch, HEADS, KEY)
    d_att_all = d_att_all.reshape(stretch, HEADS, VAL)
    keys_own = key_vals[..., :heads_key].reshape(samples_dev, sequence_bins, HEADS, KEY)
    vals_own = key_vals[..., heads_key:].reshape(samples_dev, sequence_bins, HEADS, VAL)
    score_key = (
        jnp.einsum("nihd,njhd->nhij", queries_all, keys_own, preferred_element_type=jnp.float32)
        * scale
    )
    prob_key = jnp.where(key_mask[None], jnp.exp(score_key - stats_all[:, 0][..., None]), 0.0)
    d_val_pair = jnp.einsum(
        "nhij,ihe->njhe",
        prob_key.astype(jnp.bfloat16),
        d_att_all,
        preferred_element_type=jnp.float32,
    )
    d_prob_key = jnp.einsum(
        "ihe,njhe->nhij", d_att_all, vals_own, preferred_element_type=jnp.float32
    )
    d_score_key = (prob_key * (d_prob_key - stats_all[:, 1][..., None]) * scale).astype(
        jnp.bfloat16
    )
    d_key_pair = jnp.einsum(
        "nhij,nihd->njhd", d_score_key, queries_all, preferred_element_type=jnp.float32
    )
    d_key_vals = d_key_vals + jnp.concatenate(
        [
            d_key_pair.reshape(samples_dev, sequence_bins, heads_key),
            d_val_pair.reshape(samples_dev, sequence_bins, heads_val),
        ],
        axis=2,
    )
    d_proj = jnp.concatenate(
        [d_query.reshape(samples_dev, sequence_bins, heads_key), d_key_vals], axis=2
    ).astype(jnp.bfloat16)
    d_normed = jnp.einsum("nbc,dc->nbd", d_proj, qkv_full, preferred_element_type=jnp.float32)
    gained = norm_gain * d_normed
    d_resid = (
        cot.astype(jnp.float32)[None]
        + inv_rms * gained
        - resid * inv_rms * inv_rms * inv_rms * jnp.mean(resid * gained, axis=-1, keepdims=True)
    )
    d_act = jnp.einsum(
        "nbd,cd->nbc", d_resid.astype(jnp.bfloat16), mix_full, preferred_element_type=jnp.float32
    )
    hidden_gradient = (d_act * gelu_slope(hidden_state)).astype(jnp.bfloat16)
    gradient_extended = extended(hidden_gradient, ((("sa", "sb"), 1),), DILATION_BINS)
    d_gelu_in = jnp.zeros((samples_dev, sequence_bins, base.shape[1]), jnp.float32)
    for tap_index in range(3):
        start_offset = (2 - tap_index) * DILATION_BINS
        d_gelu_in = d_gelu_in + jnp.einsum(
            "nbc,dc->nbd",
            gradient_extended[:, start_offset : start_offset + sequence_bins],
            conv_full[tap_index],
            preferred_element_type=jnp.float32,
        )
    grads = d_resid + d_gelu_in * gelu_slope(noisy)
    summed = lax.psum(jnp.sum(grads, axis=0).astype(jnp.bfloat16), "noise").astype(jnp.float32)
    return summed / (samples_dev * lax.axis_size("noise"))


def permuted(value, pairs):
    return lax.ppermute(value, ("sa", "sb", "noise"), pairs)


def routes(n_sa, route):
    flat = lambda z, y, x, c: ((z * 2 + y) * 2 + x) * 2 + c
    pairs = []
    for z in range(n_sa):
        for y in range(2):
            for x in range(2):
                for c in range(2):
                    target = route(z, y, x, c)
                    if target is not None and 0 <= target[0] < n_sa:
                        pairs.append((flat(z, y, x, c), flat(*target)))
    return pairs


def position():
    b = lax.axis_index("sb")
    return lax.axis_index("sa"), b // 2, lax.rem(b, 2), lax.axis_index("noise")


def half_index():
    return lax.rem(lax.axis_index("noise") + lax.axis_index("sa"), 2)


def pack_kernel(conv, mix, qkv, out, early, late):
    z, y, x, n = position()
    b = 2 * y + x
    part = b * 2 + n
    rows = pl.ds(pl.multiple_of(part * 48, 16), 48)
    half = pl.ds(pl.multiple_of(n * 48, 16), 48)
    columns = pl.ds(pl.multiple_of(b * 384, 128), 384)
    for t in range(3):
        early[pl.ds(48 * t, 48), :] = conv[t, rows, :]
    early[pl.ds(144, 48), :] = mix[half, columns]
    late[pl.ds(0, 48), :] = out[half, columns]
    for k in range(2):
        late[pl.ds(48 + 48 * k, 48), :] = qkv[rows, pl.ds(384 * k, 384)]
    for k in range(3):
        third = pl.ds(pl.multiple_of(part * 48 + 16 * k, 16), 16)
        late[pl.ds(144, 16), pl.ds(128 * k, 128)] = qkv[third, pl.ds(768, 128)]


def nt(a, b):
    return lax.dot_general(a, b, (((1,), (1,)), ((), ())), preferred_element_type=jnp.float32)


def tn(a, b):
    return lax.dot_general(a, b, (((0,), (0,)), ((), ())), preferred_element_type=jnp.float32)


def nn(a, b):
    return jnp.dot(a, b, preferred_element_type=jnp.float32)


CHUNK = 384


def chunk(c):
    return pl.ds(pl.multiple_of(c * CHUNK, 128), CHUNK)


def arrived(z, y, x, n, same, other):
    for j in range(3):
        for core, (straight, beside, across, diagonal_a, diagonal_b) in enumerate((same, other)):
            half = diagonal_a.shape[1]
            for dy in range(2):
                for dx in range(2):
                    if dy and dx:
                        first, second = diagonal_a[j], diagonal_b[j]
                    else:
                        whole = across if dy else beside if dx else straight
                        first, second = whole[j, pl.ds(0, half), :], whole[j, pl.ds(half, half), :]
                    yield j, z ^ (j + 1), y ^ dy, x ^ dx, n ^ core, first, second


def times(value, factor, unit):
    return pl.multiple_of(value * factor, unit)


def forward_kernel(
    blocks_even, blocks_odd, edge, other_even, other_odd, other_edge, *refs,
):
    own_conv, own_mix = refs[:2]
    same, other = refs[2:7], refs[7:12]
    (
        gain, normed_out, resid_out, inv_out, hidden_out, conv_out, mix_out,
        conv, mix, noisy, gelu_in, sems,
    ) = refs[12:]
    z, y, x, n = position()

    for t in range(3):
        conv[t, pl.ds(times(z, 384, 128), 384), :] = own_conv[t]
    mix[pl.ds(times(z, 96, 32), 96), :] = own_mix[...]
    for _, sz, sy, sx, sn, first, second in arrived(z, y, x, n, same, other):
        b = 2 * sy + sx
        rows = pl.ds(pl.multiple_of(sz * 384 + (b * 2 + sn) * 48, 16), 48)
        conv[0, rows, :] = first[:48]
        conv[1, rows, :] = first[48:]
        conv[2, rows, :] = second[:48]
        mix[pl.ds(pl.multiple_of(sz * 96 + sn * 48, 16), 48), pl.ds(times(b, 384, 128), 384)] = second[48:]
    copies = [
        pltpu.make_async_copy(s, d, sems.at[i]) for i, (s, d) in enumerate(((conv, conv_out), (mix, mix_out)))
    ]
    for copy in copies:
        copy.start()

    m = half_index()
    for half, (even, odd, outer) in (
        (m, (blocks_even, blocks_odd, edge)), (1 - m, (other_even, other_odd, other_edge))
    ):
        noisy[pl.ds(times(half, 176, 16), 48), :] = outer[...].astype(jnp.float32)
        for shift, block in enumerate((even, odd)):
            row = 48 + 64 * half + 32 * lax.rem(x + shift, 2)
            noisy[pl.ds(pl.multiple_of(row, 16), 32), :] = block[...].astype(jnp.float32)

    def activate(c, _):
        gelu_in[:, chunk(c)] = gelu_tanh(noisy[:, chunk(c)]).astype(jnp.bfloat16)
        return 0

    lax.fori_loop(0, 4, activate, 0)

    def convolve(c, total):
        for t in range(3):
            total = total + nn(gelu_in[pl.ds(16 * t, 192), chunk(c)], conv[t, chunk(c), :])
        return total

    hidden = lax.fori_loop(0, 4, convolve, jnp.zeros((192, HID), jnp.float32))
    hidden_out[...] = hidden[32:160]
    act = gelu_tanh(hidden).astype(jnp.bfloat16)

    def mixing(c, squares):
        resid = noisy[pl.ds(16, 192), chunk(c)] + nn(act, mix[:, chunk(c)])
        noisy[pl.ds(16, 192), chunk(c)] = resid
        resid_out[:, chunk(c)] = resid[32:160]
        return squares + jnp.sum(resid * resid, axis=1, keepdims=True)

    squares = lax.fori_loop(0, 4, mixing, jnp.zeros((192, 1), jnp.float32))
    inv_rms = lax.rsqrt(squares * (1.0 / 1536) + 1e-06)
    inv_out[...] = inv_rms[32:160]

    def normalise(c, _):
        normed = noisy[pl.ds(16, 192), chunk(c)] * inv_rms * gain[:, chunk(c)]
        normed_out[:, chunk(c)] = normed.astype(jnp.bfloat16)
        return 0

    lax.fori_loop(0, 4, normalise, 0)
    for copy in copies:
        copy.wait()


def attention_kernel(band, pairs, normed, cot_block, cot_beside, other_block, other_beside, *refs):
    own_qkv, own_out = refs[:2]
    same, other = refs[2:7], refs[7:12]
    d_q_out, d_kv_out, send, qkv_out, cot_out, qkv, out, sems = refs[12:]
    z, y, x, n = position()
    length = lax.axis_size("sa") * 128
    first_bin = z * 128
    pair_flag = jnp.int32(0)
    for i in range(pairs.shape[0]):
        pair_flag = pair_flag | ((pairs[i, 0] == z) & (pairs[i, 1] == z)).astype(jnp.int32)

    own_rows = pl.ds(times(z, 384, 128), 384)
    qkv[own_rows, :] = own_qkv[...]
    out[pl.ds(times(z, 96, 32), 96), :] = own_out[...]
    proj = nn(normed[:, own_rows], own_qkv[...])
    done = 0
    for j, sz, sy, sx, sn, first, second in arrived(z, y, x, n, same, other):
        b = 2 * sy + sx
        row = sz * 384 + (b * 2 + sn) * 48
        out[pl.ds(pl.multiple_of(sz * 96 + sn * 48, 16), 48), pl.ds(times(b, 384, 128), 384)] = first[:48]
        qkv[pl.ds(pl.multiple_of(row, 16), 32), pl.ds(0, 384)] = first[48:]
        qkv[pl.ds(pl.multiple_of(row + 32, 16), 16), pl.ds(0, 384)] = second[:16]
        qkv[pl.ds(pl.multiple_of(row, 16), 48), pl.ds(384, 384)] = second[16:64]
        for k in range(3):
            third = pl.ds(pl.multiple_of(row + 16 * k, 16), 16)
            qkv[third, pl.ds(768, 128)] = second[64:, 128 * k : 128 * k + 128]
        done += 1
        if done % 8 == 0:
            rows = pl.ds(times(sz, 384, 128), 384)
            proj = proj + nn(normed[:, rows], qkv[rows, :])
    proj = proj.astype(jnp.bfloat16)
    copy = pltpu.make_async_copy(qkv, qkv_out, sems.at[0])
    copy.start()
    m = half_index()
    for half, (block, beside) in ((m, (cot_block, cot_beside)), (1 - m, (other_block, other_beside))):
        for shift, rows in enumerate((block, beside)):
            row = 64 * half + 32 * lax.rem(x + shift, 2)
            cot_out[pl.ds(pl.multiple_of(row, 32), 32), :] = rows[...]
    d_att = nt(cot_out[...], out[...]).astype(jnp.bfloat16)

    row = lax.broadcasted_iota(jnp.int32, (128, 192), 0)
    column = lax.broadcasted_iota(jnp.int32, (128, 192), 1) - 32
    inside = (column + first_bin >= 0) & (column + first_bin < length)
    paired = (column >= 0) & (column < 128) & (pair_flag > 0)
    apart = jnp.abs(row - column)
    scale = KEY ** (-0.5)
    d_queries, d_keys, d_values = [], [], []
    for h in range(HEADS):
        q = proj[32:160, KEY * h : KEY * (h + 1)]
        k = proj[:, HEADS * KEY + KEY * h : HEADS * KEY + KEY * (h + 1)]
        v = proj[:, 2 * HEADS * KEY + VAL * h : 2 * HEADS * KEY + VAL * (h + 1)]
        d_att_h = d_att[:, VAL * h : VAL * (h + 1)]
        allowed = inside & (paired | (apart <= band[h]))
        score = jnp.where(allowed, nt(q, k) * scale, -1e30)
        top = jnp.max(score, axis=1, keepdims=True)
        raised = jnp.where(allowed, jnp.exp(score - top), 0.0)
        prob = raised / jnp.sum(raised, axis=1, keepdims=True)
        prob_b = prob.astype(jnp.bfloat16)
        attn = nn(prob_b, v)
        delta = jnp.sum(d_att_h.astype(jnp.float32) * attn, axis=1, keepdims=True)
        d_score = (prob * (nt(d_att_h, v) - delta) * scale).astype(jnp.bfloat16)
        d_queries.append(nn(d_score, k))
        d_keys.append(tn(d_score, q))
        d_values.append(tn(prob_b, d_att_h))
    d_q_out[...] = jnp.concatenate(d_queries, axis=1)
    d_kv = jnp.concatenate(d_keys + d_values, axis=1)
    d_kv_out[...] = d_kv[32:160]
    send[...] = jnp.where(m == 0, d_kv[:32], d_kv[160:]).astype(jnp.bfloat16)
    copy.wait()


def norm_kernel(
    d_q, d_kv, received, resid, inv_rms_ref, hidden, cot, gain, mix, qkv,
    d_hidden_out, d_resid_out, send, total_kv, gained, d_resid_all,
):
    n = half_index()
    total_kv[...] = d_kv[...]
    edge = pl.ds(pl.multiple_of(n * 96, 32), 32)
    total_kv[edge, :] = total_kv[edge, :] + received[...].astype(jnp.float32)
    d_proj = jnp.concatenate([d_q[...], total_kv[...]], axis=1).astype(jnp.bfloat16)
    inv_rms = inv_rms_ref[...]

    def back(c, mean):
        part = gain[:, chunk(c)] * nt(d_proj, qkv[chunk(c), :])
        gained[:, chunk(c)] = part
        return mean + jnp.sum(resid[:, chunk(c)] * part, axis=1, keepdims=True)

    mean = lax.fori_loop(0, 4, back, jnp.zeros((128, 1), jnp.float32)) * (1.0 / 1536)
    cubed = inv_rms * inv_rms * inv_rms * mean

    def residual(c, total):
        d_resid = (
            cot[:, chunk(c)].astype(jnp.float32)
            + inv_rms * gained[:, chunk(c)]
            - resid[:, chunk(c)] * cubed
        )
        d_resid_all[:, chunk(c)] = d_resid
        return total + nt(d_resid.astype(jnp.bfloat16), mix[:, chunk(c)])

    d_act = lax.fori_loop(0, 4, residual, jnp.zeros((128, HID), jnp.float32))
    d_hidden = (d_act * gelu_slope(hidden[...])).astype(jnp.bfloat16)
    d_hidden_out[...] = d_hidden
    d_resid_out[...] = d_resid_all[pl.ds(pl.multiple_of(n * 64, 64), 64), :]

    @pl.when(n == 0)
    def _():
        send[...] = d_hidden[:16]

    @pl.when(n == 1)
    def _():
        send[...] = d_hidden[112:]


def taps_kernel(d_hidden, received, d_resid, blocks_even, blocks_odd, conv, keep, send, extended_ref, noisy, grads):
    x, n = lax.rem(lax.axis_index("sb"), 2), half_index()

    @pl.when(n == 0)
    def _():
        extended_ref[pl.ds(0, 16), :] = received[...]
        extended_ref[pl.ds(16, 80), :] = d_hidden[pl.ds(0, 80), :]

    @pl.when(n == 1)
    def _():
        extended_ref[pl.ds(0, 80), :] = d_hidden[pl.ds(48, 80), :]
        extended_ref[pl.ds(80, 16), :] = received[...]

    for shift, block in enumerate((blocks_even, blocks_odd)):
        noisy[pl.ds(times(lax.rem(x + shift, 2), 32, 32), 32), :] = block[...].astype(jnp.float32)

    def taps(c, _):
        total = nt(extended_ref[pl.ds(32, 64), :], conv[0, chunk(c), :])
        total = total + nt(extended_ref[pl.ds(16, 64), :], conv[1, chunk(c), :])
        total = total + nt(extended_ref[pl.ds(0, 64), :], conv[2, chunk(c), :])
        grads[:, chunk(c)] = d_resid[:, chunk(c)] + total * gelu_slope(noisy[:, chunk(c)])
        return 0

    lax.fori_loop(0, 4, taps, 0)
    keep[...] = grads[pl.ds(pl.multiple_of(32 * x, 32), 32), :]
    send[...] = grads[pl.ds(pl.multiple_of(32 - 32 * x, 32), 32), :].astype(jnp.bfloat16)


def vmem(count):
    return [pl.BlockSpec(memory_space=pltpu.VMEM)] * count


def smem(count):
    return [pl.BlockSpec(memory_space=pltpu.SMEM)] * count


def hbm(count):
    return [pl.BlockSpec(memory_space=pl.ANY)] * count


def limit(mebibytes):
    return pltpu.CompilerParams(vmem_limit_bytes=mebibytes * 1024 * 1024)


f32, bf16 = (jnp.float32, jnp.bfloat16)


def shaped(*shape, dtype=jnp.float32):
    return jax.ShapeDtypeStruct(shape, dtype)


def stretch_shards(
    base, noise, cot, convolution_weight, mix_w, norm_gain, qkv_w, out_w, band_width, pairs
):
    n_sa = lax.axis_size("sa")
    b = lax.axis_index("sb")
    m = half_index()
    y, x = (b >> 1, b & 1)
    features = base.shape[1]

    early, late = pl.pallas_call(
        pack_kernel,
        out_shape=(shaped(192, CHUNK, dtype=bf16), shaped(160, CHUNK, dtype=bf16)),
        in_specs=vmem(4),
        out_specs=tuple(vmem(2)),
        compiler_params=limit(8),
    )(convolution_weight, mix_w, qkv_w, out_w)
    def along_z(step):
        return routes(n_sa, lambda z, y, x, c: (z ^ step, y, x, c))

    x_route = routes(n_sa, lambda z, y, x, c: (z, y, 1 - x, c))
    y_route = routes(n_sa, lambda z, y, x, c: (z, 1 - y, x, c))
    core_route = routes(n_sa, lambda z, y, x, c: (z, y, x, 1 - c))

    def over_z(piece):
        return [permuted(piece, along_z(step)) for step in range(1, 4)]

    def diagonals(beside, across):
        half = beside.shape[1] // 2
        return permuted(beside[:, :half], y_route), permuted(across[:, half:], x_route)

    def swapped(parts):
        return tuple(permuted(part, core_route) for part in parts)

    def after(values, *earlier):
        count = len(values)
        return lax.optimization_barrier((*values, *earlier))[:count]

    def to_sample(shift):
        return routes(n_sa, lambda z, y, x, c: (z, c, (x + shift) % 2, y ^ (z & 1)))

    noisy = (base.astype(f32)[None] + noise.astype(f32)).astype(bf16)
    even = x == 0
    straight, late, noisy, cot = after((jnp.stack(over_z(early)), late, noisy, cot))
    beside, across = permuted(straight, x_route), permuted(straight, y_route)
    late_straight = jnp.stack(over_z(late))
    blocks = [
        permuted(jnp.where(x == shift, noisy[0], noisy[1]), to_sample(shift)) for shift in range(2)
    ]
    across_cot = permuted(
        cot, routes(n_sa, lambda z, y, x, c: (z, 1 - y, x, c) if y == c ^ (z & 1) else None)
    )
    edge_route = routes(
        n_sa, lambda z, y, x, c: (z - 1, y, x, c) if c ^ (z & 1) == 0 else (z + 1, y, x, c)
    )
    low, high = jnp.where(even, blocks[0], blocks[1]), jnp.where(even, blocks[1], blocks[0])
    outer = jnp.concatenate(
        [jnp.where(m == 0, low[:16], low[16:]), jnp.where(m == 0, low[16:], high[:16]), jnp.where(m == 0, high[:16], high[16:])]
    )
    cot_block = jnp.where(y == m, cot, across_cot)
    straight, beside, across, late_straight, outer, cot_block = after(
        (straight, beside, across, late_straight, outer, cot_block)
    )
    early = (straight, beside, across) + diagonals(beside, across)
    late_beside, late_across = permuted(late_straight, x_route), permuted(late_straight, y_route)
    cot_rows = (cot_block, permuted(cot_block, x_route))
    mine = (*blocks, permuted(outer, edge_route))
    early_other = swapped(early[:3])
    early, early_other, late, cot_rows, mine = (
        lambda v: (v[:5], v[5:8], v[8:11], v[11:13], v[13:])
    )(after((*early, *early_other, late_straight, late_beside, late_across, *cot_rows, *mine)))
    late = tuple(late) + diagonals(late[1], late[2])
    early = tuple(early) + tuple(early_other) + swapped(early[3:])
    cot_rows = tuple(cot_rows) + swapped(cot_rows)
    late_other = swapped(late[:3])
    noisy_rows = tuple(mine) + swapped(mine)
    gain = norm_gain.reshape(1, features)

    normed, resid, inv_rms, hidden, conv, mix = pl.pallas_call(
        forward_kernel,
        out_shape=(
            shaped(192, features, dtype=bf16), shaped(128, features), shaped(128, 1), shaped(128, HID),
            shaped(3, features, HID, dtype=bf16), shaped(HID, features, dtype=bf16),
        ),
        in_specs=vmem(19),
        out_specs=tuple(vmem(4) + hbm(2)),
        scratch_shapes=[
            pltpu.VMEM((3, features, HID), bf16), pltpu.VMEM((HID, features), bf16),
            pltpu.VMEM((224, features), f32), pltpu.VMEM((224, features), bf16),
            pltpu.SemaphoreType.DMA((2,)),
        ],
        compiler_params=limit(18),
    )(*noisy_rows, convolution_weight, mix_w, *early, gain)
    late += late_other + swapped(late[3:])
    d_q, d_kv, send, qkv, cot_all = pl.pallas_call(
        attention_kernel,
        out_shape=(
            shaped(128, 256), shaped(128, 640), shaped(32, 640, dtype=bf16), shaped(features, 896, dtype=bf16),
            shaped(128, features, dtype=bf16),
        ),
        in_specs=smem(2) + vmem(17),
        out_specs=tuple(vmem(3) + hbm(1) + vmem(1)),
        scratch_shapes=[
            pltpu.VMEM((features, 896), bf16), pltpu.VMEM((HEADS * VAL, features), bf16),
            pltpu.SemaphoreType.DMA((1,)),
        ],
        compiler_params=limit(14),
    )(band_width, pairs, normed, *cot_rows, qkv_w, out_w, *late)

    received = permuted(send, edge_route)
    d_hidden, d_resid, send = pl.pallas_call(
        norm_kernel,
        out_shape=(shaped(128, HID, dtype=bf16), shaped(64, features), shaped(16, HID, dtype=bf16)),
        in_specs=vmem(10),
        out_specs=tuple(vmem(3)),
        scratch_shapes=[
            pltpu.VMEM((128, 640), f32), pltpu.VMEM((128, features), f32), pltpu.VMEM((128, features), f32),
        ],
        compiler_params=limit(12),
    )(d_q, d_kv, received, resid, inv_rms, hidden, cot_all, gain, mix, qkv)

    received = permuted(send, edge_route)
    keep, send = pl.pallas_call(
        taps_kernel,
        out_shape=(shaped(32, features), shaped(32, features, dtype=bf16)),
        in_specs=vmem(6),
        out_specs=tuple(vmem(2)),
        scratch_shapes=[
            pltpu.VMEM((96, HID), bf16), pltpu.VMEM((64, features), f32), pltpu.VMEM((64, features), f32),
        ],
        compiler_params=limit(6),
    )(d_hidden, received, d_resid, *blocks, conv)

    received = permuted(send, x_route)
    partial = (keep + received.astype(f32)).astype(bf16)
    first_sum = permuted(
        partial, routes(n_sa, lambda z, y, x, c: (z, 1 - y, x, c) if y != c ^ (z & 1) else (z, y, x, 1 - c))
    )
    second_sum = permuted(partial, routes(n_sa, lambda z, y, x, c: (z, 1 - y, x, 1 - c) if y != c ^ (z & 1) else None))
    other = jnp.where(y == m, partial, second_sum)
    return (first_sum.astype(f32) + other.astype(f32)) * 0.25


def solution(mesh):
    fits = mesh.shape["sb"] == 4 and mesh.shape["noise"] == 2 and HEADS == 4

    def body(*arrays):
        if fits and arrays[0].shape[0] == 32 and arrays[1].shape[0] == 2 and TILE == 128:
            if arrays[0].shape[1] == 1536 and mesh.shape["sa"] == 4:
                return stretch_shards(*arrays)
        return shards(*arrays)

    return jax.shard_map(
        body,
        mesh=mesh,
        in_specs=(
            P(("sa", "sb"), None),
            P("noise", ("sa", "sb"), None),
            P(("sa", "sb"), None),
            P(None, "sa", None),
            P("sa", None),
            P(),
            P("sa", None),
            P("sa", None),
            P(),
            P(),
        ),
        out_specs=P(("sa", "sb"), None),
        check_vma=False,
    )
```

```python
import jax
import jax.numpy as jnp
from jax import lax
from jax.experimental import pallas as pl
from jax.experimental.pallas import tpu as pltpu
from jax.sharding import PartitionSpec as P

HID = 384
HEADS = 4
KEY = 64
VAL = 96
DILATION_BINS = 16
BAND = 32
TILE = 128


ROOT_TWO_PI = 0.7978845608
CUBIC = 0.044715


def extended(value, sides, width):
    for axis, dim in sides:
        peers, length = (lax.axis_size(axis), value.shape[dim])
        up = [(i, (i + 1) % peers) for i in range(peers - 1)]
        down = [(j, i) for i, j in up]
        last = lax.slice_in_dim(value, length - width, length, axis=dim)
        leading = lax.slice_in_dim(value, 0, width, axis=dim)
        before = lax.ppermute(last, axis, up)
        after = lax.ppermute(leading, axis, down)
        value = jnp.concatenate([before, value, after], axis=dim)
    return value


def from_behind(block, axis, distance):
    devices = range(lax.axis_size(axis))
    route = [(i - distance, i) for i in devices if i - distance in devices]
    return lax.ppermute(block, axis, route)


def gelu_tanh(values):
    inner = ROOT_TWO_PI * (values + CUBIC * values * values * values)
    return 0.5 * values * (1.0 + jnp.tanh(inner))


def gelu_slope(values):
    tangent = jnp.tanh(ROOT_TWO_PI * (values + CUBIC * values * values * values))
    return 0.5 * (1.0 + tangent) + 0.5 * values * (1.0 - tangent * tangent) * ROOT_TWO_PI * (
        1.0 + 3.0 * CUBIC * values * values
    )


def shards(base, noise, cot, convolution_weight, mix_w, norm_gain, qkv_w, out_w, band_width, pairs):
    conv_full, mix_full, qkv_full, out_full = (
        lax.all_gather(convolution_weight, "sa", axis=1, tiled=True),
        lax.all_gather(mix_w, "sa", axis=0, tiled=True),
        lax.all_gather(qkv_w, "sa", axis=0, tiled=True),
        lax.all_gather(out_w, "sa", axis=0, tiled=True),
    )
    sequence_bins = base.shape[0]
    samples_dev = noise.shape[0]
    stretch = sequence_bins * lax.axis_size("sb")
    sequence_length = stretch * lax.axis_size("sa")
    heads_key = HEADS * KEY
    heads_val = HEADS * VAL
    width = sequence_bins + 2 * BAND
    scale = KEY ** (-0.5)
    stretch_first = lax.axis_index("sa") * stretch
    first_row = stretch_first + lax.axis_index("sb") * sequence_bins
    row_pos = first_row + jnp.arange(sequence_bins, dtype=jnp.int32)
    ext_pos = first_row - BAND + jnp.arange(width, dtype=jnp.int32)
    stretch_pos = stretch_first + jnp.arange(stretch, dtype=jnp.int32)
    tiles = sequence_length // TILE
    tile_ids = jnp.arange(tiles, dtype=jnp.int32)
    pick_query = (pairs[:, 0][:, None] == tile_ids[None, :]).astype(jnp.float32)
    pick_key = (pairs[:, 1][:, None] == tile_ids[None, :]).astype(jnp.float32)
    table = jnp.dot(pick_query.T, pick_key)
    own_select = ((row_pos // TILE)[:, None] == tile_ids[None, :]).astype(jnp.float32)
    stretch_select = ((stretch_pos // TILE)[:, None] == tile_ids[None, :]).astype(jnp.float32)
    pair_own_rows = jnp.dot(jnp.dot(own_select, table), stretch_select.T) > 0.5
    pair_own_keys = jnp.dot(jnp.dot(stretch_select, table), own_select.T) > 0.5
    inside = (ext_pos >= 0) & (ext_pos < sequence_length)
    band_mask = inside[None, None, :] & (
        jnp.abs(row_pos[:, None] - ext_pos[None, :])[None] <= band_width[:, None, None]
    )
    far_rows = jnp.abs(row_pos[:, None] - stretch_pos[None, :])[None] > band_width[:, None, None]
    pair_mask = pair_own_rows[None] & far_rows
    key_mask = pair_own_keys[None] & jnp.transpose(far_rows, (0, 2, 1))
    noisy = base.astype(jnp.float32)[None] + noise.astype(jnp.float32)
    gelu_input = gelu_tanh(noisy).astype(jnp.bfloat16)
    gelu_extended = extended(gelu_input, ((("sa", "sb"), 1),), DILATION_BINS)
    hidden_state = jnp.zeros((samples_dev, sequence_bins, HID), jnp.float32)
    for tap_index in range(3):
        hidden_state = hidden_state + jnp.einsum(
            "nbd,dc->nbc",
            gelu_extended[:, tap_index * DILATION_BINS : tap_index * DILATION_BINS + sequence_bins],
            conv_full[tap_index],
            preferred_element_type=jnp.float32,
        )
    act = gelu_tanh(hidden_state).astype(jnp.bfloat16)
    resid = noisy + jnp.einsum("nbc,cd->nbd", act, mix_full, preferred_element_type=jnp.float32)
    inv_rms = lax.rsqrt(jnp.mean(resid * resid, axis=-1, keepdims=True) + 1e-06)
    normed = (resid * inv_rms * norm_gain).astype(jnp.bfloat16)
    proj = jnp.einsum("nbd,dc->nbc", normed, qkv_full, preferred_element_type=jnp.float32).astype(
        jnp.bfloat16
    )
    queries = proj[..., :heads_key].reshape(samples_dev, sequence_bins, HEADS, KEY)
    key_vals = proj[..., heads_key:]
    kv_ext = extended(key_vals, ((("sa", "sb"), 1),), BAND)
    kv_all = lax.all_gather(key_vals, "sb", axis=1, tiled=True)
    keys_ext = kv_ext[..., :heads_key].reshape(samples_dev, width, HEADS, KEY)
    vals_ext = kv_ext[..., heads_key:].reshape(samples_dev, width, HEADS, VAL)
    keys_all = kv_all[..., :heads_key].reshape(samples_dev, stretch, HEADS, KEY)
    vals_all = kv_all[..., heads_key:].reshape(samples_dev, stretch, HEADS, VAL)
    score_band = (
        jnp.einsum("nihd,njhd->nhij", queries, keys_ext, preferred_element_type=jnp.float32) * scale
    )
    score_band = jnp.where(band_mask[None], score_band, -1e30)
    raw_pair = jnp.einsum("nihd,njhd->nhij", queries, keys_all, preferred_element_type=jnp.float32)
    score_pair = jnp.where(pair_mask[None], raw_pair * scale, -1e30)
    top = jnp.maximum(jnp.max(score_band, axis=-1), jnp.max(score_pair, axis=-1))
    total = jnp.sum(jnp.where(band_mask[None], jnp.exp(score_band - top[..., None]), 0.0), axis=-1)
    total = total + jnp.sum(
        jnp.where(pair_mask[None], jnp.exp(score_pair - top[..., None]), 0.0), axis=-1
    )
    lse = top + jnp.log(total)
    prob_band = jnp.where(band_mask[None], jnp.exp(score_band - lse[..., None]), 0.0)
    prob_pair = jnp.where(pair_mask[None], jnp.exp(score_pair - lse[..., None]), 0.0)
    band_b = prob_band.astype(jnp.bfloat16)
    pair_b = prob_pair.astype(jnp.bfloat16)
    attn = jnp.einsum("nhij,njhe->nihe", band_b, vals_ext, preferred_element_type=jnp.float32)
    attn = attn + jnp.einsum(
        "nhij,njhe->nihe", pair_b, vals_all, preferred_element_type=jnp.float32
    )
    d_att = jnp.dot(cot, out_full.T, preferred_element_type=jnp.float32).astype(jnp.bfloat16)
    d_att_heads = d_att.reshape(sequence_bins, HEADS, VAL)
    delta = jnp.transpose(jnp.sum(d_att_heads.astype(jnp.float32)[None] * attn, axis=-1), (0, 2, 1))
    d_prob_band = jnp.einsum(
        "ihe,njhe->nhij", d_att_heads, vals_ext, preferred_element_type=jnp.float32
    )
    d_prob_pair = jnp.einsum(
        "ihe,njhe->nhij", d_att_heads, vals_all, preferred_element_type=jnp.float32
    )
    d_score_band = (prob_band * (d_prob_band - delta[..., None]) * scale).astype(jnp.bfloat16)
    d_score_pair = (prob_pair * (d_prob_pair - delta[..., None]) * scale).astype(jnp.bfloat16)
    d_query = jnp.einsum(
        "nhij,njhd->nihd", d_score_band, keys_ext, preferred_element_type=jnp.float32
    )
    d_query = d_query + jnp.einsum(
        "nhij,njhd->nihd", d_score_pair, keys_all, preferred_element_type=jnp.float32
    )
    d_key_ext = jnp.einsum(
        "nhij,nihd->njhd", d_score_band, queries, preferred_element_type=jnp.float32
    )
    d_val_ext = jnp.einsum(
        "nhij,ihe->njhe", band_b, d_att_heads, preferred_element_type=jnp.float32
    )
    d_kv_ext = jnp.concatenate(
        [
            d_key_ext.reshape(samples_dev, width, heads_key),
            d_val_ext.reshape(samples_dev, width, heads_val),
        ],
        axis=2,
    )
    from_right = from_behind(d_kv_ext[:, :BAND].astype(jnp.bfloat16), ("sa", "sb"), -1).astype(
        jnp.float32
    )
    from_left = from_behind(
        d_kv_ext[:, BAND + sequence_bins :].astype(jnp.bfloat16), ("sa", "sb"), 1
    ).astype(jnp.float32)
    d_key_vals = d_kv_ext[:, BAND : BAND + sequence_bins]
    d_key_vals = d_key_vals + from_left
    d_key_vals = d_key_vals + from_right
    statistics = jnp.stack([lse, delta], axis=1)
    query_rows = proj[..., :heads_key]
    queries_all, d_att_all = (
        lax.all_gather(query_rows, "sb", axis=1, tiled=True),
        lax.all_gather(d_att, "sb", axis=0, tiled=True),
    )
    stats_all = lax.all_gather(statistics, "sb", axis=3, tiled=True)
    queries_all = queries_all.reshape(samples_dev, stretch, HEADS, KEY)
    d_att_all = d_att_all.reshape(stretch, HEADS, VAL)
    keys_own = key_vals[..., :heads_key].reshape(samples_dev, sequence_bins, HEADS, KEY)
    vals_own = key_vals[..., heads_key:].reshape(samples_dev, sequence_bins, HEADS, VAL)
    score_key = (
        jnp.einsum("nihd,njhd->nhij", queries_all, keys_own, preferred_element_type=jnp.float32)
        * scale
    )
    prob_key = jnp.where(key_mask[None], jnp.exp(score_key - stats_all[:, 0][..., None]), 0.0)
    d_val_pair = jnp.einsum(
        "nhij,ihe->njhe",
        prob_key.astype(jnp.bfloat16),
        d_att_all,
        preferred_element_type=jnp.float32,
    )
    d_prob_key = jnp.einsum(
        "ihe,njhe->nhij", d_att_all, vals_own, preferred_element_type=jnp.float32
    )
    d_score_key = (prob_key * (d_prob_key - stats_all[:, 1][..., None]) * scale).astype(
        jnp.bfloat16
    )
    d_key_pair = jnp.einsum(
        "nhij,nihd->njhd", d_score_key, queries_all, preferred_element_type=jnp.float32
    )
    d_key_vals = d_key_vals + jnp.concatenate(
        [
            d_key_pair.reshape(samples_dev, sequence_bins, heads_key),
            d_val_pair.reshape(samples_dev, sequence_bins, heads_val),
        ],
        axis=2,
    )
    d_proj = jnp.concatenate(
        [d_query.reshape(samples_dev, sequence_bins, heads_key), d_key_vals], axis=2
    ).astype(jnp.bfloat16)
    d_normed = jnp.einsum("nbc,dc->nbd", d_proj, qkv_full, preferred_element_type=jnp.float32)
    gained = norm_gain * d_normed
    d_resid = (
        cot.astype(jnp.float32)[None]
        + inv_rms * gained
        - resid * inv_rms * inv_rms * inv_rms * jnp.mean(resid * gained, axis=-1, keepdims=True)
    )
    d_act = jnp.einsum(
        "nbd,cd->nbc", d_resid.astype(jnp.bfloat16), mix_full, preferred_element_type=jnp.float32
    )
    hidden_gradient = (d_act * gelu_slope(hidden_state)).astype(jnp.bfloat16)
    gradient_extended = extended(hidden_gradient, ((("sa", "sb"), 1),), DILATION_BINS)
    d_gelu_in = jnp.zeros((samples_dev, sequence_bins, base.shape[1]), jnp.float32)
    for tap_index in range(3):
        start_offset = (2 - tap_index) * DILATION_BINS
        d_gelu_in = d_gelu_in + jnp.einsum(
            "nbc,dc->nbd",
            gradient_extended[:, start_offset : start_offset + sequence_bins],
            conv_full[tap_index],
            preferred_element_type=jnp.float32,
        )
    grads = d_resid + d_gelu_in * gelu_slope(noisy)
    summed = lax.psum(jnp.sum(grads, axis=0).astype(jnp.bfloat16), "noise").astype(jnp.float32)
    return summed / (samples_dev * lax.axis_size("noise"))


def permuted(value, pairs):
    return lax.ppermute(value, ("sa", "sb", "noise"), pairs)


def routes(n_sa, route):
    flat = lambda z, y, x, c: ((z * 2 + y) * 2 + x) * 2 + c
    pairs = []
    for z in range(n_sa):
        for y in range(2):
            for x in range(2):
                for c in range(2):
                    target = route(z, y, x, c)
                    if target is not None and 0 <= target[0] < n_sa:
                        pairs.append((flat(z, y, x, c), flat(*target)))
    return pairs


def position():
    b = lax.axis_index("sb")
    return lax.axis_index("sa"), b // 2, lax.rem(b, 2), lax.axis_index("noise")


def half_index():
    return lax.rem(lax.axis_index("noise") + lax.axis_index("sa"), 2)


def pack_kernel(conv, mix, qkv, out, early, late):
    z, y, x, n = position()
    b = 2 * y + x
    part = b * 2 + n
    rows = pl.ds(pl.multiple_of(part * 48, 16), 48)
    half = pl.ds(pl.multiple_of(n * 48, 16), 48)
    columns = pl.ds(pl.multiple_of(b * 384, 128), 384)
    for t in range(3):
        early[pl.ds(48 * t, 48), :] = conv[t, rows, :]
    early[pl.ds(144, 48), :] = mix[half, columns]
    late[pl.ds(0, 48), :] = out[half, columns]
    for k in range(2):
        late[pl.ds(48 + 48 * k, 48), :] = qkv[rows, pl.ds(384 * k, 384)]
    for k in range(3):
        third = pl.ds(pl.multiple_of(part * 48 + 16 * k, 16), 16)
        late[pl.ds(144, 16), pl.ds(128 * k, 128)] = qkv[third, pl.ds(768, 128)]


def nt(a, b):
    return lax.dot_general(a, b, (((1,), (1,)), ((), ())), preferred_element_type=jnp.float32)


def tn(a, b):
    return lax.dot_general(a, b, (((0,), (0,)), ((), ())), preferred_element_type=jnp.float32)


def nn(a, b):
    return jnp.dot(a, b, preferred_element_type=jnp.float32)


CHUNK = 384


def chunk(c):
    return pl.ds(pl.multiple_of(c * CHUNK, 128), CHUNK)


def arrived(z, y, x, n, same, other):
    for j in range(3):
        for core, (straight, beside, across, diagonal_a, diagonal_b) in enumerate((same, other)):
            half = diagonal_a.shape[1]
            for dy in range(2):
                for dx in range(2):
                    if dy and dx:
                        first, second = diagonal_a[j], diagonal_b[j]
                    else:
                        whole = across if dy else beside if dx else straight
                        first, second = whole[j, pl.ds(0, half), :], whole[j, pl.ds(half, half), :]
                    yield j, z ^ (j + 1), y ^ dy, x ^ dx, n ^ core, first, second


def times(value, factor, unit):
    return pl.multiple_of(value * factor, unit)


def forward_kernel(
    blocks_even, blocks_odd, edge, other_even, other_odd, other_edge, *refs,
):
    own_conv, own_mix = refs[:2]
    same, other = refs[2:7], refs[7:12]
    (
        gain, normed_out, resid_out, inv_out, hidden_out, conv_out, mix_out,
        conv, mix, noisy, gelu_in, sems,
    ) = refs[12:]
    z, y, x, n = position()

    for t in range(3):
        conv[t, pl.ds(times(z, 384, 128), 384), :] = own_conv[t]
    mix[pl.ds(times(z, 96, 32), 96), :] = own_mix[...]
    for _, sz, sy, sx, sn, first, second in arrived(z, y, x, n, same, other):
        b = 2 * sy + sx
        rows = pl.ds(pl.multiple_of(sz * 384 + (b * 2 + sn) * 48, 16), 48)
        conv[0, rows, :] = first[:48]
        conv[1, rows, :] = first[48:]
        conv[2, rows, :] = second[:48]
        mix[pl.ds(pl.multiple_of(sz * 96 + sn * 48, 16), 48), pl.ds(times(b, 384, 128), 384)] = second[48:]
    copies = [
        pltpu.make_async_copy(s, d, sems.at[i]) for i, (s, d) in enumerate(((conv, conv_out), (mix, mix_out)))
    ]
    for copy in copies:
        copy.start()

    m = half_index()
    for half, (even, odd, outer) in (
        (m, (blocks_even, blocks_odd, edge)), (1 - m, (other_even, other_odd, other_edge))
    ):
        noisy[pl.ds(times(half, 176, 16), 48), :] = outer[...].astype(jnp.float32)
        for shift, block in enumerate((even, odd)):
            row = 48 + 64 * half + 32 * lax.rem(x + shift, 2)
            noisy[pl.ds(pl.multiple_of(row, 16), 32), :] = block[...].astype(jnp.float32)

    def activate(c, _):
        gelu_in[:, chunk(c)] = gelu_tanh(noisy[:, chunk(c)]).astype(jnp.bfloat16)
        return 0

    lax.fori_loop(0, 4, activate, 0)

    def convolve(c, total):
        for t in range(3):
            total = total + nn(gelu_in[pl.ds(16 * t, 192), chunk(c)], conv[t, chunk(c), :])
        return total

    hidden = lax.fori_loop(0, 4, convolve, jnp.zeros((192, HID), jnp.float32))
    hidden_out[...] = hidden[32:160]
    act = gelu_tanh(hidden).astype(jnp.bfloat16)

    def mixing(c, squares):
        resid = noisy[pl.ds(16, 192), chunk(c)] + nn(act, mix[:, chunk(c)])
        noisy[pl.ds(16, 192), chunk(c)] = resid
        resid_out[:, chunk(c)] = resid[32:160]
        return squares + jnp.sum(resid * resid, axis=1, keepdims=True)

    squares = lax.fori_loop(0, 4, mixing, jnp.zeros((192, 1), jnp.float32))
    inv_rms = lax.rsqrt(squares * (1.0 / 1536) + 1e-06)
    inv_out[...] = inv_rms[32:160]

    def normalise(c, _):
        normed = noisy[pl.ds(16, 192), chunk(c)] * inv_rms * gain[:, chunk(c)]
        normed_out[:, chunk(c)] = normed.astype(jnp.bfloat16)
        return 0

    lax.fori_loop(0, 4, normalise, 0)
    for copy in copies:
        copy.wait()


def attention_kernel(band, flag, normed, cot_block, cot_beside, other_block, other_beside, *refs):
    own_qkv, own_out = refs[:2]
    same, other = refs[2:7], refs[7:12]
    d_q_out, d_kv_out, send, qkv_out, cot_out, qkv, out, sems = refs[12:]
    z, y, x, n = position()
    length = lax.axis_size("sa") * 128
    first_bin = z * 128
    own_rows = pl.ds(times(z, 384, 128), 384)
    qkv[own_rows, :] = own_qkv[...]
    out[pl.ds(times(z, 96, 32), 96), :] = own_out[...]
    proj = nn(normed[:, own_rows], own_qkv[...])
    done = 0
    for j, sz, sy, sx, sn, first, second in arrived(z, y, x, n, same, other):
        b = 2 * sy + sx
        row = sz * 384 + (b * 2 + sn) * 48
        out[pl.ds(pl.multiple_of(sz * 96 + sn * 48, 16), 48), pl.ds(times(b, 384, 128), 384)] = first[:48]
        qkv[pl.ds(pl.multiple_of(row, 16), 32), pl.ds(0, 384)] = first[48:]
        qkv[pl.ds(pl.multiple_of(row + 32, 16), 16), pl.ds(0, 384)] = second[:16]
        qkv[pl.ds(pl.multiple_of(row, 16), 48), pl.ds(384, 384)] = second[16:64]
        for k in range(3):
            third = pl.ds(pl.multiple_of(row + 16 * k, 16), 16)
            qkv[third, pl.ds(768, 128)] = second[64:, 128 * k : 128 * k + 128]
        done += 1
        if done % 8 == 0:
            rows = pl.ds(times(sz, 384, 128), 384)
            proj = proj + nn(normed[:, rows], qkv[rows, :])
    proj = proj.astype(jnp.bfloat16)
    copy = pltpu.make_async_copy(qkv, qkv_out, sems.at[0])
    copy.start()
    m = half_index()
    for half, (block, beside) in ((m, (cot_block, cot_beside)), (1 - m, (other_block, other_beside))):
        for shift, rows in enumerate((block, beside)):
            row = 64 * half + 32 * lax.rem(x + shift, 2)
            cot_out[pl.ds(pl.multiple_of(row, 32), 32), :] = rows[...]
    d_att = nt(cot_out[...], out[...]).astype(jnp.bfloat16)

    row = lax.broadcasted_iota(jnp.int32, (128, 192), 0)
    column = lax.broadcasted_iota(jnp.int32, (128, 192), 1) - 32
    inside = (column + first_bin >= 0) & (column + first_bin < length)
    paired = (column >= 0) & (column < 128) & (flag[0] > 0)
    apart = jnp.abs(row - column)
    scale = KEY ** (-0.5)
    d_queries, d_keys, d_values = [], [], []
    for h in range(HEADS):
        q = proj[32:160, KEY * h : KEY * (h + 1)]
        k = proj[:, HEADS * KEY + KEY * h : HEADS * KEY + KEY * (h + 1)]
        v = proj[:, 2 * HEADS * KEY + VAL * h : 2 * HEADS * KEY + VAL * (h + 1)]
        d_att_h = d_att[:, VAL * h : VAL * (h + 1)]
        allowed = inside & (paired | (apart <= band[h]))
        score = jnp.where(allowed, nt(q, k) * scale, -1e30)
        top = jnp.max(score, axis=1, keepdims=True)
        raised = jnp.where(allowed, jnp.exp(score - top), 0.0)
        prob = raised / jnp.sum(raised, axis=1, keepdims=True)
        prob_b = prob.astype(jnp.bfloat16)
        attn = nn(prob_b, v)
        delta = jnp.sum(d_att_h.astype(jnp.float32) * attn, axis=1, keepdims=True)
        d_score = (prob * (nt(d_att_h, v) - delta) * scale).astype(jnp.bfloat16)
        d_queries.append(nn(d_score, k))
        d_keys.append(tn(d_score, q))
        d_values.append(tn(prob_b, d_att_h))
    d_q_out[...] = jnp.concatenate(d_queries, axis=1)
    d_kv = jnp.concatenate(d_keys + d_values, axis=1)
    d_kv_out[...] = d_kv[32:160]
    send[...] = jnp.where(m == 0, d_kv[:32], d_kv[160:]).astype(jnp.bfloat16)
    copy.wait()


def norm_kernel(
    d_q, d_kv, received, resid, inv_rms_ref, hidden, cot, gain, mix, qkv,
    d_hidden_out, d_resid_out, send, total_kv, gained, d_resid_all,
):
    n = half_index()
    total_kv[...] = d_kv[...]
    edge = pl.ds(pl.multiple_of(n * 96, 32), 32)
    total_kv[edge, :] = total_kv[edge, :] + received[...].astype(jnp.float32)
    d_proj = jnp.concatenate([d_q[...], total_kv[...]], axis=1).astype(jnp.bfloat16)
    inv_rms = inv_rms_ref[...]

    def back(c, mean):
        part = gain[:, chunk(c)] * nt(d_proj, qkv[chunk(c), :])
        gained[:, chunk(c)] = part
        return mean + jnp.sum(resid[:, chunk(c)] * part, axis=1, keepdims=True)

    mean = lax.fori_loop(0, 4, back, jnp.zeros((128, 1), jnp.float32)) * (1.0 / 1536)
    cubed = inv_rms * inv_rms * inv_rms * mean

    def residual(c, total):
        d_resid = (
            cot[:, chunk(c)].astype(jnp.float32)
            + inv_rms * gained[:, chunk(c)]
            - resid[:, chunk(c)] * cubed
        )
        d_resid_all[:, chunk(c)] = d_resid
        return total + nt(d_resid.astype(jnp.bfloat16), mix[:, chunk(c)])

    d_act = lax.fori_loop(0, 4, residual, jnp.zeros((128, HID), jnp.float32))
    d_hidden = (d_act * gelu_slope(hidden[...])).astype(jnp.bfloat16)
    d_hidden_out[...] = d_hidden
    d_resid_out[...] = d_resid_all[pl.ds(pl.multiple_of(n * 64, 64), 64), :]

    @pl.when(n == 0)
    def _():
        send[...] = d_hidden[:16]

    @pl.when(n == 1)
    def _():
        send[...] = d_hidden[112:]


def taps_kernel(d_hidden, received, d_resid, blocks_even, blocks_odd, conv, keep, send, extended_ref, noisy, grads):
    x, n = lax.rem(lax.axis_index("sb"), 2), half_index()

    @pl.when(n == 0)
    def _():
        extended_ref[pl.ds(0, 16), :] = received[...]
        extended_ref[pl.ds(16, 80), :] = d_hidden[pl.ds(0, 80), :]

    @pl.when(n == 1)
    def _():
        extended_ref[pl.ds(0, 80), :] = d_hidden[pl.ds(48, 80), :]
        extended_ref[pl.ds(80, 16), :] = received[...]

    for shift, block in enumerate((blocks_even, blocks_odd)):
        noisy[pl.ds(times(lax.rem(x + shift, 2), 32, 32), 32), :] = block[...].astype(jnp.float32)

    def taps(c, _):
        total = nt(extended_ref[pl.ds(32, 64), :], conv[0, chunk(c), :])
        total = total + nt(extended_ref[pl.ds(16, 64), :], conv[1, chunk(c), :])
        total = total + nt(extended_ref[pl.ds(0, 64), :], conv[2, chunk(c), :])
        grads[:, chunk(c)] = d_resid[:, chunk(c)] + total * gelu_slope(noisy[:, chunk(c)])
        return 0

    lax.fori_loop(0, 4, taps, 0)
    keep[...] = grads[pl.ds(pl.multiple_of(32 * x, 32), 32), :]
    send[...] = grads[pl.ds(pl.multiple_of(32 - 32 * x, 32), 32), :].astype(jnp.bfloat16)


def vmem(count):
    return [pl.BlockSpec(memory_space=pltpu.VMEM)] * count


def smem(count):
    return [pl.BlockSpec(memory_space=pltpu.SMEM)] * count


def hbm(count):
    return [pl.BlockSpec(memory_space=pl.ANY)] * count


def limit(mebibytes):
    return pltpu.CompilerParams(vmem_limit_bytes=mebibytes * 1024 * 1024)


f32, bf16 = (jnp.float32, jnp.bfloat16)


def shaped(*shape, dtype=jnp.float32):
    return jax.ShapeDtypeStruct(shape, dtype)


def stretch_shards(
    base, noise, cot, convolution_weight, mix_w, norm_gain, qkv_w, out_w, band_width, pairs
):
    n_sa = lax.axis_size("sa")
    b = lax.axis_index("sb")
    m = half_index()
    y, x = (b >> 1, b & 1)
    features = base.shape[1]

    early, late = pl.pallas_call(
        pack_kernel,
        out_shape=(shaped(192, CHUNK, dtype=bf16), shaped(160, CHUNK, dtype=bf16)),
        in_specs=vmem(4),
        out_specs=tuple(vmem(2)),
        compiler_params=limit(8),
    )(convolution_weight, mix_w, qkv_w, out_w)
    def along_z(step):
        return routes(n_sa, lambda z, y, x, c: (z ^ step, y, x, c))

    x_route = routes(n_sa, lambda z, y, x, c: (z, y, 1 - x, c))
    y_route = routes(n_sa, lambda z, y, x, c: (z, 1 - y, x, c))
    core_route = routes(n_sa, lambda z, y, x, c: (z, y, x, 1 - c))

    def over_z(piece):
        return [permuted(piece, along_z(step)) for step in range(1, 4)]

    def diagonals(beside, across):
        half = beside.shape[1] // 2
        return permuted(beside[:, :half], y_route), permuted(across[:, half:], x_route)

    def swapped(parts):
        return tuple(permuted(part, core_route) for part in parts)

    def after(values, *earlier):
        count = len(values)
        return lax.optimization_barrier((*values, *earlier))[:count]

    def to_sample(shift):
        return routes(n_sa, lambda z, y, x, c: (z, c, (x + shift) % 2, y ^ (z & 1)))

    noisy = (base.astype(f32)[None] + noise.astype(f32)).astype(bf16)
    even = x == 0
    edge_route = routes(
        n_sa, lambda z, y, x, c: (z - 1, y, x, c) if c ^ (z & 1) == 0 else (z + 1, y, x, c)
    )
    z = lax.axis_index("sa")
    flag = jnp.any((pairs[:, 0] == z) & (pairs[:, 1] == z)).astype(jnp.int32).reshape(1)
    straight = over_z(early)
    noisy, cot = after((noisy, cot), *straight[:1])
    blocks = [
        permuted(jnp.where(x == shift, noisy[0], noisy[1]), to_sample(shift)) for shift in range(2)
    ]
    across_cot = permuted(
        cot, routes(n_sa, lambda z, y, x, c: (z, 1 - y, x, c) if y == c ^ (z & 1) else None)
    )
    low, high = jnp.where(even, blocks[0], blocks[1]), jnp.where(even, blocks[1], blocks[0])
    outer = jnp.concatenate(
        [jnp.where(m == 0, low[:16], low[16:]), jnp.where(m == 0, low[16:], high[:16]), jnp.where(m == 0, high[:16], high[16:])]
    )
    cot_block = jnp.where(y == m, cot, across_cot)
    straight = jnp.stack(straight)
    straight, late, flag, outer, cot_block = after((straight, late, flag, outer, cot_block))
    beside, across = permuted(straight, x_route), permuted(straight, y_route)
    late_straight = jnp.stack(over_z(late))
    edge = permuted(outer, edge_route)
    straight, beside, across, late_straight, edge, cot_block, *blocks = after(
        (straight, beside, across, late_straight, edge, cot_block, *blocks)
    )
    early = (straight, beside, across) + diagonals(beside, across)
    late_beside, late_across = permuted(late_straight, x_route), permuted(late_straight, y_route)
    early, late, cot_block, mine = (
        lambda v: (v[:5], v[5:8], v[8], v[9:])
    )(after((*early, late_straight, late_beside, late_across, cot_block, *blocks, edge)))
    late = tuple(late) + diagonals(late[1], late[2])
    noisy_rows = tuple(mine) + swapped(mine)
    early = tuple(early) + swapped(early)
    cot_rows = (cot_block, permuted(cot_block, x_route))
    cot_rows = cot_rows + swapped(cot_rows)
    late_other = swapped(late[:3])
    gain = norm_gain.reshape(1, features)

    normed, resid, inv_rms, hidden, conv, mix = pl.pallas_call(
        forward_kernel,
        out_shape=(
            shaped(192, features, dtype=bf16), shaped(128, features), shaped(128, 1), shaped(128, HID),
            shaped(3, features, HID, dtype=bf16), shaped(HID, features, dtype=bf16),
        ),
        in_specs=vmem(19),
        out_specs=tuple(vmem(4) + hbm(2)),
        scratch_shapes=[
            pltpu.VMEM((3, features, HID), bf16), pltpu.VMEM((HID, features), bf16),
            pltpu.VMEM((224, features), f32), pltpu.VMEM((224, features), bf16),
            pltpu.SemaphoreType.DMA((2,)),
        ],
        compiler_params=limit(18),
    )(*noisy_rows, convolution_weight, mix_w, *early, gain)
    late += late_other + swapped(late[3:])
    d_q, d_kv, send, qkv, cot_all = pl.pallas_call(
        attention_kernel,
        out_shape=(
            shaped(128, 256), shaped(128, 640), shaped(32, 640, dtype=bf16), shaped(features, 896, dtype=bf16),
            shaped(128, features, dtype=bf16),
        ),
        in_specs=smem(2) + vmem(17),
        out_specs=tuple(vmem(3) + hbm(1) + vmem(1)),
        scratch_shapes=[
            pltpu.VMEM((features, 896), bf16), pltpu.VMEM((HEADS * VAL, features), bf16),
            pltpu.SemaphoreType.DMA((1,)),
        ],
        compiler_params=limit(14),
    )(band_width, flag, normed, *cot_rows, qkv_w, out_w, *late)

    received = permuted(send, edge_route)
    d_hidden, d_resid, send = pl.pallas_call(
        norm_kernel,
        out_shape=(shaped(128, HID, dtype=bf16), shaped(64, features), shaped(16, HID, dtype=bf16)),
        in_specs=vmem(10),
        out_specs=tuple(vmem(3)),
        scratch_shapes=[
            pltpu.VMEM((128, 640), f32), pltpu.VMEM((128, features), f32), pltpu.VMEM((128, features), f32),
        ],
        compiler_params=limit(12),
    )(d_q, d_kv, received, resid, inv_rms, hidden, cot_all, gain, mix, qkv)

    received = permuted(send, edge_route)
    keep, send = pl.pallas_call(
        taps_kernel,
        out_shape=(shaped(32, features), shaped(32, features, dtype=bf16)),
        in_specs=vmem(6),
        out_specs=tuple(vmem(2)),
        scratch_shapes=[
            pltpu.VMEM((96, HID), bf16), pltpu.VMEM((64, features), f32), pltpu.VMEM((64, features), f32),
        ],
        compiler_params=limit(6),
    )(d_hidden, received, d_resid, *blocks, conv)

    received = permuted(send, x_route)
    partial = (keep + received.astype(f32)).astype(bf16)
    first_sum = permuted(
        partial, routes(n_sa, lambda z, y, x, c: (z, 1 - y, x, c) if y != c ^ (z & 1) else (z, y, x, 1 - c))
    )
    second_sum = permuted(partial, routes(n_sa, lambda z, y, x, c: (z, 1 - y, x, 1 - c) if y != c ^ (z & 1) else None))
    other = jnp.where(y == m, partial, second_sum)
    return (first_sum.astype(f32) + other.astype(f32)) * 0.25


def solution(mesh):
    fits = mesh.shape["sb"] == 4 and mesh.shape["noise"] == 2 and HEADS == 4

    def body(*arrays):
        if fits and arrays[0].shape[0] == 32 and arrays[1].shape[0] == 2 and TILE == 128:
            if arrays[0].shape[1] == 1536 and mesh.shape["sa"] == 4:
                return stretch_shards(*arrays)
        return shards(*arrays)

    return jax.shard_map(
        body,
        mesh=mesh,
        in_specs=(
            P(("sa", "sb"), None),
            P("noise", ("sa", "sb"), None),
            P(("sa", "sb"), None),
            P(None, "sa", None),
            P("sa", None),
            P(),
            P("sa", None),
            P("sa", None),
            P(),
            P(),
        ),
        out_specs=P(("sa", "sb"), None),
        check_vma=False,
    )
```

```python
import jax
import jax.numpy as jnp
from jax import lax
from jax.experimental import pallas as pl
from jax.experimental.pallas import tpu as pltpu
from jax.sharding import PartitionSpec as P

HID = 384
HEADS = 4
KEY = 64
VAL = 96
DILATION_BINS = 16
BAND = 32
TILE = 128


ROOT_TWO_PI = 0.7978845608
CUBIC = 0.044715


def extended(value, sides, width):
    for axis, dim in sides:
        peers, length = (lax.axis_size(axis), value.shape[dim])
        up = [(i, (i + 1) % peers) for i in range(peers - 1)]
        down = [(j, i) for i, j in up]
        last = lax.slice_in_dim(value, length - width, length, axis=dim)
        leading = lax.slice_in_dim(value, 0, width, axis=dim)
        before = lax.ppermute(last, axis, up)
        after = lax.ppermute(leading, axis, down)
        value = jnp.concatenate([before, value, after], axis=dim)
    return value


def from_behind(block, axis, distance):
    devices = range(lax.axis_size(axis))
    route = [(i - distance, i) for i in devices if i - distance in devices]
    return lax.ppermute(block, axis, route)


def gelu_tanh(values):
    inner = ROOT_TWO_PI * (values + CUBIC * values * values * values)
    return 0.5 * values * (1.0 + jnp.tanh(inner))


def gelu_slope(values):
    tangent = jnp.tanh(ROOT_TWO_PI * (values + CUBIC * values * values * values))
    return 0.5 * (1.0 + tangent) + 0.5 * values * (1.0 - tangent * tangent) * ROOT_TWO_PI * (
        1.0 + 3.0 * CUBIC * values * values
    )


def shards(base, noise, cot, convolution_weight, mix_w, norm_gain, qkv_w, out_w, band_width, pairs):
    conv_full, mix_full, qkv_full, out_full = (
        lax.all_gather(convolution_weight, "sa", axis=1, tiled=True),
        lax.all_gather(mix_w, "sa", axis=0, tiled=True),
        lax.all_gather(qkv_w, "sa", axis=0, tiled=True),
        lax.all_gather(out_w, "sa", axis=0, tiled=True),
    )
    sequence_bins = base.shape[0]
    samples_dev = noise.shape[0]
    stretch = sequence_bins * lax.axis_size("sb")
    sequence_length = stretch * lax.axis_size("sa")
    heads_key = HEADS * KEY
    heads_val = HEADS * VAL
    width = sequence_bins + 2 * BAND
    scale = KEY ** (-0.5)
    stretch_first = lax.axis_index("sa") * stretch
    first_row = stretch_first + lax.axis_index("sb") * sequence_bins
    row_pos = first_row + jnp.arange(sequence_bins, dtype=jnp.int32)
    ext_pos = first_row - BAND + jnp.arange(width, dtype=jnp.int32)
    stretch_pos = stretch_first + jnp.arange(stretch, dtype=jnp.int32)
    tiles = sequence_length // TILE
    tile_ids = jnp.arange(tiles, dtype=jnp.int32)
    pick_query = (pairs[:, 0][:, None] == tile_ids[None, :]).astype(jnp.float32)
    pick_key = (pairs[:, 1][:, None] == tile_ids[None, :]).astype(jnp.float32)
    table = jnp.dot(pick_query.T, pick_key)
    own_select = ((row_pos // TILE)[:, None] == tile_ids[None, :]).astype(jnp.float32)
    stretch_select = ((stretch_pos // TILE)[:, None] == tile_ids[None, :]).astype(jnp.float32)
    pair_own_rows = jnp.dot(jnp.dot(own_select, table), stretch_select.T) > 0.5
    pair_own_keys = jnp.dot(jnp.dot(stretch_select, table), own_select.T) > 0.5
    inside = (ext_pos >= 0) & (ext_pos < sequence_length)
    band_mask = inside[None, None, :] & (
        jnp.abs(row_pos[:, None] - ext_pos[None, :])[None] <= band_width[:, None, None]
    )
    far_rows = jnp.abs(row_pos[:, None] - stretch_pos[None, :])[None] > band_width[:, None, None]
    pair_mask = pair_own_rows[None] & far_rows
    key_mask = pair_own_keys[None] & jnp.transpose(far_rows, (0, 2, 1))
    noisy = base.astype(jnp.float32)[None] + noise.astype(jnp.float32)
    gelu_input = gelu_tanh(noisy).astype(jnp.bfloat16)
    gelu_extended = extended(gelu_input, ((("sa", "sb"), 1),), DILATION_BINS)
    hidden_state = jnp.zeros((samples_dev, sequence_bins, HID), jnp.float32)
    for tap_index in range(3):
        hidden_state = hidden_state + jnp.einsum(
            "nbd,dc->nbc",
            gelu_extended[:, tap_index * DILATION_BINS : tap_index * DILATION_BINS + sequence_bins],
            conv_full[tap_index],
            preferred_element_type=jnp.float32,
        )
    act = gelu_tanh(hidden_state).astype(jnp.bfloat16)
    resid = noisy + jnp.einsum("nbc,cd->nbd", act, mix_full, preferred_element_type=jnp.float32)
    inv_rms = lax.rsqrt(jnp.mean(resid * resid, axis=-1, keepdims=True) + 1e-06)
    normed = (resid * inv_rms * norm_gain).astype(jnp.bfloat16)
    proj = jnp.einsum("nbd,dc->nbc", normed, qkv_full, preferred_element_type=jnp.float32).astype(
        jnp.bfloat16
    )
    queries = proj[..., :heads_key].reshape(samples_dev, sequence_bins, HEADS, KEY)
    key_vals = proj[..., heads_key:]
    kv_ext = extended(key_vals, ((("sa", "sb"), 1),), BAND)
    kv_all = lax.all_gather(key_vals, "sb", axis=1, tiled=True)
    keys_ext = kv_ext[..., :heads_key].reshape(samples_dev, width, HEADS, KEY)
    vals_ext = kv_ext[..., heads_key:].reshape(samples_dev, width, HEADS, VAL)
    keys_all = kv_all[..., :heads_key].reshape(samples_dev, stretch, HEADS, KEY)
    vals_all = kv_all[..., heads_key:].reshape(samples_dev, stretch, HEADS, VAL)
    score_band = (
        jnp.einsum("nihd,njhd->nhij", queries, keys_ext, preferred_element_type=jnp.float32) * scale
    )
    score_band = jnp.where(band_mask[None], score_band, -1e30)
    raw_pair = jnp.einsum("nihd,njhd->nhij", queries, keys_all, preferred_element_type=jnp.float32)
    score_pair = jnp.where(pair_mask[None], raw_pair * scale, -1e30)
    top = jnp.maximum(jnp.max(score_band, axis=-1), jnp.max(score_pair, axis=-1))
    total = jnp.sum(jnp.where(band_mask[None], jnp.exp(score_band - top[..., None]), 0.0), axis=-1)
    total = total + jnp.sum(
        jnp.where(pair_mask[None], jnp.exp(score_pair - top[..., None]), 0.0), axis=-1
    )
    lse = top + jnp.log(total)
    prob_band = jnp.where(band_mask[None], jnp.exp(score_band - lse[..., None]), 0.0)
    prob_pair = jnp.where(pair_mask[None], jnp.exp(score_pair - lse[..., None]), 0.0)
    band_b = prob_band.astype(jnp.bfloat16)
    pair_b = prob_pair.astype(jnp.bfloat16)
    attn = jnp.einsum("nhij,njhe->nihe", band_b, vals_ext, preferred_element_type=jnp.float32)
    attn = attn + jnp.einsum(
        "nhij,njhe->nihe", pair_b, vals_all, preferred_element_type=jnp.float32
    )
    d_att = jnp.dot(cot, out_full.T, preferred_element_type=jnp.float32).astype(jnp.bfloat16)
    d_att_heads = d_att.reshape(sequence_bins, HEADS, VAL)
    delta = jnp.transpose(jnp.sum(d_att_heads.astype(jnp.float32)[None] * attn, axis=-1), (0, 2, 1))
    d_prob_band = jnp.einsum(
        "ihe,njhe->nhij", d_att_heads, vals_ext, preferred_element_type=jnp.float32
    )
    d_prob_pair = jnp.einsum(
        "ihe,njhe->nhij", d_att_heads, vals_all, preferred_element_type=jnp.float32
    )
    d_score_band = (prob_band * (d_prob_band - delta[..., None]) * scale).astype(jnp.bfloat16)
    d_score_pair = (prob_pair * (d_prob_pair - delta[..., None]) * scale).astype(jnp.bfloat16)
    d_query = jnp.einsum(
        "nhij,njhd->nihd", d_score_band, keys_ext, preferred_element_type=jnp.float32
    )
    d_query = d_query + jnp.einsum(
        "nhij,njhd->nihd", d_score_pair, keys_all, preferred_element_type=jnp.float32
    )
    d_key_ext = jnp.einsum(
        "nhij,nihd->njhd", d_score_band, queries, preferred_element_type=jnp.float32
    )
    d_val_ext = jnp.einsum(
        "nhij,ihe->njhe", band_b, d_att_heads, preferred_element_type=jnp.float32
    )
    d_kv_ext = jnp.concatenate(
        [
            d_key_ext.reshape(samples_dev, width, heads_key),
            d_val_ext.reshape(samples_dev, width, heads_val),
        ],
        axis=2,
    )
    from_right = from_behind(d_kv_ext[:, :BAND].astype(jnp.bfloat16), ("sa", "sb"), -1).astype(
        jnp.float32
    )
    from_left = from_behind(
        d_kv_ext[:, BAND + sequence_bins :].astype(jnp.bfloat16), ("sa", "sb"), 1
    ).astype(jnp.float32)
    d_key_vals = d_kv_ext[:, BAND : BAND + sequence_bins]
    d_key_vals = d_key_vals + from_left
    d_key_vals = d_key_vals + from_right
    statistics = jnp.stack([lse, delta], axis=1)
    query_rows = proj[..., :heads_key]
    queries_all, d_att_all = (
        lax.all_gather(query_rows, "sb", axis=1, tiled=True),
        lax.all_gather(d_att, "sb", axis=0, tiled=True),
    )
    stats_all = lax.all_gather(statistics, "sb", axis=3, tiled=True)
    queries_all = queries_all.reshape(samples_dev, stretch, HEADS, KEY)
    d_att_all = d_att_all.reshape(stretch, HEADS, VAL)
    keys_own = key_vals[..., :heads_key].reshape(samples_dev, sequence_bins, HEADS, KEY)
    vals_own = key_vals[..., heads_key:].reshape(samples_dev, sequence_bins, HEADS, VAL)
    score_key = (
        jnp.einsum("nihd,njhd->nhij", queries_all, keys_own, preferred_element_type=jnp.float32)
        * scale
    )
    prob_key = jnp.where(key_mask[None], jnp.exp(score_key - stats_all[:, 0][..., None]), 0.0)
    d_val_pair = jnp.einsum(
        "nhij,ihe->njhe",
        prob_key.astype(jnp.bfloat16),
        d_att_all,
        preferred_element_type=jnp.float32,
    )
    d_prob_key = jnp.einsum(
        "ihe,njhe->nhij", d_att_all, vals_own, preferred_element_type=jnp.float32
    )
    d_score_key = (prob_key * (d_prob_key - stats_all[:, 1][..., None]) * scale).astype(
        jnp.bfloat16
    )
    d_key_pair = jnp.einsum(
        "nhij,nihd->njhd", d_score_key, queries_all, preferred_element_type=jnp.float32
    )
    d_key_vals = d_key_vals + jnp.concatenate(
        [
            d_key_pair.reshape(samples_dev, sequence_bins, heads_key),
            d_val_pair.reshape(samples_dev, sequence_bins, heads_val),
        ],
        axis=2,
    )
    d_proj = jnp.concatenate(
        [d_query.reshape(samples_dev, sequence_bins, heads_key), d_key_vals], axis=2
    ).astype(jnp.bfloat16)
    d_normed = jnp.einsum("nbc,dc->nbd", d_proj, qkv_full, preferred_element_type=jnp.float32)
    gained = norm_gain * d_normed
    d_resid = (
        cot.astype(jnp.float32)[None]
        + inv_rms * gained
        - resid * inv_rms * inv_rms * inv_rms * jnp.mean(resid * gained, axis=-1, keepdims=True)
    )
    d_act = jnp.einsum(
        "nbd,cd->nbc", d_resid.astype(jnp.bfloat16), mix_full, preferred_element_type=jnp.float32
    )
    hidden_gradient = (d_act * gelu_slope(hidden_state)).astype(jnp.bfloat16)
    gradient_extended = extended(hidden_gradient, ((("sa", "sb"), 1),), DILATION_BINS)
    d_gelu_in = jnp.zeros((samples_dev, sequence_bins, base.shape[1]), jnp.float32)
    for tap_index in range(3):
        start_offset = (2 - tap_index) * DILATION_BINS
        d_gelu_in = d_gelu_in + jnp.einsum(
            "nbc,dc->nbd",
            gradient_extended[:, start_offset : start_offset + sequence_bins],
            conv_full[tap_index],
            preferred_element_type=jnp.float32,
        )
    grads = d_resid + d_gelu_in * gelu_slope(noisy)
    summed = lax.psum(jnp.sum(grads, axis=0).astype(jnp.bfloat16), "noise").astype(jnp.float32)
    return summed / (samples_dev * lax.axis_size("noise"))


def permuted(value, pairs):
    return lax.ppermute(value, ("sa", "sb", "noise"), pairs)


def routes(n_sa, route):
    flat = lambda z, y, x, c: ((z * 2 + y) * 2 + x) * 2 + c
    pairs = []
    for z in range(n_sa):
        for y in range(2):
            for x in range(2):
                for c in range(2):
                    target = route(z, y, x, c)
                    if target is not None and 0 <= target[0] < n_sa:
                        pairs.append((flat(z, y, x, c), flat(*target)))
    return pairs


def position():
    b = lax.axis_index("sb")
    return lax.axis_index("sa"), b // 2, lax.rem(b, 2), lax.axis_index("noise")


def half_index():
    return lax.rem(lax.axis_index("noise") + lax.axis_index("sa"), 2)


def pack_kernel(conv, mix, qkv, out, early, late, taps, rows_qkv, sems):
    z, y, x, n = position()
    b = 2 * y + x
    part = b * 2 + n
    rows = pl.ds(pl.multiple_of(part * 48, 16), 48)
    half = pl.ds(pl.multiple_of(n * 48, 16), 48)
    columns = pl.ds(pl.multiple_of(b * 384, 128), 384)
    pairs = (
        (conv.at[:, rows, :], taps), (mix.at[half, columns], early.at[pl.ds(144, 48), :]),
        (qkv.at[rows, :], rows_qkv), (out.at[half, columns], late.at[pl.ds(0, 48), :]),
    )
    copies = [pltpu.make_async_copy(source, target, sems.at[i]) for i, (source, target) in enumerate(pairs)]
    for copy in copies:
        copy.start()
    for copy in copies:
        copy.wait()
    for t in range(3):
        early[pl.ds(48 * t, 48), :] = taps[t]
    for k in range(2):
        late[pl.ds(48 + 48 * k, 48), :] = rows_qkv[:, pl.ds(384 * k, 384)]
    for k in range(3):
        late[pl.ds(144, 16), pl.ds(128 * k, 128)] = rows_qkv[pl.ds(16 * k, 16), pl.ds(768, 128)]


def nt(a, b):
    return lax.dot_general(a, b, (((1,), (1,)), ((), ())), preferred_element_type=jnp.float32)


def tn(a, b):
    return lax.dot_general(a, b, (((0,), (0,)), ((), ())), preferred_element_type=jnp.float32)


def nn(a, b):
    return jnp.dot(a, b, preferred_element_type=jnp.float32)


CHUNK = 384


def chunk(c):
    return pl.ds(pl.multiple_of(c * CHUNK, 128), CHUNK)


def arrived(z, y, x, n, same, other):
    for j in range(3):
        for core, (straight, beside, across, diagonal_a, diagonal_b) in enumerate((same, other)):
            half = diagonal_a.shape[1]
            for dy in range(2):
                for dx in range(2):
                    if dy and dx:
                        first, second = diagonal_a[j], diagonal_b[j]
                    else:
                        whole = across if dy else beside if dx else straight
                        first, second = whole[j, pl.ds(0, half), :], whole[j, pl.ds(half, half), :]
                    yield j, z ^ (j + 1), y ^ dy, x ^ dx, n ^ core, first, second


def times(value, factor, unit):
    return pl.multiple_of(value * factor, unit)


def forward_kernel(
    blocks_even, blocks_odd, edge, other_even, other_odd, other_edge, *refs,
):
    own_conv, own_mix = refs[:2]
    same, other = refs[2:7], refs[7:12]
    (
        gain, normed_out, resid_out, inv_out, hidden_out, conv_out, mix_out,
        conv, mix, noisy, gelu_in, sems,
    ) = refs[12:]
    z, y, x, n = position()

    for t in range(3):
        conv[t, pl.ds(times(z, 384, 128), 384), :] = own_conv[t]
    mix[pl.ds(times(z, 96, 32), 96), :] = own_mix[...]
    for _, sz, sy, sx, sn, first, second in arrived(z, y, x, n, same, other):
        b = 2 * sy + sx
        rows = pl.ds(pl.multiple_of(sz * 384 + (b * 2 + sn) * 48, 16), 48)
        conv[0, rows, :] = first[:48]
        conv[1, rows, :] = first[48:]
        conv[2, rows, :] = second[:48]
        mix[pl.ds(pl.multiple_of(sz * 96 + sn * 48, 16), 48), pl.ds(times(b, 384, 128), 384)] = second[48:]
    copies = [
        pltpu.make_async_copy(s, d, sems.at[i]) for i, (s, d) in enumerate(((conv, conv_out), (mix, mix_out)))
    ]
    for copy in copies:
        copy.start()

    m = half_index()
    for half, (even, odd, outer) in (
        (m, (blocks_even, blocks_odd, edge)), (1 - m, (other_even, other_odd, other_edge))
    ):
        noisy[pl.ds(times(half, 176, 16), 48), :] = outer[...].astype(jnp.float32)
        for shift, block in enumerate((even, odd)):
            row = 48 + 64 * half + 32 * lax.rem(x + shift, 2)
            noisy[pl.ds(pl.multiple_of(row, 16), 32), :] = block[...].astype(jnp.float32)

    def activate(c, _):
        gelu_in[:, chunk(c)] = gelu_tanh(noisy[:, chunk(c)]).astype(jnp.bfloat16)
        return 0

    lax.fori_loop(0, 4, activate, 0)

    def convolve(c, total):
        for t in range(3):
            total = total + nn(gelu_in[pl.ds(16 * t, 192), chunk(c)], conv[t, chunk(c), :])
        return total

    hidden = lax.fori_loop(0, 4, convolve, jnp.zeros((192, HID), jnp.float32))
    hidden_out[...] = hidden[32:160]
    act = gelu_tanh(hidden).astype(jnp.bfloat16)

    def mixing(c, squares):
        resid = noisy[pl.ds(16, 192), chunk(c)] + nn(act, mix[:, chunk(c)])
        noisy[pl.ds(16, 192), chunk(c)] = resid
        resid_out[:, chunk(c)] = resid[32:160]
        return squares + jnp.sum(resid * resid, axis=1, keepdims=True)

    squares = lax.fori_loop(0, 4, mixing, jnp.zeros((192, 1), jnp.float32))
    inv_rms = lax.rsqrt(squares * (1.0 / 1536) + 1e-06)
    inv_out[...] = inv_rms[32:160]

    def normalise(c, _):
        normed = noisy[pl.ds(16, 192), chunk(c)] * inv_rms * gain[:, chunk(c)]
        normed_out[:, chunk(c)] = normed.astype(jnp.bfloat16)
        return 0

    lax.fori_loop(0, 4, normalise, 0)
    for copy in copies:
        copy.wait()


def attention_kernel(band, flag, normed, cot_block, cot_beside, other_block, other_beside, *refs):
    own_qkv, own_out = refs[:2]
    same, other = refs[2:7], refs[7:12]
    d_q_out, d_kv_out, send, qkv_out, cot_out, qkv, out, sems = refs[12:]
    z, y, x, n = position()
    length = lax.axis_size("sa") * 128
    first_bin = z * 128
    own_rows = pl.ds(times(z, 384, 128), 384)
    qkv[own_rows, :] = own_qkv[...]
    out[pl.ds(times(z, 96, 32), 96), :] = own_out[...]
    proj = nn(normed[:, own_rows], own_qkv[...])
    done = 0
    for j, sz, sy, sx, sn, first, second in arrived(z, y, x, n, same, other):
        b = 2 * sy + sx
        row = sz * 384 + (b * 2 + sn) * 48
        out[pl.ds(pl.multiple_of(sz * 96 + sn * 48, 16), 48), pl.ds(times(b, 384, 128), 384)] = first[:48]
        qkv[pl.ds(pl.multiple_of(row, 16), 32), pl.ds(0, 384)] = first[48:]
        qkv[pl.ds(pl.multiple_of(row + 32, 16), 16), pl.ds(0, 384)] = second[:16]
        qkv[pl.ds(pl.multiple_of(row, 16), 48), pl.ds(384, 384)] = second[16:64]
        for k in range(3):
            third = pl.ds(pl.multiple_of(row + 16 * k, 16), 16)
            qkv[third, pl.ds(768, 128)] = second[64:, 128 * k : 128 * k + 128]
        done += 1
        if done % 8 == 0:
            rows = pl.ds(times(sz, 384, 128), 384)
            proj = proj + nn(normed[:, rows], qkv[rows, :])
    proj = proj.astype(jnp.bfloat16)
    copy = pltpu.make_async_copy(qkv, qkv_out, sems.at[0])
    copy.start()
    m = half_index()
    for half, (block, beside) in ((m, (cot_block, cot_beside)), (1 - m, (other_block, other_beside))):
        for shift, rows in enumerate((block, beside)):
            row = 64 * half + 32 * lax.rem(x + shift, 2)
            cot_out[pl.ds(pl.multiple_of(row, 32), 32), :] = rows[...]
    d_att = nt(cot_out[...], out[...]).astype(jnp.bfloat16)

    row = lax.broadcasted_iota(jnp.int32, (128, 192), 0)
    column = lax.broadcasted_iota(jnp.int32, (128, 192), 1) - 32
    inside = (column + first_bin >= 0) & (column + first_bin < length)
    paired = (column >= 0) & (column < 128) & (flag[0] > 0)
    apart = jnp.abs(row - column)
    scale = KEY ** (-0.5)
    d_queries, d_keys, d_values = [], [], []
    for h in range(HEADS):
        q = proj[32:160, KEY * h : KEY * (h + 1)]
        k = proj[:, HEADS * KEY + KEY * h : HEADS * KEY + KEY * (h + 1)]
        v = proj[:, 2 * HEADS * KEY + VAL * h : 2 * HEADS * KEY + VAL * (h + 1)]
        d_att_h = d_att[:, VAL * h : VAL * (h + 1)]
        allowed = inside & (paired | (apart <= band[h]))
        score = jnp.where(allowed, nt(q, k) * scale, -1e30)
        top = jnp.max(score, axis=1, keepdims=True)
        raised = jnp.where(allowed, jnp.exp(score - top), 0.0)
        prob = raised / jnp.sum(raised, axis=1, keepdims=True)
        prob_b = prob.astype(jnp.bfloat16)
        attn = nn(prob_b, v)
        delta = jnp.sum(d_att_h.astype(jnp.float32) * attn, axis=1, keepdims=True)
        d_score = (prob * (nt(d_att_h, v) - delta) * scale).astype(jnp.bfloat16)
        d_queries.append(nn(d_score, k))
        d_keys.append(tn(d_score, q))
        d_values.append(tn(prob_b, d_att_h))
    d_q_out[...] = jnp.concatenate(d_queries, axis=1)
    d_kv = jnp.concatenate(d_keys + d_values, axis=1)
    d_kv_out[...] = d_kv[32:160]
    send[...] = jnp.where(m == 0, d_kv[:32], d_kv[160:]).astype(jnp.bfloat16)
    copy.wait()


def norm_kernel(
    d_q, d_kv, received, resid, inv_rms_ref, hidden, cot, gain, mix, qkv,
    d_hidden_out, d_resid_out, send, total_kv, gained, d_resid_all,
):
    n = half_index()
    total_kv[...] = d_kv[...]
    edge = pl.ds(pl.multiple_of(n * 96, 32), 32)
    total_kv[edge, :] = total_kv[edge, :] + received[...].astype(jnp.float32)
    d_proj = jnp.concatenate([d_q[...], total_kv[...]], axis=1).astype(jnp.bfloat16)
    inv_rms = inv_rms_ref[...]

    def back(c, mean):
        part = gain[:, chunk(c)] * nt(d_proj, qkv[chunk(c), :])
        gained[:, chunk(c)] = part
        return mean + jnp.sum(resid[:, chunk(c)] * part, axis=1, keepdims=True)

    mean = lax.fori_loop(0, 4, back, jnp.zeros((128, 1), jnp.float32)) * (1.0 / 1536)
    cubed = inv_rms * inv_rms * inv_rms * mean

    def residual(c, total):
        d_resid = (
            cot[:, chunk(c)].astype(jnp.float32)
            + inv_rms * gained[:, chunk(c)]
            - resid[:, chunk(c)] * cubed
        )
        d_resid_all[:, chunk(c)] = d_resid
        return total + nt(d_resid.astype(jnp.bfloat16), mix[:, chunk(c)])

    d_act = lax.fori_loop(0, 4, residual, jnp.zeros((128, HID), jnp.float32))
    d_hidden = (d_act * gelu_slope(hidden[...])).astype(jnp.bfloat16)
    d_hidden_out[...] = d_hidden
    d_resid_out[...] = d_resid_all[pl.ds(pl.multiple_of(n * 64, 64), 64), :]

    @pl.when(n == 0)
    def _():
        send[...] = d_hidden[:16]

    @pl.when(n == 1)
    def _():
        send[...] = d_hidden[112:]


def taps_kernel(d_hidden, received, d_resid, blocks_even, blocks_odd, conv, keep, send, extended_ref, noisy, grads):
    x, n = lax.rem(lax.axis_index("sb"), 2), half_index()

    @pl.when(n == 0)
    def _():
        extended_ref[pl.ds(0, 16), :] = received[...]
        extended_ref[pl.ds(16, 80), :] = d_hidden[pl.ds(0, 80), :]

    @pl.when(n == 1)
    def _():
        extended_ref[pl.ds(0, 80), :] = d_hidden[pl.ds(48, 80), :]
        extended_ref[pl.ds(80, 16), :] = received[...]

    for shift, block in enumerate((blocks_even, blocks_odd)):
        noisy[pl.ds(times(lax.rem(x + shift, 2), 32, 32), 32), :] = block[...].astype(jnp.float32)

    def taps(c, _):
        total = nt(extended_ref[pl.ds(32, 64), :], conv[0, chunk(c), :])
        total = total + nt(extended_ref[pl.ds(16, 64), :], conv[1, chunk(c), :])
        total = total + nt(extended_ref[pl.ds(0, 64), :], conv[2, chunk(c), :])
        grads[:, chunk(c)] = d_resid[:, chunk(c)] + total * gelu_slope(noisy[:, chunk(c)])
        return 0

    lax.fori_loop(0, 4, taps, 0)
    keep[...] = grads[pl.ds(pl.multiple_of(32 * x, 32), 32), :]
    send[...] = grads[pl.ds(pl.multiple_of(32 - 32 * x, 32), 32), :].astype(jnp.bfloat16)


def vmem(count):
    return [pl.BlockSpec(memory_space=pltpu.VMEM)] * count


def smem(count):
    return [pl.BlockSpec(memory_space=pltpu.SMEM)] * count


def hbm(count):
    return [pl.BlockSpec(memory_space=pl.ANY)] * count


def limit(mebibytes):
    return pltpu.CompilerParams(vmem_limit_bytes=mebibytes * 1024 * 1024)


f32, bf16 = (jnp.float32, jnp.bfloat16)


def shaped(*shape, dtype=jnp.float32):
    return jax.ShapeDtypeStruct(shape, dtype)


def stretch_shards(
    base, noise, cot, convolution_weight, mix_w, norm_gain, qkv_w, out_w, band_width, pairs
):
    n_sa = lax.axis_size("sa")
    b = lax.axis_index("sb")
    m = half_index()
    y, x = (b >> 1, b & 1)
    features = base.shape[1]

    early, late = pl.pallas_call(
        pack_kernel,
        out_shape=(shaped(192, CHUNK, dtype=bf16), shaped(160, CHUNK, dtype=bf16)),
        in_specs=hbm(4),
        out_specs=tuple(vmem(2)),
        scratch_shapes=[
            pltpu.VMEM((3, 48, HID), bf16), pltpu.VMEM((48, 896), bf16), pltpu.SemaphoreType.DMA((4,))
        ],
        compiler_params=limit(4),
    )(convolution_weight, mix_w, qkv_w, out_w)
    def along_z(step):
        return routes(n_sa, lambda z, y, x, c: (z ^ step, y, x, c))

    x_route = routes(n_sa, lambda z, y, x, c: (z, y, 1 - x, c))
    y_route = routes(n_sa, lambda z, y, x, c: (z, 1 - y, x, c))
    core_route = routes(n_sa, lambda z, y, x, c: (z, y, x, 1 - c))

    def over_z(piece):
        return [permuted(piece, along_z(step)) for step in range(1, 4)]

    def diagonals(beside, across):
        half = beside.shape[1] // 2
        return permuted(beside[:, :half], y_route), permuted(across[:, half:], x_route)

    def swapped(parts):
        return tuple(permuted(part, core_route) for part in parts)

    def after(values, *earlier):
        count = len(values)
        return lax.optimization_barrier((*values, *earlier))[:count]

    def to_sample(shift):
        return routes(n_sa, lambda z, y, x, c: (z, c, (x + shift) % 2, y ^ (z & 1)))

    noisy = (base.astype(f32)[None] + noise.astype(f32)).astype(bf16)
    even = x == 0
    edge_route = routes(
        n_sa, lambda z, y, x, c: (z - 1, y, x, c) if c ^ (z & 1) == 0 else (z + 1, y, x, c)
    )
    z = lax.axis_index("sa")
    flag = jnp.any((pairs[:, 0] == z) & (pairs[:, 1] == z)).astype(jnp.int32).reshape(1)
    straight = over_z(early)
    noisy, cot = after((noisy, cot), *straight[:1])
    blocks = [
        permuted(jnp.where(x == shift, noisy[0], noisy[1]), to_sample(shift)) for shift in range(2)
    ]
    across_cot = permuted(
        cot, routes(n_sa, lambda z, y, x, c: (z, 1 - y, x, c) if y == c ^ (z & 1) else None)
    )
    low, high = jnp.where(even, blocks[0], blocks[1]), jnp.where(even, blocks[1], blocks[0])
    outer = jnp.concatenate(
        [jnp.where(m == 0, low[:16], low[16:]), jnp.where(m == 0, low[16:], high[:16]), jnp.where(m == 0, high[:16], high[16:])]
    )
    cot_block = jnp.where(y == m, cot, across_cot)
    straight = jnp.stack(straight)
    straight, late, flag, outer, cot_block = after((straight, late, flag, outer, cot_block))
    beside, across = permuted(straight, x_route), permuted(straight, y_route)
    late_straight = jnp.stack(over_z(late))
    straight_other = permuted(straight, core_route)
    straight, beside, across, late_straight, outer, cot_block, straight_other, *blocks = after(
        (straight, beside, across, late_straight, outer, cot_block, straight_other, *blocks)
    )
    early = (straight, beside, across) + diagonals(beside, across)
    late_beside, late_across = permuted(late_straight, x_route), permuted(late_straight, y_route)
    cot_rows = (cot_block, permuted(cot_block, x_route))
    mine = (*blocks, permuted(outer, edge_route))
    early, late, cot_rows, mine = (
        lambda v: (v[:5], v[5:8], v[8:10], v[10:])
    )(after((*early, late_straight, late_beside, late_across, *cot_rows, *mine)))
    late = tuple(late) + diagonals(late[1], late[2])
    noisy_rows = tuple(mine) + swapped(mine)
    early = tuple(early) + (straight_other,) + swapped(early[1:])
    cot_rows = tuple(cot_rows) + swapped(cot_rows)
    late_other = swapped(late[:3])
    gain = norm_gain.reshape(1, features)

    normed, resid, inv_rms, hidden, conv, mix = pl.pallas_call(
        forward_kernel,
        out_shape=(
            shaped(192, features, dtype=bf16), shaped(128, features), shaped(128, 1), shaped(128, HID),
            shaped(3, features, HID, dtype=bf16), shaped(HID, features, dtype=bf16),
        ),
        in_specs=vmem(19),
        out_specs=tuple(vmem(4) + hbm(2)),
        scratch_shapes=[
            pltpu.VMEM((3, features, HID), bf16), pltpu.VMEM((HID, features), bf16),
            pltpu.VMEM((224, features), f32), pltpu.VMEM((224, features), bf16),
            pltpu.SemaphoreType.DMA((2,)),
        ],
        compiler_params=limit(18),
    )(*noisy_rows, convolution_weight, mix_w, *early, gain)
    late += late_other + swapped(late[3:])
    d_q, d_kv, send, qkv, cot_all = pl.pallas_call(
        attention_kernel,
        out_shape=(
            shaped(128, 256), shaped(128, 640), shaped(32, 640, dtype=bf16), shaped(features, 896, dtype=bf16),
            shaped(128, features, dtype=bf16),
        ),
        in_specs=smem(2) + vmem(17),
        out_specs=tuple(vmem(3) + hbm(1) + vmem(1)),
        scratch_shapes=[
            pltpu.VMEM((features, 896), bf16), pltpu.VMEM((HEADS * VAL, features), bf16),
            pltpu.SemaphoreType.DMA((1,)),
        ],
        compiler_params=limit(14),
    )(band_width, flag, normed, *cot_rows, qkv_w, out_w, *late)

    received = permuted(send, edge_route)
    d_hidden, d_resid, send = pl.pallas_call(
        norm_kernel,
        out_shape=(shaped(128, HID, dtype=bf16), shaped(64, features), shaped(16, HID, dtype=bf16)),
        in_specs=vmem(10),
        out_specs=tuple(vmem(3)),
        scratch_shapes=[
            pltpu.VMEM((128, 640), f32), pltpu.VMEM((128, features), f32), pltpu.VMEM((128, features), f32),
        ],
        compiler_params=limit(12),
    )(d_q, d_kv, received, resid, inv_rms, hidden, cot_all, gain, mix, qkv)

    received = permuted(send, edge_route)
    keep, send = pl.pallas_call(
        taps_kernel,
        out_shape=(shaped(32, features), shaped(32, features, dtype=bf16)),
        in_specs=vmem(6),
        out_specs=tuple(vmem(2)),
        scratch_shapes=[
            pltpu.VMEM((96, HID), bf16), pltpu.VMEM((64, features), f32), pltpu.VMEM((64, features), f32),
        ],
        compiler_params=limit(6),
    )(d_hidden, received, d_resid, *blocks, conv)

    received = permuted(send, x_route)
    partial = (keep + received.astype(f32)).astype(bf16)
    received = permuted(partial, y_route)
    total = (partial.astype(f32) + received.astype(f32)) * 0.25
    swapped_total = permuted(total, core_route)
    return jnp.where(y == m, total, swapped_total)


def solution(mesh):
    fits = mesh.shape["sb"] == 4 and mesh.shape["noise"] == 2 and HEADS == 4

    def body(*arrays):
        if fits and arrays[0].shape[0] == 32 and arrays[1].shape[0] == 2 and TILE == 128:
            if arrays[0].shape[1] == 1536 and mesh.shape["sa"] == 4:
                return stretch_shards(*arrays)
        return shards(*arrays)

    return jax.shard_map(
        body,
        mesh=mesh,
        in_specs=(
            P(("sa", "sb"), None),
            P("noise", ("sa", "sb"), None),
            P(("sa", "sb"), None),
            P(None, "sa", None),
            P("sa", None),
            P(),
            P("sa", None),
            P("sa", None),
            P(),
            P(),
        ),
        out_specs=P(("sa", "sb"), None),
        check_vma=False,
    )
```

```python
import jax
import jax.numpy as jnp
from jax import lax
from jax.experimental import pallas as pl
from jax.experimental.pallas import tpu as pltpu
from jax.sharding import PartitionSpec as P

HID = 384
HEADS = 4
KEY = 64
VAL = 96
DILATION_BINS = 16
BAND = 32
TILE = 128


ROOT_TWO_PI = 0.7978845608
CUBIC = 0.044715


def extended(value, sides, width):
    for axis, dim in sides:
        peers, length = (lax.axis_size(axis), value.shape[dim])
        up = [(i, (i + 1) % peers) for i in range(peers - 1)]
        down = [(j, i) for i, j in up]
        last = lax.slice_in_dim(value, length - width, length, axis=dim)
        leading = lax.slice_in_dim(value, 0, width, axis=dim)
        before = lax.ppermute(last, axis, up)
        after = lax.ppermute(leading, axis, down)
        value = jnp.concatenate([before, value, after], axis=dim)
    return value


def from_behind(block, axis, distance):
    devices = range(lax.axis_size(axis))
    route = [(i - distance, i) for i in devices if i - distance in devices]
    return lax.ppermute(block, axis, route)


def gelu_tanh(values):
    inner = ROOT_TWO_PI * (values + CUBIC * values * values * values)
    return 0.5 * values * (1.0 + jnp.tanh(inner))


def gelu_slope(values):
    tangent = jnp.tanh(ROOT_TWO_PI * (values + CUBIC * values * values * values))
    return 0.5 * (1.0 + tangent) + 0.5 * values * (1.0 - tangent * tangent) * ROOT_TWO_PI * (
        1.0 + 3.0 * CUBIC * values * values
    )


def shards(base, noise, cot, convolution_weight, mix_w, norm_gain, qkv_w, out_w, band_width, pairs):
    conv_full, mix_full, qkv_full, out_full = (
        lax.all_gather(convolution_weight, "sa", axis=1, tiled=True),
        lax.all_gather(mix_w, "sa", axis=0, tiled=True),
        lax.all_gather(qkv_w, "sa", axis=0, tiled=True),
        lax.all_gather(out_w, "sa", axis=0, tiled=True),
    )
    sequence_bins = base.shape[0]
    samples_dev = noise.shape[0]
    stretch = sequence_bins * lax.axis_size("sb")
    sequence_length = stretch * lax.axis_size("sa")
    heads_key = HEADS * KEY
    heads_val = HEADS * VAL
    width = sequence_bins + 2 * BAND
    scale = KEY ** (-0.5)
    stretch_first = lax.axis_index("sa") * stretch
    first_row = stretch_first + lax.axis_index("sb") * sequence_bins
    row_pos = first_row + jnp.arange(sequence_bins, dtype=jnp.int32)
    ext_pos = first_row - BAND + jnp.arange(width, dtype=jnp.int32)
    stretch_pos = stretch_first + jnp.arange(stretch, dtype=jnp.int32)
    tiles = sequence_length // TILE
    tile_ids = jnp.arange(tiles, dtype=jnp.int32)
    pick_query = (pairs[:, 0][:, None] == tile_ids[None, :]).astype(jnp.float32)
    pick_key = (pairs[:, 1][:, None] == tile_ids[None, :]).astype(jnp.float32)
    table = jnp.dot(pick_query.T, pick_key)
    own_select = ((row_pos // TILE)[:, None] == tile_ids[None, :]).astype(jnp.float32)
    stretch_select = ((stretch_pos // TILE)[:, None] == tile_ids[None, :]).astype(jnp.float32)
    pair_own_rows = jnp.dot(jnp.dot(own_select, table), stretch_select.T) > 0.5
    pair_own_keys = jnp.dot(jnp.dot(stretch_select, table), own_select.T) > 0.5
    inside = (ext_pos >= 0) & (ext_pos < sequence_length)
    band_mask = inside[None, None, :] & (
        jnp.abs(row_pos[:, None] - ext_pos[None, :])[None] <= band_width[:, None, None]
    )
    far_rows = jnp.abs(row_pos[:, None] - stretch_pos[None, :])[None] > band_width[:, None, None]
    pair_mask = pair_own_rows[None] & far_rows
    key_mask = pair_own_keys[None] & jnp.transpose(far_rows, (0, 2, 1))
    noisy = base.astype(jnp.float32)[None] + noise.astype(jnp.float32)
    gelu_input = gelu_tanh(noisy).astype(jnp.bfloat16)
    gelu_extended = extended(gelu_input, ((("sa", "sb"), 1),), DILATION_BINS)
    hidden_state = jnp.zeros((samples_dev, sequence_bins, HID), jnp.float32)
    for tap_index in range(3):
        hidden_state = hidden_state + jnp.einsum(
            "nbd,dc->nbc",
            gelu_extended[:, tap_index * DILATION_BINS : tap_index * DILATION_BINS + sequence_bins],
            conv_full[tap_index],
            preferred_element_type=jnp.float32,
        )
    act = gelu_tanh(hidden_state).astype(jnp.bfloat16)
    resid = noisy + jnp.einsum("nbc,cd->nbd", act, mix_full, preferred_element_type=jnp.float32)
    inv_rms = lax.rsqrt(jnp.mean(resid * resid, axis=-1, keepdims=True) + 1e-06)
    normed = (resid * inv_rms * norm_gain).astype(jnp.bfloat16)
    proj = jnp.einsum("nbd,dc->nbc", normed, qkv_full, preferred_element_type=jnp.float32).astype(
        jnp.bfloat16
    )
    queries = proj[..., :heads_key].reshape(samples_dev, sequence_bins, HEADS, KEY)
    key_vals = proj[..., heads_key:]
    kv_ext = extended(key_vals, ((("sa", "sb"), 1),), BAND)
    kv_all = lax.all_gather(key_vals, "sb", axis=1, tiled=True)
    keys_ext = kv_ext[..., :heads_key].reshape(samples_dev, width, HEADS, KEY)
    vals_ext = kv_ext[..., heads_key:].reshape(samples_dev, width, HEADS, VAL)
    keys_all = kv_all[..., :heads_key].reshape(samples_dev, stretch, HEADS, KEY)
    vals_all = kv_all[..., heads_key:].reshape(samples_dev, stretch, HEADS, VAL)
    score_band = (
        jnp.einsum("nihd,njhd->nhij", queries, keys_ext, preferred_element_type=jnp.float32) * scale
    )
    score_band = jnp.where(band_mask[None], score_band, -1e30)
    raw_pair = jnp.einsum("nihd,njhd->nhij", queries, keys_all, preferred_element_type=jnp.float32)
    score_pair = jnp.where(pair_mask[None], raw_pair * scale, -1e30)
    top = jnp.maximum(jnp.max(score_band, axis=-1), jnp.max(score_pair, axis=-1))
    total = jnp.sum(jnp.where(band_mask[None], jnp.exp(score_band - top[..., None]), 0.0), axis=-1)
    total = total + jnp.sum(
        jnp.where(pair_mask[None], jnp.exp(score_pair - top[..., None]), 0.0), axis=-1
    )
    lse = top + jnp.log(total)
    prob_band = jnp.where(band_mask[None], jnp.exp(score_band - lse[..., None]), 0.0)
    prob_pair = jnp.where(pair_mask[None], jnp.exp(score_pair - lse[..., None]), 0.0)
    band_b = prob_band.astype(jnp.bfloat16)
    pair_b = prob_pair.astype(jnp.bfloat16)
    attn = jnp.einsum("nhij,njhe->nihe", band_b, vals_ext, preferred_element_type=jnp.float32)
    attn = attn + jnp.einsum(
        "nhij,njhe->nihe", pair_b, vals_all, preferred_element_type=jnp.float32
    )
    d_att = jnp.dot(cot, out_full.T, preferred_element_type=jnp.float32).astype(jnp.bfloat16)
    d_att_heads = d_att.reshape(sequence_bins, HEADS, VAL)
    delta = jnp.transpose(jnp.sum(d_att_heads.astype(jnp.float32)[None] * attn, axis=-1), (0, 2, 1))
    d_prob_band = jnp.einsum(
        "ihe,njhe->nhij", d_att_heads, vals_ext, preferred_element_type=jnp.float32
    )
    d_prob_pair = jnp.einsum(
        "ihe,njhe->nhij", d_att_heads, vals_all, preferred_element_type=jnp.float32
    )
    d_score_band = (prob_band * (d_prob_band - delta[..., None]) * scale).astype(jnp.bfloat16)
    d_score_pair = (prob_pair * (d_prob_pair - delta[..., None]) * scale).astype(jnp.bfloat16)
    d_query = jnp.einsum(
        "nhij,njhd->nihd", d_score_band, keys_ext, preferred_element_type=jnp.float32
    )
    d_query = d_query + jnp.einsum(
        "nhij,njhd->nihd", d_score_pair, keys_all, preferred_element_type=jnp.float32
    )
    d_key_ext = jnp.einsum(
        "nhij,nihd->njhd", d_score_band, queries, preferred_element_type=jnp.float32
    )
    d_val_ext = jnp.einsum(
        "nhij,ihe->njhe", band_b, d_att_heads, preferred_element_type=jnp.float32
    )
    d_kv_ext = jnp.concatenate(
        [
            d_key_ext.reshape(samples_dev, width, heads_key),
            d_val_ext.reshape(samples_dev, width, heads_val),
        ],
        axis=2,
    )
    from_right = from_behind(d_kv_ext[:, :BAND].astype(jnp.bfloat16), ("sa", "sb"), -1).astype(
        jnp.float32
    )
    from_left = from_behind(
        d_kv_ext[:, BAND + sequence_bins :].astype(jnp.bfloat16), ("sa", "sb"), 1
    ).astype(jnp.float32)
    d_key_vals = d_kv_ext[:, BAND : BAND + sequence_bins]
    d_key_vals = d_key_vals + from_left
    d_key_vals = d_key_vals + from_right
    statistics = jnp.stack([lse, delta], axis=1)
    query_rows = proj[..., :heads_key]
    queries_all, d_att_all = (
        lax.all_gather(query_rows, "sb", axis=1, tiled=True),
        lax.all_gather(d_att, "sb", axis=0, tiled=True),
    )
    stats_all = lax.all_gather(statistics, "sb", axis=3, tiled=True)
    queries_all = queries_all.reshape(samples_dev, stretch, HEADS, KEY)
    d_att_all = d_att_all.reshape(stretch, HEADS, VAL)
    keys_own = key_vals[..., :heads_key].reshape(samples_dev, sequence_bins, HEADS, KEY)
    vals_own = key_vals[..., heads_key:].reshape(samples_dev, sequence_bins, HEADS, VAL)
    score_key = (
        jnp.einsum("nihd,njhd->nhij", queries_all, keys_own, preferred_element_type=jnp.float32)
        * scale
    )
    prob_key = jnp.where(key_mask[None], jnp.exp(score_key - stats_all[:, 0][..., None]), 0.0)
    d_val_pair = jnp.einsum(
        "nhij,ihe->njhe",
        prob_key.astype(jnp.bfloat16),
        d_att_all,
        preferred_element_type=jnp.float32,
    )
    d_prob_key = jnp.einsum(
        "ihe,njhe->nhij", d_att_all, vals_own, preferred_element_type=jnp.float32
    )
    d_score_key = (prob_key * (d_prob_key - stats_all[:, 1][..., None]) * scale).astype(
        jnp.bfloat16
    )
    d_key_pair = jnp.einsum(
        "nhij,nihd->njhd", d_score_key, queries_all, preferred_element_type=jnp.float32
    )
    d_key_vals = d_key_vals + jnp.concatenate(
        [
            d_key_pair.reshape(samples_dev, sequence_bins, heads_key),
            d_val_pair.reshape(samples_dev, sequence_bins, heads_val),
        ],
        axis=2,
    )
    d_proj = jnp.concatenate(
        [d_query.reshape(samples_dev, sequence_bins, heads_key), d_key_vals], axis=2
    ).astype(jnp.bfloat16)
    d_normed = jnp.einsum("nbc,dc->nbd", d_proj, qkv_full, preferred_element_type=jnp.float32)
    gained = norm_gain * d_normed
    d_resid = (
        cot.astype(jnp.float32)[None]
        + inv_rms * gained
        - resid * inv_rms * inv_rms * inv_rms * jnp.mean(resid * gained, axis=-1, keepdims=True)
    )
    d_act = jnp.einsum(
        "nbd,cd->nbc", d_resid.astype(jnp.bfloat16), mix_full, preferred_element_type=jnp.float32
    )
    hidden_gradient = (d_act * gelu_slope(hidden_state)).astype(jnp.bfloat16)
    gradient_extended = extended(hidden_gradient, ((("sa", "sb"), 1),), DILATION_BINS)
    d_gelu_in = jnp.zeros((samples_dev, sequence_bins, base.shape[1]), jnp.float32)
    for tap_index in range(3):
        start_offset = (2 - tap_index) * DILATION_BINS
        d_gelu_in = d_gelu_in + jnp.einsum(
            "nbc,dc->nbd",
            gradient_extended[:, start_offset : start_offset + sequence_bins],
            conv_full[tap_index],
            preferred_element_type=jnp.float32,
        )
    grads = d_resid + d_gelu_in * gelu_slope(noisy)
    summed = lax.psum(jnp.sum(grads, axis=0).astype(jnp.bfloat16), "noise").astype(jnp.float32)
    return summed / (samples_dev * lax.axis_size("noise"))


def permuted(value, pairs):
    return lax.ppermute(value, ("sa", "sb", "noise"), pairs)


def routes(n_sa, route):
    flat = lambda z, y, x, c: ((z * 2 + y) * 2 + x) * 2 + c
    pairs = []
    for z in range(n_sa):
        for y in range(2):
            for x in range(2):
                for c in range(2):
                    target = route(z, y, x, c)
                    if target is not None and 0 <= target[0] < n_sa:
                        pairs.append((flat(z, y, x, c), flat(*target)))
    return pairs


def position():
    b = lax.axis_index("sb")
    return lax.axis_index("sa"), b // 2, lax.rem(b, 2), lax.axis_index("noise")


def half_index():
    return lax.rem(lax.axis_index("noise") + lax.axis_index("sa"), 2)


def pack_kernel(conv, mix, qkv, out, early, late, taps, rows_qkv, sems):
    z, y, x, n = position()
    b = 2 * y + x
    part = b * 2 + n
    rows = pl.ds(pl.multiple_of(part * 48, 16), 48)
    half = pl.ds(pl.multiple_of(n * 48, 16), 48)
    columns = pl.ds(pl.multiple_of(b * 384, 128), 384)
    pairs = (
        (conv.at[:, rows, :], taps), (mix.at[half, columns], early.at[pl.ds(144, 48), :]),
        (qkv.at[rows, :], rows_qkv), (out.at[half, columns], late.at[pl.ds(0, 48), :]),
    )
    copies = [pltpu.make_async_copy(source, target, sems.at[i]) for i, (source, target) in enumerate(pairs)]
    for copy in copies:
        copy.start()
    for copy in copies:
        copy.wait()
    for t in range(3):
        early[pl.ds(48 * t, 48), :] = taps[t]
    for k in range(2):
        late[pl.ds(48 + 48 * k, 48), :] = rows_qkv[:, pl.ds(384 * k, 384)]
    for k in range(3):
        late[pl.ds(144, 16), pl.ds(128 * k, 128)] = rows_qkv[pl.ds(16 * k, 16), pl.ds(768, 128)]


def nt(a, b):
    return lax.dot_general(a, b, (((1,), (1,)), ((), ())), preferred_element_type=jnp.float32)


def tn(a, b):
    return lax.dot_general(a, b, (((0,), (0,)), ((), ())), preferred_element_type=jnp.float32)


def nn(a, b):
    return jnp.dot(a, b, preferred_element_type=jnp.float32)


CHUNK = 384


def chunk(c):
    return pl.ds(pl.multiple_of(c * CHUNK, 128), CHUNK)


def arrived(z, y, x, n, same, other):
    for j in range(3):
        for core, (straight, beside, across, diagonal_a, diagonal_b) in enumerate((same, other)):
            half = diagonal_a.shape[1]
            for dy in range(2):
                for dx in range(2):
                    if dy and dx:
                        first, second = diagonal_a[j], diagonal_b[j]
                    else:
                        whole = across if dy else beside if dx else straight
                        first, second = whole[j, pl.ds(0, half), :], whole[j, pl.ds(half, half), :]
                    yield j, z ^ (j + 1), y ^ dy, x ^ dx, n ^ core, first, second


def times(value, factor, unit):
    return pl.multiple_of(value * factor, unit)


def forward_kernel(
    blocks_even, blocks_odd, edge, other_even, other_odd, other_edge, *refs,
):
    own_conv, own_mix = refs[:2]
    same, other = refs[2:7], refs[7:12]
    (
        gain, normed_out, resid_out, inv_out, hidden_out, conv_out, mix_out,
        conv, mix, noisy, gelu_in, sems,
    ) = refs[12:]
    z, y, x, n = position()

    for t in range(3):
        conv[t, pl.ds(times(z, 384, 128), 384), :] = own_conv[t]
    mix[pl.ds(times(z, 96, 32), 96), :] = own_mix[...]
    for _, sz, sy, sx, sn, first, second in arrived(z, y, x, n, same, other):
        b = 2 * sy + sx
        rows = pl.ds(pl.multiple_of(sz * 384 + (b * 2 + sn) * 48, 16), 48)
        conv[0, rows, :] = first[:48]
        conv[1, rows, :] = first[48:]
        conv[2, rows, :] = second[:48]
        mix[pl.ds(pl.multiple_of(sz * 96 + sn * 48, 16), 48), pl.ds(times(b, 384, 128), 384)] = second[48:]
    copies = [
        pltpu.make_async_copy(s, d, sems.at[i]) for i, (s, d) in enumerate(((conv, conv_out), (mix, mix_out)))
    ]
    for copy in copies:
        copy.start()

    m = half_index()
    for half, (even, odd, outer) in (
        (m, (blocks_even, blocks_odd, edge)), (1 - m, (other_even, other_odd, other_edge))
    ):
        noisy[pl.ds(times(half, 176, 16), 48), :] = outer[...].astype(jnp.float32)
        for shift, block in enumerate((even, odd)):
            row = 48 + 64 * half + 32 * lax.rem(x + shift, 2)
            noisy[pl.ds(pl.multiple_of(row, 16), 32), :] = block[...].astype(jnp.float32)

    def activate(c, _):
        gelu_in[:, chunk(c)] = gelu_tanh(noisy[:, chunk(c)]).astype(jnp.bfloat16)
        return 0

    lax.fori_loop(0, 4, activate, 0)

    def convolve(c, total):
        for t in range(3):
            total = total + nn(gelu_in[pl.ds(16 * t, 192), chunk(c)], conv[t, chunk(c), :])
        return total

    hidden = lax.fori_loop(0, 4, convolve, jnp.zeros((192, HID), jnp.float32))
    hidden_out[...] = hidden[32:160]
    act = gelu_tanh(hidden).astype(jnp.bfloat16)

    def mixing(c, squares):
        resid = noisy[pl.ds(16, 192), chunk(c)] + nn(act, mix[:, chunk(c)])
        noisy[pl.ds(16, 192), chunk(c)] = resid
        resid_out[:, chunk(c)] = resid[32:160]
        return squares + jnp.sum(resid * resid, axis=1, keepdims=True)

    squares = lax.fori_loop(0, 4, mixing, jnp.zeros((192, 1), jnp.float32))
    inv_rms = lax.rsqrt(squares * (1.0 / 1536) + 1e-06)
    inv_out[...] = inv_rms[32:160]

    def normalise(c, _):
        normed = noisy[pl.ds(16, 192), chunk(c)] * inv_rms * gain[:, chunk(c)]
        normed_out[:, chunk(c)] = normed.astype(jnp.bfloat16)
        return 0

    lax.fori_loop(0, 4, normalise, 0)
    for copy in copies:
        copy.wait()


def attention_kernel(band, flag, normed, cot_block, cot_beside, other_block, other_beside, *refs):
    own_qkv, own_out = refs[:2]
    same, other = refs[2:7], refs[7:12]
    d_q_out, d_kv_out, send, qkv_out, cot_out, qkv, out, sems = refs[12:]
    z, y, x, n = position()
    length = lax.axis_size("sa") * 128
    first_bin = z * 128
    own_rows = pl.ds(times(z, 384, 128), 384)
    qkv[own_rows, :] = own_qkv[...]
    out[pl.ds(times(z, 96, 32), 96), :] = own_out[...]
    proj = nn(normed[:, own_rows], own_qkv[...])
    done = 0
    for j, sz, sy, sx, sn, first, second in arrived(z, y, x, n, same, other):
        b = 2 * sy + sx
        row = sz * 384 + (b * 2 + sn) * 48
        out[pl.ds(pl.multiple_of(sz * 96 + sn * 48, 16), 48), pl.ds(times(b, 384, 128), 384)] = first[:48]
        qkv[pl.ds(pl.multiple_of(row, 16), 32), pl.ds(0, 384)] = first[48:]
        qkv[pl.ds(pl.multiple_of(row + 32, 16), 16), pl.ds(0, 384)] = second[:16]
        qkv[pl.ds(pl.multiple_of(row, 16), 48), pl.ds(384, 384)] = second[16:64]
        for k in range(3):
            third = pl.ds(pl.multiple_of(row + 16 * k, 16), 16)
            qkv[third, pl.ds(768, 128)] = second[64:, 128 * k : 128 * k + 128]
        done += 1
        if done % 8 == 0:
            rows = pl.ds(times(sz, 384, 128), 384)
            proj = proj + nn(normed[:, rows], qkv[rows, :])
    proj = proj.astype(jnp.bfloat16)
    copy = pltpu.make_async_copy(qkv, qkv_out, sems.at[0])
    copy.start()
    m = half_index()
    for half, (block, beside) in ((m, (cot_block, cot_beside)), (1 - m, (other_block, other_beside))):
        for shift, rows in enumerate((block, beside)):
            row = 64 * half + 32 * lax.rem(x + shift, 2)
            cot_out[pl.ds(pl.multiple_of(row, 32), 32), :] = rows[...]
    d_att = nt(cot_out[...], out[...]).astype(jnp.bfloat16)

    row = lax.broadcasted_iota(jnp.int32, (128, 192), 0)
    column = lax.broadcasted_iota(jnp.int32, (128, 192), 1) - 32
    inside = (column + first_bin >= 0) & (column + first_bin < length)
    paired = (column >= 0) & (column < 128) & (flag[0] > 0)
    apart = jnp.abs(row - column)
    scale = KEY ** (-0.5)
    d_queries, d_keys, d_values = [], [], []
    for h in range(HEADS):
        q = proj[32:160, KEY * h : KEY * (h + 1)]
        k = proj[:, HEADS * KEY + KEY * h : HEADS * KEY + KEY * (h + 1)]
        v = proj[:, 2 * HEADS * KEY + VAL * h : 2 * HEADS * KEY + VAL * (h + 1)]
        d_att_h = d_att[:, VAL * h : VAL * (h + 1)]
        allowed = inside & (paired | (apart <= band[h]))
        score = jnp.where(allowed, nt(q, k) * scale, -1e30)
        top = jnp.max(score, axis=1, keepdims=True)
        raised = jnp.where(allowed, jnp.exp(score - top), 0.0)
        prob = raised / jnp.sum(raised, axis=1, keepdims=True)
        prob_b = prob.astype(jnp.bfloat16)
        attn = nn(prob_b, v)
        delta = jnp.sum(d_att_h.astype(jnp.float32) * attn, axis=1, keepdims=True)
        d_score = (prob * (nt(d_att_h, v) - delta) * scale).astype(jnp.bfloat16)
        d_queries.append(nn(d_score, k))
        d_keys.append(tn(d_score, q))
        d_values.append(tn(prob_b, d_att_h))
    d_q_out[...] = jnp.concatenate(d_queries, axis=1)
    d_kv = jnp.concatenate(d_keys + d_values, axis=1)
    d_kv_out[...] = d_kv[32:160]
    send[...] = jnp.where(m == 0, d_kv[:32], d_kv[160:]).astype(jnp.bfloat16)
    copy.wait()


def norm_kernel(
    d_q, d_kv, received, resid, inv_rms_ref, hidden, cot, gain, mix, qkv,
    d_hidden_out, d_resid_out, send, total_kv, gained, d_resid_all,
):
    n = half_index()
    total_kv[...] = d_kv[...]
    edge = pl.ds(pl.multiple_of(n * 96, 32), 32)
    total_kv[edge, :] = total_kv[edge, :] + received[...].astype(jnp.float32)
    d_proj = jnp.concatenate([d_q[...], total_kv[...]], axis=1).astype(jnp.bfloat16)
    inv_rms = inv_rms_ref[...]

    def back(c, mean):
        part = gain[:, chunk(c)] * nt(d_proj, qkv[chunk(c), :])
        gained[:, chunk(c)] = part
        return mean + jnp.sum(resid[:, chunk(c)] * part, axis=1, keepdims=True)

    mean = lax.fori_loop(0, 4, back, jnp.zeros((128, 1), jnp.float32)) * (1.0 / 1536)
    cubed = inv_rms * inv_rms * inv_rms * mean

    def residual(c, total):
        d_resid = (
            cot[:, chunk(c)].astype(jnp.float32)
            + inv_rms * gained[:, chunk(c)]
            - resid[:, chunk(c)] * cubed
        )
        d_resid_all[:, chunk(c)] = d_resid
        return total + nt(d_resid.astype(jnp.bfloat16), mix[:, chunk(c)])

    d_act = lax.fori_loop(0, 4, residual, jnp.zeros((128, HID), jnp.float32))
    d_hidden = (d_act * gelu_slope(hidden[...])).astype(jnp.bfloat16)
    d_hidden_out[...] = d_hidden
    d_resid_out[...] = d_resid_all[pl.ds(pl.multiple_of(n * 64, 64), 64), :]

    @pl.when(n == 0)
    def _():
        send[...] = d_hidden[:16]

    @pl.when(n == 1)
    def _():
        send[...] = d_hidden[112:]


def taps_kernel(d_hidden, received, d_resid, blocks_even, blocks_odd, conv, keep, send, extended_ref, noisy, grads):
    x, n = lax.rem(lax.axis_index("sb"), 2), half_index()

    @pl.when(n == 0)
    def _():
        extended_ref[pl.ds(0, 16), :] = received[...]
        extended_ref[pl.ds(16, 80), :] = d_hidden[pl.ds(0, 80), :]

    @pl.when(n == 1)
    def _():
        extended_ref[pl.ds(0, 80), :] = d_hidden[pl.ds(48, 80), :]
        extended_ref[pl.ds(80, 16), :] = received[...]

    for shift, block in enumerate((blocks_even, blocks_odd)):
        noisy[pl.ds(times(lax.rem(x + shift, 2), 32, 32), 32), :] = block[...].astype(jnp.float32)

    def taps(c, _):
        total = nt(extended_ref[pl.ds(32, 64), :], conv[0, chunk(c), :])
        total = total + nt(extended_ref[pl.ds(16, 64), :], conv[1, chunk(c), :])
        total = total + nt(extended_ref[pl.ds(0, 64), :], conv[2, chunk(c), :])
        grads[:, chunk(c)] = d_resid[:, chunk(c)] + total * gelu_slope(noisy[:, chunk(c)])
        return 0

    lax.fori_loop(0, 4, taps, 0)
    keep[...] = grads[pl.ds(pl.multiple_of(32 * x, 32), 32), :]
    send[...] = grads[pl.ds(pl.multiple_of(32 - 32 * x, 32), 32), :].astype(jnp.bfloat16)


def vmem(count):
    return [pl.BlockSpec(memory_space=pltpu.VMEM)] * count


def smem(count):
    return [pl.BlockSpec(memory_space=pltpu.SMEM)] * count


def hbm(count):
    return [pl.BlockSpec(memory_space=pl.ANY)] * count


def limit(mebibytes):
    return pltpu.CompilerParams(vmem_limit_bytes=mebibytes * 1024 * 1024)


f32, bf16 = (jnp.float32, jnp.bfloat16)


def shaped(*shape, dtype=jnp.float32):
    return jax.ShapeDtypeStruct(shape, dtype)


def stretch_shards(
    base, noise, cot, convolution_weight, mix_w, norm_gain, qkv_w, out_w, band_width, pairs
):
    n_sa = lax.axis_size("sa")
    b = lax.axis_index("sb")
    m = half_index()
    y, x = (b >> 1, b & 1)
    features = base.shape[1]

    early, late = pl.pallas_call(
        pack_kernel,
        out_shape=(shaped(192, CHUNK, dtype=bf16), shaped(160, CHUNK, dtype=bf16)),
        in_specs=[pl.BlockSpec(memory_space=pltpu.HBM)] * 4,
        out_specs=tuple(vmem(2)),
        scratch_shapes=[
            pltpu.VMEM((3, 48, HID), bf16), pltpu.VMEM((48, 896), bf16), pltpu.SemaphoreType.DMA((4,))
        ],
        compiler_params=limit(60),
    )(convolution_weight, mix_w, qkv_w, out_w)
    def along_z(step):
        return routes(n_sa, lambda z, y, x, c: (z ^ step, y, x, c))

    x_route = routes(n_sa, lambda z, y, x, c: (z, y, 1 - x, c))
    y_route = routes(n_sa, lambda z, y, x, c: (z, 1 - y, x, c))
    core_route = routes(n_sa, lambda z, y, x, c: (z, y, x, 1 - c))

    def over_z(piece):
        return [permuted(piece, along_z(step)) for step in range(1, 4)]

    def diagonals(beside, across):
        half = beside.shape[1] // 2
        return permuted(beside[:, :half], y_route), permuted(across[:, half:], x_route)

    def swapped(parts):
        return tuple(permuted(part, core_route) for part in parts)

    def after(values, *earlier):
        count = len(values)
        return lax.optimization_barrier((*values, *earlier))[:count]

    def to_sample(shift):
        return routes(n_sa, lambda z, y, x, c: (z, c, (x + shift) % 2, y ^ (z & 1)))

    noisy = (base.astype(f32)[None] + noise.astype(f32)).astype(bf16)
    even = x == 0
    edge_route = routes(
        n_sa, lambda z, y, x, c: (z - 1, y, x, c) if c ^ (z & 1) == 0 else (z + 1, y, x, c)
    )
    z = lax.axis_index("sa")
    flag = jnp.any((pairs[:, 0] == z) & (pairs[:, 1] == z)).astype(jnp.int32).reshape(1)
    straight = over_z(early)
    noisy, cot = after((noisy, cot), *straight[:1])
    blocks = [
        permuted(jnp.where(x == shift, noisy[0], noisy[1]), to_sample(shift)) for shift in range(2)
    ]
    across_cot = permuted(
        cot, routes(n_sa, lambda z, y, x, c: (z, 1 - y, x, c) if y == c ^ (z & 1) else None)
    )
    low, high = jnp.where(even, blocks[0], blocks[1]), jnp.where(even, blocks[1], blocks[0])
    outer = jnp.concatenate(
        [jnp.where(m == 0, low[:16], low[16:]), jnp.where(m == 0, low[16:], high[:16]), jnp.where(m == 0, high[:16], high[16:])]
    )
    cot_block = jnp.where(y == m, cot, across_cot)
    straight = jnp.stack(straight)
    straight, late, flag, outer, cot_block = after((straight, late, flag, outer, cot_block))
    beside, across = permuted(straight, x_route), permuted(straight, y_route)
    late_straight = jnp.stack(over_z(late))
    edge = permuted(outer, edge_route)
    straight, beside, across, late_straight, edge, cot_block, *blocks = after(
        (straight, beside, across, late_straight, edge, cot_block, *blocks)
    )
    early = (straight, beside, across) + diagonals(beside, across)
    late_beside, late_across = permuted(late_straight, x_route), permuted(late_straight, y_route)
    cot_rows = (cot_block, permuted(cot_block, x_route))
    early, late, cot_rows, mine = (
        lambda v: (v[:5], v[5:8], v[8:10], v[10:])
    )(after((*early, late_straight, late_beside, late_across, *cot_rows, *blocks, edge)))
    late = tuple(late) + diagonals(late[1], late[2])
    noisy_rows = tuple(mine) + swapped(mine)
    early = tuple(early) + swapped(early)
    cot_rows = tuple(cot_rows) + swapped(cot_rows)
    late_other = swapped(late[:3])
    gain = norm_gain.reshape(1, features)

    normed, resid, inv_rms, hidden, conv, mix = pl.pallas_call(
        forward_kernel,
        out_shape=(
            shaped(192, features, dtype=bf16), shaped(128, features), shaped(128, 1), shaped(128, HID),
            shaped(3, features, HID, dtype=bf16), shaped(HID, features, dtype=bf16),
        ),
        in_specs=vmem(19),
        out_specs=tuple(vmem(4) + hbm(2)),
        scratch_shapes=[
            pltpu.VMEM((3, features, HID), bf16), pltpu.VMEM((HID, features), bf16),
            pltpu.VMEM((224, features), f32), pltpu.VMEM((224, features), bf16),
            pltpu.SemaphoreType.DMA((2,)),
        ],
        compiler_params=limit(18),
    )(*noisy_rows, convolution_weight, mix_w, *early, gain)
    late += late_other + swapped(late[3:])
    d_q, d_kv, send, qkv, cot_all = pl.pallas_call(
        attention_kernel,
        out_shape=(
            shaped(128, 256), shaped(128, 640), shaped(32, 640, dtype=bf16), shaped(features, 896, dtype=bf16),
            shaped(128, features, dtype=bf16),
        ),
        in_specs=smem(2) + vmem(17),
        out_specs=tuple(vmem(3) + hbm(1) + vmem(1)),
        scratch_shapes=[
            pltpu.VMEM((features, 896), bf16), pltpu.VMEM((HEADS * VAL, features), bf16),
            pltpu.SemaphoreType.DMA((1,)),
        ],
        compiler_params=limit(14),
    )(band_width, flag, normed, *cot_rows, qkv_w, out_w, *late)

    received = permuted(send, edge_route)
    d_hidden, d_resid, send = pl.pallas_call(
        norm_kernel,
        out_shape=(shaped(128, HID, dtype=bf16), shaped(64, features), shaped(16, HID, dtype=bf16)),
        in_specs=vmem(10),
        out_specs=tuple(vmem(3)),
        scratch_shapes=[
            pltpu.VMEM((128, 640), f32), pltpu.VMEM((128, features), f32), pltpu.VMEM((128, features), f32),
        ],
        compiler_params=limit(12),
    )(d_q, d_kv, received, resid, inv_rms, hidden, cot_all, gain, mix, qkv)

    received = permuted(send, edge_route)
    keep, send = pl.pallas_call(
        taps_kernel,
        out_shape=(shaped(32, features), shaped(32, features, dtype=bf16)),
        in_specs=vmem(6),
        out_specs=tuple(vmem(2)),
        scratch_shapes=[
            pltpu.VMEM((96, HID), bf16), pltpu.VMEM((64, features), f32), pltpu.VMEM((64, features), f32),
        ],
        compiler_params=limit(6),
    )(d_hidden, received, d_resid, *blocks, conv)

    received = permuted(send, x_route)
    partial = (keep + received.astype(f32)).astype(bf16)
    first_sum = permuted(
        partial, routes(n_sa, lambda z, y, x, c: (z, 1 - y, x, c) if y != c ^ (z & 1) else (z, y, x, 1 - c))
    )
    second_sum = permuted(partial, routes(n_sa, lambda z, y, x, c: (z, 1 - y, x, 1 - c) if y != c ^ (z & 1) else None))
    other = jnp.where(y == m, partial, second_sum)
    return (first_sum.astype(f32) + other.astype(f32)) * 0.25


def solution(mesh):
    fits = mesh.shape["sb"] == 4 and mesh.shape["noise"] == 2 and HEADS == 4

    def body(*arrays):
        if fits and arrays[0].shape[0] == 32 and arrays[1].shape[0] == 2 and TILE == 128:
            if arrays[0].shape[1] == 1536 and mesh.shape["sa"] == 4:
                return stretch_shards(*arrays)
        return shards(*arrays)

    return jax.shard_map(
        body,
        mesh=mesh,
        in_specs=(
            P(("sa", "sb"), None),
            P("noise", ("sa", "sb"), None),
            P(("sa", "sb"), None),
            P(None, "sa", None),
            P("sa", None),
            P(),
            P("sa", None),
            P("sa", None),
            P(),
            P(),
        ),
        out_specs=P(("sa", "sb"), None),
        check_vma=False,
    )
```

```python
import jax
import jax.numpy as jnp
from jax import lax
from jax.experimental import pallas as pl
from jax.experimental.pallas import tpu as pltpu
from jax.sharding import PartitionSpec as P

HID = 384
HEADS = 4
KEY = 64
VAL = 96
DILATION_BINS = 16
BAND = 32
TILE = 128


ROOT_TWO_PI = 0.7978845608
CUBIC = 0.044715


def extended(value, sides, width):
    for axis, dim in sides:
        peers, length = (lax.axis_size(axis), value.shape[dim])
        up = [(i, (i + 1) % peers) for i in range(peers - 1)]
        down = [(j, i) for i, j in up]
        last = lax.slice_in_dim(value, length - width, length, axis=dim)
        leading = lax.slice_in_dim(value, 0, width, axis=dim)
        before = lax.ppermute(last, axis, up)
        after = lax.ppermute(leading, axis, down)
        value = jnp.concatenate([before, value, after], axis=dim)
    return value


def from_behind(block, axis, distance):
    devices = range(lax.axis_size(axis))
    route = [(i - distance, i) for i in devices if i - distance in devices]
    return lax.ppermute(block, axis, route)


def gelu_tanh(values):
    inner = ROOT_TWO_PI * (values + CUBIC * values * values * values)
    return 0.5 * values * (1.0 + jnp.tanh(inner))


def gelu_slope(values):
    tangent = jnp.tanh(ROOT_TWO_PI * (values + CUBIC * values * values * values))
    return 0.5 * (1.0 + tangent) + 0.5 * values * (1.0 - tangent * tangent) * ROOT_TWO_PI * (
        1.0 + 3.0 * CUBIC * values * values
    )


def shards(base, noise, cot, convolution_weight, mix_w, norm_gain, qkv_w, out_w, band_width, pairs):
    conv_full, mix_full, qkv_full, out_full = (
        lax.all_gather(convolution_weight, "sa", axis=1, tiled=True),
        lax.all_gather(mix_w, "sa", axis=0, tiled=True),
        lax.all_gather(qkv_w, "sa", axis=0, tiled=True),
        lax.all_gather(out_w, "sa", axis=0, tiled=True),
    )
    sequence_bins = base.shape[0]
    samples_dev = noise.shape[0]
    stretch = sequence_bins * lax.axis_size("sb")
    sequence_length = stretch * lax.axis_size("sa")
    heads_key = HEADS * KEY
    heads_val = HEADS * VAL
    width = sequence_bins + 2 * BAND
    scale = KEY ** (-0.5)
    stretch_first = lax.axis_index("sa") * stretch
    first_row = stretch_first + lax.axis_index("sb") * sequence_bins
    row_pos = first_row + jnp.arange(sequence_bins, dtype=jnp.int32)
    ext_pos = first_row - BAND + jnp.arange(width, dtype=jnp.int32)
    stretch_pos = stretch_first + jnp.arange(stretch, dtype=jnp.int32)
    tiles = sequence_length // TILE
    tile_ids = jnp.arange(tiles, dtype=jnp.int32)
    pick_query = (pairs[:, 0][:, None] == tile_ids[None, :]).astype(jnp.float32)
    pick_key = (pairs[:, 1][:, None] == tile_ids[None, :]).astype(jnp.float32)
    table = jnp.dot(pick_query.T, pick_key)
    own_select = ((row_pos // TILE)[:, None] == tile_ids[None, :]).astype(jnp.float32)
    stretch_select = ((stretch_pos // TILE)[:, None] == tile_ids[None, :]).astype(jnp.float32)
    pair_own_rows = jnp.dot(jnp.dot(own_select, table), stretch_select.T) > 0.5
    pair_own_keys = jnp.dot(jnp.dot(stretch_select, table), own_select.T) > 0.5
    inside = (ext_pos >= 0) & (ext_pos < sequence_length)
    band_mask = inside[None, None, :] & (
        jnp.abs(row_pos[:, None] - ext_pos[None, :])[None] <= band_width[:, None, None]
    )
    far_rows = jnp.abs(row_pos[:, None] - stretch_pos[None, :])[None] > band_width[:, None, None]
    pair_mask = pair_own_rows[None] & far_rows
    key_mask = pair_own_keys[None] & jnp.transpose(far_rows, (0, 2, 1))
    noisy = base.astype(jnp.float32)[None] + noise.astype(jnp.float32)
    gelu_input = gelu_tanh(noisy).astype(jnp.bfloat16)
    gelu_extended = extended(gelu_input, ((("sa", "sb"), 1),), DILATION_BINS)
    hidden_state = jnp.zeros((samples_dev, sequence_bins, HID), jnp.float32)
    for tap_index in range(3):
        hidden_state = hidden_state + jnp.einsum(
            "nbd,dc->nbc",
            gelu_extended[:, tap_index * DILATION_BINS : tap_index * DILATION_BINS + sequence_bins],
            conv_full[tap_index],
            preferred_element_type=jnp.float32,
        )
    act = gelu_tanh(hidden_state).astype(jnp.bfloat16)
    resid = noisy + jnp.einsum("nbc,cd->nbd", act, mix_full, preferred_element_type=jnp.float32)
    inv_rms = lax.rsqrt(jnp.mean(resid * resid, axis=-1, keepdims=True) + 1e-06)
    normed = (resid * inv_rms * norm_gain).astype(jnp.bfloat16)
    proj = jnp.einsum("nbd,dc->nbc", normed, qkv_full, preferred_element_type=jnp.float32).astype(
        jnp.bfloat16
    )
    queries = proj[..., :heads_key].reshape(samples_dev, sequence_bins, HEADS, KEY)
    key_vals = proj[..., heads_key:]
    kv_ext = extended(key_vals, ((("sa", "sb"), 1),), BAND)
    kv_all = lax.all_gather(key_vals, "sb", axis=1, tiled=True)
    keys_ext = kv_ext[..., :heads_key].reshape(samples_dev, width, HEADS, KEY)
    vals_ext = kv_ext[..., heads_key:].reshape(samples_dev, width, HEADS, VAL)
    keys_all = kv_all[..., :heads_key].reshape(samples_dev, stretch, HEADS, KEY)
    vals_all = kv_all[..., heads_key:].reshape(samples_dev, stretch, HEADS, VAL)
    score_band = (
        jnp.einsum("nihd,njhd->nhij", queries, keys_ext, preferred_element_type=jnp.float32) * scale
    )
    score_band = jnp.where(band_mask[None], score_band, -1e30)
    raw_pair = jnp.einsum("nihd,njhd->nhij", queries, keys_all, preferred_element_type=jnp.float32)
    score_pair = jnp.where(pair_mask[None], raw_pair * scale, -1e30)
    top = jnp.maximum(jnp.max(score_band, axis=-1), jnp.max(score_pair, axis=-1))
    total = jnp.sum(jnp.where(band_mask[None], jnp.exp(score_band - top[..., None]), 0.0), axis=-1)
    total = total + jnp.sum(
        jnp.where(pair_mask[None], jnp.exp(score_pair - top[..., None]), 0.0), axis=-1
    )
    lse = top + jnp.log(total)
    prob_band = jnp.where(band_mask[None], jnp.exp(score_band - lse[..., None]), 0.0)
    prob_pair = jnp.where(pair_mask[None], jnp.exp(score_pair - lse[..., None]), 0.0)
    band_b = prob_band.astype(jnp.bfloat16)
    pair_b = prob_pair.astype(jnp.bfloat16)
    attn = jnp.einsum("nhij,njhe->nihe", band_b, vals_ext, preferred_element_type=jnp.float32)
    attn = attn + jnp.einsum(
        "nhij,njhe->nihe", pair_b, vals_all, preferred_element_type=jnp.float32
    )
    d_att = jnp.dot(cot, out_full.T, preferred_element_type=jnp.float32).astype(jnp.bfloat16)
    d_att_heads = d_att.reshape(sequence_bins, HEADS, VAL)
    delta = jnp.transpose(jnp.sum(d_att_heads.astype(jnp.float32)[None] * attn, axis=-1), (0, 2, 1))
    d_prob_band = jnp.einsum(
        "ihe,njhe->nhij", d_att_heads, vals_ext, preferred_element_type=jnp.float32
    )
    d_prob_pair = jnp.einsum(
        "ihe,njhe->nhij", d_att_heads, vals_all, preferred_element_type=jnp.float32
    )
    d_score_band = (prob_band * (d_prob_band - delta[..., None]) * scale).astype(jnp.bfloat16)
    d_score_pair = (prob_pair * (d_prob_pair - delta[..., None]) * scale).astype(jnp.bfloat16)
    d_query = jnp.einsum(
        "nhij,njhd->nihd", d_score_band, keys_ext, preferred_element_type=jnp.float32
    )
    d_query = d_query + jnp.einsum(
        "nhij,njhd->nihd", d_score_pair, keys_all, preferred_element_type=jnp.float32
    )
    d_key_ext = jnp.einsum(
        "nhij,nihd->njhd", d_score_band, queries, preferred_element_type=jnp.float32
    )
    d_val_ext = jnp.einsum(
        "nhij,ihe->njhe", band_b, d_att_heads, preferred_element_type=jnp.float32
    )
    d_kv_ext = jnp.concatenate(
        [
            d_key_ext.reshape(samples_dev, width, heads_key),
            d_val_ext.reshape(samples_dev, width, heads_val),
        ],
        axis=2,
    )
    from_right = from_behind(d_kv_ext[:, :BAND].astype(jnp.bfloat16), ("sa", "sb"), -1).astype(
        jnp.float32
    )
    from_left = from_behind(
        d_kv_ext[:, BAND + sequence_bins :].astype(jnp.bfloat16), ("sa", "sb"), 1
    ).astype(jnp.float32)
    d_key_vals = d_kv_ext[:, BAND : BAND + sequence_bins]
    d_key_vals = d_key_vals + from_left
    d_key_vals = d_key_vals + from_right
    statistics = jnp.stack([lse, delta], axis=1)
    query_rows = proj[..., :heads_key]
    queries_all, d_att_all = (
        lax.all_gather(query_rows, "sb", axis=1, tiled=True),
        lax.all_gather(d_att, "sb", axis=0, tiled=True),
    )
    stats_all = lax.all_gather(statistics, "sb", axis=3, tiled=True)
    queries_all = queries_all.reshape(samples_dev, stretch, HEADS, KEY)
    d_att_all = d_att_all.reshape(stretch, HEADS, VAL)
    keys_own = key_vals[..., :heads_key].reshape(samples_dev, sequence_bins, HEADS, KEY)
    vals_own = key_vals[..., heads_key:].reshape(samples_dev, sequence_bins, HEADS, VAL)
    score_key = (
        jnp.einsum("nihd,njhd->nhij", queries_all, keys_own, preferred_element_type=jnp.float32)
        * scale
    )
    prob_key = jnp.where(key_mask[None], jnp.exp(score_key - stats_all[:, 0][..., None]), 0.0)
    d_val_pair = jnp.einsum(
        "nhij,ihe->njhe",
        prob_key.astype(jnp.bfloat16),
        d_att_all,
        preferred_element_type=jnp.float32,
    )
    d_prob_key = jnp.einsum(
        "ihe,njhe->nhij", d_att_all, vals_own, preferred_element_type=jnp.float32
    )
    d_score_key = (prob_key * (d_prob_key - stats_all[:, 1][..., None]) * scale).astype(
        jnp.bfloat16
    )
    d_key_pair = jnp.einsum(
        "nhij,nihd->njhd", d_score_key, queries_all, preferred_element_type=jnp.float32
    )
    d_key_vals = d_key_vals + jnp.concatenate(
        [
            d_key_pair.reshape(samples_dev, sequence_bins, heads_key),
            d_val_pair.reshape(samples_dev, sequence_bins, heads_val),
        ],
        axis=2,
    )
    d_proj = jnp.concatenate(
        [d_query.reshape(samples_dev, sequence_bins, heads_key), d_key_vals], axis=2
    ).astype(jnp.bfloat16)
    d_normed = jnp.einsum("nbc,dc->nbd", d_proj, qkv_full, preferred_element_type=jnp.float32)
    gained = norm_gain * d_normed
    d_resid = (
        cot.astype(jnp.float32)[None]
        + inv_rms * gained
        - resid * inv_rms * inv_rms * inv_rms * jnp.mean(resid * gained, axis=-1, keepdims=True)
    )
    d_act = jnp.einsum(
        "nbd,cd->nbc", d_resid.astype(jnp.bfloat16), mix_full, preferred_element_type=jnp.float32
    )
    hidden_gradient = (d_act * gelu_slope(hidden_state)).astype(jnp.bfloat16)
    gradient_extended = extended(hidden_gradient, ((("sa", "sb"), 1),), DILATION_BINS)
    d_gelu_in = jnp.zeros((samples_dev, sequence_bins, base.shape[1]), jnp.float32)
    for tap_index in range(3):
        start_offset = (2 - tap_index) * DILATION_BINS
        d_gelu_in = d_gelu_in + jnp.einsum(
            "nbc,dc->nbd",
            gradient_extended[:, start_offset : start_offset + sequence_bins],
            conv_full[tap_index],
            preferred_element_type=jnp.float32,
        )
    grads = d_resid + d_gelu_in * gelu_slope(noisy)
    summed = lax.psum(jnp.sum(grads, axis=0).astype(jnp.bfloat16), "noise").astype(jnp.float32)
    return summed / (samples_dev * lax.axis_size("noise"))


def permuted(value, pairs):
    return lax.ppermute(value, ("sa", "sb", "noise"), pairs)


def routes(n_sa, route):
    flat = lambda z, y, x, c: ((z * 2 + y) * 2 + x) * 2 + c
    pairs = []
    for z in range(n_sa):
        for y in range(2):
            for x in range(2):
                for c in range(2):
                    target = route(z, y, x, c)
                    if target is not None and 0 <= target[0] < n_sa:
                        pairs.append((flat(z, y, x, c), flat(*target)))
    return pairs


def position():
    b = lax.axis_index("sb")
    return lax.axis_index("sa"), b // 2, lax.rem(b, 2), lax.axis_index("noise")


def half_index():
    return lax.rem(lax.axis_index("noise") + lax.axis_index("sa"), 2)


def pack_kernel(conv, mix, qkv, out, early, late, taps, rows_qkv, sems):
    z, y, x, n = position()
    b = 2 * y + x
    part = b * 2 + n
    rows = pl.ds(pl.multiple_of(part * 48, 16), 48)
    half = pl.ds(pl.multiple_of(n * 48, 16), 48)
    columns = pl.ds(pl.multiple_of(b * 384, 128), 384)
    pairs = (
        (conv.at[:, rows, :], taps), (mix.at[half, columns], early.at[pl.ds(144, 48), :]),
        (qkv.at[rows, :], rows_qkv), (out.at[half, columns], late.at[pl.ds(0, 48), :]),
    )
    copies = [pltpu.make_async_copy(source, target, sems.at[i]) for i, (source, target) in enumerate(pairs)]
    for copy in copies:
        copy.start()
    for copy in copies:
        copy.wait()
    for t in range(3):
        early[pl.ds(48 * t, 48), :] = taps[t]
    for k in range(2):
        late[pl.ds(48 + 48 * k, 48), :] = rows_qkv[:, pl.ds(384 * k, 384)]
    for k in range(3):
        late[pl.ds(144, 16), pl.ds(128 * k, 128)] = rows_qkv[pl.ds(16 * k, 16), pl.ds(768, 128)]


def nt(a, b):
    return lax.dot_general(a, b, (((1,), (1,)), ((), ())), preferred_element_type=jnp.float32)


def tn(a, b):
    return lax.dot_general(a, b, (((0,), (0,)), ((), ())), preferred_element_type=jnp.float32)


def nn(a, b):
    return jnp.dot(a, b, preferred_element_type=jnp.float32)


CHUNK = 384


def chunk(c):
    return pl.ds(pl.multiple_of(c * CHUNK, 128), CHUNK)


def arrived(z, y, x, n, same, other):
    for j in range(3):
        for core, (straight, beside, across, diagonal_a, diagonal_b) in enumerate((same, other)):
            half = diagonal_a.shape[1]
            for dy in range(2):
                for dx in range(2):
                    if dy and dx:
                        first, second = diagonal_a[j], diagonal_b[j]
                    else:
                        whole = across if dy else beside if dx else straight
                        first, second = whole[j, pl.ds(0, half), :], whole[j, pl.ds(half, half), :]
                    yield j, z ^ (j + 1), y ^ dy, x ^ dx, n ^ core, first, second


def times(value, factor, unit):
    return pl.multiple_of(value * factor, unit)


def forward_kernel(
    blocks_even, blocks_odd, edge, other_even, other_odd, other_edge, *refs,
):
    own_conv, own_mix = refs[:2]
    same, other = refs[2:7], refs[7:12]
    (
        gain, normed_out, resid_out, inv_out, hidden_out, conv_out, mix_out,
        conv, mix, noisy, gelu_in, sems,
    ) = refs[12:]
    z, y, x, n = position()

    for t in range(3):
        conv[t, pl.ds(times(z, 384, 128), 384), :] = own_conv[t]
    mix[pl.ds(times(z, 96, 32), 96), :] = own_mix[...]
    for _, sz, sy, sx, sn, first, second in arrived(z, y, x, n, same, other):
        b = 2 * sy + sx
        rows = pl.ds(pl.multiple_of(sz * 384 + (b * 2 + sn) * 48, 16), 48)
        conv[0, rows, :] = first[:48]
        conv[1, rows, :] = first[48:]
        conv[2, rows, :] = second[:48]
        mix[pl.ds(pl.multiple_of(sz * 96 + sn * 48, 16), 48), pl.ds(times(b, 384, 128), 384)] = second[48:]
    copies = [
        pltpu.make_async_copy(s, d, sems.at[i]) for i, (s, d) in enumerate(((conv, conv_out), (mix, mix_out)))
    ]
    for copy in copies:
        copy.start()

    m = half_index()
    for half, (even, odd, outer) in (
        (m, (blocks_even, blocks_odd, edge)), (1 - m, (other_even, other_odd, other_edge))
    ):
        noisy[pl.ds(times(half, 176, 16), 48), :] = outer[...].astype(jnp.float32)
        for shift, block in enumerate((even, odd)):
            row = 48 + 64 * half + 32 * lax.rem(x + shift, 2)
            noisy[pl.ds(pl.multiple_of(row, 16), 32), :] = block[...].astype(jnp.float32)

    def activate(c, _):
        gelu_in[:, chunk(c)] = gelu_tanh(noisy[:, chunk(c)]).astype(jnp.bfloat16)
        return 0

    lax.fori_loop(0, 4, activate, 0)

    def convolve(c, total):
        for t in range(3):
            total = total + nn(gelu_in[pl.ds(16 * t, 192), chunk(c)], conv[t, chunk(c), :])
        return total

    hidden = lax.fori_loop(0, 4, convolve, jnp.zeros((192, HID), jnp.float32))
    hidden_out[...] = hidden[32:160]
    act = gelu_tanh(hidden).astype(jnp.bfloat16)

    def mixing(c, squares):
        resid = noisy[pl.ds(16, 192), chunk(c)] + nn(act, mix[:, chunk(c)])
        noisy[pl.ds(16, 192), chunk(c)] = resid
        resid_out[:, chunk(c)] = resid[32:160]
        return squares + jnp.sum(resid * resid, axis=1, keepdims=True)

    squares = lax.fori_loop(0, 4, mixing, jnp.zeros((192, 1), jnp.float32))
    inv_rms = lax.rsqrt(squares * (1.0 / 1536) + 1e-06)
    inv_out[...] = inv_rms[32:160]

    def normalise(c, _):
        normed = noisy[pl.ds(16, 192), chunk(c)] * inv_rms * gain[:, chunk(c)]
        normed_out[:, chunk(c)] = normed.astype(jnp.bfloat16)
        return 0

    lax.fori_loop(0, 4, normalise, 0)
    for copy in copies:
        copy.wait()


def attention_kernel(band, flag, normed, cot_block, cot_beside, other_block, other_beside, *refs):
    own_qkv, own_out = refs[:2]
    same, other = refs[2:7], refs[7:12]
    d_q_out, d_kv_out, send, qkv_out, cot_out, qkv, out, sems = refs[12:]
    z, y, x, n = position()
    length = lax.axis_size("sa") * 128
    first_bin = z * 128
    own_rows = pl.ds(times(z, 384, 128), 384)
    qkv[own_rows, :] = own_qkv[...]
    out[pl.ds(times(z, 96, 32), 96), :] = own_out[...]
    proj = nn(normed[:, own_rows], own_qkv[...])
    done = 0
    for j, sz, sy, sx, sn, first, second in arrived(z, y, x, n, same, other):
        b = 2 * sy + sx
        row = sz * 384 + (b * 2 + sn) * 48
        out[pl.ds(pl.multiple_of(sz * 96 + sn * 48, 16), 48), pl.ds(times(b, 384, 128), 384)] = first[:48]
        qkv[pl.ds(pl.multiple_of(row, 16), 32), pl.ds(0, 384)] = first[48:]
        qkv[pl.ds(pl.multiple_of(row + 32, 16), 16), pl.ds(0, 384)] = second[:16]
        qkv[pl.ds(pl.multiple_of(row, 16), 48), pl.ds(384, 384)] = second[16:64]
        for k in range(3):
            third = pl.ds(pl.multiple_of(row + 16 * k, 16), 16)
            qkv[third, pl.ds(768, 128)] = second[64:, 128 * k : 128 * k + 128]
        done += 1
        if done % 8 == 0:
            rows = pl.ds(times(sz, 384, 128), 384)
            proj = proj + nn(normed[:, rows], qkv[rows, :])
    proj = proj.astype(jnp.bfloat16)
    copy = pltpu.make_async_copy(qkv, qkv_out, sems.at[0])
    copy.start()
    m = half_index()
    for half, (block, beside) in ((m, (cot_block, cot_beside)), (1 - m, (other_block, other_beside))):
        for shift, rows in enumerate((block, beside)):
            row = 64 * half + 32 * lax.rem(x + shift, 2)
            cot_out[pl.ds(pl.multiple_of(row, 32), 32), :] = rows[...]
    d_att = nt(cot_out[...], out[...]).astype(jnp.bfloat16)

    row = lax.broadcasted_iota(jnp.int32, (128, 192), 0)
    column = lax.broadcasted_iota(jnp.int32, (128, 192), 1) - 32
    inside = (column + first_bin >= 0) & (column + first_bin < length)
    paired = (column >= 0) & (column < 128) & (flag[0] > 0)
    apart = jnp.abs(row - column)
    scale = KEY ** (-0.5)
    d_queries, d_keys, d_values = [], [], []
    for h in range(HEADS):
        q = proj[32:160, KEY * h : KEY * (h + 1)]
        k = proj[:, HEADS * KEY + KEY * h : HEADS * KEY + KEY * (h + 1)]
        v = proj[:, 2 * HEADS * KEY + VAL * h : 2 * HEADS * KEY + VAL * (h + 1)]
        d_att_h = d_att[:, VAL * h : VAL * (h + 1)]
        allowed = inside & (paired | (apart <= band[h]))
        score = jnp.where(allowed, nt(q, k) * scale, -1e30)
        top = jnp.max(score, axis=1, keepdims=True)
        raised = jnp.where(allowed, jnp.exp(score - top), 0.0)
        prob = raised / jnp.sum(raised, axis=1, keepdims=True)
        prob_b = prob.astype(jnp.bfloat16)
        attn = nn(prob_b, v)
        delta = jnp.sum(d_att_h.astype(jnp.float32) * attn, axis=1, keepdims=True)
        d_score = (prob * (nt(d_att_h, v) - delta) * scale).astype(jnp.bfloat16)
        d_queries.append(nn(d_score, k))
        d_keys.append(tn(d_score, q))
        d_values.append(tn(prob_b, d_att_h))
    d_q_out[...] = jnp.concatenate(d_queries, axis=1)
    d_kv = jnp.concatenate(d_keys + d_values, axis=1)
    d_kv_out[...] = d_kv[32:160]
    send[...] = jnp.where(m == 0, d_kv[:32], d_kv[160:]).astype(jnp.bfloat16)
    copy.wait()


def norm_kernel(
    d_q, d_kv, received, resid, inv_rms_ref, hidden, cot, gain, mix, qkv,
    d_hidden_out, d_resid_out, send, total_kv, gained, d_resid_all,
):
    n = half_index()
    total_kv[...] = d_kv[...]
    edge = pl.ds(pl.multiple_of(n * 96, 32), 32)
    total_kv[edge, :] = total_kv[edge, :] + received[...].astype(jnp.float32)
    d_proj = jnp.concatenate([d_q[...], total_kv[...]], axis=1).astype(jnp.bfloat16)
    inv_rms = inv_rms_ref[...]

    def back(c, mean):
        part = gain[:, chunk(c)] * nt(d_proj, qkv[chunk(c), :])
        gained[:, chunk(c)] = part
        return mean + jnp.sum(resid[:, chunk(c)] * part, axis=1, keepdims=True)

    mean = lax.fori_loop(0, 4, back, jnp.zeros((128, 1), jnp.float32)) * (1.0 / 1536)
    cubed = inv_rms * inv_rms * inv_rms * mean

    def residual(c, total):
        d_resid = (
            cot[:, chunk(c)].astype(jnp.float32)
            + inv_rms * gained[:, chunk(c)]
            - resid[:, chunk(c)] * cubed
        )
        d_resid_all[:, chunk(c)] = d_resid
        return total + nt(d_resid.astype(jnp.bfloat16), mix[:, chunk(c)])

    d_act = lax.fori_loop(0, 4, residual, jnp.zeros((128, HID), jnp.float32))
    d_hidden = (d_act * gelu_slope(hidden[...])).astype(jnp.bfloat16)
    d_hidden_out[...] = d_hidden
    d_resid_out[...] = d_resid_all[pl.ds(pl.multiple_of(n * 64, 64), 64), :]

    @pl.when(n == 0)
    def _():
        send[...] = d_hidden[:16]

    @pl.when(n == 1)
    def _():
        send[...] = d_hidden[112:]


def taps_kernel(d_hidden, received, d_resid, blocks_even, blocks_odd, conv, keep, send, extended_ref, noisy, grads):
    x, n = lax.rem(lax.axis_index("sb"), 2), half_index()

    @pl.when(n == 0)
    def _():
        extended_ref[pl.ds(0, 16), :] = received[...]
        extended_ref[pl.ds(16, 80), :] = d_hidden[pl.ds(0, 80), :]

    @pl.when(n == 1)
    def _():
        extended_ref[pl.ds(0, 80), :] = d_hidden[pl.ds(48, 80), :]
        extended_ref[pl.ds(80, 16), :] = received[...]

    for shift, block in enumerate((blocks_even, blocks_odd)):
        noisy[pl.ds(times(lax.rem(x + shift, 2), 32, 32), 32), :] = block[...].astype(jnp.float32)

    def taps(c, _):
        total = nt(extended_ref[pl.ds(32, 64), :], conv[0, chunk(c), :])
        total = total + nt(extended_ref[pl.ds(16, 64), :], conv[1, chunk(c), :])
        total = total + nt(extended_ref[pl.ds(0, 64), :], conv[2, chunk(c), :])
        grads[:, chunk(c)] = d_resid[:, chunk(c)] + total * gelu_slope(noisy[:, chunk(c)])
        return 0

    lax.fori_loop(0, 4, taps, 0)
    keep[...] = grads[pl.ds(pl.multiple_of(32 * x, 32), 32), :]
    send[...] = grads[pl.ds(pl.multiple_of(32 - 32 * x, 32), 32), :].astype(jnp.bfloat16)


def vmem(count):
    return [pl.BlockSpec(memory_space=pltpu.VMEM)] * count


def smem(count):
    return [pl.BlockSpec(memory_space=pltpu.SMEM)] * count


def hbm(count):
    return [pl.BlockSpec(memory_space=pl.ANY)] * count


def limit(mebibytes):
    return pltpu.CompilerParams(vmem_limit_bytes=mebibytes * 1024 * 1024)


f32, bf16 = (jnp.float32, jnp.bfloat16)


def shaped(*shape, dtype=jnp.float32):
    return jax.ShapeDtypeStruct(shape, dtype)


def stretch_shards(
    base, noise, cot, convolution_weight, mix_w, norm_gain, qkv_w, out_w, band_width, pairs
):
    n_sa = lax.axis_size("sa")
    b = lax.axis_index("sb")
    m = half_index()
    y, x = (b >> 1, b & 1)
    features = base.shape[1]

    early, late = pl.pallas_call(
        pack_kernel,
        out_shape=(shaped(192, CHUNK, dtype=bf16), shaped(160, CHUNK, dtype=bf16)),
        in_specs=[pl.BlockSpec(memory_space=pltpu.HBM)] * 4,
        out_specs=tuple(vmem(2)),
        scratch_shapes=[
            pltpu.VMEM((3, 48, HID), bf16), pltpu.VMEM((48, 896), bf16), pltpu.SemaphoreType.DMA((4,))
        ],
        compiler_params=limit(60),
    )(convolution_weight, mix_w, qkv_w, out_w)
    def along_z(step):
        return routes(n_sa, lambda z, y, x, c: (z ^ step, y, x, c))

    x_route = routes(n_sa, lambda z, y, x, c: (z, y, 1 - x, c))
    y_route = routes(n_sa, lambda z, y, x, c: (z, 1 - y, x, c))
    core_route = routes(n_sa, lambda z, y, x, c: (z, y, x, 1 - c))

    def over_z(piece):
        return [permuted(piece, along_z(step)) for step in range(1, 4)]

    def diagonals(beside, across):
        half = beside.shape[1] // 2
        return permuted(beside[:, :half], y_route), permuted(across[:, half:], x_route)

    def swapped(parts):
        return tuple(permuted(part, core_route) for part in parts)

    def after(values, *earlier):
        count = len(values)
        return lax.optimization_barrier((*values, *earlier))[:count]

    def to_sample(shift):
        return routes(n_sa, lambda z, y, x, c: (z, c, (x + shift) % 2, y ^ (z & 1)))

    noisy = (base.astype(f32)[None] + noise.astype(f32)).astype(bf16)
    even = x == 0
    edge_route = routes(
        n_sa, lambda z, y, x, c: (z - 1, y, x, c) if c ^ (z & 1) == 0 else (z + 1, y, x, c)
    )
    z = lax.axis_index("sa")
    flag = jnp.any((pairs[:, 0] == z) & (pairs[:, 1] == z)).astype(jnp.int32).reshape(1)
    straight = over_z(early)
    noisy, cot = after((noisy, cot), *straight[:1])
    blocks = [
        permuted(jnp.where(x == shift, noisy[0], noisy[1]), to_sample(shift)) for shift in range(2)
    ]
    across_cot = permuted(
        cot, routes(n_sa, lambda z, y, x, c: (z, 1 - y, x, c) if y == c ^ (z & 1) else None)
    )
    low, high = jnp.where(even, blocks[0], blocks[1]), jnp.where(even, blocks[1], blocks[0])
    outer = jnp.concatenate(
        [jnp.where(m == 0, low[:16], low[16:]), jnp.where(m == 0, low[16:], high[:16]), jnp.where(m == 0, high[:16], high[16:])]
    )
    cot_block = jnp.where(y == m, cot, across_cot)
    straight = jnp.stack(straight)
    straight, late, flag, outer, cot_block = after((straight, late, flag, outer, cot_block))
    beside, across = permuted(straight, x_route), permuted(straight, y_route)
    late_straight = jnp.stack(over_z(late))
    straight, beside, across, late_straight, outer, cot_block, *blocks = after(
        (straight, beside, across, late_straight, outer, cot_block, *blocks)
    )
    early = (straight, beside, across) + diagonals(beside, across)
    late_beside, late_across = permuted(late_straight, x_route), permuted(late_straight, y_route)
    edge = permuted(outer, edge_route)
    early, late, cot_block, mine = (
        lambda v: (v[:5], v[5:8], v[8], v[9:])
    )(after((*early, late_straight, late_beside, late_across, cot_block, *blocks, edge)))
    late = tuple(late) + diagonals(late[1], late[2])
    noisy_rows = tuple(mine) + swapped(mine)
    early = tuple(early) + swapped(early)
    cot_rows = (cot_block, permuted(cot_block, x_route))
    cot_rows = cot_rows + swapped(cot_rows)
    late_other = swapped(late[:3])
    gain = norm_gain.reshape(1, features)

    normed, resid, inv_rms, hidden, conv, mix = pl.pallas_call(
        forward_kernel,
        out_shape=(
            shaped(192, features, dtype=bf16), shaped(128, features), shaped(128, 1), shaped(128, HID),
            shaped(3, features, HID, dtype=bf16), shaped(HID, features, dtype=bf16),
        ),
        in_specs=vmem(19),
        out_specs=tuple(vmem(4) + hbm(2)),
        scratch_shapes=[
            pltpu.VMEM((3, features, HID), bf16), pltpu.VMEM((HID, features), bf16),
            pltpu.VMEM((224, features), f32), pltpu.VMEM((224, features), bf16),
            pltpu.SemaphoreType.DMA((2,)),
        ],
        compiler_params=limit(18),
    )(*noisy_rows, convolution_weight, mix_w, *early, gain)
    late += late_other + swapped(late[3:])
    d_q, d_kv, send, qkv, cot_all = pl.pallas_call(
        attention_kernel,
        out_shape=(
            shaped(128, 256), shaped(128, 640), shaped(32, 640, dtype=bf16), shaped(features, 896, dtype=bf16),
            shaped(128, features, dtype=bf16),
        ),
        in_specs=smem(2) + vmem(17),
        out_specs=tuple(vmem(3) + hbm(1) + vmem(1)),
        scratch_shapes=[
            pltpu.VMEM((features, 896), bf16), pltpu.VMEM((HEADS * VAL, features), bf16),
            pltpu.SemaphoreType.DMA((1,)),
        ],
        compiler_params=limit(14),
    )(band_width, flag, normed, *cot_rows, qkv_w, out_w, *late)

    received = permuted(send, edge_route)
    d_hidden, d_resid, send = pl.pallas_call(
        norm_kernel,
        out_shape=(shaped(128, HID, dtype=bf16), shaped(64, features), shaped(16, HID, dtype=bf16)),
        in_specs=vmem(10),
        out_specs=tuple(vmem(3)),
        scratch_shapes=[
            pltpu.VMEM((128, 640), f32), pltpu.VMEM((128, features), f32), pltpu.VMEM((128, features), f32),
        ],
        compiler_params=limit(12),
    )(d_q, d_kv, received, resid, inv_rms, hidden, cot_all, gain, mix, qkv)

    received = permuted(send, edge_route)
    keep, send = pl.pallas_call(
        taps_kernel,
        out_shape=(shaped(32, features), shaped(32, features, dtype=bf16)),
        in_specs=vmem(6),
        out_specs=tuple(vmem(2)),
        scratch_shapes=[
            pltpu.VMEM((96, HID), bf16), pltpu.VMEM((64, features), f32), pltpu.VMEM((64, features), f32),
        ],
        compiler_params=limit(6),
    )(d_hidden, received, d_resid, *blocks, conv)

    received = permuted(send, x_route)
    partial = (keep + received.astype(f32)).astype(bf16)
    first_sum = permuted(
        partial, routes(n_sa, lambda z, y, x, c: (z, 1 - y, x, c) if y != c ^ (z & 1) else (z, y, x, 1 - c))
    )
    second_sum = permuted(partial, routes(n_sa, lambda z, y, x, c: (z, 1 - y, x, 1 - c) if y != c ^ (z & 1) else None))
    other = jnp.where(y == m, partial, second_sum)
    return (first_sum.astype(f32) + other.astype(f32)) * 0.25


def solution(mesh):
    fits = mesh.shape["sb"] == 4 and mesh.shape["noise"] == 2 and HEADS == 4

    def body(*arrays):
        if fits and arrays[0].shape[0] == 32 and arrays[1].shape[0] == 2 and TILE == 128:
            if arrays[0].shape[1] == 1536 and mesh.shape["sa"] == 4:
                return stretch_shards(*arrays)
        return shards(*arrays)

    return jax.shard_map(
        body,
        mesh=mesh,
        in_specs=(
            P(("sa", "sb"), None),
            P("noise", ("sa", "sb"), None),
            P(("sa", "sb"), None),
            P(None, "sa", None),
            P("sa", None),
            P(),
            P("sa", None),
            P("sa", None),
            P(),
            P(),
        ),
        out_specs=P(("sa", "sb"), None),
        check_vma=False,
    )
```

```python
import jax
import jax.numpy as jnp
from jax import lax
from jax.experimental import pallas as pl
from jax.experimental.pallas import tpu as pltpu
from jax.sharding import PartitionSpec as P

HID = 384
HEADS = 4
KEY = 64
VAL = 96
DILATION_BINS = 16
BAND = 32
TILE = 128


ROOT_TWO_PI = 0.7978845608
CUBIC = 0.044715


def extended(value, sides, width):
    for axis, dim in sides:
        peers, length = (lax.axis_size(axis), value.shape[dim])
        up = [(i, (i + 1) % peers) for i in range(peers - 1)]
        down = [(j, i) for i, j in up]
        last = lax.slice_in_dim(value, length - width, length, axis=dim)
        leading = lax.slice_in_dim(value, 0, width, axis=dim)
        before = lax.ppermute(last, axis, up)
        after = lax.ppermute(leading, axis, down)
        value = jnp.concatenate([before, value, after], axis=dim)
    return value


def from_behind(block, axis, distance):
    devices = range(lax.axis_size(axis))
    route = [(i - distance, i) for i in devices if i - distance in devices]
    return lax.ppermute(block, axis, route)


def gelu_tanh(values):
    inner = ROOT_TWO_PI * (values + CUBIC * values * values * values)
    return 0.5 * values * (1.0 + jnp.tanh(inner))


def gelu_slope(values):
    tangent = jnp.tanh(ROOT_TWO_PI * (values + CUBIC * values * values * values))
    return 0.5 * (1.0 + tangent) + 0.5 * values * (1.0 - tangent * tangent) * ROOT_TWO_PI * (
        1.0 + 3.0 * CUBIC * values * values
    )


def shards(base, noise, cot, convolution_weight, mix_w, norm_gain, qkv_w, out_w, band_width, pairs):
    conv_full, mix_full, qkv_full, out_full = (
        lax.all_gather(convolution_weight, "sa", axis=1, tiled=True),
        lax.all_gather(mix_w, "sa", axis=0, tiled=True),
        lax.all_gather(qkv_w, "sa", axis=0, tiled=True),
        lax.all_gather(out_w, "sa", axis=0, tiled=True),
    )
    sequence_bins = base.shape[0]
    samples_dev = noise.shape[0]
    stretch = sequence_bins * lax.axis_size("sb")
    sequence_length = stretch * lax.axis_size("sa")
    heads_key = HEADS * KEY
    heads_val = HEADS * VAL
    width = sequence_bins + 2 * BAND
    scale = KEY ** (-0.5)
    stretch_first = lax.axis_index("sa") * stretch
    first_row = stretch_first + lax.axis_index("sb") * sequence_bins
    row_pos = first_row + jnp.arange(sequence_bins, dtype=jnp.int32)
    ext_pos = first_row - BAND + jnp.arange(width, dtype=jnp.int32)
    stretch_pos = stretch_first + jnp.arange(stretch, dtype=jnp.int32)
    tiles = sequence_length // TILE
    tile_ids = jnp.arange(tiles, dtype=jnp.int32)
    pick_query = (pairs[:, 0][:, None] == tile_ids[None, :]).astype(jnp.float32)
    pick_key = (pairs[:, 1][:, None] == tile_ids[None, :]).astype(jnp.float32)
    table = jnp.dot(pick_query.T, pick_key)
    own_select = ((row_pos // TILE)[:, None] == tile_ids[None, :]).astype(jnp.float32)
    stretch_select = ((stretch_pos // TILE)[:, None] == tile_ids[None, :]).astype(jnp.float32)
    pair_own_rows = jnp.dot(jnp.dot(own_select, table), stretch_select.T) > 0.5
    pair_own_keys = jnp.dot(jnp.dot(stretch_select, table), own_select.T) > 0.5
    inside = (ext_pos >= 0) & (ext_pos < sequence_length)
    band_mask = inside[None, None, :] & (
        jnp.abs(row_pos[:, None] - ext_pos[None, :])[None] <= band_width[:, None, None]
    )
    far_rows = jnp.abs(row_pos[:, None] - stretch_pos[None, :])[None] > band_width[:, None, None]
    pair_mask = pair_own_rows[None] & far_rows
    key_mask = pair_own_keys[None] & jnp.transpose(far_rows, (0, 2, 1))
    noisy = base.astype(jnp.float32)[None] + noise.astype(jnp.float32)
    gelu_input = gelu_tanh(noisy).astype(jnp.bfloat16)
    gelu_extended = extended(gelu_input, ((("sa", "sb"), 1),), DILATION_BINS)
    hidden_state = jnp.zeros((samples_dev, sequence_bins, HID), jnp.float32)
    for tap_index in range(3):
        hidden_state = hidden_state + jnp.einsum(
            "nbd,dc->nbc",
            gelu_extended[:, tap_index * DILATION_BINS : tap_index * DILATION_BINS + sequence_bins],
            conv_full[tap_index],
            preferred_element_type=jnp.float32,
        )
    act = gelu_tanh(hidden_state).astype(jnp.bfloat16)
    resid = noisy + jnp.einsum("nbc,cd->nbd", act, mix_full, preferred_element_type=jnp.float32)
    inv_rms = lax.rsqrt(jnp.mean(resid * resid, axis=-1, keepdims=True) + 1e-06)
    normed = (resid * inv_rms * norm_gain).astype(jnp.bfloat16)
    proj = jnp.einsum("nbd,dc->nbc", normed, qkv_full, preferred_element_type=jnp.float32).astype(
        jnp.bfloat16
    )
    queries = proj[..., :heads_key].reshape(samples_dev, sequence_bins, HEADS, KEY)
    key_vals = proj[..., heads_key:]
    kv_ext = extended(key_vals, ((("sa", "sb"), 1),), BAND)
    kv_all = lax.all_gather(key_vals, "sb", axis=1, tiled=True)
    keys_ext = kv_ext[..., :heads_key].reshape(samples_dev, width, HEADS, KEY)
    vals_ext = kv_ext[..., heads_key:].reshape(samples_dev, width, HEADS, VAL)
    keys_all = kv_all[..., :heads_key].reshape(samples_dev, stretch, HEADS, KEY)
    vals_all = kv_all[..., heads_key:].reshape(samples_dev, stretch, HEADS, VAL)
    score_band = (
        jnp.einsum("nihd,njhd->nhij", queries, keys_ext, preferred_element_type=jnp.float32) * scale
    )
    score_band = jnp.where(band_mask[None], score_band, -1e30)
    raw_pair = jnp.einsum("nihd,njhd->nhij", queries, keys_all, preferred_element_type=jnp.float32)
    score_pair = jnp.where(pair_mask[None], raw_pair * scale, -1e30)
    top = jnp.maximum(jnp.max(score_band, axis=-1), jnp.max(score_pair, axis=-1))
    total = jnp.sum(jnp.where(band_mask[None], jnp.exp(score_band - top[..., None]), 0.0), axis=-1)
    total = total + jnp.sum(
        jnp.where(pair_mask[None], jnp.exp(score_pair - top[..., None]), 0.0), axis=-1
    )
    lse = top + jnp.log(total)
    prob_band = jnp.where(band_mask[None], jnp.exp(score_band - lse[..., None]), 0.0)
    prob_pair = jnp.where(pair_mask[None], jnp.exp(score_pair - lse[..., None]), 0.0)
    band_b = prob_band.astype(jnp.bfloat16)
    pair_b = prob_pair.astype(jnp.bfloat16)
    attn = jnp.einsum("nhij,njhe->nihe", band_b, vals_ext, preferred_element_type=jnp.float32)
    attn = attn + jnp.einsum(
        "nhij,njhe->nihe", pair_b, vals_all, preferred_element_type=jnp.float32
    )
    d_att = jnp.dot(cot, out_full.T, preferred_element_type=jnp.float32).astype(jnp.bfloat16)
    d_att_heads = d_att.reshape(sequence_bins, HEADS, VAL)
    delta = jnp.transpose(jnp.sum(d_att_heads.astype(jnp.float32)[None] * attn, axis=-1), (0, 2, 1))
    d_prob_band = jnp.einsum(
        "ihe,njhe->nhij", d_att_heads, vals_ext, preferred_element_type=jnp.float32
    )
    d_prob_pair = jnp.einsum(
        "ihe,njhe->nhij", d_att_heads, vals_all, preferred_element_type=jnp.float32
    )
    d_score_band = (prob_band * (d_prob_band - delta[..., None]) * scale).astype(jnp.bfloat16)
    d_score_pair = (prob_pair * (d_prob_pair - delta[..., None]) * scale).astype(jnp.bfloat16)
    d_query = jnp.einsum(
        "nhij,njhd->nihd", d_score_band, keys_ext, preferred_element_type=jnp.float32
    )
    d_query = d_query + jnp.einsum(
        "nhij,njhd->nihd", d_score_pair, keys_all, preferred_element_type=jnp.float32
    )
    d_key_ext = jnp.einsum(
        "nhij,nihd->njhd", d_score_band, queries, preferred_element_type=jnp.float32
    )
    d_val_ext = jnp.einsum(
        "nhij,ihe->njhe", band_b, d_att_heads, preferred_element_type=jnp.float32
    )
    d_kv_ext = jnp.concatenate(
        [
            d_key_ext.reshape(samples_dev, width, heads_key),
            d_val_ext.reshape(samples_dev, width, heads_val),
        ],
        axis=2,
    )
    from_right = from_behind(d_kv_ext[:, :BAND].astype(jnp.bfloat16), ("sa", "sb"), -1).astype(
        jnp.float32
    )
    from_left = from_behind(
        d_kv_ext[:, BAND + sequence_bins :].astype(jnp.bfloat16), ("sa", "sb"), 1
    ).astype(jnp.float32)
    d_key_vals = d_kv_ext[:, BAND : BAND + sequence_bins]
    d_key_vals = d_key_vals + from_left
    d_key_vals = d_key_vals + from_right
    statistics = jnp.stack([lse, delta], axis=1)
    query_rows = proj[..., :heads_key]
    queries_all, d_att_all = (
        lax.all_gather(query_rows, "sb", axis=1, tiled=True),
        lax.all_gather(d_att, "sb", axis=0, tiled=True),
    )
    stats_all = lax.all_gather(statistics, "sb", axis=3, tiled=True)
    queries_all = queries_all.reshape(samples_dev, stretch, HEADS, KEY)
    d_att_all = d_att_all.reshape(stretch, HEADS, VAL)
    keys_own = key_vals[..., :heads_key].reshape(samples_dev, sequence_bins, HEADS, KEY)
    vals_own = key_vals[..., heads_key:].reshape(samples_dev, sequence_bins, HEADS, VAL)
    score_key = (
        jnp.einsum("nihd,njhd->nhij", queries_all, keys_own, preferred_element_type=jnp.float32)
        * scale
    )
    prob_key = jnp.where(key_mask[None], jnp.exp(score_key - stats_all[:, 0][..., None]), 0.0)
    d_val_pair = jnp.einsum(
        "nhij,ihe->njhe",
        prob_key.astype(jnp.bfloat16),
        d_att_all,
        preferred_element_type=jnp.float32,
    )
    d_prob_key = jnp.einsum(
        "ihe,njhe->nhij", d_att_all, vals_own, preferred_element_type=jnp.float32
    )
    d_score_key = (prob_key * (d_prob_key - stats_all[:, 1][..., None]) * scale).astype(
        jnp.bfloat16
    )
    d_key_pair = jnp.einsum(
        "nhij,nihd->njhd", d_score_key, queries_all, preferred_element_type=jnp.float32
    )
    d_key_vals = d_key_vals + jnp.concatenate(
        [
            d_key_pair.reshape(samples_dev, sequence_bins, heads_key),
            d_val_pair.reshape(samples_dev, sequence_bins, heads_val),
        ],
        axis=2,
    )
    d_proj = jnp.concatenate(
        [d_query.reshape(samples_dev, sequence_bins, heads_key), d_key_vals], axis=2
    ).astype(jnp.bfloat16)
    d_normed = jnp.einsum("nbc,dc->nbd", d_proj, qkv_full, preferred_element_type=jnp.float32)
    gained = norm_gain * d_normed
    d_resid = (
        cot.astype(jnp.float32)[None]
        + inv_rms * gained
        - resid * inv_rms * inv_rms * inv_rms * jnp.mean(resid * gained, axis=-1, keepdims=True)
    )
    d_act = jnp.einsum(
        "nbd,cd->nbc", d_resid.astype(jnp.bfloat16), mix_full, preferred_element_type=jnp.float32
    )
    hidden_gradient = (d_act * gelu_slope(hidden_state)).astype(jnp.bfloat16)
    gradient_extended = extended(hidden_gradient, ((("sa", "sb"), 1),), DILATION_BINS)
    d_gelu_in = jnp.zeros((samples_dev, sequence_bins, base.shape[1]), jnp.float32)
    for tap_index in range(3):
        start_offset = (2 - tap_index) * DILATION_BINS
        d_gelu_in = d_gelu_in + jnp.einsum(
            "nbc,dc->nbd",
            gradient_extended[:, start_offset : start_offset + sequence_bins],
            conv_full[tap_index],
            preferred_element_type=jnp.float32,
        )
    grads = d_resid + d_gelu_in * gelu_slope(noisy)
    summed = lax.psum(jnp.sum(grads, axis=0).astype(jnp.bfloat16), "noise").astype(jnp.float32)
    return summed / (samples_dev * lax.axis_size("noise"))


def permuted(value, pairs):
    return lax.ppermute(value, ("sa", "sb", "noise"), pairs)


def routes(n_sa, route):
    flat = lambda z, y, x, c: ((z * 2 + y) * 2 + x) * 2 + c
    pairs = []
    for z in range(n_sa):
        for y in range(2):
            for x in range(2):
                for c in range(2):
                    target = route(z, y, x, c)
                    if target is not None and 0 <= target[0] < n_sa:
                        pairs.append((flat(z, y, x, c), flat(*target)))
    return pairs


def position():
    b = lax.axis_index("sb")
    return lax.axis_index("sa"), b // 2, lax.rem(b, 2), lax.axis_index("noise")


def half_index():
    return lax.rem(lax.axis_index("noise") + lax.axis_index("sa"), 2)


def pack_kernel(conv, mix, qkv, out, early, late, taps, rows_qkv, sems):
    z, y, x, n = position()
    b = 2 * y + x
    part = b * 2 + n
    rows = pl.ds(pl.multiple_of(part * 48, 16), 48)
    half = pl.ds(pl.multiple_of(n * 48, 16), 48)
    columns = pl.ds(pl.multiple_of(b * 384, 128), 384)
    pairs = (
        (conv.at[:, rows, :], taps), (mix.at[half, columns], early.at[pl.ds(144, 48), :]),
        (qkv.at[rows, :], rows_qkv), (out.at[half, columns], late.at[pl.ds(0, 48), :]),
    )
    copies = [pltpu.make_async_copy(source, target, sems.at[i]) for i, (source, target) in enumerate(pairs)]
    for copy in copies:
        copy.start()
    for copy in copies:
        copy.wait()
    for t in range(3):
        early[pl.ds(48 * t, 48), :] = taps[t]
    for k in range(2):
        late[pl.ds(48 + 48 * k, 48), :] = rows_qkv[:, pl.ds(384 * k, 384)]
    for k in range(3):
        late[pl.ds(144, 16), pl.ds(128 * k, 128)] = rows_qkv[pl.ds(16 * k, 16), pl.ds(768, 128)]


def nt(a, b):
    return lax.dot_general(a, b, (((1,), (1,)), ((), ())), preferred_element_type=jnp.float32)


def tn(a, b):
    return lax.dot_general(a, b, (((0,), (0,)), ((), ())), preferred_element_type=jnp.float32)


def nn(a, b):
    return jnp.dot(a, b, preferred_element_type=jnp.float32)


CHUNK = 384


def chunk(c):
    return pl.ds(pl.multiple_of(c * CHUNK, 128), CHUNK)


def arrived(z, y, x, n, same, other):
    for j in range(3):
        for core, (straight, beside, across, diagonal_a, diagonal_b) in enumerate((same, other)):
            half = diagonal_a.shape[1]
            for dy in range(2):
                for dx in range(2):
                    if dy and dx:
                        first, second = diagonal_a[j], diagonal_b[j]
                    else:
                        whole = across if dy else beside if dx else straight
                        first, second = whole[j, pl.ds(0, half), :], whole[j, pl.ds(half, half), :]
                    yield j, z ^ (j + 1), y ^ dy, x ^ dx, n ^ core, first, second


def times(value, factor, unit):
    return pl.multiple_of(value * factor, unit)


def forward_kernel(
    blocks_even, blocks_odd, edge, other_even, other_odd, other_edge, *refs,
):
    own_conv, own_mix = refs[:2]
    same, other = refs[2:7], refs[7:12]
    (
        gain, normed_out, resid_out, inv_out, hidden_out, conv_out, mix_out,
        conv, mix, noisy, gelu_in, sems,
    ) = refs[12:]
    z, y, x, n = position()

    for t in range(3):
        conv[t, pl.ds(times(z, 384, 128), 384), :] = own_conv[t]
    mix[pl.ds(times(z, 96, 32), 96), :] = own_mix[...]
    for _, sz, sy, sx, sn, first, second in arrived(z, y, x, n, same, other):
        b = 2 * sy + sx
        rows = pl.ds(pl.multiple_of(sz * 384 + (b * 2 + sn) * 48, 16), 48)
        conv[0, rows, :] = first[:48]
        conv[1, rows, :] = first[48:]
        conv[2, rows, :] = second[:48]
        mix[pl.ds(pl.multiple_of(sz * 96 + sn * 48, 16), 48), pl.ds(times(b, 384, 128), 384)] = second[48:]
    copies = [
        pltpu.make_async_copy(s, d, sems.at[i]) for i, (s, d) in enumerate(((conv, conv_out), (mix, mix_out)))
    ]
    for copy in copies:
        copy.start()

    m = half_index()
    for half, (even, odd, outer) in (
        (m, (blocks_even, blocks_odd, edge)), (1 - m, (other_even, other_odd, other_edge))
    ):
        noisy[pl.ds(times(half, 176, 16), 48), :] = outer[...].astype(jnp.float32)
        for shift, block in enumerate((even, odd)):
            row = 48 + 64 * half + 32 * lax.rem(x + shift, 2)
            noisy[pl.ds(pl.multiple_of(row, 16), 32), :] = block[...].astype(jnp.float32)

    def activate(c, _):
        gelu_in[:, chunk(c)] = gelu_tanh(noisy[:, chunk(c)]).astype(jnp.bfloat16)
        return 0

    lax.fori_loop(0, 4, activate, 0)

    def convolve(c, total):
        for t in range(3):
            total = total + nn(gelu_in[pl.ds(16 * t, 192), chunk(c)], conv[t, chunk(c), :])
        return total

    hidden = lax.fori_loop(0, 4, convolve, jnp.zeros((192, HID), jnp.float32))
    hidden_out[...] = hidden[32:160]
    act = gelu_tanh(hidden).astype(jnp.bfloat16)

    def mixing(c, squares):
        resid = noisy[pl.ds(16, 192), chunk(c)] + nn(act, mix[:, chunk(c)])
        noisy[pl.ds(16, 192), chunk(c)] = resid
        resid_out[:, chunk(c)] = resid[32:160]
        return squares + jnp.sum(resid * resid, axis=1, keepdims=True)

    squares = lax.fori_loop(0, 4, mixing, jnp.zeros((192, 1), jnp.float32))
    inv_rms = lax.rsqrt(squares * (1.0 / 1536) + 1e-06)
    inv_out[...] = inv_rms[32:160]

    def normalise(c, _):
        normed = noisy[pl.ds(16, 192), chunk(c)] * inv_rms * gain[:, chunk(c)]
        normed_out[:, chunk(c)] = normed.astype(jnp.bfloat16)
        return 0

    lax.fori_loop(0, 4, normalise, 0)
    for copy in copies:
        copy.wait()


def attention_kernel(band, flag, normed, cot_block, cot_beside, other_block, other_beside, *refs):
    own_qkv, own_out = refs[:2]
    same, other = refs[2:7], refs[7:12]
    d_q_out, d_kv_out, send, qkv_out, cot_out, qkv, out, sems = refs[12:]
    z, y, x, n = position()
    length = lax.axis_size("sa") * 128
    first_bin = z * 128
    own_rows = pl.ds(times(z, 384, 128), 384)
    qkv[own_rows, :] = own_qkv[...]
    out[pl.ds(times(z, 96, 32), 96), :] = own_out[...]
    proj = nn(normed[:, own_rows], own_qkv[...])
    done = 0
    for j, sz, sy, sx, sn, first, second in arrived(z, y, x, n, same, other):
        b = 2 * sy + sx
        row = sz * 384 + (b * 2 + sn) * 48
        out[pl.ds(pl.multiple_of(sz * 96 + sn * 48, 16), 48), pl.ds(times(b, 384, 128), 384)] = first[:48]
        qkv[pl.ds(pl.multiple_of(row, 16), 32), pl.ds(0, 384)] = first[48:]
        qkv[pl.ds(pl.multiple_of(row + 32, 16), 16), pl.ds(0, 384)] = second[:16]
        qkv[pl.ds(pl.multiple_of(row, 16), 48), pl.ds(384, 384)] = second[16:64]
        for k in range(3):
            third = pl.ds(pl.multiple_of(row + 16 * k, 16), 16)
            qkv[third, pl.ds(768, 128)] = second[64:, 128 * k : 128 * k + 128]
        done += 1
        if done % 8 == 0:
            rows = pl.ds(times(sz, 384, 128), 384)
            proj = proj + nn(normed[:, rows], qkv[rows, :])
    proj = proj.astype(jnp.bfloat16)
    copy = pltpu.make_async_copy(qkv, qkv_out, sems.at[0])
    copy.start()
    m = half_index()
    for half, (block, beside) in ((m, (cot_block, cot_beside)), (1 - m, (other_block, other_beside))):
        for shift, rows in enumerate((block, beside)):
            row = 64 * half + 32 * lax.rem(x + shift, 2)
            cot_out[pl.ds(pl.multiple_of(row, 32), 32), :] = rows[...]
    d_att = nt(cot_out[...], out[...]).astype(jnp.bfloat16)

    row = lax.broadcasted_iota(jnp.int32, (128, 192), 0)
    column = lax.broadcasted_iota(jnp.int32, (128, 192), 1) - 32
    inside = (column + first_bin >= 0) & (column + first_bin < length)
    paired = (column >= 0) & (column < 128) & (flag[0] > 0)
    apart = jnp.abs(row - column)
    scale = KEY ** (-0.5)
    d_queries, d_keys, d_values = [], [], []
    for h in range(HEADS):
        q = proj[32:160, KEY * h : KEY * (h + 1)]
        k = proj[:, HEADS * KEY + KEY * h : HEADS * KEY + KEY * (h + 1)]
        v = proj[:, 2 * HEADS * KEY + VAL * h : 2 * HEADS * KEY + VAL * (h + 1)]
        d_att_h = d_att[:, VAL * h : VAL * (h + 1)]
        allowed = inside & (paired | (apart <= band[h]))
        score = jnp.where(allowed, nt(q, k) * scale, -1e30)
        top = jnp.max(score, axis=1, keepdims=True)
        raised = jnp.where(allowed, jnp.exp(score - top), 0.0)
        prob = raised / jnp.sum(raised, axis=1, keepdims=True)
        prob_b = prob.astype(jnp.bfloat16)
        attn = nn(prob_b, v)
        delta = jnp.sum(d_att_h.astype(jnp.float32) * attn, axis=1, keepdims=True)
        d_score = (prob * (nt(d_att_h, v) - delta) * scale).astype(jnp.bfloat16)
        d_queries.append(nn(d_score, k))
        d_keys.append(tn(d_score, q))
        d_values.append(tn(prob_b, d_att_h))
    d_q_out[...] = jnp.concatenate(d_queries, axis=1)
    d_kv = jnp.concatenate(d_keys + d_values, axis=1)
    d_kv_out[...] = d_kv[32:160]
    send[...] = jnp.where(m == 0, d_kv[:32], d_kv[160:]).astype(jnp.bfloat16)
    copy.wait()


def norm_kernel(
    d_q, d_kv, received, resid, inv_rms_ref, hidden, cot, gain, mix, qkv,
    d_hidden_out, d_resid_out, send, total_kv, gained, d_resid_all,
):
    n = half_index()
    total_kv[...] = d_kv[...]
    edge = pl.ds(pl.multiple_of(n * 96, 32), 32)
    total_kv[edge, :] = total_kv[edge, :] + received[...].astype(jnp.float32)
    d_proj = jnp.concatenate([d_q[...], total_kv[...]], axis=1).astype(jnp.bfloat16)
    inv_rms = inv_rms_ref[...]

    def back(c, mean):
        part = gain[:, chunk(c)] * nt(d_proj, qkv[chunk(c), :])
        gained[:, chunk(c)] = part
        return mean + jnp.sum(resid[:, chunk(c)] * part, axis=1, keepdims=True)

    mean = lax.fori_loop(0, 4, back, jnp.zeros((128, 1), jnp.float32)) * (1.0 / 1536)
    cubed = inv_rms * inv_rms * inv_rms * mean

    def residual(c, total):
        d_resid = (
            cot[:, chunk(c)].astype(jnp.float32)
            + inv_rms * gained[:, chunk(c)]
            - resid[:, chunk(c)] * cubed
        )
        d_resid_all[:, chunk(c)] = d_resid
        return total + nt(d_resid.astype(jnp.bfloat16), mix[:, chunk(c)])

    d_act = lax.fori_loop(0, 4, residual, jnp.zeros((128, HID), jnp.float32))
    d_hidden = (d_act * gelu_slope(hidden[...])).astype(jnp.bfloat16)
    d_hidden_out[...] = d_hidden
    d_resid_out[...] = d_resid_all[pl.ds(pl.multiple_of(n * 64, 64), 64), :]

    @pl.when(n == 0)
    def _():
        send[...] = d_hidden[:16]

    @pl.when(n == 1)
    def _():
        send[...] = d_hidden[112:]


def taps_kernel(d_hidden, received, d_resid, blocks_even, blocks_odd, conv, keep, send, extended_ref, noisy, grads):
    x, n = lax.rem(lax.axis_index("sb"), 2), half_index()

    @pl.when(n == 0)
    def _():
        extended_ref[pl.ds(0, 16), :] = received[...]
        extended_ref[pl.ds(16, 80), :] = d_hidden[pl.ds(0, 80), :]

    @pl.when(n == 1)
    def _():
        extended_ref[pl.ds(0, 80), :] = d_hidden[pl.ds(48, 80), :]
        extended_ref[pl.ds(80, 16), :] = received[...]

    for shift, block in enumerate((blocks_even, blocks_odd)):
        noisy[pl.ds(times(lax.rem(x + shift, 2), 32, 32), 32), :] = block[...].astype(jnp.float32)

    def taps(c, _):
        total = nt(extended_ref[pl.ds(32, 64), :], conv[0, chunk(c), :])
        total = total + nt(extended_ref[pl.ds(16, 64), :], conv[1, chunk(c), :])
        total = total + nt(extended_ref[pl.ds(0, 64), :], conv[2, chunk(c), :])
        grads[:, chunk(c)] = d_resid[:, chunk(c)] + total * gelu_slope(noisy[:, chunk(c)])
        return 0

    lax.fori_loop(0, 4, taps, 0)
    keep[...] = grads[pl.ds(pl.multiple_of(32 * x, 32), 32), :]
    send[...] = grads[pl.ds(pl.multiple_of(32 - 32 * x, 32), 32), :].astype(jnp.bfloat16)


def vmem(count):
    return [pl.BlockSpec(memory_space=pltpu.VMEM)] * count


def smem(count):
    return [pl.BlockSpec(memory_space=pltpu.SMEM)] * count


def hbm(count):
    return [pl.BlockSpec(memory_space=pl.ANY)] * count


def limit(mebibytes):
    return pltpu.CompilerParams(vmem_limit_bytes=mebibytes * 1024 * 1024)


f32, bf16 = (jnp.float32, jnp.bfloat16)


def shaped(*shape, dtype=jnp.float32):
    return jax.ShapeDtypeStruct(shape, dtype)


def stretch_shards(
    base, noise, cot, convolution_weight, mix_w, norm_gain, qkv_w, out_w, band_width, pairs
):
    n_sa = lax.axis_size("sa")
    b = lax.axis_index("sb")
    m = half_index()
    y, x = (b >> 1, b & 1)
    features = base.shape[1]

    early, late = pl.pallas_call(
        pack_kernel,
        out_shape=(shaped(192, CHUNK, dtype=bf16), shaped(160, CHUNK, dtype=bf16)),
        in_specs=[pl.BlockSpec(memory_space=pltpu.HBM)] * 4,
        out_specs=tuple(vmem(2)),
        scratch_shapes=[
            pltpu.VMEM((3, 48, HID), bf16), pltpu.VMEM((48, 896), bf16), pltpu.SemaphoreType.DMA((4,))
        ],
        compiler_params=limit(60),
    )(convolution_weight, mix_w, qkv_w, out_w)
    def along_z(step):
        return routes(n_sa, lambda z, y, x, c: (z ^ step, y, x, c))

    x_route = routes(n_sa, lambda z, y, x, c: (z, y, 1 - x, c))
    y_route = routes(n_sa, lambda z, y, x, c: (z, 1 - y, x, c))
    core_route = routes(n_sa, lambda z, y, x, c: (z, y, x, 1 - c))

    def over_z(piece):
        return [permuted(piece, along_z(step)) for step in range(1, 4)]

    def diagonals(beside, across):
        half = beside.shape[1] // 2
        return permuted(beside[:, :half], y_route), permuted(across[:, half:], x_route)

    def swapped(parts):
        return tuple(permuted(part, core_route) for part in parts)

    def after(values, *earlier):
        count = len(values)
        return lax.optimization_barrier((*values, *earlier))[:count]

    def to_sample(shift):
        return routes(n_sa, lambda z, y, x, c: (z, c, (x + shift) % 2, y ^ (z & 1)))

    noisy = (base.astype(f32)[None] + noise.astype(f32)).astype(bf16)
    even = x == 0
    edge_route = routes(
        n_sa, lambda z, y, x, c: (z - 1, y, x, c) if c ^ (z & 1) == 0 else (z + 1, y, x, c)
    )
    z = lax.axis_index("sa")
    flag = jnp.any((pairs[:, 0] == z) & (pairs[:, 1] == z)).astype(jnp.int32).reshape(1)
    straight = over_z(early)
    noisy, cot = after((noisy, cot), *straight[:1])
    blocks = [
        permuted(jnp.where(x == shift, noisy[0], noisy[1]), to_sample(shift)) for shift in range(2)
    ]
    across_cot = permuted(
        cot, routes(n_sa, lambda z, y, x, c: (z, 1 - y, x, c) if y == c ^ (z & 1) else None)
    )
    low, high = jnp.where(even, blocks[0], blocks[1]), jnp.where(even, blocks[1], blocks[0])
    outer = jnp.concatenate(
        [jnp.where(m == 0, low[:16], low[16:]), jnp.where(m == 0, low[16:], high[:16]), jnp.where(m == 0, high[:16], high[16:])]
    )
    cot_block = jnp.where(y == m, cot, across_cot)
    straight = jnp.stack(straight)
    straight, late, flag, outer, cot_block = after((straight, late, flag, outer, cot_block))
    beside, across = permuted(straight, x_route), permuted(straight, y_route)
    late_straight = jnp.stack(over_z(late))
    edge = permuted(outer, edge_route)
    straight, beside, across, late_straight, edge, cot_block, *blocks = after(
        (straight, beside, across, late_straight, edge, cot_block, *blocks)
    )
    early = (straight, beside, across) + diagonals(beside, across)
    late_beside, late_across = permuted(late_straight, x_route), permuted(late_straight, y_route)
    moved = swapped((straight, *blocks))
    early, late, cot_block, mine, moved = (
        lambda v: (v[:5], v[5:8], v[8], v[9:12], v[12:])
    )(after((*early, late_straight, late_beside, late_across, cot_block, *blocks, edge, *moved)))
    late = tuple(late) + diagonals(late[1], late[2])
    noisy_rows = tuple(mine) + tuple(moved[1:]) + swapped(mine[2:])
    early = tuple(early) + tuple(moved[:1]) + swapped(early[1:])
    cot_rows = (cot_block, permuted(cot_block, x_route))
    cot_rows = cot_rows + swapped(cot_rows)
    late_other = swapped(late[:3])
    gain = norm_gain.reshape(1, features)

    normed, resid, inv_rms, hidden, conv, mix = pl.pallas_call(
        forward_kernel,
        out_shape=(
            shaped(192, features, dtype=bf16), shaped(128, features), shaped(128, 1), shaped(128, HID),
            shaped(3, features, HID, dtype=bf16), shaped(HID, features, dtype=bf16),
        ),
        in_specs=vmem(19),
        out_specs=tuple(vmem(4) + hbm(2)),
        scratch_shapes=[
            pltpu.VMEM((3, features, HID), bf16), pltpu.VMEM((HID, features), bf16),
            pltpu.VMEM((224, features), f32), pltpu.VMEM((224, features), bf16),
            pltpu.SemaphoreType.DMA((2,)),
        ],
        compiler_params=limit(18),
    )(*noisy_rows, convolution_weight, mix_w, *early, gain)
    late += late_other + swapped(late[3:])
    d_q, d_kv, send, qkv, cot_all = pl.pallas_call(
        attention_kernel,
        out_shape=(
            shaped(128, 256), shaped(128, 640), shaped(32, 640, dtype=bf16), shaped(features, 896, dtype=bf16),
            shaped(128, features, dtype=bf16),
        ),
        in_specs=smem(2) + vmem(17),
        out_specs=tuple(vmem(3) + hbm(1) + vmem(1)),
        scratch_shapes=[
            pltpu.VMEM((features, 896), bf16), pltpu.VMEM((HEADS * VAL, features), bf16),
            pltpu.SemaphoreType.DMA((1,)),
        ],
        compiler_params=limit(14),
    )(band_width, flag, normed, *cot_rows, qkv_w, out_w, *late)

    received = permuted(send, edge_route)
    d_hidden, d_resid, send = pl.pallas_call(
        norm_kernel,
        out_shape=(shaped(128, HID, dtype=bf16), shaped(64, features), shaped(16, HID, dtype=bf16)),
        in_specs=vmem(10),
        out_specs=tuple(vmem(3)),
        scratch_shapes=[
            pltpu.VMEM((128, 640), f32), pltpu.VMEM((128, features), f32), pltpu.VMEM((128, features), f32),
        ],
        compiler_params=limit(12),
    )(d_q, d_kv, received, resid, inv_rms, hidden, cot_all, gain, mix, qkv)

    received = permuted(send, edge_route)
    keep, send = pl.pallas_call(
        taps_kernel,
        out_shape=(shaped(32, features), shaped(32, features, dtype=bf16)),
        in_specs=vmem(6),
        out_specs=tuple(vmem(2)),
        scratch_shapes=[
            pltpu.VMEM((96, HID), bf16), pltpu.VMEM((64, features), f32), pltpu.VMEM((64, features), f32),
        ],
        compiler_params=limit(6),
    )(d_hidden, received, d_resid, *blocks, conv)

    received = permuted(send, x_route)
    partial = (keep + received.astype(f32)).astype(bf16)
    first_sum = permuted(
        partial, routes(n_sa, lambda z, y, x, c: (z, 1 - y, x, c) if y != c ^ (z & 1) else (z, y, x, 1 - c))
    )
    second_sum = permuted(partial, routes(n_sa, lambda z, y, x, c: (z, 1 - y, x, 1 - c) if y != c ^ (z & 1) else None))
    other = jnp.where(y == m, partial, second_sum)
    return (first_sum.astype(f32) + other.astype(f32)) * 0.25


def solution(mesh):
    fits = mesh.shape["sb"] == 4 and mesh.shape["noise"] == 2 and HEADS == 4

    def body(*arrays):
        if fits and arrays[0].shape[0] == 32 and arrays[1].shape[0] == 2 and TILE == 128:
            if arrays[0].shape[1] == 1536 and mesh.shape["sa"] == 4:
                return stretch_shards(*arrays)
        return shards(*arrays)

    return jax.shard_map(
        body,
        mesh=mesh,
        in_specs=(
            P(("sa", "sb"), None),
            P("noise", ("sa", "sb"), None),
            P(("sa", "sb"), None),
            P(None, "sa", None),
            P("sa", None),
            P(),
            P("sa", None),
            P("sa", None),
            P(),
            P(),
        ),
        out_specs=P(("sa", "sb"), None),
        check_vma=False,
    )
```

```python
import jax
import jax.numpy as jnp
from jax import lax
from jax.experimental import pallas as pl
from jax.experimental.pallas import tpu as pltpu
from jax.sharding import PartitionSpec as P

HID = 384
HEADS = 4
KEY = 64
VAL = 96
DILATION_BINS = 16
BAND = 32
TILE = 128


ROOT_TWO_PI = 0.7978845608
CUBIC = 0.044715


def extended(value, sides, width):
    for axis, dim in sides:
        peers, length = (lax.axis_size(axis), value.shape[dim])
        up = [(i, (i + 1) % peers) for i in range(peers - 1)]
        down = [(j, i) for i, j in up]
        last = lax.slice_in_dim(value, length - width, length, axis=dim)
        leading = lax.slice_in_dim(value, 0, width, axis=dim)
        before = lax.ppermute(last, axis, up)
        after = lax.ppermute(leading, axis, down)
        value = jnp.concatenate([before, value, after], axis=dim)
    return value


def from_behind(block, axis, distance):
    devices = range(lax.axis_size(axis))
    route = [(i - distance, i) for i in devices if i - distance in devices]
    return lax.ppermute(block, axis, route)


def gelu_tanh(values):
    inner = ROOT_TWO_PI * (values + CUBIC * values * values * values)
    return 0.5 * values * (1.0 + jnp.tanh(inner))


def gelu_slope(values):
    tangent = jnp.tanh(ROOT_TWO_PI * (values + CUBIC * values * values * values))
    return 0.5 * (1.0 + tangent) + 0.5 * values * (1.0 - tangent * tangent) * ROOT_TWO_PI * (
        1.0 + 3.0 * CUBIC * values * values
    )


def shards(base, noise, cot, convolution_weight, mix_w, norm_gain, qkv_w, out_w, band_width, pairs):
    conv_full, mix_full, qkv_full, out_full = (
        lax.all_gather(convolution_weight, "sa", axis=1, tiled=True),
        lax.all_gather(mix_w, "sa", axis=0, tiled=True),
        lax.all_gather(qkv_w, "sa", axis=0, tiled=True),
        lax.all_gather(out_w, "sa", axis=0, tiled=True),
    )
    sequence_bins = base.shape[0]
    samples_dev = noise.shape[0]
    stretch = sequence_bins * lax.axis_size("sb")
    sequence_length = stretch * lax.axis_size("sa")
    heads_key = HEADS * KEY
    heads_val = HEADS * VAL
    width = sequence_bins + 2 * BAND
    scale = KEY ** (-0.5)
    stretch_first = lax.axis_index("sa") * stretch
    first_row = stretch_first + lax.axis_index("sb") * sequence_bins
    row_pos = first_row + jnp.arange(sequence_bins, dtype=jnp.int32)
    ext_pos = first_row - BAND + jnp.arange(width, dtype=jnp.int32)
    stretch_pos = stretch_first + jnp.arange(stretch, dtype=jnp.int32)
    tiles = sequence_length // TILE
    tile_ids = jnp.arange(tiles, dtype=jnp.int32)
    pick_query = (pairs[:, 0][:, None] == tile_ids[None, :]).astype(jnp.float32)
    pick_key = (pairs[:, 1][:, None] == tile_ids[None, :]).astype(jnp.float32)
    table = jnp.dot(pick_query.T, pick_key)
    own_select = ((row_pos // TILE)[:, None] == tile_ids[None, :]).astype(jnp.float32)
    stretch_select = ((stretch_pos // TILE)[:, None] == tile_ids[None, :]).astype(jnp.float32)
    pair_own_rows = jnp.dot(jnp.dot(own_select, table), stretch_select.T) > 0.5
    pair_own_keys = jnp.dot(jnp.dot(stretch_select, table), own_select.T) > 0.5
    inside = (ext_pos >= 0) & (ext_pos < sequence_length)
    band_mask = inside[None, None, :] & (
        jnp.abs(row_pos[:, None] - ext_pos[None, :])[None] <= band_width[:, None, None]
    )
    far_rows = jnp.abs(row_pos[:, None] - stretch_pos[None, :])[None] > band_width[:, None, None]
    pair_mask = pair_own_rows[None] & far_rows
    key_mask = pair_own_keys[None] & jnp.transpose(far_rows, (0, 2, 1))
    noisy = base.astype(jnp.float32)[None] + noise.astype(jnp.float32)
    gelu_input = gelu_tanh(noisy).astype(jnp.bfloat16)
    gelu_extended = extended(gelu_input, ((("sa", "sb"), 1),), DILATION_BINS)
    hidden_state = jnp.zeros((samples_dev, sequence_bins, HID), jnp.float32)
    for tap_index in range(3):
        hidden_state = hidden_state + jnp.einsum(
            "nbd,dc->nbc",
            gelu_extended[:, tap_index * DILATION_BINS : tap_index * DILATION_BINS + sequence_bins],
            conv_full[tap_index],
            preferred_element_type=jnp.float32,
        )
    act = gelu_tanh(hidden_state).astype(jnp.bfloat16)
    resid = noisy + jnp.einsum("nbc,cd->nbd", act, mix_full, preferred_element_type=jnp.float32)
    inv_rms = lax.rsqrt(jnp.mean(resid * resid, axis=-1, keepdims=True) + 1e-06)
    normed = (resid * inv_rms * norm_gain).astype(jnp.bfloat16)
    proj = jnp.einsum("nbd,dc->nbc", normed, qkv_full, preferred_element_type=jnp.float32).astype(
        jnp.bfloat16
    )
    queries = proj[..., :heads_key].reshape(samples_dev, sequence_bins, HEADS, KEY)
    key_vals = proj[..., heads_key:]
    kv_ext = extended(key_vals, ((("sa", "sb"), 1),), BAND)
    kv_all = lax.all_gather(key_vals, "sb", axis=1, tiled=True)
    keys_ext = kv_ext[..., :heads_key].reshape(samples_dev, width, HEADS, KEY)
    vals_ext = kv_ext[..., heads_key:].reshape(samples_dev, width, HEADS, VAL)
    keys_all = kv_all[..., :heads_key].reshape(samples_dev, stretch, HEADS, KEY)
    vals_all = kv_all[..., heads_key:].reshape(samples_dev, stretch, HEADS, VAL)
    score_band = (
        jnp.einsum("nihd,njhd->nhij", queries, keys_ext, preferred_element_type=jnp.float32) * scale
    )
    score_band = jnp.where(band_mask[None], score_band, -1e30)
    raw_pair = jnp.einsum("nihd,njhd->nhij", queries, keys_all, preferred_element_type=jnp.float32)
    score_pair = jnp.where(pair_mask[None], raw_pair * scale, -1e30)
    top = jnp.maximum(jnp.max(score_band, axis=-1), jnp.max(score_pair, axis=-1))
    total = jnp.sum(jnp.where(band_mask[None], jnp.exp(score_band - top[..., None]), 0.0), axis=-1)
    total = total + jnp.sum(
        jnp.where(pair_mask[None], jnp.exp(score_pair - top[..., None]), 0.0), axis=-1
    )
    lse = top + jnp.log(total)
    prob_band = jnp.where(band_mask[None], jnp.exp(score_band - lse[..., None]), 0.0)
    prob_pair = jnp.where(pair_mask[None], jnp.exp(score_pair - lse[..., None]), 0.0)
    band_b = prob_band.astype(jnp.bfloat16)
    pair_b = prob_pair.astype(jnp.bfloat16)
    attn = jnp.einsum("nhij,njhe->nihe", band_b, vals_ext, preferred_element_type=jnp.float32)
    attn = attn + jnp.einsum(
        "nhij,njhe->nihe", pair_b, vals_all, preferred_element_type=jnp.float32
    )
    d_att = jnp.dot(cot, out_full.T, preferred_element_type=jnp.float32).astype(jnp.bfloat16)
    d_att_heads = d_att.reshape(sequence_bins, HEADS, VAL)
    delta = jnp.transpose(jnp.sum(d_att_heads.astype(jnp.float32)[None] * attn, axis=-1), (0, 2, 1))
    d_prob_band = jnp.einsum(
        "ihe,njhe->nhij", d_att_heads, vals_ext, preferred_element_type=jnp.float32
    )
    d_prob_pair = jnp.einsum(
        "ihe,njhe->nhij", d_att_heads, vals_all, preferred_element_type=jnp.float32
    )
    d_score_band = (prob_band * (d_prob_band - delta[..., None]) * scale).astype(jnp.bfloat16)
    d_score_pair = (prob_pair * (d_prob_pair - delta[..., None]) * scale).astype(jnp.bfloat16)
    d_query = jnp.einsum(
        "nhij,njhd->nihd", d_score_band, keys_ext, preferred_element_type=jnp.float32
    )
    d_query = d_query + jnp.einsum(
        "nhij,njhd->nihd", d_score_pair, keys_all, preferred_element_type=jnp.float32
    )
    d_key_ext = jnp.einsum(
        "nhij,nihd->njhd", d_score_band, queries, preferred_element_type=jnp.float32
    )
    d_val_ext = jnp.einsum(
        "nhij,ihe->njhe", band_b, d_att_heads, preferred_element_type=jnp.float32
    )
    d_kv_ext = jnp.concatenate(
        [
            d_key_ext.reshape(samples_dev, width, heads_key),
            d_val_ext.reshape(samples_dev, width, heads_val),
        ],
        axis=2,
    )
    from_right = from_behind(d_kv_ext[:, :BAND].astype(jnp.bfloat16), ("sa", "sb"), -1).astype(
        jnp.float32
    )
    from_left = from_behind(
        d_kv_ext[:, BAND + sequence_bins :].astype(jnp.bfloat16), ("sa", "sb"), 1
    ).astype(jnp.float32)
    d_key_vals = d_kv_ext[:, BAND : BAND + sequence_bins]
    d_key_vals = d_key_vals + from_left
    d_key_vals = d_key_vals + from_right
    statistics = jnp.stack([lse, delta], axis=1)
    query_rows = proj[..., :heads_key]
    queries_all, d_att_all = (
        lax.all_gather(query_rows, "sb", axis=1, tiled=True),
        lax.all_gather(d_att, "sb", axis=0, tiled=True),
    )
    stats_all = lax.all_gather(statistics, "sb", axis=3, tiled=True)
    queries_all = queries_all.reshape(samples_dev, stretch, HEADS, KEY)
    d_att_all = d_att_all.reshape(stretch, HEADS, VAL)
    keys_own = key_vals[..., :heads_key].reshape(samples_dev, sequence_bins, HEADS, KEY)
    vals_own = key_vals[..., heads_key:].reshape(samples_dev, sequence_bins, HEADS, VAL)
    score_key = (
        jnp.einsum("nihd,njhd->nhij", queries_all, keys_own, preferred_element_type=jnp.float32)
        * scale
    )
    prob_key = jnp.where(key_mask[None], jnp.exp(score_key - stats_all[:, 0][..., None]), 0.0)
    d_val_pair = jnp.einsum(
        "nhij,ihe->njhe",
        prob_key.astype(jnp.bfloat16),
        d_att_all,
        preferred_element_type=jnp.float32,
    )
    d_prob_key = jnp.einsum(
        "ihe,njhe->nhij", d_att_all, vals_own, preferred_element_type=jnp.float32
    )
    d_score_key = (prob_key * (d_prob_key - stats_all[:, 1][..., None]) * scale).astype(
        jnp.bfloat16
    )
    d_key_pair = jnp.einsum(
        "nhij,nihd->njhd", d_score_key, queries_all, preferred_element_type=jnp.float32
    )
    d_key_vals = d_key_vals + jnp.concatenate(
        [
            d_key_pair.reshape(samples_dev, sequence_bins, heads_key),
            d_val_pair.reshape(samples_dev, sequence_bins, heads_val),
        ],
        axis=2,
    )
    d_proj = jnp.concatenate(
        [d_query.reshape(samples_dev, sequence_bins, heads_key), d_key_vals], axis=2
    ).astype(jnp.bfloat16)
    d_normed = jnp.einsum("nbc,dc->nbd", d_proj, qkv_full, preferred_element_type=jnp.float32)
    gained = norm_gain * d_normed
    d_resid = (
        cot.astype(jnp.float32)[None]
        + inv_rms * gained
        - resid * inv_rms * inv_rms * inv_rms * jnp.mean(resid * gained, axis=-1, keepdims=True)
    )
    d_act = jnp.einsum(
        "nbd,cd->nbc", d_resid.astype(jnp.bfloat16), mix_full, preferred_element_type=jnp.float32
    )
    hidden_gradient = (d_act * gelu_slope(hidden_state)).astype(jnp.bfloat16)
    gradient_extended = extended(hidden_gradient, ((("sa", "sb"), 1),), DILATION_BINS)
    d_gelu_in = jnp.zeros((samples_dev, sequence_bins, base.shape[1]), jnp.float32)
    for tap_index in range(3):
        start_offset = (2 - tap_index) * DILATION_BINS
        d_gelu_in = d_gelu_in + jnp.einsum(
            "nbc,dc->nbd",
            gradient_extended[:, start_offset : start_offset + sequence_bins],
            conv_full[tap_index],
            preferred_element_type=jnp.float32,
        )
    grads = d_resid + d_gelu_in * gelu_slope(noisy)
    summed = lax.psum(jnp.sum(grads, axis=0).astype(jnp.bfloat16), "noise").astype(jnp.float32)
    return summed / (samples_dev * lax.axis_size("noise"))


def permuted(value, pairs):
    return lax.ppermute(value, ("sa", "sb", "noise"), pairs)


def routes(n_sa, route):
    flat = lambda z, y, x, c: ((z * 2 + y) * 2 + x) * 2 + c
    pairs = []
    for z in range(n_sa):
        for y in range(2):
            for x in range(2):
                for c in range(2):
                    target = route(z, y, x, c)
                    if target is not None and 0 <= target[0] < n_sa:
                        pairs.append((flat(z, y, x, c), flat(*target)))
    return pairs


def position():
    b = lax.axis_index("sb")
    return lax.axis_index("sa"), b // 2, lax.rem(b, 2), lax.axis_index("noise")


def half_index():
    return lax.rem(lax.axis_index("noise") + lax.axis_index("sa"), 2)


def pack_kernel(conv, mix, qkv, out, early, late, taps, rows_qkv, sems):
    z, y, x, n = position()
    b = 2 * y + x
    part = b * 2 + n
    rows = pl.ds(pl.multiple_of(part * 48, 16), 48)
    half = pl.ds(pl.multiple_of(n * 48, 16), 48)
    columns = pl.ds(pl.multiple_of(b * 384, 128), 384)
    pairs = (
        (conv.at[:, rows, :], taps), (mix.at[half, columns], early.at[pl.ds(144, 48), :]),
        (qkv.at[rows, :], rows_qkv), (out.at[half, columns], late.at[pl.ds(0, 48), :]),
    )
    copies = [pltpu.make_async_copy(source, target, sems.at[i]) for i, (source, target) in enumerate(pairs)]
    for copy in copies:
        copy.start()
    for copy in copies:
        copy.wait()
    for t in range(3):
        early[pl.ds(48 * t, 48), :] = taps[t]
    for k in range(2):
        late[pl.ds(48 + 48 * k, 48), :] = rows_qkv[:, pl.ds(384 * k, 384)]
    for k in range(3):
        late[pl.ds(144, 16), pl.ds(128 * k, 128)] = rows_qkv[pl.ds(16 * k, 16), pl.ds(768, 128)]


def nt(a, b):
    return lax.dot_general(a, b, (((1,), (1,)), ((), ())), preferred_element_type=jnp.float32)


def tn(a, b):
    return lax.dot_general(a, b, (((0,), (0,)), ((), ())), preferred_element_type=jnp.float32)


def nn(a, b):
    return jnp.dot(a, b, preferred_element_type=jnp.float32)


CHUNK = 384


def chunk(c):
    return pl.ds(pl.multiple_of(c * CHUNK, 128), CHUNK)


def arrived(z, y, x, n, same, other):
    for j in range(3):
        for core, (straight, beside, across, diagonal_a, diagonal_b) in enumerate((same, other)):
            half = diagonal_a.shape[1]
            for dy in range(2):
                for dx in range(2):
                    if dy and dx:
                        first, second = diagonal_a[j], diagonal_b[j]
                    else:
                        whole = across if dy else beside if dx else straight
                        first, second = whole[j, pl.ds(0, half), :], whole[j, pl.ds(half, half), :]
                    yield j, z ^ (j + 1), y ^ dy, x ^ dx, n ^ core, first, second


def times(value, factor, unit):
    return pl.multiple_of(value * factor, unit)


def forward_kernel(
    blocks_even, blocks_odd, edge, other_even, other_odd, other_edge, *refs,
):
    own_conv, own_mix = refs[:2]
    same, other = refs[2:7], refs[7:12]
    (
        gain, normed_out, resid_out, inv_out, hidden_out, conv_out, mix_out,
        conv, mix, noisy, gelu_in, sems,
    ) = refs[12:]
    z, y, x, n = position()

    for t in range(3):
        conv[t, pl.ds(times(z, 384, 128), 384), :] = own_conv[t]
    mix[pl.ds(times(z, 96, 32), 96), :] = own_mix[...]
    for _, sz, sy, sx, sn, first, second in arrived(z, y, x, n, same, other):
        b = 2 * sy + sx
        rows = pl.ds(pl.multiple_of(sz * 384 + (b * 2 + sn) * 48, 16), 48)
        conv[0, rows, :] = first[:48]
        conv[1, rows, :] = first[48:]
        conv[2, rows, :] = second[:48]
        mix[pl.ds(pl.multiple_of(sz * 96 + sn * 48, 16), 48), pl.ds(times(b, 384, 128), 384)] = second[48:]
    copies = [
        pltpu.make_async_copy(s, d, sems.at[i]) for i, (s, d) in enumerate(((conv, conv_out), (mix, mix_out)))
    ]
    for copy in copies:
        copy.start()

    m = half_index()
    for half, (even, odd, outer) in (
        (m, (blocks_even, blocks_odd, edge)), (1 - m, (other_even, other_odd, other_edge))
    ):
        noisy[pl.ds(times(half, 176, 16), 48), :] = outer[...].astype(jnp.float32)
        for shift, block in enumerate((even, odd)):
            row = 48 + 64 * half + 32 * lax.rem(x + shift, 2)
            noisy[pl.ds(pl.multiple_of(row, 16), 32), :] = block[...].astype(jnp.float32)

    def activate(c, _):
        gelu_in[:, chunk(c)] = gelu_tanh(noisy[:, chunk(c)]).astype(jnp.bfloat16)
        return 0

    lax.fori_loop(0, 4, activate, 0)

    def convolve(c, total):
        for t in range(3):
            total = total + nn(gelu_in[pl.ds(16 * t, 192), chunk(c)], conv[t, chunk(c), :])
        return total

    hidden = lax.fori_loop(0, 4, convolve, jnp.zeros((192, HID), jnp.float32))
    hidden_out[...] = hidden[32:160]
    act = gelu_tanh(hidden).astype(jnp.bfloat16)

    def mixing(c, squares):
        resid = noisy[pl.ds(16, 192), chunk(c)] + nn(act, mix[:, chunk(c)])
        noisy[pl.ds(16, 192), chunk(c)] = resid
        resid_out[:, chunk(c)] = resid[32:160]
        return squares + jnp.sum(resid * resid, axis=1, keepdims=True)

    squares = lax.fori_loop(0, 4, mixing, jnp.zeros((192, 1), jnp.float32))
    inv_rms = lax.rsqrt(squares * (1.0 / 1536) + 1e-06)
    inv_out[...] = inv_rms[32:160]

    def normalise(c, _):
        normed = noisy[pl.ds(16, 192), chunk(c)] * inv_rms * gain[:, chunk(c)]
        normed_out[:, chunk(c)] = normed.astype(jnp.bfloat16)
        return 0

    lax.fori_loop(0, 4, normalise, 0)
    for copy in copies:
        copy.wait()


def attention_kernel(band, flag, normed, cot_block, cot_beside, other_block, other_beside, *refs):
    own_qkv, own_out = refs[:2]
    same, other = refs[2:7], refs[7:12]
    d_q_out, d_kv_out, send, qkv_out, cot_out, qkv, out, sems = refs[12:]
    z, y, x, n = position()
    length = lax.axis_size("sa") * 128
    first_bin = z * 128
    own_rows = pl.ds(times(z, 384, 128), 384)
    qkv[own_rows, :] = own_qkv[...]
    out[pl.ds(times(z, 96, 32), 96), :] = own_out[...]
    proj = nn(normed[:, own_rows], own_qkv[...])
    done = 0
    for j, sz, sy, sx, sn, first, second in arrived(z, y, x, n, same, other):
        b = 2 * sy + sx
        row = sz * 384 + (b * 2 + sn) * 48
        out[pl.ds(pl.multiple_of(sz * 96 + sn * 48, 16), 48), pl.ds(times(b, 384, 128), 384)] = first[:48]
        qkv[pl.ds(pl.multiple_of(row, 16), 32), pl.ds(0, 384)] = first[48:]
        qkv[pl.ds(pl.multiple_of(row + 32, 16), 16), pl.ds(0, 384)] = second[:16]
        qkv[pl.ds(pl.multiple_of(row, 16), 48), pl.ds(384, 384)] = second[16:64]
        for k in range(3):
            third = pl.ds(pl.multiple_of(row + 16 * k, 16), 16)
            qkv[third, pl.ds(768, 128)] = second[64:, 128 * k : 128 * k + 128]
        done += 1
        if done % 8 == 0:
            rows = pl.ds(times(sz, 384, 128), 384)
            proj = proj + nn(normed[:, rows], qkv[rows, :])
    proj = proj.astype(jnp.bfloat16)
    copy = pltpu.make_async_copy(qkv, qkv_out, sems.at[0])
    copy.start()
    m = half_index()
    for half, (block, beside) in ((m, (cot_block, cot_beside)), (1 - m, (other_block, other_beside))):
        for shift, rows in enumerate((block, beside)):
            row = 64 * half + 32 * lax.rem(x + shift, 2)
            cot_out[pl.ds(pl.multiple_of(row, 32), 32), :] = rows[...]
    d_att = nt(cot_out[...], out[...]).astype(jnp.bfloat16)

    row = lax.broadcasted_iota(jnp.int32, (128, 192), 0)
    column = lax.broadcasted_iota(jnp.int32, (128, 192), 1) - 32
    inside = (column + first_bin >= 0) & (column + first_bin < length)
    paired = (column >= 0) & (column < 128) & (flag[0] > 0)
    apart = jnp.abs(row - column)
    scale = KEY ** (-0.5)
    d_queries, d_keys, d_values = [], [], []
    for h in range(HEADS):
        q = proj[32:160, KEY * h : KEY * (h + 1)]
        k = proj[:, HEADS * KEY + KEY * h : HEADS * KEY + KEY * (h + 1)]
        v = proj[:, 2 * HEADS * KEY + VAL * h : 2 * HEADS * KEY + VAL * (h + 1)]
        d_att_h = d_att[:, VAL * h : VAL * (h + 1)]
        allowed = inside & (paired | (apart <= band[h]))
        score = jnp.where(allowed, nt(q, k) * scale, -1e30)
        top = jnp.max(score, axis=1, keepdims=True)
        raised = jnp.where(allowed, jnp.exp(score - top), 0.0)
        prob = raised / jnp.sum(raised, axis=1, keepdims=True)
        prob_b = prob.astype(jnp.bfloat16)
        attn = nn(prob_b, v)
        delta = jnp.sum(d_att_h.astype(jnp.float32) * attn, axis=1, keepdims=True)
        d_score = (prob * (nt(d_att_h, v) - delta) * scale).astype(jnp.bfloat16)
        d_queries.append(nn(d_score, k))
        d_keys.append(tn(d_score, q))
        d_values.append(tn(prob_b, d_att_h))
    d_q_out[...] = jnp.concatenate(d_queries, axis=1)
    d_kv = jnp.concatenate(d_keys + d_values, axis=1)
    d_kv_out[...] = d_kv[32:160]
    send[...] = jnp.where(m == 0, d_kv[:32], d_kv[160:]).astype(jnp.bfloat16)
    copy.wait()


def norm_kernel(
    d_q, d_kv, received, resid, inv_rms_ref, hidden, cot, gain, mix, qkv,
    d_hidden_out, d_resid_out, send, total_kv, gained, d_resid_all,
):
    n = half_index()
    total_kv[...] = d_kv[...]
    edge = pl.ds(pl.multiple_of(n * 96, 32), 32)
    total_kv[edge, :] = total_kv[edge, :] + received[...].astype(jnp.float32)
    d_proj = jnp.concatenate([d_q[...], total_kv[...]], axis=1).astype(jnp.bfloat16)
    inv_rms = inv_rms_ref[...]

    def back(c, mean):
        part = gain[:, chunk(c)] * nt(d_proj, qkv[chunk(c), :])
        gained[:, chunk(c)] = part
        return mean + jnp.sum(resid[:, chunk(c)] * part, axis=1, keepdims=True)

    mean = lax.fori_loop(0, 4, back, jnp.zeros((128, 1), jnp.float32)) * (1.0 / 1536)
    cubed = inv_rms * inv_rms * inv_rms * mean

    def residual(c, total):
        d_resid = (
            cot[:, chunk(c)].astype(jnp.float32)
            + inv_rms * gained[:, chunk(c)]
            - resid[:, chunk(c)] * cubed
        )
        d_resid_all[:, chunk(c)] = d_resid
        return total + nt(d_resid.astype(jnp.bfloat16), mix[:, chunk(c)])

    d_act = lax.fori_loop(0, 4, residual, jnp.zeros((128, HID), jnp.float32))
    d_hidden = (d_act * gelu_slope(hidden[...])).astype(jnp.bfloat16)
    d_hidden_out[...] = d_hidden
    d_resid_out[...] = d_resid_all[pl.ds(pl.multiple_of(n * 64, 64), 64), :]

    @pl.when(n == 0)
    def _():
        send[...] = d_hidden[:16]

    @pl.when(n == 1)
    def _():
        send[...] = d_hidden[112:]


def taps_kernel(d_hidden, received, d_resid, blocks_even, blocks_odd, conv, keep, send, extended_ref, noisy, grads):
    x, n = lax.rem(lax.axis_index("sb"), 2), half_index()

    @pl.when(n == 0)
    def _():
        extended_ref[pl.ds(0, 16), :] = received[...]
        extended_ref[pl.ds(16, 80), :] = d_hidden[pl.ds(0, 80), :]

    @pl.when(n == 1)
    def _():
        extended_ref[pl.ds(0, 80), :] = d_hidden[pl.ds(48, 80), :]
        extended_ref[pl.ds(80, 16), :] = received[...]

    for shift, block in enumerate((blocks_even, blocks_odd)):
        noisy[pl.ds(times(lax.rem(x + shift, 2), 32, 32), 32), :] = block[...].astype(jnp.float32)

    def taps(c, _):
        total = nt(extended_ref[pl.ds(32, 64), :], conv[0, chunk(c), :])
        total = total + nt(extended_ref[pl.ds(16, 64), :], conv[1, chunk(c), :])
        total = total + nt(extended_ref[pl.ds(0, 64), :], conv[2, chunk(c), :])
        grads[:, chunk(c)] = d_resid[:, chunk(c)] + total * gelu_slope(noisy[:, chunk(c)])
        return 0

    lax.fori_loop(0, 4, taps, 0)
    keep[...] = grads[pl.ds(pl.multiple_of(32 * x, 32), 32), :]
    send[...] = grads[pl.ds(pl.multiple_of(32 - 32 * x, 32), 32), :].astype(jnp.bfloat16)


def vmem(count):
    return [pl.BlockSpec(memory_space=pltpu.VMEM)] * count


def smem(count):
    return [pl.BlockSpec(memory_space=pltpu.SMEM)] * count


def hbm(count):
    return [pl.BlockSpec(memory_space=pl.ANY)] * count


def limit(mebibytes):
    return pltpu.CompilerParams(vmem_limit_bytes=mebibytes * 1024 * 1024)


f32, bf16 = (jnp.float32, jnp.bfloat16)


def shaped(*shape, dtype=jnp.float32):
    return jax.ShapeDtypeStruct(shape, dtype)


def stretch_shards(
    base, noise, cot, convolution_weight, mix_w, norm_gain, qkv_w, out_w, band_width, pairs
):
    n_sa = lax.axis_size("sa")
    b = lax.axis_index("sb")
    m = half_index()
    y, x = (b >> 1, b & 1)
    features = base.shape[1]

    early, late = pl.pallas_call(
        pack_kernel,
        out_shape=(shaped(192, CHUNK, dtype=bf16), shaped(160, CHUNK, dtype=bf16)),
        in_specs=[pl.BlockSpec(memory_space=pltpu.HBM)] * 4,
        out_specs=tuple(vmem(2)),
        scratch_shapes=[
            pltpu.VMEM((3, 48, HID), bf16), pltpu.VMEM((48, 896), bf16), pltpu.SemaphoreType.DMA((4,))
        ],
        compiler_params=limit(60),
    )(convolution_weight, mix_w, qkv_w, out_w)
    def along_z(step):
        return routes(n_sa, lambda z, y, x, c: (z ^ step, y, x, c))

    x_route = routes(n_sa, lambda z, y, x, c: (z, y, 1 - x, c))
    y_route = routes(n_sa, lambda z, y, x, c: (z, 1 - y, x, c))
    core_route = routes(n_sa, lambda z, y, x, c: (z, y, x, 1 - c))

    def over_z(piece):
        return [permuted(piece, along_z(step)) for step in range(1, 4)]

    def diagonals(beside, across):
        half = beside.shape[1] // 2
        return permuted(beside[:, :half], y_route), permuted(across[:, half:], x_route)

    def swapped(parts):
        return tuple(permuted(part, core_route) for part in parts)

    def after(values, *earlier):
        count = len(values)
        return lax.optimization_barrier((*values, *earlier))[:count]

    def to_sample(shift):
        return routes(n_sa, lambda z, y, x, c: (z, c, (x + shift) % 2, y ^ (z & 1)))

    noisy = (base.astype(f32)[None] + noise.astype(f32)).astype(bf16)
    even = x == 0
    edge_route = routes(
        n_sa, lambda z, y, x, c: (z - 1, y, x, c) if c ^ (z & 1) == 0 else (z + 1, y, x, c)
    )
    z = lax.axis_index("sa")
    flag = jnp.any((pairs[:, 0] == z) & (pairs[:, 1] == z)).astype(jnp.int32).reshape(1)
    straight = over_z(early)
    noisy, cot = after((noisy, cot), *straight[:1])
    blocks = [
        permuted(jnp.where(x == shift, noisy[0], noisy[1]), to_sample(shift)) for shift in range(2)
    ]
    across_cot = permuted(
        cot, routes(n_sa, lambda z, y, x, c: (z, 1 - y, x, c) if y == c ^ (z & 1) else None)
    )
    low, high = jnp.where(even, blocks[0], blocks[1]), jnp.where(even, blocks[1], blocks[0])
    outer = jnp.concatenate(
        [jnp.where(m == 0, low[:16], low[16:]), jnp.where(m == 0, low[16:], high[:16]), jnp.where(m == 0, high[:16], high[16:])]
    )
    cot_block = jnp.where(y == m, cot, across_cot)
    straight = jnp.stack(straight)
    straight, late, flag, outer, cot_block = after((straight, late, flag, outer, cot_block))
    beside, across = permuted(straight, x_route), permuted(straight, y_route)
    late_straight = jnp.stack(over_z(late))
    edge = permuted(outer, edge_route)
    straight, beside, across, late_straight, edge, cot_block, *blocks = after(
        (straight, beside, across, late_straight, edge, cot_block, *blocks)
    )
    early = (straight, beside, across) + diagonals(beside, across)
    late_beside, late_across = permuted(late_straight, x_route), permuted(late_straight, y_route)
    cot_rows = (cot_block, permuted(cot_block, x_route))
    early, late, cot_rows, mine = (
        lambda v: (v[:5], v[5:8], v[8:10], v[10:])
    )(after((*early, late_straight, late_beside, late_across, *cot_rows, *blocks, edge)))
    late = tuple(late) + diagonals(late[1], late[2])
    noisy_rows = tuple(mine) + swapped(mine)
    early = tuple(early) + swapped(early)
    cot_rows = tuple(cot_rows) + swapped(cot_rows)
    late_other = swapped(late[:3])
    gain = norm_gain.reshape(1, features)

    normed, resid, inv_rms, hidden, conv, mix = pl.pallas_call(
        forward_kernel,
        out_shape=(
            shaped(192, features, dtype=bf16), shaped(128, features), shaped(128, 1), shaped(128, HID),
            shaped(3, features, HID, dtype=bf16), shaped(HID, features, dtype=bf16),
        ),
        in_specs=vmem(19),
        out_specs=tuple(vmem(4) + hbm(2)),
        scratch_shapes=[
            pltpu.VMEM((3, features, HID), bf16), pltpu.VMEM((HID, features), bf16),
            pltpu.VMEM((224, features), f32), pltpu.VMEM((224, features), bf16),
            pltpu.SemaphoreType.DMA((2,)),
        ],
        compiler_params=limit(18),
    )(*noisy_rows, convolution_weight, mix_w, *early, gain)
    late += late_other + swapped(late[3:])
    d_q, d_kv, send, qkv, cot_all = pl.pallas_call(
        attention_kernel,
        out_shape=(
            shaped(128, 256), shaped(128, 640), shaped(32, 640, dtype=bf16), shaped(features, 896, dtype=bf16),
            shaped(128, features, dtype=bf16),
        ),
        in_specs=smem(2) + vmem(17),
        out_specs=tuple(vmem(3) + hbm(1) + vmem(1)),
        scratch_shapes=[
            pltpu.VMEM((features, 896), bf16), pltpu.VMEM((HEADS * VAL, features), bf16),
            pltpu.SemaphoreType.DMA((1,)),
        ],
        compiler_params=limit(14),
    )(band_width, flag, normed, *cot_rows, qkv_w, out_w, *late)

    received = permuted(send, edge_route)
    d_hidden, d_resid, send = pl.pallas_call(
        norm_kernel,
        out_shape=(shaped(128, HID, dtype=bf16), shaped(64, features), shaped(16, HID, dtype=bf16)),
        in_specs=vmem(10),
        out_specs=tuple(vmem(3)),
        scratch_shapes=[
            pltpu.VMEM((128, 640), f32), pltpu.VMEM((128, features), f32), pltpu.VMEM((128, features), f32),
        ],
        compiler_params=limit(12),
    )(d_q, d_kv, received, resid, inv_rms, hidden, cot_all, gain, mix, qkv)

    received = permuted(send, edge_route)
    keep, send = pl.pallas_call(
        taps_kernel,
        out_shape=(shaped(32, features), shaped(32, features, dtype=bf16)),
        in_specs=vmem(6),
        out_specs=tuple(vmem(2)),
        scratch_shapes=[
            pltpu.VMEM((96, HID), bf16), pltpu.VMEM((64, features), f32), pltpu.VMEM((64, features), f32),
        ],
        compiler_params=limit(6),
    )(d_hidden, received, d_resid, *blocks, conv)

    received = permuted(send, x_route)
    partial = (keep + received.astype(f32)).astype(bf16)
    received = permuted(partial, y_route)
    total = (partial.astype(f32) + received.astype(f32)) * 0.25
    swapped_total = permuted(total, core_route)
    return jnp.where(y == m, total, swapped_total)


def solution(mesh):
    fits = mesh.shape["sb"] == 4 and mesh.shape["noise"] == 2 and HEADS == 4

    def body(*arrays):
        if fits and arrays[0].shape[0] == 32 and arrays[1].shape[0] == 2 and TILE == 128:
            if arrays[0].shape[1] == 1536 and mesh.shape["sa"] == 4:
                return stretch_shards(*arrays)
        return shards(*arrays)

    return jax.shard_map(
        body,
        mesh=mesh,
        in_specs=(
            P(("sa", "sb"), None),
            P("noise", ("sa", "sb"), None),
            P(("sa", "sb"), None),
            P(None, "sa", None),
            P("sa", None),
            P(),
            P("sa", None),
            P("sa", None),
            P(),
            P(),
        ),
        out_specs=P(("sa", "sb"), None),
        check_vma=False,
    )
```
